128 devices in a mesh: rep: 16 (over y, z_hi, core), shard: 8 (over x, z_lo).
Axes of the slice: x: 4, y: 4, z: 4 (z_hi: 2, z_lo: 2; z = z_hi * 2 + z_lo), core: 2. Of those that a mesh axis runs over, the one named last changes fastest.
Arguments:
- tokens: bfloat16 [16, 1536, 1280], P('rep', 'shard'), may hold values from -6 to 6
- lengths: int32 [16], P('rep'), may hold values from 1345 to 1500, as said below
- w_query: bfloat16 [1280, 1280], P('shard'), may hold values from -0.25 to 0.25
- w_key: bfloat16 [1280, 1280], P('shard'), may hold values from -0.25 to 0.25
- w_value: bfloat16 [1280, 1280], P('shard'), may hold values from -0.15625 to 0.15625
- w_out: bfloat16 [1280, 1280], P('shard'), may hold values from -0.625 to 0.625
- w_up: bfloat16 [1280, 5120], P('shard'), may hold values from -0.15625 to 0.15625
- w_down: bfloat16 [5120, 1280], P('shard'), may hold values from -0.078125 to 0.078125
- b_query: bfloat16 [1280], P('shard'), may hold values from -3 to 3
- b_value: bfloat16 [1280], P('shard'), may hold values from -3 to 3
- b_out: bfloat16 [1280], P('shard'), may hold values from -3 to 3
- b_up: bfloat16 [5120], P('shard'), may hold values from -3 to 3
- b_down: bfloat16 [1280], P('shard'), may hold values from -3 to 3
- gain_attn: bfloat16 [1280], P('shard'), may hold values from 0.25 to 1.75
- shift_attn: bfloat16 [1280], P('shard'), may hold values from -3 to 3
- gain_ffn: bfloat16 [1280], P('shard'), may hold values from 0.25 to 1.75
- shift_ffn: bfloat16 [1280], P('shard'), may hold values from -3 to 3
- cotangent: bfloat16 [16, 1536, 1280], P('rep', 'shard'), may hold values from -6 to 6
Outputs:
- output: bfloat16 [16, 1536, 1280], P('rep', 'shard')
- input_grad: float32 [16, 1536, 1280], P('rep', 'shard')
- grad_w_query: float32 [1280, 1280], P('shard')
- grad_w_key: float32 [1280, 1280], P('shard')
- grad_w_value: float32 [1280, 1280], P('shard')
- grad_w_out: float32 [1280, 1280], P('shard')
- grad_w_up: float32 [1280, 5120], P('shard')
- grad_w_down: float32 [5120, 1280], P('shard')
- grad_b_query: float32 [1280], P('shard')
- grad_b_value: float32 [1280], P('shard')
- grad_b_out: float32 [1280], P('shard')
- grad_b_up: float32 [5120], P('shard')
- grad_b_down: float32 [1280], P('shard')
- grad_gain_attn: float32 [1280], P('shard')
- grad_shift_attn: float32 [1280], P('shard')
- grad_gain_ffn: float32 [1280], P('shard')
- grad_shift_ffn: float32 [1280], P('shard')
The draws below stay inside these ranges and needn't reach their ends.
Inputs may be any that keep to these rules, and one draw needn't show every extreme that they name: tokens of each clip, slots from lengths[c] on are padding; the longest clip has exactly 1500 tokens, and every clip, being the only one on its index of rep, has 1345 tokens or more.
All inputs are finite; a program needn't handle non-finite values.
Results may differ from the reference program's by a relative error of at most 0.02.
Values may be sent and summed in bfloat16 or wider, within the bound.
A program may use at most 448 MiB of HBM per device.

```python
import jax
import jax.numpy as jnp
from jax import lax

D = 1280
H = 16
HD = 80
FF = 5120
SLOT = 1536
LONGEST = 1500
SHORTEST = 1100
CLIPS_GRP = 1
CLIPS = 16
REACH = 1345


def draw_lengths(key, part):
    key = jax.random.fold_in(key, 7)
    key_base, key_reach, key_pick, key_top = jax.random.split(key, 4)
    group_count = CLIPS // CLIPS_GRP
    base_len = jax.random.randint(key_base, (CLIPS,), SHORTEST, LONGEST + 1)
    reach_len = jax.random.randint(key_reach, (CLIPS,), REACH, LONGEST + 1)
    picked = jax.random.randint(key_pick, (group_count,), 0, CLIPS_GRP)
    picked_full = jnp.repeat(picked, CLIPS_GRP, total_repeat_length=CLIPS)
    position = jnp.arange(CLIPS)
    chosen = position % CLIPS_GRP == picked_full
    top_clip = jax.random.randint(key_top, (), 0, CLIPS)
    low_group = (top_clip // CLIPS_GRP + 1) % group_count
    low_clip = low_group * CLIPS_GRP + (picked[low_group] + 1) % CLIPS_GRP
    low_value = jnp.where(chosen, REACH, SHORTEST)
    result = jnp.where(chosen, reach_len, base_len)
    result = jnp.where(position == low_clip, low_value, result)
    result = jnp.where(position == top_clip, LONGEST, result)
    return result.astype(jnp.int32)


def block_scale(rng, dims, pieces, low, high):
    level, own = 1.0, jax.random.fold_in(rng, 6)
    for dim, blocks in pieces:
        heights = jnp.exp(jax.random.uniform(jax.random.fold_in(own, dim), (blocks,), jnp.float32, low / len(pieces), high / len(pieces)))
        level = level * jnp.repeat(heights, dims[dim] // blocks).reshape([-1 if axis == dim else 1 for axis in range(len(dims))])
    return level


def bell_draw(rng, dims, scale, bound, pieces=(), held_as=jnp.bfloat16):
    drawn = jax.random.normal(rng, dims, jnp.float32) * scale
    if len(pieces) > 0:
        drawn = block_scale(rng, dims, pieces, -0.22, 0.18) * drawn
    return jnp.clip(drawn, min=-bound, max=bound).astype(held_as)


def setup_inputs(seed: int = 0) -> dict:
    key_of = jax.random.split(jax.random.key(seed), 19)
    return {
        "tokens": bell_draw(key_of[0], (CLIPS, SLOT, D), 1.0, 6.0, ((0, 16), (1, 8))),
        "lengths": draw_lengths(jax.random.fold_in(key_of[18], 71), 0),
        "w_query": bell_draw(key_of[2], (D, D), (D // 2) ** -0.5, 0.25, ((0, 8),)),
        "w_key": bell_draw(key_of[3], (D, D), (D // 2) ** -0.5, 0.25, ((0, 8),)),
        "w_value": bell_draw(key_of[4], (D, D), D ** -0.5, 0.15625, ((0, 8),)),
        "w_out": bell_draw(key_of[5], (D, D), (D // 16) ** -0.5, 0.625, ((0, 8),)),
        "w_up": bell_draw(key_of[6], (D, FF), D ** -0.5, 0.15625, ((0, 8),)),
        "w_down": bell_draw(key_of[7], (FF, D), FF ** -0.5, 0.078125, ((0, 8),)),
        "b_query": bell_draw(key_of[8], (D,), 0.5, 3.0, ((0, 8),)),
        "b_value": bell_draw(key_of[9], (D,), 0.5, 3.0, ((0, 8),)),
        "b_out": bell_draw(key_of[10], (D,), 0.5, 3.0, ((0, 8),)),
        "b_up": bell_draw(key_of[11], (FF,), 0.5, 3.0, ((0, 8),)),
        "b_down": bell_draw(key_of[12], (D,), 0.5, 3.0, ((0, 8),)),
        "gain_attn": jnp.clip(1.0 + 0.15 * jax.random.normal(key_of[13], (D,), jnp.float32), 0.25, 1.75).astype(jnp.bfloat16),
        "shift_attn": bell_draw(key_of[14], (D,), 0.5, 3.0, ((0, 8),)),
        "gain_ffn": jnp.clip(1.0 + 0.15 * jax.random.normal(key_of[15], (D,), jnp.float32), 0.25, 1.75).astype(jnp.bfloat16),
        "shift_ffn": bell_draw(key_of[16], (D,), 0.5, 3.0, ((0, 8),)),
        "cotangent": bell_draw(key_of[17], (CLIPS, SLOT, D), 1.0, 6.0, ((0, 16), (1, 8))),
    }


@jax.custom_vjp
def low(v):
    return lax.optimization_barrier(v.astype(jnp.bfloat16)).astype(jnp.float32)

@jax.custom_vjp
def low_back(v):
    return v

def low_keep(v):
    return (low(v), None)

def low_pass(kept, grad):
    return (grad,)

def back_keep(v):
    return (v, None)

def back_low(kept, grad):
    return (low(grad),)
low.defvjp(low_keep, low_pass)
low_back.defvjp(back_keep, back_low)

def norm_rows(values, gain, shift):
    center = values - lax.optimization_barrier(jnp.mean(values, axis=-1, keepdims=True))
    spread = lax.optimization_barrier(jnp.mean(center * center, axis=-1, keepdims=True))
    return center * lax.rsqrt(spread + 1e-05) * gain + shift

def matmul(left, right):
    return jnp.dot(left, right, precision=lax.Precision.HIGHEST)

def layer(clip_rows, params, length):
    w_query, w_key, w_value, w_out, w_up, w_down, b_query, b_value, b_out, b_up, b_down, gain_attn, shift_attn, gain_ffn, shift_ffn = params
    seq_len = clip_rows.shape[0]
    normed = low(norm_rows(clip_rows, gain_attn, shift_attn))
    queries = low(low_back(matmul(normed, w_query) + b_query)).reshape(seq_len, H, HD)
    keys_all = low(low_back(matmul(normed, w_key))).reshape(seq_len, H, HD)
    values_all = low(low_back(matmul(normed, w_value) + b_value)).reshape(seq_len, H, HD)
    scores = jnp.einsum('thd,shd->hts', queries, keys_all, precision=lax.Precision.HIGHEST) * HD ** (-0.5)
    valid = jnp.arange(seq_len) < length
    scores = low_back(jnp.where(valid[None, None, :], scores, -1e+30))
    probs = low(jax.nn.softmax(scores, axis=-1))
    attended = jnp.einsum('hts,shd->thd', probs, values_all, precision=lax.Precision.HIGHEST).reshape(seq_len, D)
    attended = low(low_back(attended))
    middle = clip_rows + low_back(matmul(attended, w_out) + b_out)
    second = low(norm_rows(middle, gain_ffn, shift_ffn))
    hidden_pre = low_back(matmul(second, w_up) + b_up)
    activated = low(jax.nn.gelu(hidden_pre, approximate=False))
    return middle + low_back(matmul(activated, w_down) + b_down)

def reference(tokens, lengths, w_query, w_key, w_value, w_out, w_up, w_down, b_query, b_value, b_out, b_up, b_down, gain_attn, shift_attn, gain_ffn, shift_ffn, cotangent):
    params = tuple((item.astype(jnp.float32) for item in (w_query, w_key, w_value, w_out, w_up, w_down, b_query, b_value, b_out, b_up, b_down, gain_attn, shift_attn, gain_ffn, shift_ffn)))

    def one_clip(totals, item):
        clip_rows, length, clip_cot = item
        live = (jnp.arange(SLOT) < length).astype(jnp.float32)[:, None]
        result, pullback = jax.vjp(lambda inputs, weights: layer(inputs, weights, length), clip_rows.astype(jnp.float32), params)
        grad_in, grad_params = pullback(clip_cot.astype(jnp.float32) * live)
        totals = jax.tree.map(lambda acc, new: acc + new, totals, grad_params)
        return (totals, (result.astype(jnp.bfloat16), grad_in))
    zeros = tuple((jnp.zeros_like(item) for item in params))
    totals, (outputs, input_grad) = lax.scan(one_clip, zeros, (tokens, lengths, cotangent))
    return (outputs, input_grad, totals[0], totals[1], totals[2], totals[3], totals[4], totals[5], totals[6], totals[7], totals[8], totals[9], totals[10], totals[11], totals[12], totals[13], totals[14])
```

```python
import functools

import jax
import jax.numpy as jnp
from jax import lax
from jax.experimental import pallas as pl
from jax.experimental.pallas import tpu as pltpu
from jax.sharding import PartitionSpec as P

H = 16
HD = 80
EPS = 1e-05
AXES = ("rep", "shard")
F32 = jnp.float32
BF16 = jnp.bfloat16
NT = (((1,), (1,)), ((), ()))
TN = (((0,), (0,)), ((), ()))


def flat_index(y, zh, c, x, zl):
    return ((y % 4) * 4 + (zh % 2) * 2 + c % 2) * 8 + (x % 4) * 2 + zl % 2


def pairs(move):
    found = []
    for y in range(4):
        for zh in range(2):
            for c in range(2):
                for x in range(4):
                    for zl in range(2):
                        here = flat_index(y, zh, c, x, zl)
                        found.append((here, flat_index(*move(y, zh, c, x, zl))))
    return found


def send(value, move):
    return lax.ppermute(value, AXES, pairs(move))


def along_x(value, dx):
    return send(value, lambda y, zh, c, x, zl: (y, zh, c, x + dx, zl))


def along_y(value, dy):
    return send(value, lambda y, zh, c, x, zl: (y + dy, zh, c, x, zl))


def along_z(value, dz):
    def move(y, zh, c, x, zl):
        z = (2 * zh + zl + dz) % 4
        return (y, z // 2, c, x, z % 2)

    return send(value, move)


def to_sibling(value):
    return send(value, lambda y, zh, c, x, zl: (y, zh, c + 1, x, zl))


def cross(value):
    return send(value, lambda y, zh, c, x, zl: (y, zh, zl, x, c))


def gather_group(own):
    near = [own] + [along_x(own, dx) for dx in (1, 2, 3)]
    return [[block, to_sibling(block)] for block in near]


def scatter_group(parts):
    total = None
    for dx in (2, 1, 3, 0):
        both = parts[dx][0].astype(F32) + to_sibling(parts[dx][1]).astype(F32)
        if dx > 0:
            both = along_x(both.astype(BF16), -dx).astype(F32)
        total = both if total is None else total + both
    return total


def sum_four(value, along):
    one, two, three = (along(value, step).astype(F32) for step in (1, 2, 3))
    return (value.astype(F32) + two) + (one + three)


def place(blocks, indices):
    held = jnp.zeros((len(blocks),) + blocks[0].shape, blocks[0].dtype)
    for block, index in zip(blocks, indices):
        held = lax.dynamic_update_index_in_dim(held, block, index, 0)
    return held


def pick(array, index, axis=0):
    return lax.dynamic_index_in_dim(array, index, axis, keepdims=False)


def norm_fwd(values, gain, shift):
    center = values - jnp.mean(values, axis=-1, keepdims=True)
    inverse = lax.rsqrt(jnp.mean(center * center, axis=-1, keepdims=True) + EPS)
    normed = center * inverse
    return (normed, inverse, normed * gain + shift)


def norm_back(grad_rows, normed, inverse, gain):
    scaled = grad_rows * gain
    grad_in = inverse * (
        scaled
        - jnp.mean(scaled, axis=-1, keepdims=True)
        - normed * jnp.mean(scaled * normed, axis=-1, keepdims=True)
    )
    return (grad_in, jnp.sum(grad_rows * normed, axis=0), jnp.sum(grad_rows, axis=0))


def attend_kernel(scale, queries, everything, mask, mixed, probs, keys, values):
    @pl.when(pl.program_id(0) == 0)
    def _():
        for h in range(2):
            keys[h] = everything[:, 160 + h * HD : 160 + (h + 1) * HD]
            values[h] = everything[:, 320 + h * HD : 320 + (h + 1) * HD]

    for h in range(2):
        mine = queries[:, h * HD : (h + 1) * HD]
        scores = lax.dot_general(mine, keys[h], NT, preferred_element_type=F32) * scale
        scores = scores + mask[...]
        top = jnp.max(scores, axis=-1, keepdims=True)
        risen = jnp.exp(scores - top)
        share = 1.0 / jnp.sum(risen, axis=-1, keepdims=True)
        low = (risen * share).astype(BF16)
        probs[h] = low
        mixed[:, h * HD : (h + 1) * HD] = jnp.dot(
            low, values[h], preferred_element_type=F32
        ).astype(BF16)


def attend(qkv, mask, tile):
    rows = qkv.shape[0]
    return pl.pallas_call(
        functools.partial(attend_kernel, HD**-0.5),
        grid=(rows // tile,),
        in_specs=[
            pl.BlockSpec((tile, 480), lambda i: (i, 0)),
            pl.BlockSpec((rows, 480), lambda i: (0, 0)),
            pl.BlockSpec((1, rows), lambda i: (0, 0)),
        ],
        out_specs=[
            pl.BlockSpec((tile, 160), lambda i: (i, 0)),
            pl.BlockSpec((2, tile, rows), lambda i: (0, i, 0)),
        ],
        out_shape=[
            jax.ShapeDtypeStruct((rows, 160), BF16),
            jax.ShapeDtypeStruct((2, rows, rows), BF16),
        ],
        scratch_shapes=[pltpu.VMEM((2, rows, HD), BF16), pltpu.VMEM((2, rows, HD), BF16)],
        compiler_params=pltpu.CompilerParams(vmem_limit_bytes=48 << 20),
        cost_estimate=pl.CostEstimate(
            flops=8 * rows * rows * 256, bytes_accessed=16 << 20, transcendentals=2 * rows * rows
        ),
    )(qkv, qkv, mask)


def attend_back_kernel(
    scale, queries, everything, probs, mixed, grad_mixed, grads, keys, values, sum_k, sum_v
):
    step = pl.program_id(0)
    tile = queries.shape[0]

    @pl.when(step == 0)
    def _():
        for h in range(2):
            keys[h] = everything[:, 160 + h * HD : 160 + (h + 1) * HD]
            values[h] = everything[:, 320 + h * HD : 320 + (h + 1) * HD]
        sum_k[...] = jnp.zeros_like(sum_k)
        sum_v[...] = jnp.zeros_like(sum_v)

    here = pl.ds(pl.multiple_of(step * tile, tile), tile)
    for h in range(2):
        cols = slice(h * HD, (h + 1) * HD)
        mine, back, low = queries[:, cols], grad_mixed[:, cols], probs[h]
        row_total = jnp.sum(
            back.astype(F32) * mixed[:, cols].astype(F32), axis=-1, keepdims=True
        )
        grad_probs = lax.dot_general(back, values[h], NT, preferred_element_type=F32)
        grad_scores = (low.astype(F32) * (grad_probs - row_total)).astype(BF16)
        sum_v[h] += lax.dot_general(low, back, TN, preferred_element_type=F32)
        sum_k[h] += lax.dot_general(grad_scores, mine, TN, preferred_element_type=F32)
        grad_q = jnp.dot(grad_scores, keys[h], preferred_element_type=F32) * scale
        grads[here, cols] = grad_q.astype(BF16)

    @pl.when(step == pl.num_programs(0) - 1)
    def _():
        for h in range(2):
            grads[:, 160 + h * HD : 160 + (h + 1) * HD] = (sum_k[h] * scale).astype(BF16)
            grads[:, 320 + h * HD : 320 + (h + 1) * HD] = sum_v[h].astype(BF16)


def attend_back(qkv, probs, mixed, grad_mixed, tile):
    rows = qkv.shape[0]
    return pl.pallas_call(
        functools.partial(attend_back_kernel, HD**-0.5),
        grid=(rows // tile,),
        in_specs=[
            pl.BlockSpec((tile, 480), lambda i: (i, 0)),
            pl.BlockSpec((rows, 480), lambda i: (0, 0)),
            pl.BlockSpec((2, tile, rows), lambda i: (0, i, 0)),
            pl.BlockSpec((tile, 160), lambda i: (i, 0)),
            pl.BlockSpec((tile, 160), lambda i: (i, 0)),
        ],
        out_specs=pl.BlockSpec((rows, 480), lambda i: (0, 0)),
        out_shape=jax.ShapeDtypeStruct((rows, 480), BF16),
        scratch_shapes=[
            pltpu.VMEM((2, rows, HD), BF16),
            pltpu.VMEM((2, rows, HD), BF16),
            pltpu.VMEM((2, rows, HD), F32),
            pltpu.VMEM((2, rows, HD), F32),
        ],
        compiler_params=pltpu.CompilerParams(vmem_limit_bytes=48 << 20),
        cost_estimate=pl.CostEstimate(
            flops=16 * rows * rows * 256, bytes_accessed=16 << 20, transcendentals=0
        ),
    )(qkv, qkv, probs, mixed, grad_mixed)


def dot(a, b):
    return jnp.dot(a, b, preferred_element_type=F32)


def dot_nt(a, b):
    return lax.dot_general(a, b, NT, preferred_element_type=F32)


def dot_tn(a, b):
    return lax.dot_general(a, b, TN, preferred_element_type=F32)


def rejoin_rows(part, y, c, zl):
    pieces = part.astype(BF16).reshape((4, part.shape[0] // 4) + part.shape[1:])
    total = pick(pieces, y).astype(F32)
    for dy in (2, 1, 3):
        total = total + along_y(pick(pieces, (y + dy) % 4), dy).astype(F32)
    total = sum_four(total.astype(BF16), along_z).astype(BF16)
    other = to_sibling(total)
    total = jnp.where(c == zl, total, other)
    blocks = [total] + [along_y(total, dy) for dy in (1, 2, 3)]
    held = place(blocks, [(y - dy) % 4 for dy in range(4)])
    return held.reshape((-1,) + held.shape[2:]).astype(F32)


def rejoin_columns(part, y, c, x, zl):
    depth = part.shape[0] // 32
    pieces = part.astype(BF16).reshape(8, 4, depth, part.shape[1])
    total = pick(pieces, y, 1).astype(F32)
    for dy in (2, 1, 3):
        total = total + along_y(pick(pieces, (y + dy) % 4, 1), dy).astype(F32)
    total = sum_four(total.astype(BF16), along_z).astype(BF16)
    near = [pick(total, 2 * x + zl)]
    near += [along_x(pick(total, 2 * ((x + dx) % 4) + zl), dx) for dx in (1, 2, 3)]
    near = jnp.stack(near)
    far = to_sibling(near)
    blocks, indices = [], []
    for dx in range(4):
        for dc, source in enumerate((near, far)):
            blocks.append(source[dx])
            indices.append(2 * ((x - dx) % 4) + (c ^ dc))
    whole = place(blocks, indices)
    blocks = [whole] + [along_y(whole, dy) for dy in (1, 2, 3)]
    return place(blocks, [(y - dy) % 4 for dy in range(4)])


def per_device(
    tokens,
    lengths,
    w_query,
    w_key,
    w_value,
    w_out,
    w_up,
    w_down,
    b_query,
    b_value,
    b_out,
    b_up,
    b_down,
    gain_attn,
    shift_attn,
    gain_ffn,
    shift_ffn,
    cotangent,
):
    rep, shard = lax.axis_index("rep"), lax.axis_index("shard")
    y, c, x, zl = rep // 4, rep % 2, shard // 2, shard % 2
    rows, width = tokens.shape[1:]

    own = cross(tokens[0])
    length = jnp.where(c == zl, lengths, to_sibling(lengths))[0]

    small = jnp.concatenate(
        [b_query, b_value, b_out, b_down, gain_attn, shift_attn, gain_ffn, shift_ffn, b_up]
    ).reshape(4, 480)
    cut = jnp.stack([w_query, w_key, w_value]).reshape(3, 160, 8, 160)
    cut = cut.transpose(2, 1, 0, 3).reshape(8, 160, 480)

    def spread(get):
        blocks, indices = [], []
        for dx in range(4):
            for dz in range(2):
                block = get(2 * ((x + dx) % 4) + c)
                if dx or dz:
                    block = send(
                        block,
                        lambda y, zh, c, x, zl, dx=dx, dz=dz: (y, zh, c, x + dx, zl + dz),
                    )
                blocks.append(block)
                indices.append(2 * ((x - dx) % 4) + (zl ^ dz))
        return place(blocks, indices)

    held = spread(lambda index: jnp.concatenate([pick(cut, index), small]))
    w_qkv = held[:, :160].reshape(width, 480)
    small = held[:, 160:].reshape(8, 1920)
    full = small[:, :1280].reshape(8, 8, 160).transpose(1, 0, 2).reshape(8, width).astype(F32)
    bias_out, bias_down, gain_one, shift_one, gain_two, shift_two = (full[k] for k in range(2, 8))
    me = 2 * x + c
    mine_small = pick(small, me).astype(F32)
    bias_qkv = jnp.concatenate([mine_small[:160], jnp.zeros((160,), F32), mine_small[160:320]])
    bias_up = mine_small[1280:]

    token_blocks = gather_group(own)

    def first_norm(block):
        return norm_fwd(block.astype(F32), gain_one, shift_one)

    first_in, qkv = [], []
    for dx in range(4):
        normed = first_norm(jnp.concatenate(token_blocks[dx]))[2].astype(BF16)
        first_in.append(normed)
        qkv.append((dot(normed, w_qkv) + bias_qkv).astype(BF16))
    first_in, qkv = jnp.concatenate(first_in), jnp.concatenate(qkv)

    starts = jnp.stack([2 * ((x - dx) % 4) + (c ^ dc) for dx in range(4) for dc in range(2)])
    position = (starts[:, None] * rows + jnp.arange(rows)[None, :]).reshape(1, 8 * rows)
    mask = jnp.where(position < length, 0.0, -1e30).astype(F32)
    live = (position < length).astype(F32).reshape(4, 2 * rows, 1)

    out_blocks = gather_group(cross(w_out))
    out_full = jnp.concatenate([block for both in out_blocks for block in both])
    up_mine = spread(
        lambda index: lax.dynamic_slice_in_dim(w_up, index * 640, 640, axis=1)
    ).reshape(width, 640)
    down_mine = cross(w_down)
    grad_blocks = gather_group(cross(cotangent[0]))
    grad_top = [
        (jnp.concatenate(grad_blocks[dx]).astype(F32) * live[dx]).astype(BF16) for dx in range(4)
    ]

    mixed, probs = attend(qkv, mask, 384)

    def exchange(blocks):
        got = [[None, None] for _ in range(4)]
        for dx in range(4):
            for dc in range(2):
                block = blocks[dx][dc]
                if dx or dc:
                    block = send(
                        block,
                        lambda y, zh, c, x, zl, dx=dx, dc=dc: (y, zh, c + dc, x - dx, zl),
                    )
                got[-dx % 4][dc] = block
        return got

    split = mixed.reshape(4, 2, rows, 160)
    attended = exchange([[split[dx, dc] for dc in range(2)] for dx in range(4)])
    attended = jnp.concatenate([block for both in attended for block in both], axis=1)
    middle = own.astype(F32) + dot(attended, out_full) + bias_out
    normed_two, inverse_two, second_own = norm_fwd(middle, gain_two, shift_two)
    second_blocks = gather_group(second_own.astype(BF16))

    second_in, active, grad_hidden, out_parts, second_parts = [], [], [], [], []
    for dx in range(4):
        block = jnp.concatenate(second_blocks[dx])
        hidden = dot(block, up_mine) + bias_up
        bell = 0.5 * (1.0 + lax.erf(hidden * 0.7071067811865476))
        act = (hidden * bell).astype(BF16)
        slope = bell + hidden * jnp.exp(-0.5 * hidden * hidden) * 0.3989422804014327
        grad_z = (dot_nt(grad_top[dx], down_mine) * slope).astype(BF16)
        second_in.append(block)
        active.append(act)
        grad_hidden.append(grad_z)
        second_parts.append(dot_nt(grad_z, up_mine).astype(BF16).reshape(2, rows, width))
        out_parts.append(dot(act, down_mine).astype(BF16).reshape(2, rows, width))
    grad_second = scatter_group(second_parts)
    result = scatter_group(out_parts)
    output = cross((middle + result + bias_down).astype(BF16))

    grad_hidden = jnp.concatenate(grad_hidden)
    g_w_up = dot_tn(jnp.concatenate(second_in), grad_hidden)
    g_w_down = dot_tn(jnp.concatenate(active), jnp.concatenate(grad_top))
    g_b_up = jnp.sum(grad_hidden.astype(F32), axis=0)

    top_own = grad_top[0][:rows].astype(F32)
    grad_ln, g_gain_ffn, g_shift_ffn = norm_back(grad_second, normed_two, inverse_two, gain_two)
    grad_middle = top_own + grad_ln
    branch = grad_middle.astype(BF16)
    grad_attended = dot_nt(branch, out_full).astype(BF16)
    back = exchange(
        [
            [grad_attended[:, (2 * dx + dc) * 160 : (2 * dx + dc + 1) * 160] for dc in range(2)]
            for dx in range(4)
        ]
    )
    grad_mixed = jnp.concatenate([block for both in back for block in both])
    grad_qkv = attend_back(qkv, probs, mixed, grad_mixed, 384)

    branch_blocks = gather_group(branch)
    branch_all = jnp.concatenate([block for both in branch_blocks for block in both])
    g_w_out = dot_tn(mixed, branch_all)

    first_parts = []
    for dx in range(4):
        part = dot_nt(grad_qkv[2 * rows * dx : 2 * rows * (dx + 1)], w_qkv)
        first_parts.append(part.astype(BF16).reshape(2, rows, width))
    grad_first = scatter_group(first_parts)
    g_w_qkv = dot_tn(first_in, grad_qkv)
    sums = jnp.sum(grad_qkv.astype(F32), axis=0)
    normed_one, inverse_one, _ = first_norm(own)
    grad_ln, g_gain_attn, g_shift_attn = norm_back(grad_first, normed_one, inverse_one, gain_one)
    input_grad = cross(grad_middle + grad_ln)

    grad_down = rejoin_rows(g_w_down, y, c, zl)
    grad_out = rejoin_rows(g_w_out, y, c, zl)
    grad_up = rejoin_columns(g_w_up, y, c, x, zl)
    grad_up = grad_up.transpose(0, 2, 1, 3).reshape(160, 5120).astype(F32)
    three = rejoin_columns(g_w_qkv, y, c, x, zl).reshape(4, 8, 40, 3, 160)
    three = three.transpose(3, 0, 2, 1, 4).reshape(3, 160, width).astype(F32)

    vectors = jnp.stack(
        [
            jnp.sum(branch.astype(F32), axis=0),
            jnp.sum(top_own, axis=0),
            g_gain_attn,
            g_shift_attn,
            g_gain_ffn,
            g_shift_ffn,
        ]
    )
    vectors = vectors + to_sibling(vectors)
    vectors = sum_four(vectors, along_x)
    sliced = jnp.concatenate([sums[:160], sums[320:], g_b_up])
    packed = jnp.concatenate([vectors.reshape(-1), sliced])
    packed = sum_four(packed, along_y)
    packed = sum_four(packed, along_z)
    sliced = packed[6 * width :]
    sliced = jnp.where(c == zl, sliced, to_sibling(sliced))
    vectors = lax.dynamic_slice_in_dim(packed[: 6 * width].reshape(6, width), shard * 160, 160, 1)
    return (
        output[None],
        input_grad[None],
        three[0],
        three[1],
        three[2],
        grad_out,
        grad_up,
        grad_down,
        sliced[:160],
        sliced[160:320],
        vectors[0],
        sliced[320:],
        vectors[1],
        vectors[2],
        vectors[3],
        vectors[4],
        vectors[5],
    )


def solution(mesh):
    by_clip, matrix, vector = P("rep", "shard", None), P("shard", None), P("shard")
    return jax.shard_map(
        per_device,
        mesh=mesh,
        in_specs=(by_clip, P("rep")) + (matrix,) * 6 + (vector,) * 9 + (by_clip,),
        out_specs=(by_clip, by_clip) + (matrix,) * 6 + (vector,) * 9,
        check_vma=False,
    )
```

```python
import functools

import jax
import jax.numpy as jnp
from jax import lax
from jax.experimental import pallas as pl
from jax.experimental.pallas import tpu as pltpu
from jax.sharding import PartitionSpec as P

H = 16
HD = 80
EPS = 1e-05
AXES = ("rep", "shard")
F32 = jnp.float32
BF16 = jnp.bfloat16
NT = (((1,), (1,)), ((), ()))
TN = (((0,), (0,)), ((), ()))


def flat_index(y, zh, c, x, zl):
    return ((y % 4) * 4 + (zh % 2) * 2 + c % 2) * 8 + (x % 4) * 2 + zl % 2


def pairs(move):
    found = []
    for y in range(4):
        for zh in range(2):
            for c in range(2):
                for x in range(4):
                    for zl in range(2):
                        here = flat_index(y, zh, c, x, zl)
                        found.append((here, flat_index(*move(y, zh, c, x, zl))))
    return found


def send(value, move):
    return lax.ppermute(value, AXES, pairs(move))


def along_x(value, dx):
    return send(value, lambda y, zh, c, x, zl: (y, zh, c, x + dx, zl))


def along_y(value, dy):
    return send(value, lambda y, zh, c, x, zl: (y + dy, zh, c, x, zl))


def along_z(value, dz):
    def move(y, zh, c, x, zl):
        z = (2 * zh + zl + dz) % 4
        return (y, z // 2, c, x, z % 2)

    return send(value, move)


def to_sibling(value):
    return send(value, lambda y, zh, c, x, zl: (y, zh, c + 1, x, zl))


def cross(value):
    return send(value, lambda y, zh, c, x, zl: (y, zh, zl, x, c))


def gather_group(own):
    near = [own] + [along_x(own, dx) for dx in (1, 2, 3)]
    return [[block, to_sibling(block)] for block in near]


def scatter_group(parts):
    total = None
    for dx in (2, 1, 3, 0):
        both = parts[dx][0].astype(F32) + to_sibling(parts[dx][1]).astype(F32)
        if dx > 0:
            both = along_x(both.astype(BF16), -dx).astype(F32)
        total = both if total is None else total + both
    return total


def sum_four(value, along):
    one, two, three = (along(value, step).astype(F32) for step in (1, 2, 3))
    return (value.astype(F32) + two) + (one + three)


def place(blocks, indices):
    held = jnp.zeros((len(blocks),) + blocks[0].shape, blocks[0].dtype)
    for block, index in zip(blocks, indices):
        held = lax.dynamic_update_index_in_dim(held, block, index, 0)
    return held


def pick(array, index, axis=0):
    return lax.dynamic_index_in_dim(array, index, axis, keepdims=False)


def norm_fwd(values, gain, shift):
    center = values - jnp.mean(values, axis=-1, keepdims=True)
    inverse = lax.rsqrt(jnp.mean(center * center, axis=-1, keepdims=True) + EPS)
    normed = center * inverse
    return (normed, inverse, normed * gain + shift)


def norm_back(grad_rows, normed, inverse, gain):
    scaled = grad_rows * gain
    grad_in = inverse * (
        scaled
        - jnp.mean(scaled, axis=-1, keepdims=True)
        - normed * jnp.mean(scaled * normed, axis=-1, keepdims=True)
    )
    return (grad_in, jnp.sum(grad_rows * normed, axis=0), jnp.sum(grad_rows, axis=0))


MESH = pl.DeviceIdType.MESH
VMEM = pl.BlockSpec(memory_space=pltpu.VMEM)
HBM = pl.BlockSpec(memory_space=pl.ANY)


class Net:
    def __init__(self, sent, got, still):
        rep, shard = lax.axis_index("rep"), lax.axis_index("shard")
        self.y, self.zh, self.c = rep // 4, rep // 2 % 2, rep % 2
        self.x, self.zl = shard // 2, shard % 2
        self.me, self.shard = 2 * self.x + self.c, shard
        self.sent, self.got, self.still, self.used, self.started = sent, got, still, 0, []

    def device(self, dx=0, dc=0, dz=0, dy=0):
        z = (2 * self.zh + self.zl + dz) % 4
        return (
            (self.y + dy) % 4 * 4 + z // 2 * 2 + (self.c + dc) % 2,
            (self.x + dx) % 4 * 2 + z % 2,
        )

    def in_pair(self, dx, dz):
        return (
            self.y * 4 + self.zh * 2 + self.c,
            (self.x + dx) % 4 * 2 + (self.zl + dz) % 2,
        )

    def partner(self):
        return (self.y * 4 + self.zh * 2 + self.zl, 2 * self.x + self.c)

    def greet(self, devices):
        barrier = pltpu.get_barrier_semaphore()
        for device in devices:
            pl.semaphore_signal(barrier, inc=1, device_id=device, device_id_type=MESH)
        return lambda: pl.semaphore_wait(barrier, len(devices))

    def reserve(self, count):
        first = self.used
        self.used += count
        return first

    def copy(self, index, source, target, device):
        return pltpu.make_async_remote_copy(
            src_ref=source,
            dst_ref=target,
            send_sem=self.sent.at[index],
            recv_sem=self.got.at[index],
            device_id=device,
            device_id_type=MESH,
        )

    def go(self, source, target, device):
        copy = self.copy(self.reserve(1), source, target, device)
        copy.start()
        self.started.append(copy)
        return copy

    def cross(self, source, target):
        index = self.reserve(1)
        copy = self.copy(index, source, target, self.partner())
        local = pltpu.make_async_copy(source, target, self.still.at[index])

        @pl.when(self.c != self.zl)
        def _():
            copy.start()

        @pl.when(self.c == self.zl)
        def _():
            local.start()

        def arrived():
            @pl.when(self.c != self.zl)
            def _():
                copy.wait_recv()

            @pl.when(self.c == self.zl)
            def _():
                local.wait()

        def left():
            @pl.when(self.c != self.zl)
            def _():
                copy.wait_send()

        return arrived, left

    def all_sent(self):
        for copy in self.started:
            copy.wait_send()


def order(k):
    return 1 + 2 * k - 3 * (k // 2)


def aligned(index, size):
    return pl.ds(pl.multiple_of(index * size, size), size)


def scratch_for(copies):
    return [pltpu.SemaphoreType.DMA((copies,)) for _ in range(3)]


def begin_kernel(
    tokens,
    w_query,
    w_key,
    w_value,
    small,
    w_out,
    w_up,
    w_down,
    cotangent,
    length,
    h1,
    heads,
    probs,
    mixed,
    attended,
    w_qkv,
    smalls,
    own,
    clip,
    out_full,
    up_mine,
    down_mine,
    top,
    gathered,
    cut,
    lens,
    vectors,
    sent,
    got,
    still,
):
    net = Net(sent, got, still)
    x, c, zl, me, shard = net.x, net.c, net.zl, net.me, net.shard
    rows, width = tokens.shape
    plane = [net.device(dx, dc) for dx in range(4) for dc in range(2) if dx or dc]
    across = [net.in_pair(dx, 1) for dx in range(4)]
    everyone = plane + across + [(net.y * 4 + net.zh * 2 + 1 - c, 2 * x + 1 - zl)]
    wait = net.greet(everyone)
    for block in range(8):
        cols = slice(160 * block, 160 * block + 160)
        cut[block, :, :160] = w_query[:, cols]
        cut[block, :, 160:320] = w_key[:, cols]
        cut[block, :, 320:] = w_value[:, cols]
    wait()

    token_arrived, token_left = net.cross(tokens, gathered.at[2 * x + zl])
    base = net.reserve(4)

    def token_send(k, source):
        dx = order(k)
        return net.copy(base + dx, source, gathered.at[me], net.device(dx))

    @pl.when(c == zl)
    def _():
        for k in range(3):
            token_send(k, tokens).start()

    @pl.when(c == 0)
    def _():
        lens[0] = length[...]

    @pl.when(c == 1)
    def _():
        lens[1] = length[...]

    lens_copy = net.go(length, lens.at[c], net.device(0, 1))
    arriving = []
    for dx in (0, 1, 3, 2):
        for dz in range(2):
            if dx or dz:
                device = net.in_pair(dx, dz)
                arriving.append(net.go(small, smalls.at[shard], device))
                target = 2 * ((x + dx) % 4) + c
                arriving.append(net.go(cut.at[target], w_qkv.at[aligned(shard, 160)], device))
    smalls[shard] = small[...]
    w_qkv[aligned(shard, 160)] = cut[me]
    token_arrived()

    @pl.when(c != zl)
    def _():
        for k in range(3):
            token_send(k, gathered.at[me]).start()

    sibling = net.device(0, 1)
    own_over = net.go(gathered.at[me], gathered.at[me], sibling)
    out_arrived, out_left = net.cross(w_out, out_full.at[2 * x + zl])
    top_arrived, top_left = net.cross(cotangent, top.at[2 * x + zl])
    down_arrived, down_left = net.cross(w_down, down_mine)
    own[...] = gathered[me]

    for copy in arriving:
        copy.wait_recv()
    for block in range(8):
        vectors[:, 160 * block : 160 * block + 160] = smalls[block, :8, :160].astype(F32)
    gain, shift = vectors[4:5, :], vectors[5:6, :]
    bias_q = smalls[me, 0:1, :160].astype(F32)
    bias_v = smalls[me, 1:2, :160].astype(F32)

    def project(slot):
        values = gathered[slot].astype(F32)
        center = values - jnp.mean(values, axis=-1, keepdims=True)
        inverse = lax.rsqrt(jnp.mean(center * center, axis=-1, keepdims=True) + EPS)
        normed = (center * inverse * gain + shift).astype(BF16)
        h1[slot] = normed
        made = jnp.dot(normed, w_qkv[...], preferred_element_type=F32)
        here = aligned(slot, rows)
        for h in range(2):
            cols = slice(h * HD, (h + 1) * HD)
            heads[h, here, :] = (made[:, cols] + bias_q[:, cols]).astype(BF16)
            heads[2 + h, here, :] = made[:, 160 + h * HD : 240 + h * HD].astype(BF16)
            heads[4 + h, here, :] = (
                made[:, 320 + h * HD : 400 + h * HD] + bias_v[:, cols]
            ).astype(BF16)

    project(me)
    own_over.wait_recv()
    project(2 * x + 1 - c)
    over = net.reserve(4)

    def passed(dx, slot):
        return net.copy(over + dx, gathered.at[slot], gathered.at[slot], sibling)

    @pl.loop(0, 3)
    def _(k):
        dx = order(k)
        from_x = (x - dx + 4) % 4
        token_send(k, gathered.at[me]).wait_recv()
        passed(dx, 2 * from_x + c).start()
        project(2 * from_x + c)
        passed(dx, 2 * from_x + c).wait_recv()
        project(2 * from_x + 1 - c)

    later = []
    top_arrived()
    for dx in (1, 3, 2):
        later.append((net.go(top.at[me], top.at[me], net.device(dx)), top, dx))
    out_arrived()
    for dx in (1, 3, 2):
        later.append((net.go(out_full.at[me], out_full.at[me], net.device(dx)), out_full, dx))
    last = [
        net.go(top.at[me], top.at[me], sibling),
        net.go(out_full.at[me], out_full.at[me], sibling),
    ]
    for dx in (0, 1, 3, 2):
        for dz in range(2):
            if dx or dz:
                target = 2 * ((x + dx) % 4) + c
                source = w_up.at[:, pl.ds(pl.multiple_of(target * 640, 128), 640)]
                last.append(net.go(source, up_mine.at[shard], net.in_pair(dx, dz)))
    mine_up = pltpu.make_async_copy(
        w_up.at[:, pl.ds(pl.multiple_of(me * 640, 128), 640)],
        up_mine.at[shard],
        still.at[net.reserve(1)],
    )
    mine_up.start()

    lens_copy.wait_recv()
    clip[...] = lens[zl]
    clip_length = clip[0:1, 0:1]
    position = lax.broadcasted_iota(jnp.int32, (1, 8 * rows), 1).astype(F32)
    mask = jnp.where(position < clip_length, 0.0, -1e30)

    def attend_rows(to_x):
        here = aligned(to_x, 2 * rows)
        for h in range(2):
            cols = slice(h * HD, (h + 1) * HD)
            scores = lax.dot_general(heads[h, here, :], heads[2 + h], NT, preferred_element_type=F32)
            scores = scores * HD**-0.5 + mask
            risen = jnp.exp(scores - jnp.max(scores, axis=-1, keepdims=True))
            share = 1.0 / jnp.sum(risen, axis=-1, keepdims=True)
            low = (risen * share).astype(BF16)
            probs[h, here, :] = low
            made = jnp.dot(low, heads[4 + h], preferred_element_type=F32).astype(BF16)
            mixed[2 * to_x, :, cols] = made[:rows]
            mixed[2 * to_x + 1, :, cols] = made[rows:]

    mixed_base = net.reserve(8)

    def mixed_send(dx, dc):
        slot = 2 * ((x + dx) % 4) + (c + dc) % 2
        return net.copy(
            mixed_base + 2 * dx + dc, mixed.at[slot], attended.at[me], net.device(dx, dc)
        )

    @pl.loop(1, 5)
    def _(step):
        dx = step % 4
        attend_rows((x + dx) % 4)
        mixed_send(dx, 1).start()

        @pl.when(dx != 0)
        def _():
            mixed_send(dx, 0).start()

    attended[me] = mixed[me]
    for copy, array, dx in later:
        copy.wait_recv()
        slot = 2 * ((x - dx + 4) % 4) + c
        last.append(net.go(array.at[slot], array.at[slot], sibling))

    for dx in range(4):
        for dc in range(2):
            if dx or dc:
                mixed_send(dx, dc).wait()
    for copy in last:
        copy.wait_recv()
    mine_up.wait()
    down_arrived()
    for left in (token_left, out_left, top_left, down_left):
        left()
    for k in range(3):
        token_send(k, gathered.at[me]).wait_send()
        dx = order(k)
        passed(dx, me).wait_send()
    net.all_sent()


def begin(tokens, w_query, w_key, w_value, small, w_out, w_up, w_down, cotangent, length):
    rows, width = tokens.shape

    def shape(*dims):
        return jax.ShapeDtypeStruct(dims, BF16)

    return pl.pallas_call(
        begin_kernel,
        in_specs=[VMEM] * 5 + [HBM] * 4 + [VMEM],
        out_specs=[VMEM] * 9 + [HBM] * 4,
        out_shape=[
            shape(8, rows, width),
            shape(6, 8 * rows, HD),
            shape(2, 8 * rows, 8 * rows),
            shape(8, rows, 160),
            shape(8, rows, 160),
            shape(width, 480),
            shape(8, 16, 640),
            shape(rows, width),
            jax.ShapeDtypeStruct((8, 128), F32),
            shape(8, 160, width),
            shape(8, 160, 640),
            shape(640, width),
            shape(8, rows, width),
        ],
        scratch_shapes=[
            pltpu.VMEM((8, rows, width), BF16),
            pltpu.VMEM((8, 160, 480), BF16),
            pltpu.VMEM((2, 8, 128), F32),
            pltpu.VMEM((8, width), F32),
        ]
        + scratch_for(80),
        compiler_params=pltpu.CompilerParams(
            collective_id=0, has_side_effects=True, vmem_limit_bytes=58 << 20
        ),
    )(tokens, w_query, w_key, w_value, small, w_out, w_up, w_down, cotangent, length)


def middle_kernel(
    attended,
    own,
    smalls,
    clip,
    out_full,
    up_mine,
    down_mine,
    top,
    middle,
    grad_middle,
    branch,
    out_parts,
    g_up,
    g_down,
    g_up_bias,
    g_vectors,
    grad_mixed,
    vectors,
    second,
    masked,
    active,
    hidden,
    parts,
    over,
    sums,
    arrived,
    joined,
    by_head,
    sent,
    got,
    still,
):
    net = Net(sent, got, still)
    x, c, me = net.x, net.c, net.me
    rows, width = own.shape
    wait = net.greet([net.device(dx, dc) for dx in range(4) for dc in range(2) if dx or dc])
    for block in range(8):
        vectors[:, 160 * block : 160 * block + 160] = smalls[block, :8, :160].astype(F32)
    bias_up = smalls[me, 8:9, :].astype(F32)
    mine = aligned(me, rows)
    for block in range(8):
        joined[:, 160 * block : 160 * block + 160] = attended[block]
    made = jnp.dot(joined[...], out_full[...], preferred_element_type=F32)
    middle[...] = own[...].astype(F32) + made + vectors[2:3, :]

    def normalised():
        values = middle[...]
        center = values - jnp.mean(values, axis=-1, keepdims=True)
        inverse = lax.rsqrt(jnp.mean(center * center, axis=-1, keepdims=True) + EPS)
        return center * inverse, inverse

    second[mine, :] = (normalised()[0] * vectors[6:7, :] + vectors[7:8, :]).astype(BF16)
    wait()

    near, pass_on, swap, add = (net.reserve(4) for _ in range(4))

    def near_copy(dx):
        return net.copy(near + dx, second.at[mine], second.at[mine], net.device(dx))

    def pass_copy(dx, slot):
        here = second.at[aligned(slot, rows)]
        return net.copy(pass_on + dx, here, here, net.device(0, 1))

    def swap_copy(dx, to_x):
        source = parts.at[aligned(2 * to_x + 1 - c, rows)]
        return net.copy(swap + dx, source, over.at[to_x], net.device(0, 1))

    def add_copy(dx, to_x):
        return net.copy(add + dx, sums.at[to_x], arrived.at[dx], net.device(4 - dx))

    for dx in (1, 3, 2):
        near_copy(dx).start()

    @pl.loop(0, 4)
    def _(k):
        dx = k ^ (k >> 1)
        to_x = (x - dx + 4) % 4

        @pl.when(dx != 0)
        def _():
            near_copy(dx).wait_recv()

        pass_copy(dx, 2 * to_x + c).start()
        here = aligned(to_x, 2 * rows)
        position = lax.broadcasted_iota(jnp.int32, (2 * rows, 1), 0) + to_x * 2 * rows
        live = position.astype(F32) < clip[0:1, 0:1]
        low_top = jnp.where(live, top[here, :].astype(F32), 0.0).astype(BF16)
        masked[here, :] = low_top
        grad_act = lax.dot_general(low_top, down_mine[...], NT, preferred_element_type=F32)
        pass_copy(dx, 2 * to_x + c).wait_recv()
        z = jnp.dot(second[here, :], up_mine[...], preferred_element_type=F32) + bias_up
        bell = 0.5 * (1.0 + lax.erf(z * 0.7071067811865476))
        active[here, :] = (z * bell).astype(BF16)
        slope = bell + z * jnp.exp(-0.5 * z * z) * 0.3989422804014327
        grad_z = (grad_act * slope).astype(BF16)
        hidden[here, :] = grad_z
        parts[here, :] = lax.dot_general(
            grad_z, up_mine[...], NT, preferred_element_type=F32
        ).astype(BF16)
        swap_copy(dx, to_x).start()
        out_parts[here, :] = jnp.dot(
            active[here, :], down_mine[...], preferred_element_type=F32
        ).astype(BF16)
        swap_copy(dx, to_x).wait_recv()

        @pl.when(dx != 0)
        def _():
            kept = parts[aligned(2 * to_x + c, rows), :].astype(F32)
            sums[to_x] = (kept + over[to_x].astype(F32)).astype(BF16)
            add_copy(dx, to_x).start()

    @pl.loop(0, 5)
    def _(i):
        cols = pl.ds(pl.multiple_of(i * 256, 256), 256)
        g_up[cols, :] = lax.dot_general(
            second[:, cols], hidden[...], TN, preferred_element_type=F32
        ).astype(BF16)
        cols = pl.ds(pl.multiple_of(i * 128, 128), 128)
        g_down[cols, :] = lax.dot_general(
            active[:, cols], masked[...], TN, preferred_element_type=F32
        ).astype(BF16)

    g_up_bias[...] = jnp.sum(hidden[...].astype(F32), axis=0, keepdims=True)
    grad_second = parts[mine, :].astype(F32) + over[x].astype(F32)
    for dx in (1, 3, 2):
        add_copy(dx, (x - dx + 4) % 4).wait_recv()
        grad_second = grad_second + arrived[dx].astype(F32)
    normed, inverse = normalised()
    scaled = grad_second * vectors[6:7, :]
    back = inverse * (
        scaled
        - jnp.mean(scaled, axis=-1, keepdims=True)
        - normed * jnp.mean(scaled * normed, axis=-1, keepdims=True)
    )
    top_own = masked[mine, :].astype(F32)
    total = top_own + back
    grad_middle[...] = total
    low = total.astype(BF16)
    branch[...] = low
    grad_attended = lax.dot_general(low, out_full[...], NT, preferred_element_type=F32)
    grad_attended = grad_attended.astype(BF16)
    for block in range(8):
        by_head[block] = grad_attended[:, 160 * block : 160 * block + 160]
    mixing = []
    for dx in (2, 1, 3, 0):
        for dc in (1, 0):
            if dx or dc:
                slot = 2 * ((x + dx) % 4) + (c + dc) % 2
                mixing.append(net.go(by_head.at[slot], grad_mixed.at[me], net.device(dx, dc)))
    grad_mixed[me] = by_head[me]
    g_vectors[0:1, :] = jnp.sum(low.astype(F32), axis=0, keepdims=True)
    g_vectors[1:2, :] = jnp.sum(top_own, axis=0, keepdims=True)
    g_vectors[2:3, :] = jnp.sum(grad_second * normed, axis=0, keepdims=True)
    g_vectors[3:4, :] = jnp.sum(grad_second, axis=0, keepdims=True)
    for copy in mixing:
        copy.wait_recv()
    for dx in range(4):
        to_x = (x - dx + 4) % 4
        pass_copy(dx, 2 * to_x + c).wait_send()
        swap_copy(dx, to_x).wait_send()
        if dx:
            near_copy(dx).wait_send()
            add_copy(dx, to_x).wait_send()
    net.all_sent()


def middle_part(attended, own, smalls, clip, out_full, up_mine, down_mine, top):
    rows, width = own.shape

    def shape(*dims, dtype=BF16):
        return jax.ShapeDtypeStruct(dims, dtype)

    def buffer(*dims, dtype=BF16):
        return pltpu.VMEM(dims, dtype)

    return pl.pallas_call(
        middle_kernel,
        in_specs=[VMEM] * 8,
        out_specs=[VMEM] * 9,
        out_shape=[
            shape(rows, width, dtype=F32),
            shape(rows, width, dtype=F32),
            shape(rows, width),
            shape(8 * rows, width),
            shape(width, 640),
            shape(640, width),
            shape(1, 640, dtype=F32),
            shape(4, width, dtype=F32),
            shape(8, rows, 160),
        ],
        scratch_shapes=[
            buffer(8, width, dtype=F32),
            buffer(8 * rows, width),
            buffer(8 * rows, width),
            buffer(8 * rows, 640),
            buffer(8 * rows, 640),
            buffer(8 * rows, width),
            buffer(4, rows, width),
            buffer(4, rows, width),
            buffer(4, rows, width),
            buffer(rows, width),
            buffer(8, rows, 160),
        ]
        + scratch_for(24),
        compiler_params=pltpu.CompilerParams(
            collective_id=1, has_side_effects=True, vmem_limit_bytes=60 << 20
        ),
    )(attended, own, smalls, clip, out_full, up_mine, down_mine, top)


def attend_back_kernel(scale, queries, keys, values, probs, mixed, grad_mixed, grads, sum_k, sum_v):
    step = pl.program_id(0)
    tile = queries.shape[1]

    @pl.when(step == 0)
    def _():
        sum_k[...] = jnp.zeros_like(sum_k)
        sum_v[...] = jnp.zeros_like(sum_v)

    here = pl.ds(pl.multiple_of(step * tile, tile), tile)
    for h in range(2):
        cols = slice(h * HD, (h + 1) * HD)
        mine, back, low = queries[h], grad_mixed[:, cols], probs[h]
        row_total = jnp.sum(
            back.astype(F32) * mixed[:, cols].astype(F32), axis=-1, keepdims=True
        )
        grad_probs = lax.dot_general(back, values[h], NT, preferred_element_type=F32)
        grad_scores = (low.astype(F32) * (grad_probs - row_total)).astype(BF16)
        sum_v[h] += lax.dot_general(low, back, TN, preferred_element_type=F32)
        sum_k[h] += lax.dot_general(grad_scores, mine, TN, preferred_element_type=F32)
        grad_q = jnp.dot(grad_scores, keys[h], preferred_element_type=F32) * scale
        grads[here, cols] = grad_q.astype(BF16)

    @pl.when(step == pl.num_programs(0) - 1)
    def _():
        for h in range(2):
            grads[:, 160 + h * HD : 160 + (h + 1) * HD] = (sum_k[h] * scale).astype(BF16)
            grads[:, 320 + h * HD : 320 + (h + 1) * HD] = sum_v[h].astype(BF16)


def attend_back(heads, probs, mixed, grad_mixed, tile):
    rows = heads.shape[1]
    return pl.pallas_call(
        functools.partial(attend_back_kernel, HD**-0.5),
        grid=(rows // tile,),
        in_specs=[
            pl.BlockSpec((2, tile, HD), lambda i: (0, i, 0)),
            pl.BlockSpec((2, rows, HD), lambda i: (1, 0, 0)),
            pl.BlockSpec((2, rows, HD), lambda i: (2, 0, 0)),
            pl.BlockSpec((2, tile, rows), lambda i: (0, i, 0)),
            pl.BlockSpec((tile, 160), lambda i: (i, 0)),
            pl.BlockSpec((tile, 160), lambda i: (i, 0)),
        ],
        out_specs=pl.BlockSpec((rows, 480), lambda i: (0, 0)),
        out_shape=jax.ShapeDtypeStruct((rows, 480), BF16),
        scratch_shapes=[
            pltpu.VMEM((2, rows, HD), F32),
            pltpu.VMEM((2, rows, HD), F32),
        ],
        compiler_params=pltpu.CompilerParams(vmem_limit_bytes=48 << 20),
        cost_estimate=pl.CostEstimate(
            flops=16 * rows * rows * 256, bytes_accessed=16 << 20, transcendentals=0
        ),
    )(heads, heads, heads, probs, mixed, grad_mixed)


def dot(a, b):
    return jnp.dot(a, b, preferred_element_type=F32)


def dot_nt(a, b):
    return lax.dot_general(a, b, NT, preferred_element_type=F32)


def dot_tn(a, b):
    return lax.dot_general(a, b, TN, preferred_element_type=F32)


def rejoin_rows(part, y, c, zl):
    pieces = part.astype(BF16).reshape((4, part.shape[0] // 4) + part.shape[1:])
    total = pick(pieces, y).astype(F32)
    for dy in (2, 1, 3):
        total = total + along_y(pick(pieces, (y + dy) % 4), dy).astype(F32)
    total = sum_four(total.astype(BF16), along_z).astype(BF16)
    other = to_sibling(total)
    total = jnp.where(c == zl, total, other)
    blocks = [total] + [along_y(total, dy) for dy in (1, 2, 3)]
    held = place(blocks, [(y - dy) % 4 for dy in range(4)])
    return held.reshape((-1,) + held.shape[2:]).astype(F32)


def rejoin_columns(part, y, c, x, zl):
    depth = part.shape[0] // 32
    pieces = part.astype(BF16).reshape(8, 4, depth, part.shape[1])
    total = pick(pieces, y, 1).astype(F32)
    for dy in (2, 1, 3):
        total = total + along_y(pick(pieces, (y + dy) % 4, 1), dy).astype(F32)
    total = sum_four(total.astype(BF16), along_z).astype(BF16)
    near = [pick(total, 2 * x + zl)]
    near += [along_x(pick(total, 2 * ((x + dx) % 4) + zl), dx) for dx in (1, 2, 3)]
    near = jnp.stack(near)
    far = to_sibling(near)
    blocks, indices = [], []
    for dx in range(4):
        for dc, source in enumerate((near, far)):
            blocks.append(source[dx])
            indices.append(2 * ((x - dx) % 4) + (c ^ dc))
    whole = place(blocks, indices)
    blocks = [whole] + [along_y(whole, dy) for dy in (1, 2, 3)]
    return place(blocks, [(y - dy) % 4 for dy in range(4)])


def per_device(
    tokens,
    lengths,
    w_query,
    w_key,
    w_value,
    w_out,
    w_up,
    w_down,
    b_query,
    b_value,
    b_out,
    b_up,
    b_down,
    gain_attn,
    shift_attn,
    gain_ffn,
    shift_ffn,
    cotangent,
):
    rep, shard = lax.axis_index("rep"), lax.axis_index("shard")
    y, c, x, zl = rep // 4, rep % 2, shard // 2, shard % 2
    rows, width = tokens.shape[1:]

    eight = [b_query, b_value, b_out, b_down, gain_attn, shift_attn, gain_ffn, shift_ffn]
    small = jnp.zeros((16, 640), BF16)
    small = small.at[:8, :160].set(jnp.stack(eight)).at[8].set(b_up)
    known = jnp.full((8, 128), lengths[0], F32)
    (
        h1,
        heads,
        probs,
        mixed,
        attended,
        w_qkv,
        smalls,
        own,
        clip,
        out_full,
        up_mine,
        down_mine,
        top,
    ) = begin(
        tokens[0], w_query, w_key, w_value, small, w_out, w_up, w_down, cotangent[0], known
    )

    (
        middle,
        grad_middle,
        branch,
        out_parts,
        g_w_up,
        g_w_down,
        g_b_up,
        g_vectors,
        grad_mixed,
    ) = middle_part(
        attended,
        own,
        smalls,
        clip,
        out_full.reshape(width, width),
        up_mine.reshape(width, 640),
        down_mine,
        top.reshape(8 * rows, width),
    )
    g_b_up = g_b_up[0]

    def relative(blocks):
        blocks = blocks.reshape(8, rows, width)
        return [
            [pick(blocks, 2 * ((x - dx) % 4) + (c ^ dc)) for dc in range(2)] for dx in range(4)
        ]

    full = smalls[:, :8, :160].transpose(1, 0, 2).reshape(8, width).astype(F32)
    bias_down, gain_one, shift_one = full[3], full[4], full[5]
    mixed = mixed.reshape(8 * rows, 160)
    grad_qkv = attend_back(heads, probs, mixed, grad_mixed.reshape(8 * rows, 160), 384)
    result = scatter_group(relative(out_parts))
    output = cross((middle + result + bias_down).astype(BF16))
    branch_blocks = gather_group(branch)
    branch_all = place(
        [block for both in branch_blocks for block in both],
        [2 * ((x - dx) % 4) + (c ^ dc) for dx in range(4) for dc in range(2)],
    ).reshape(8 * rows, width)
    g_w_out = dot_tn(mixed, branch_all)

    grad_first = scatter_group(relative(dot_nt(grad_qkv, w_qkv).astype(BF16)))
    g_w_qkv = dot_tn(h1.reshape(8 * rows, width), grad_qkv)
    sums = jnp.sum(grad_qkv.astype(F32), axis=0)
    normed_one, inverse_one, _ = norm_fwd(own.astype(F32), gain_one, shift_one)
    grad_ln, g_gain_attn, g_shift_attn = norm_back(grad_first, normed_one, inverse_one, gain_one)
    input_grad = cross(grad_middle + grad_ln)

    grad_down = rejoin_rows(g_w_down, y, c, zl)
    grad_out = rejoin_rows(g_w_out, y, c, zl)
    grad_up = rejoin_columns(g_w_up, y, c, x, zl)
    grad_up = grad_up.transpose(0, 2, 1, 3).reshape(160, 5120).astype(F32)
    three = rejoin_columns(g_w_qkv, y, c, x, zl).reshape(4, 8, 40, 3, 160)
    three = three.transpose(3, 0, 2, 1, 4).reshape(3, 160, width).astype(F32)

    vectors = jnp.stack(
        [g_vectors[0], g_vectors[1], g_gain_attn, g_shift_attn, g_vectors[2], g_vectors[3]]
    )
    vectors = vectors + to_sibling(vectors)
    vectors = sum_four(vectors, along_x)
    sliced = jnp.concatenate([sums[:160], sums[320:], g_b_up])
    packed = jnp.concatenate([vectors.reshape(-1), sliced])
    packed = sum_four(packed, along_y)
    packed = sum_four(packed, along_z)
    sliced = packed[6 * width :]
    sliced = jnp.where(c == zl, sliced, to_sibling(sliced))
    vectors = lax.dynamic_slice_in_dim(packed[: 6 * width].reshape(6, width), shard * 160, 160, 1)
    return (
        output[None],
        input_grad[None],
        three[0],
        three[1],
        three[2],
        grad_out,
        grad_up,
        grad_down,
        sliced[:160],
        sliced[160:320],
        vectors[0],
        sliced[320:],
        vectors[1],
        vectors[2],
        vectors[3],
        vectors[4],
        vectors[5],
    )


def solution(mesh):
    by_clip, matrix, vector = P("rep", "shard", None), P("shard", None), P("shard")
    return jax.shard_map(
        per_device,
        mesh=mesh,
        in_specs=(by_clip, P("rep")) + (matrix,) * 6 + (vector,) * 9 + (by_clip,),
        out_specs=(by_clip, by_clip) + (matrix,) * 6 + (vector,) * 9,
        check_vma=False,
    )
```

```python
import functools

import jax
import jax.numpy as jnp
from jax import lax
from jax.experimental import pallas as pl
from jax.experimental.pallas import tpu as pltpu
from jax.sharding import PartitionSpec as P

H = 16
HD = 80
EPS = 1e-05
AXES = ("rep", "shard")
F32 = jnp.float32
BF16 = jnp.bfloat16
NT = (((1,), (1,)), ((), ()))
TN = (((0,), (0,)), ((), ()))


def flat_index(y, zh, c, x, zl):
    return ((y % 4) * 4 + (zh % 2) * 2 + c % 2) * 8 + (x % 4) * 2 + zl % 2


def pairs(move):
    found = []
    for y in range(4):
        for zh in range(2):
            for c in range(2):
                for x in range(4):
                    for zl in range(2):
                        here = flat_index(y, zh, c, x, zl)
                        found.append((here, flat_index(*move(y, zh, c, x, zl))))
    return found


def send(value, move):
    return lax.ppermute(value, AXES, pairs(move))


def along_x(value, dx):
    return send(value, lambda y, zh, c, x, zl: (y, zh, c, x + dx, zl))


def along_y(value, dy):
    return send(value, lambda y, zh, c, x, zl: (y + dy, zh, c, x, zl))


def along_z(value, dz):
    def move(y, zh, c, x, zl):
        z = (2 * zh + zl + dz) % 4
        return (y, z // 2, c, x, z % 2)

    return send(value, move)


def to_sibling(value):
    return send(value, lambda y, zh, c, x, zl: (y, zh, c + 1, x, zl))


def cross(value):
    return send(value, lambda y, zh, c, x, zl: (y, zh, zl, x, c))


def gather_group(own):
    near = [own] + [along_x(own, dx) for dx in (1, 2, 3)]
    return [[block, to_sibling(block)] for block in near]


def scatter_group(parts):
    total = None
    for dx in (2, 1, 3, 0):
        both = parts[dx][0].astype(F32) + to_sibling(parts[dx][1]).astype(F32)
        if dx > 0:
            both = along_x(both.astype(BF16), -dx).astype(F32)
        total = both if total is None else total + both
    return total


def sum_four(value, along):
    one, two, three = (along(value, step).astype(F32) for step in (1, 2, 3))
    return (value.astype(F32) + two) + (one + three)


def place(blocks, indices):
    held = jnp.zeros((len(blocks),) + blocks[0].shape, blocks[0].dtype)
    for block, index in zip(blocks, indices):
        held = lax.dynamic_update_index_in_dim(held, block, index, 0)
    return held


def pick(array, index, axis=0):
    return lax.dynamic_index_in_dim(array, index, axis, keepdims=False)


def norm_fwd(values, gain, shift):
    center = values - jnp.mean(values, axis=-1, keepdims=True)
    inverse = lax.rsqrt(jnp.mean(center * center, axis=-1, keepdims=True) + EPS)
    normed = center * inverse
    return (normed, inverse, normed * gain + shift)


def norm_back(grad_rows, normed, inverse, gain):
    scaled = grad_rows * gain
    grad_in = inverse * (
        scaled
        - jnp.mean(scaled, axis=-1, keepdims=True)
        - normed * jnp.mean(scaled * normed, axis=-1, keepdims=True)
    )
    return (grad_in, jnp.sum(grad_rows * normed, axis=0), jnp.sum(grad_rows, axis=0))


MESH = pl.DeviceIdType.MESH
VMEM = pl.BlockSpec(memory_space=pltpu.VMEM)
HBM = pl.BlockSpec(memory_space=pl.ANY)


class Net:
    def __init__(self, sent, got, still):
        rep, shard = lax.axis_index("rep"), lax.axis_index("shard")
        self.y, self.zh, self.c = rep // 4, rep // 2 % 2, rep % 2
        self.x, self.zl = shard // 2, shard % 2
        self.me, self.shard = 2 * self.x + self.c, shard
        self.sent, self.got, self.still, self.used, self.started = sent, got, still, 0, []

    def device(self, dx=0, dc=0, dz=0, dy=0):
        z = (2 * self.zh + self.zl + dz) % 4
        return (
            (self.y + dy) % 4 * 4 + z // 2 * 2 + (self.c + dc) % 2,
            (self.x + dx) % 4 * 2 + z % 2,
        )

    def in_pair(self, dx, dz):
        return (
            self.y * 4 + self.zh * 2 + self.c,
            (self.x + dx) % 4 * 2 + (self.zl + dz) % 2,
        )

    def partner(self):
        return (self.y * 4 + self.zh * 2 + self.zl, 2 * self.x + self.c)

    def greet(self, devices):
        barrier = pltpu.get_barrier_semaphore()
        for device in devices:
            pl.semaphore_signal(barrier, inc=1, device_id=device, device_id_type=MESH)
        return lambda: pl.semaphore_wait(barrier, len(devices))

    def reserve(self, count):
        first = self.used
        self.used += count
        return first

    def copy(self, index, source, target, device):
        return pltpu.make_async_remote_copy(
            src_ref=source,
            dst_ref=target,
            send_sem=self.sent.at[index],
            recv_sem=self.got.at[index],
            device_id=device,
            device_id_type=MESH,
        )

    def go(self, source, target, device):
        copy = self.copy(self.reserve(1), source, target, device)
        copy.start()
        self.started.append(copy)
        return copy

    def cross(self, source, target):
        index = self.reserve(1)
        copy = self.copy(index, source, target, self.partner())
        local = pltpu.make_async_copy(source, target, self.still.at[index])

        @pl.when(self.c != self.zl)
        def _():
            copy.start()

        @pl.when(self.c == self.zl)
        def _():
            local.start()

        def arrived():
            @pl.when(self.c != self.zl)
            def _():
                copy.wait_recv()

            @pl.when(self.c == self.zl)
            def _():
                local.wait()

        def left():
            @pl.when(self.c != self.zl)
            def _():
                copy.wait_send()

        return arrived, left

    def all_sent(self):
        for copy in self.started:
            copy.wait_send()


def order(k):
    return 1 + 2 * k - 3 * (k // 2)


def aligned(index, size):
    return pl.ds(pl.multiple_of(index * size, size), size)


def scratch_for(copies):
    return [pltpu.SemaphoreType.DMA((copies,)) for _ in range(3)]


def begin_kernel(
    tokens,
    w_query,
    w_key,
    w_value,
    small,
    w_out,
    w_up,
    w_down,
    cotangent,
    length,
    h1,
    heads,
    probs,
    mixed,
    attended,
    w_qkv,
    smalls,
    own,
    clip,
    out_full,
    up_mine,
    down_mine,
    top,
    gathered,
    cut,
    lens,
    vectors,
    sent,
    got,
    still,
):
    net = Net(sent, got, still)
    x, c, zl, me, shard = net.x, net.c, net.zl, net.me, net.shard
    rows, width = tokens.shape
    plane = [net.device(dx, dc) for dx in range(4) for dc in range(2) if dx or dc]
    across = [net.in_pair(dx, 1) for dx in range(4)]
    everyone = plane + across + [(net.y * 4 + net.zh * 2 + 1 - c, 2 * x + 1 - zl)]
    wait = net.greet(everyone)
    for block in range(8):
        cols = slice(160 * block, 160 * block + 160)
        cut[block, :, :160] = w_query[:, cols]
        cut[block, :, 160:320] = w_key[:, cols]
        cut[block, :, 320:] = w_value[:, cols]
    wait()

    token_arrived, token_left = net.cross(tokens, gathered.at[2 * x + zl])
    base = net.reserve(4)

    def token_send(k, source):
        dx = order(k)
        return net.copy(base + dx, source, gathered.at[me], net.device(dx))

    @pl.when(c == zl)
    def _():
        for k in range(3):
            token_send(k, tokens).start()

    @pl.when(c == 0)
    def _():
        lens[0] = length[...]

    @pl.when(c == 1)
    def _():
        lens[1] = length[...]

    lens_copy = net.go(length, lens.at[c], net.device(0, 1))
    arriving = []
    for dx in (0, 1, 3, 2):
        for dz in range(2):
            if dx or dz:
                device = net.in_pair(dx, dz)
                arriving.append(net.go(small, smalls.at[shard], device))
                target = 2 * ((x + dx) % 4) + c
                arriving.append(net.go(cut.at[target], w_qkv.at[aligned(shard, 160)], device))
    smalls[shard] = small[...]
    w_qkv[aligned(shard, 160)] = cut[me]
    token_arrived()

    @pl.when(c != zl)
    def _():
        for k in range(3):
            token_send(k, gathered.at[me]).start()

    sibling = net.device(0, 1)
    own_over = net.go(gathered.at[me], gathered.at[me], sibling)
    out_arrived, out_left = net.cross(w_out, out_full.at[2 * x + zl])
    top_arrived, top_left = net.cross(cotangent, top.at[2 * x + zl])
    down_arrived, down_left = net.cross(w_down, down_mine)
    own[...] = gathered[me]

    for copy in arriving:
        copy.wait_recv()
    for block in range(8):
        vectors[:, 160 * block : 160 * block + 160] = smalls[block, :8, :160].astype(F32)
    gain, shift = vectors[4:5, :], vectors[5:6, :]
    bias_q = smalls[me, 0:1, :160].astype(F32)
    bias_v = smalls[me, 1:2, :160].astype(F32)

    def project(slot):
        values = gathered[slot].astype(F32)
        center = values - jnp.mean(values, axis=-1, keepdims=True)
        inverse = lax.rsqrt(jnp.mean(center * center, axis=-1, keepdims=True) + EPS)
        normed = (center * inverse * gain + shift).astype(BF16)
        h1[slot] = normed
        made = jnp.dot(normed, w_qkv[...], preferred_element_type=F32)
        here = aligned(slot, rows)
        for h in range(2):
            cols = slice(h * HD, (h + 1) * HD)
            heads[h, here, :] = (made[:, cols] + bias_q[:, cols]).astype(BF16)
            heads[2 + h, here, :] = made[:, 160 + h * HD : 240 + h * HD].astype(BF16)
            heads[4 + h, here, :] = (
                made[:, 320 + h * HD : 400 + h * HD] + bias_v[:, cols]
            ).astype(BF16)

    project(me)
    own_over.wait_recv()
    project(2 * x + 1 - c)
    over = net.reserve(4)

    def passed(dx, slot):
        return net.copy(over + dx, gathered.at[slot], gathered.at[slot], sibling)

    @pl.loop(0, 3)
    def _(k):
        dx = order(k)
        from_x = (x - dx + 4) % 4
        token_send(k, gathered.at[me]).wait_recv()
        passed(dx, 2 * from_x + c).start()
        project(2 * from_x + c)
        passed(dx, 2 * from_x + c).wait_recv()
        project(2 * from_x + 1 - c)

    later = []
    top_arrived()
    for dx in (1, 3, 2):
        later.append((net.go(top.at[me], top.at[me], net.device(dx)), top, dx))
    out_arrived()
    for dx in (1, 3, 2):
        later.append((net.go(out_full.at[me], out_full.at[me], net.device(dx)), out_full, dx))
    last = [
        net.go(top.at[me], top.at[me], sibling),
        net.go(out_full.at[me], out_full.at[me], sibling),
    ]
    for dx in (0, 1, 3, 2):
        for dz in range(2):
            if dx or dz:
                target = 2 * ((x + dx) % 4) + c
                source = w_up.at[:, pl.ds(pl.multiple_of(target * 640, 128), 640)]
                last.append(net.go(source, up_mine.at[shard], net.in_pair(dx, dz)))
    mine_up = pltpu.make_async_copy(
        w_up.at[:, pl.ds(pl.multiple_of(me * 640, 128), 640)],
        up_mine.at[shard],
        still.at[net.reserve(1)],
    )
    mine_up.start()

    lens_copy.wait_recv()
    clip[...] = lens[zl]
    clip_length = clip[0:1, 0:1]
    position = lax.broadcasted_iota(jnp.int32, (1, 8 * rows), 1).astype(F32)
    mask = jnp.where(position < clip_length, 0.0, -1e30)

    def attend_rows(to_x):
        here = aligned(to_x, 2 * rows)
        for h in range(2):
            cols = slice(h * HD, (h + 1) * HD)
            scores = lax.dot_general(heads[h, here, :], heads[2 + h], NT, preferred_element_type=F32)
            scores = scores * HD**-0.5 + mask
            risen = jnp.exp(scores - jnp.max(scores, axis=-1, keepdims=True))
            share = 1.0 / jnp.sum(risen, axis=-1, keepdims=True)
            low = (risen * share).astype(BF16)
            probs[h, here, :] = low
            made = jnp.dot(low, heads[4 + h], preferred_element_type=F32).astype(BF16)
            mixed[2 * to_x, :, cols] = made[:rows]
            mixed[2 * to_x + 1, :, cols] = made[rows:]

    mixed_base = net.reserve(8)

    def mixed_send(dx, dc):
        slot = 2 * ((x + dx) % 4) + (c + dc) % 2
        return net.copy(
            mixed_base + 2 * dx + dc, mixed.at[slot], attended.at[me], net.device(dx, dc)
        )

    @pl.loop(1, 5)
    def _(step):
        dx = step % 4
        attend_rows((x + dx) % 4)
        mixed_send(dx, 1).start()

        @pl.when(dx != 0)
        def _():
            mixed_send(dx, 0).start()

    attended[me] = mixed[me]
    for copy, array, dx in later:
        copy.wait_recv()
        slot = 2 * ((x - dx + 4) % 4) + c
        last.append(net.go(array.at[slot], array.at[slot], sibling))

    for dx in range(4):
        for dc in range(2):
            if dx or dc:
                mixed_send(dx, dc).wait()
    for copy in last:
        copy.wait_recv()
    mine_up.wait()
    down_arrived()
    for left in (token_left, out_left, top_left, down_left):
        left()
    for k in range(3):
        token_send(k, gathered.at[me]).wait_send()
        dx = order(k)
        passed(dx, me).wait_send()
    net.all_sent()


def begin(tokens, w_query, w_key, w_value, small, w_out, w_up, w_down, cotangent, length):
    rows, width = tokens.shape

    def shape(*dims):
        return jax.ShapeDtypeStruct(dims, BF16)

    return pl.pallas_call(
        begin_kernel,
        in_specs=[VMEM] * 5 + [HBM] * 4 + [VMEM],
        out_specs=[VMEM] * 9 + [HBM] * 4,
        out_shape=[
            shape(8, rows, width),
            shape(6, 8 * rows, HD),
            shape(2, 8 * rows, 8 * rows),
            shape(8, rows, 160),
            shape(8, rows, 160),
            shape(width, 480),
            shape(8, 16, 640),
            shape(rows, width),
            jax.ShapeDtypeStruct((8, 128), F32),
            shape(8, 160, width),
            shape(8, 160, 640),
            shape(640, width),
            shape(8, rows, width),
        ],
        scratch_shapes=[
            pltpu.VMEM((8, rows, width), BF16),
            pltpu.VMEM((8, 160, 480), BF16),
            pltpu.VMEM((2, 8, 128), F32),
            pltpu.VMEM((8, width), F32),
        ]
        + scratch_for(80),
        compiler_params=pltpu.CompilerParams(
            collective_id=0, has_side_effects=True, vmem_limit_bytes=58 << 20
        ),
    )(tokens, w_query, w_key, w_value, small, w_out, w_up, w_down, cotangent, length)


def middle_kernel(
    attended,
    own,
    smalls,
    clip,
    out_full,
    up_mine,
    down_mine,
    top,
    result,
    grad_middle,
    branch,
    out_sums,
    g_up,
    g_down,
    g_up_bias,
    g_vectors,
    grad_mixed,
    vectors,
    middle,
    second,
    masked,
    active,
    hidden,
    parts,
    over,
    sums,
    arrived,
    out_parts,
    out_over,
    joined,
    by_head,
    sent,
    got,
    still,
):
    net = Net(sent, got, still)
    x, c, me = net.x, net.c, net.me
    rows, width = own.shape
    wait = net.greet([net.device(dx, dc) for dx in range(4) for dc in range(2) if dx or dc])
    for block in range(8):
        vectors[:, 160 * block : 160 * block + 160] = smalls[block, :8, :160].astype(F32)
    bias_up = smalls[me, 8:9, :].astype(F32)
    mine = aligned(me, rows)
    for block in range(8):
        joined[:, 160 * block : 160 * block + 160] = attended[block]
    made = jnp.dot(joined[...], out_full[...], preferred_element_type=F32)
    middle[...] = own[...].astype(F32) + made + vectors[2:3, :]

    def normalised():
        values = middle[...]
        center = values - jnp.mean(values, axis=-1, keepdims=True)
        inverse = lax.rsqrt(jnp.mean(center * center, axis=-1, keepdims=True) + EPS)
        return center * inverse, inverse

    second[mine, :] = (normalised()[0] * vectors[6:7, :] + vectors[7:8, :]).astype(BF16)
    wait()

    near, pass_on, swap, add, out_swap = (net.reserve(4) for _ in range(5))

    def out_copy(dx, to_x):
        source = out_parts.at[aligned(2 * to_x + 1 - c, rows)]
        return net.copy(out_swap + dx, source, out_over.at[to_x], net.device(0, 1))

    def near_copy(dx):
        return net.copy(near + dx, second.at[mine], second.at[mine], net.device(dx))

    def pass_copy(dx, slot):
        here = second.at[aligned(slot, rows)]
        return net.copy(pass_on + dx, here, here, net.device(0, 1))

    def swap_copy(dx, to_x):
        source = parts.at[aligned(2 * to_x + 1 - c, rows)]
        return net.copy(swap + dx, source, over.at[to_x], net.device(0, 1))

    def add_copy(dx, to_x):
        return net.copy(add + dx, sums.at[to_x], arrived.at[dx], net.device(4 - dx))

    for dx in (1, 3, 2):
        near_copy(dx).start()

    @pl.loop(0, 4)
    def _(k):
        dx = k ^ (k >> 1)
        to_x = (x - dx + 4) % 4

        @pl.when(dx != 0)
        def _():
            near_copy(dx).wait_recv()

        pass_copy(dx, 2 * to_x + c).start()
        here = aligned(to_x, 2 * rows)
        position = lax.broadcasted_iota(jnp.int32, (2 * rows, 1), 0) + to_x * 2 * rows
        live = position.astype(F32) < clip[0:1, 0:1]
        low_top = jnp.where(live, top[here, :].astype(F32), 0.0).astype(BF16)
        masked[here, :] = low_top
        grad_act = lax.dot_general(low_top, down_mine[...], NT, preferred_element_type=F32)
        pass_copy(dx, 2 * to_x + c).wait_recv()
        z = jnp.dot(second[here, :], up_mine[...], preferred_element_type=F32) + bias_up
        bell = 0.5 * (1.0 + lax.erf(z * 0.7071067811865476))
        active[here, :] = (z * bell).astype(BF16)
        slope = bell + z * jnp.exp(-0.5 * z * z) * 0.3989422804014327
        grad_z = (grad_act * slope).astype(BF16)
        hidden[here, :] = grad_z
        parts[here, :] = lax.dot_general(
            grad_z, up_mine[...], NT, preferred_element_type=F32
        ).astype(BF16)
        swap_copy(dx, to_x).start()
        out_parts[here, :] = jnp.dot(
            active[here, :], down_mine[...], preferred_element_type=F32
        ).astype(BF16)
        out_copy(dx, to_x).start()
        swap_copy(dx, to_x).wait_recv()

        @pl.when(dx != 0)
        def _():
            kept = parts[aligned(2 * to_x + c, rows), :].astype(F32)
            sums[to_x] = (kept + over[to_x].astype(F32)).astype(BF16)
            add_copy(dx, to_x).start()

    @pl.loop(0, 5)
    def _(i):
        cols = pl.ds(pl.multiple_of(i * 256, 256), 256)
        g_up[cols, :] = lax.dot_general(
            second[:, cols], hidden[...], TN, preferred_element_type=F32
        ).astype(BF16)
        cols = pl.ds(pl.multiple_of(i * 128, 128), 128)
        g_down[cols, :] = lax.dot_general(
            active[:, cols], masked[...], TN, preferred_element_type=F32
        ).astype(BF16)

    for dx in range(4):
        to_x = (x - dx + 4) % 4
        out_copy(dx, to_x).wait_recv()
        kept = out_parts[aligned(2 * to_x + c, rows), :].astype(F32) + out_over[to_x].astype(F32)
        if dx:
            out_sums[to_x] = kept.astype(BF16)
        else:
            result[...] = middle[...] + kept + vectors[3:4, :]
    g_up_bias[...] = jnp.sum(hidden[...].astype(F32), axis=0, keepdims=True)
    grad_second = parts[mine, :].astype(F32) + over[x].astype(F32)
    for dx in (1, 3, 2):
        add_copy(dx, (x - dx + 4) % 4).wait_recv()
        grad_second = grad_second + arrived[dx].astype(F32)
    normed, inverse = normalised()
    scaled = grad_second * vectors[6:7, :]
    back = inverse * (
        scaled
        - jnp.mean(scaled, axis=-1, keepdims=True)
        - normed * jnp.mean(scaled * normed, axis=-1, keepdims=True)
    )
    top_own = masked[mine, :].astype(F32)
    total = top_own + back
    grad_middle[...] = total
    low = total.astype(BF16)
    branch[...] = low
    grad_attended = lax.dot_general(low, out_full[...], NT, preferred_element_type=F32)
    grad_attended = grad_attended.astype(BF16)
    for block in range(8):
        by_head[block] = grad_attended[:, 160 * block : 160 * block + 160]
    mixing = []
    for dx in (2, 1, 3, 0):
        for dc in (1, 0):
            if dx or dc:
                slot = 2 * ((x + dx) % 4) + (c + dc) % 2
                mixing.append(net.go(by_head.at[slot], grad_mixed.at[me], net.device(dx, dc)))
    grad_mixed[me] = by_head[me]
    g_vectors[0:1, :] = jnp.sum(low.astype(F32), axis=0, keepdims=True)
    g_vectors[1:2, :] = jnp.sum(top_own, axis=0, keepdims=True)
    g_vectors[2:3, :] = jnp.sum(grad_second * normed, axis=0, keepdims=True)
    g_vectors[3:4, :] = jnp.sum(grad_second, axis=0, keepdims=True)
    for copy in mixing:
        copy.wait_recv()
    for dx in range(4):
        to_x = (x - dx + 4) % 4
        pass_copy(dx, 2 * to_x + c).wait_send()
        swap_copy(dx, to_x).wait_send()
        out_copy(dx, to_x).wait_send()
        if dx:
            near_copy(dx).wait_send()
            add_copy(dx, to_x).wait_send()
    net.all_sent()


def middle_part(attended, own, smalls, clip, out_full, up_mine, down_mine, top):
    rows, width = own.shape

    def shape(*dims, dtype=BF16):
        return jax.ShapeDtypeStruct(dims, dtype)

    def buffer(*dims, dtype=BF16):
        return pltpu.VMEM(dims, dtype)

    return pl.pallas_call(
        middle_kernel,
        in_specs=[VMEM] * 8,
        out_specs=[VMEM] * 9,
        out_shape=[
            shape(rows, width, dtype=F32),
            shape(rows, width, dtype=F32),
            shape(rows, width),
            shape(4, rows, width),
            shape(width, 640),
            shape(640, width),
            shape(1, 640, dtype=F32),
            shape(4, width, dtype=F32),
            shape(8, rows, 160),
        ],
        scratch_shapes=[
            buffer(8, width, dtype=F32),
            buffer(rows, width, dtype=F32),
            buffer(8 * rows, width),
            buffer(8 * rows, width),
            buffer(8 * rows, 640),
            buffer(8 * rows, 640),
            buffer(8 * rows, width),
            buffer(4, rows, width),
            buffer(4, rows, width),
            buffer(4, rows, width),
            buffer(8 * rows, width),
            buffer(4, rows, width),
            buffer(rows, width),
            buffer(8, rows, 160),
        ]
        + scratch_for(32),
        compiler_params=pltpu.CompilerParams(
            collective_id=1, has_side_effects=True, vmem_limit_bytes=60 << 20
        ),
    )(attended, own, smalls, clip, out_full, up_mine, down_mine, top)


def piece_start(index):
    return pl.multiple_of(48 * index - 32 * (index // 3), 16)


def column_flow(net, source, r1, s1, r2, s2, planes, landed, place_of):
    y, z, x, c = net.y, 2 * net.zh + net.zl, net.x, net.c
    b1, b2, b3, b4, b5 = (net.reserve(4) for _ in range(5))
    sibling = net.device(0, 1)

    def copy_1(d):
        rows = pl.ds(piece_start((y + d) % 4), 48)
        return net.copy(b1 + d, source.at[:, rows, :], r1.at[d], net.device(dy=d))

    mine = pltpu.make_async_copy(
        source.at[:, pl.ds(piece_start(y), 48), :], r1.at[0], net.still.at[b1]
    )

    def copy_2(d):
        part = s1.at[pl.ds(2 * ((z + d) % 4), 2)]
        return net.copy(b2 + d, part, r2.at[d], net.device(dz=d))

    def copy_3(d):
        return net.copy(b3 + d, s2.at[(z + d) % 2], planes.at[z], net.device(dz=d))

    def copy_4(d):
        target = place_of(landed, 2 * x + c)
        return net.copy(b4 + d, planes.at[(x + d) % 4], target, net.device(d))

    def copy_5(d):
        here = place_of(landed, 2 * ((x - d + 4) % 4) + c)
        return net.copy(b5 + d, here, here, sibling)

    def first():
        mine.start()
        for d in (2, 1, 3):
            copy_1(d).start()

    def second():
        mine.wait()
        for d in (1, 2, 3):
            copy_1(d).wait_recv()
        total = r1[0].astype(F32)
        for d in (1, 2, 3):
            total = total + r1[d].astype(F32)
        s1[...] = total.astype(BF16)
        for d in (2, 1, 3):
            copy_2(d).start()

    def third():
        total = s1[pl.ds(2 * z, 2)].astype(F32)
        for d in (1, 2, 3):
            copy_2(d).wait_recv()
            total = total + r2[d].astype(F32)
        s2[...] = total.astype(BF16)
        for d in (2, 1, 3):
            copy_3(d).start()
        planes[z] = s2[z % 2]

    def fourth():
        for d in (1, 2, 3):
            copy_3(d).wait_recv()
        for d in (2, 1, 3):
            copy_4(d).start()
        place_of(landed, 2 * x + c)[...] = planes[x]
        copy_5(0).start()

    def fifth():
        for d in (1, 3, 2):
            copy_4(d).wait_recv()
            copy_5(d).start()
        for d in range(4):
            copy_5(d).wait_recv()

    def sent():
        for d in range(4):
            copy_5(d).wait_send()
        for d in (1, 2, 3):
            for copy in (copy_1, copy_2, copy_3, copy_4):
                copy(d).wait_send()

    return first, second, third, fourth, fifth, sent


def share_over_y(net, whole, final, half_of):
    y = net.y
    near, over = net.reserve(4), net.reserve(4)
    own = pltpu.make_async_copy(whole, final.at[y], net.still.at[near])

    def copy(d):
        return net.copy(near + d, half_of(whole), half_of(final.at[y]), net.device(dy=d))

    def forward(d):
        here = half_of(final.at[(y - d + 4) % 4])
        return net.copy(over + d, here, here, net.device(0, 1))

    def first():
        own.start()
        for d in (2, 1, 3):
            copy(d).start()

    def second():
        for d in (1, 3, 2):
            copy(d).wait_recv()
            forward(d).start()

    def third():
        own.wait()
        for d in (1, 2, 3):
            forward(d).wait_recv()
            forward(d).wait_send()
            copy(d).wait_send()

    return first, second, third


def four_way(net, base, held, position, device_of):
    def copy(d):
        return net.copy(base + d, held.at[position], held.at[position], device_of(d))

    def go():
        for d in (2, 1, 3):
            copy(d).start()

    def total():
        for d in (1, 2, 3):
            copy(d).wait_recv()
        return (held[0].astype(F32) + held[1].astype(F32)) + (
            held[2].astype(F32) + held[3].astype(F32)
        )

    def sent():
        for d in (1, 2, 3):
            copy(d).wait_send()

    return go, total, sent


def finish_kernel(
    heads,
    mixed,
    grad_mixed,
    w_qkv,
    own,
    smalls,
    result,
    grad_middle,
    branch,
    out_sums,
    g_up_bias,
    g_vectors,
    probs,
    h1,
    g_up,
    g_down,
    hb_out,
    vec_out,
    output,
    input_grad,
    fin_up,
    fin_qkv,
    fin_down,
    fin_out,
    branch_all,
    tall,
    prob_buf,
    grads,
    sum_k,
    sum_v,
    give,
    over,
    sums,
    arrived,
    out_arrived,
    final_rows,
    final_grad,
    up_r1,
    up_s1,
    up_r2,
    up_s2,
    up_planes,
    up_landed,
    g_qkv,
    qkv_r1,
    qkv_s1,
    qkv_r2,
    qkv_s2,
    qkv_planes,
    qkv_landed,
    qkv_rows,
    down_r1,
    down_s1,
    down_r2,
    down_l3,
    down_p,
    g_out,
    out_r1,
    out_z,
    out_t,
    head_y,
    head_z,
    head_sib,
    vec_cut,
    vec_1,
    vec_1s,
    vec_2,
    vec_3,
    vectors,
    sent,
    got,
    still,
):
    net = Net(sent, got, still)
    x, y, c, zl, me = net.x, net.y, net.c, net.zl, net.me
    z = 2 * net.zh + zl
    rows, width = own.shape
    sibling = net.device(0, 1)
    wait = net.greet(
        [net.device(dx, dc) for dx in range(4) for dc in range(2) if dx or dc]
        + [net.device(dy=d) for d in (1, 2, 3)]
        + [net.device(dz=d) for d in (1, 2, 3)]
        + [(y * 4 + net.zh * 2 + 1 - c, 2 * x + 1 - zl)]
    )

    tile = 2 * rows
    slots = net.reserve(2)

    def load_probs(i):
        slot = i % 2
        return pltpu.make_async_copy(
            probs.at[:, aligned(i, tile), :], prob_buf.at[slot], still.at[slots + slot]
        )

    load_probs(0).start()
    load_h1 = pltpu.make_async_copy(h1, tall, still.at[net.reserve(1)])
    load_h1.start()
    own_branch = pltpu.make_async_copy(
        branch, branch_all.at[aligned(me, rows)], still.at[net.reserve(1)]
    )
    own_branch.start()
    for block in range(8):
        vectors[:, 160 * block : 160 * block + 160] = smalls[block, :8, :160].astype(F32)
    sum_k[...] = jnp.zeros_like(sum_k)
    sum_v[...] = jnp.zeros_like(sum_v)

    up = column_flow(
        net,
        g_up,
        up_r1,
        up_s1,
        up_r2,
        up_s2,
        up_planes,
        up_landed,
        lambda ref, hb: ref.at[:, pl.ds(pl.multiple_of(hb * 640, 128), 640)],
    )
    three = column_flow(
        net,
        g_qkv,
        qkv_r1,
        qkv_s1,
        qkv_r2,
        qkv_s2,
        qkv_planes,
        qkv_landed,
        lambda ref, hb: ref.at[hb],
    )
    up_share = share_over_y(
        net,
        up_landed,
        fin_up,
        lambda ref: ref.at[:, pl.ds(pl.multiple_of(c * 2560, 128), 2560)],
    )
    three_share = share_over_y(
        net,
        qkv_rows,
        fin_qkv,
        lambda ref: ref.at[:, :, pl.ds(pl.multiple_of(c * 640, 128), 640)],
    )

    d1, d2, d4, d5 = (net.reserve(4) for _ in range(4))
    d3_go, _, d3_sent = four_way(net, d3 := net.reserve(4), down_l3, y, lambda d: net.device(dy=d))
    down_mine = pltpu.make_async_copy(
        g_down.at[aligned(z, 160)], down_r1.at[0], still.at[d1]
    )

    def down_1(d):
        return net.copy(d1 + d, g_down.at[aligned((z + d) % 4, 160)], down_r1.at[d], net.device(dz=d))

    def down_2(d):
        part = down_s1.at[pl.ds(piece_start((y + d) % 4), 48)]
        return net.copy(d2 + d, part, down_r2.at[d], net.device(dy=d))

    def down_4(k, source_z):
        to_z = c + 2 * k
        return pltpu.make_async_remote_copy(
            src_ref=down_p,
            dst_ref=fin_down.at[aligned(source_z, 160)],
            send_sem=sent.at[d4 + k],
            recv_sem=got.at[d4 + source_z],
            device_id=(y * 4 + to_z // 2 * 2 + c, 2 * x + to_z % 2),
            device_id_type=MESH,
        )

    down_local = pltpu.make_async_copy(down_p, fin_down.at[aligned(z, 160)], still.at[d4])

    def down_5(source_z):
        here = fin_down.at[aligned(source_z, 160)]
        return net.copy(d5 + source_z, here, here, sibling)

    e1, e3, e4 = (net.reserve(4) for _ in range(3))
    out_go, out_total, out_sent = four_way(
        net, net.reserve(4), out_z, z, lambda d: net.device(dz=d)
    )

    def out_1(d):
        part = g_out.at[pl.ds(piece_start((y + d) % 4), 48)]
        return net.copy(e1 + d, part, out_r1.at[d], net.device(dy=d))

    def out_3(d):
        return net.copy(e3 + d, out_t, fin_out.at[y], net.device(dy=d))

    out_local = pltpu.make_async_copy(out_t, fin_out.at[y], still.at[e3])

    def out_4(source_y):
        return net.copy(e4 + source_y, fin_out.at[source_y], fin_out.at[source_y], sibling)

    near, pass_on, swap, add, out_add = (net.reserve(4) for _ in range(5))

    def near_copy(dx):
        return net.copy(near + dx, branch, branch_all.at[aligned(me, rows)], net.device(dx))

    def pass_copy(dx):
        here = branch_all.at[aligned(2 * ((x - dx + 4) % 4) + c, rows)]
        return net.copy(pass_on + dx, here, here, sibling)

    def swap_copy(dx, to_x):
        return net.copy(swap + dx, give.at[to_x], over.at[to_x], sibling)

    def add_copy(dx, to_x):
        return net.copy(add + dx, sums.at[to_x], arrived.at[dx], net.device(4 - dx))

    def out_add_copy(dx):
        to_x = (x - dx + 4) % 4
        return net.copy(out_add + dx, out_sums.at[to_x], out_arrived.at[dx], net.device(4 - dx))

    wait()
    for dx in (1, 3, 2):
        near_copy(dx).start()
    up[0]()
    down_mine.start()
    for d in (2, 1, 3):
        down_1(d).start()

    @pl.loop(0, 4)
    def _(i):
        @pl.when(i < 3)
        def _():
            load_probs(i + 1).start()

        load_probs(i).wait()
        here = aligned(i, tile)
        for h in range(2):
            cols = slice(h * HD, (h + 1) * HD)
            back = jnp.concatenate([grad_mixed[2 * i, :, cols], grad_mixed[2 * i + 1, :, cols]])
            seen = jnp.concatenate([mixed[2 * i, :, cols], mixed[2 * i + 1, :, cols]])
            low = prob_buf[i % 2, h]
            row_total = jnp.sum(back.astype(F32) * seen.astype(F32), axis=-1, keepdims=True)
            grad_probs = lax.dot_general(back, heads[4 + h], NT, preferred_element_type=F32)
            grad_scores = (low.astype(F32) * (grad_probs - row_total)).astype(BF16)
            sum_v[h] += lax.dot_general(low, back, TN, preferred_element_type=F32)
            sum_k[h] += lax.dot_general(
                grad_scores, heads[h, here, :], TN, preferred_element_type=F32
            )
            grad_q = jnp.dot(grad_scores, heads[2 + h], preferred_element_type=F32)
            grads[here, cols] = (grad_q * HD**-0.5).astype(BF16)

    for h in range(2):
        grads[:, 160 + h * HD : 160 + (h + 1) * HD] = (sum_k[h] * HD**-0.5).astype(BF16)
        grads[:, 320 + h * HD : 320 + (h + 1) * HD] = sum_v[h].astype(BF16)

    @pl.loop(0, 4)
    def _(k):
        dx = order(k)
        dx = jnp.where(k == 3, 0, dx)
        to_x = (x - dx + 4) % 4
        part = lax.dot_general(
            grads[aligned(to_x, tile), :], w_qkv[...], NT, preferred_element_type=F32
        )
        low, high = part[:rows], part[rows:]
        give[to_x] = jnp.where(c == 0, high, low).astype(BF16)
        swap_copy(dx, to_x).start()
        kept = jnp.where(c == 0, low, high)
        swap_copy(dx, to_x).wait_recv()
        kept = kept + over[to_x].astype(F32)

        @pl.when(dx != 0)
        def _():
            sums[to_x] = kept.astype(BF16)
            add_copy(dx, to_x).start()

        @pl.when(dx == 0)
        def _():
            final_grad[...] = kept

    for dx in (1, 3, 2):
        out_add_copy(dx).start()
    load_h1.wait()

    @pl.loop(0, 2)
    def _(i):
        cols = pl.ds(pl.multiple_of(i * 640, 128), 640)
        made = lax.dot_general(tall[:, cols], grads[...], TN, preferred_element_type=F32)
        g_qkv[pl.ds(4 * i, 4)] = made.astype(BF16).reshape(4, 160, 480)

    three[0]()
    head_y[y] = jnp.zeros((8, 640), F32)
    head_y[y, 0:1, :] = g_up_bias[...]
    column_sums = jnp.sum(grads[...].astype(F32), axis=0, keepdims=True)
    head_y[y, 1:2, :160] = column_sums[:, :160]
    head_y[y, 2:3, :160] = column_sums[:, 320:]
    head_y_go, head_y_total, head_y_sent = four_way(
        net, net.reserve(4), head_y, y, lambda d: net.device(dy=d)
    )
    head_y_go()

    own_branch.wait()
    pass_copy(0).start()
    for dx in (1, 3, 2):
        near_copy(dx).wait_recv()
        pass_copy(dx).start()

    up[1]()
    down_mine.wait()
    total = down_r1[0].astype(F32)
    for d in (1, 2, 3):
        down_1(d).wait_recv()
        total = total + down_r1[d].astype(F32)
    down_s1[...] = total.astype(BF16)
    for d in (2, 1, 3):
        down_2(d).start()

    for dx in range(4):
        pass_copy(dx).wait_recv()
        pass_copy(dx).wait_send()
    load_branch = pltpu.make_async_copy(branch_all, tall, still.at[net.reserve(1)])
    load_branch.start()
    load_branch.wait()
    seen = jnp.concatenate([mixed[block] for block in range(8)])
    g_out[...] = lax.dot_general(seen, tall[...], TN, preferred_element_type=F32).astype(BF16)
    for d in (2, 1, 3):
        out_1(d).start()

    up[2]()
    total = down_s1[pl.ds(piece_start(y), 48), :].astype(F32)
    for d in (1, 2, 3):
        down_2(d).wait_recv()
        total = total + down_r2[d].astype(F32)
    down_l3[y] = total.astype(BF16)
    d3_go()

    grad_first = final_grad[...]
    for dx in (1, 3, 2):
        add_copy(dx, (x - dx + 4) % 4).wait_recv()
        grad_first = grad_first + arrived[dx].astype(F32)
    values = own[...].astype(F32)
    center = values - jnp.mean(values, axis=-1, keepdims=True)
    inverse = lax.rsqrt(jnp.mean(center * center, axis=-1, keepdims=True) + EPS)
    normed = center * inverse
    scaled = grad_first * vectors[4:5, :]
    back = inverse * (
        scaled
        - jnp.mean(scaled, axis=-1, keepdims=True)
        - normed * jnp.mean(scaled * normed, axis=-1, keepdims=True)
    )
    final_grad[...] = grad_middle[...] + back
    grad_arrived, grad_left = net.cross(final_grad, input_grad)
    gain = jnp.sum(grad_first * normed, axis=0, keepdims=True)
    shift = jnp.sum(grad_first, axis=0, keepdims=True)
    for block in range(8):
        cols = slice(160 * block, 160 * block + 160)
        here = vec_cut.at[block // 2, block % 2]
        here[0:4, :] = g_vectors[:, cols]
        here[4:5, :] = gain[:, cols]
        here[5:6, :] = shift[:, cols]
        here[6:8, :] = jnp.zeros((2, 160), F32)
    v1 = net.reserve(8)

    def vec_copy(dx, dc):
        return net.copy(
            v1 + 2 * dx + dc, vec_cut.at[(x + dx) % 4], vec_1.at[me], net.device(dx, dc)
        )

    others = [(dx, dc) for dx in (2, 1, 3, 0) for dc in (1, 0) if dx or dc]
    for dx, dc in others:
        vec_copy(dx, dc).start()
    vec_1[me] = vec_cut[x]

    total = g_out[pl.ds(piece_start(y), 48), :].astype(F32)
    for d in (1, 2, 3):
        out_1(d).wait_recv()
        total = total + out_r1[d].astype(F32)
    out_z[z] = total.astype(BF16)
    out_go()
    up[3]()
    for d in (1, 2, 3):
        net.copy(d3 + d, down_l3.at[y], down_l3.at[y], net.device(dy=d)).wait_recv()
    for i in range(3):
        down_p[48 * i : 48 * i + 48, :] = down_l3[i]
    down_p[144:160, :] = down_l3[3, 32:48, :]
    for k in range(2):

        @pl.when(c + 2 * k != z)
        def _():
            down_4(k, z).start()

    @pl.when(c == zl)
    def _():
        down_local.start()

    three[1]()
    head_z[z] = head_y_total()
    head_z_go, head_z_total, head_z_sent = four_way(
        net, net.reserve(4), head_z, z, lambda d: net.device(dz=d)
    )
    head_z_go()
    for dx, dc in others:
        vec_copy(dx, dc).wait_recv()
    total = vec_1[0]
    for block in range(1, 8):
        total = total + vec_1[block]
    vec_1s[...] = total
    v2 = net.reserve(4)

    def vec_z(d):
        return net.copy(v2 + d, vec_1s.at[(z + d) % 2], vec_2.at[z], net.device(dz=d))

    for d in (2, 1, 3):
        vec_z(d).start()
    vec_2[z] = vec_1s[zl]
    out_t[...] = out_total().astype(BF16)

    @pl.when(c == zl)
    def _():
        out_local.start()
        for d in (2, 1, 3):
            out_3(d).start()

    up[4]()
    up_share[0]()
    three[2]()

    total = result[...]
    for dx in (1, 3, 2):
        out_add_copy(dx).wait_recv()
        total = total + out_arrived[dx].astype(F32)
    final_rows[...] = total.astype(BF16)
    output_arrived, output_left = net.cross(final_rows, output)

    head_sib[0] = head_z_total()
    head_copy = net.go(head_sib.at[0], head_sib.at[1], sibling)
    for d in (1, 2, 3):
        vec_z(d).wait_recv()
    vec_3[y] = (vec_2[0] + vec_2[1]) + (vec_2[2] + vec_2[3])
    vec_y_go, vec_y_total, vec_y_sent = four_way(
        net, net.reserve(4), vec_3, y, lambda d: net.device(dy=d)
    )
    vec_y_go()

    @pl.when(c == zl)
    def _():
        down_local.wait()
        down_5(z).start()
        for d in (1, 2, 3):
            source_z = (z + d) % 4
            down_4(0, source_z).wait_recv()
            down_5(source_z).start()
        out_local.wait()
        out_4(y).start()
        for d in (1, 2, 3):
            out_3(d).wait_recv()
            out_4((y + 4 - d) % 4).start()

    three[3]()
    three[4]()
    for block in range(8):
        cols = slice(160 * block, 160 * block + 160)
        for k in range(3):
            qkv_rows[k, :, cols] = qkv_landed[block, :, 160 * k : 160 * k + 160]
    three_share[0]()
    up_share[1]()
    head_copy.wait_recv()
    hb_out[...] = jnp.where(c == zl, head_sib[0], head_sib[1])
    vec_out[...] = vec_y_total()
    three_share[1]()

    @pl.when(c == zl)
    def _():
        for i in range(4):
            down_5(i).wait_send()
            out_4(i).wait_send()
        for d in (1, 2, 3):
            out_3(d).wait_send()

    @pl.when(c != zl)
    def _():
        for i in range(4):
            down_5(i).wait_recv()
            out_4(i).wait_recv()

    for k in range(2):

        @pl.when(c + 2 * k != z)
        def _():
            down_4(k, z).wait_send()

    up_share[2]()
    three_share[2]()
    grad_arrived()
    grad_left()
    output_arrived()
    output_left()
    for done in (up[5], three[5], d3_sent, out_sent, head_y_sent, head_z_sent, vec_y_sent):
        done()
    for d in (1, 2, 3):
        down_1(d).wait_send()
        down_2(d).wait_send()
        out_1(d).wait_send()
        vec_z(d).wait_send()
        near_copy(d).wait_send()
        add_copy(d, (x - d + 4) % 4).wait_send()
        out_add_copy(d).wait_send()
    for d in range(4):
        swap_copy(d, (x - d + 4) % 4).wait_send()
    for dx, dc in others:
        vec_copy(dx, dc).wait_send()
    net.all_sent()


def finish(
    heads,
    mixed,
    grad_mixed,
    w_qkv,
    own,
    smalls,
    result,
    grad_middle,
    branch,
    out_sums,
    g_up_bias,
    g_vectors,
    probs,
    h1,
    g_up,
    g_down,
):
    rows, width = own.shape

    def shape(*dims, dtype=BF16):
        return jax.ShapeDtypeStruct(dims, dtype)

    def buffer(*dims, dtype=BF16):
        return pltpu.VMEM(dims, dtype)

    def column_buffers(columns):
        return [
            buffer(4, 8, 48, columns),
            buffer(8, 48, columns),
            buffer(4, 2, 48, columns),
            buffer(2, 48, columns),
            buffer(4, 48, columns),
        ]

    return pl.pallas_call(
        finish_kernel,
        in_specs=[VMEM] * 12 + [HBM] * 4,
        out_specs=[VMEM] * 2 + [HBM] * 7,
        out_shape=[
            shape(8, 640, dtype=F32),
            shape(8, 160, dtype=F32),
            shape(rows, width),
            shape(rows, width, dtype=F32),
            shape(4, 48, 5120),
            shape(4, 3, 48, width),
            shape(640, width),
            shape(4, 48, width),
            shape(8 * rows, width),
        ],
        scratch_shapes=[
            buffer(8 * rows, width),
            buffer(2, 2, 2 * rows, 8 * rows),
            buffer(8 * rows, 480),
            buffer(2, 8 * rows, HD, dtype=F32),
            buffer(2, 8 * rows, HD, dtype=F32),
            buffer(4, rows, width),
            buffer(4, rows, width),
            buffer(4, rows, width),
            buffer(4, rows, width),
            buffer(4, rows, width),
            buffer(rows, width),
            buffer(rows, width, dtype=F32),
        ]
        + column_buffers(640)
        + [buffer(48, 5120), buffer(8, 160, 480)]
        + column_buffers(480)
        + [
            buffer(8, 48, 480),
            buffer(3, 48, width),
            buffer(4, 160, width),
            buffer(160, width),
            buffer(4, 48, width),
            buffer(4, 48, width),
            buffer(160, width),
            buffer(160, width),
            buffer(4, 48, width),
            buffer(4, 48, width),
            buffer(48, width),
            buffer(4, 8, 640, dtype=F32),
            buffer(4, 8, 640, dtype=F32),
            buffer(2, 8, 640, dtype=F32),
            buffer(4, 2, 8, 160, dtype=F32),
            buffer(8, 2, 8, 160, dtype=F32),
            buffer(2, 8, 160, dtype=F32),
            buffer(4, 8, 160, dtype=F32),
            buffer(4, 8, 160, dtype=F32),
            buffer(8, width, dtype=F32),
        ]
        + scratch_for(192),
        compiler_params=pltpu.CompilerParams(
            collective_id=2, has_side_effects=True, vmem_limit_bytes=62 << 20
        ),
    )(
        heads,
        mixed,
        grad_mixed,
        w_qkv,
        own,
        smalls,
        result,
        grad_middle,
        branch,
        out_sums,
        g_up_bias,
        g_vectors,
        probs,
        h1,
        g_up,
        g_down,
    )


def per_device(
    tokens,
    lengths,
    w_query,
    w_key,
    w_value,
    w_out,
    w_up,
    w_down,
    b_query,
    b_value,
    b_out,
    b_up,
    b_down,
    gain_attn,
    shift_attn,
    gain_ffn,
    shift_ffn,
    cotangent,
):
    rep, shard = lax.axis_index("rep"), lax.axis_index("shard")
    y, c, x, zl = rep // 4, rep % 2, shard // 2, shard % 2
    rows, width = tokens.shape[1:]

    eight = [b_query, b_value, b_out, b_down, gain_attn, shift_attn, gain_ffn, shift_ffn]
    small = jnp.zeros((16, 640), BF16)
    small = small.at[:8, :160].set(jnp.stack(eight)).at[8].set(b_up)
    known = jnp.full((8, 128), lengths[0], F32)
    (
        h1,
        heads,
        probs,
        mixed,
        attended,
        w_qkv,
        smalls,
        own,
        clip,
        out_full,
        up_mine,
        down_mine,
        top,
    ) = begin(
        tokens[0], w_query, w_key, w_value, small, w_out, w_up, w_down, cotangent[0], known
    )

    (
        result,
        grad_middle,
        branch,
        out_sums,
        g_up,
        g_down,
        g_up_bias,
        g_vectors,
        grad_mixed,
    ) = middle_part(
        attended,
        own,
        smalls,
        clip,
        out_full.reshape(width, width),
        up_mine.reshape(width, 640),
        down_mine,
        top.reshape(8 * rows, width),
    )
    hb_out, vec_out, output, input_grad, fin_up, fin_qkv, fin_down, fin_out, _ = finish(
        heads,
        mixed,
        grad_mixed,
        w_qkv,
        own,
        smalls,
        result,
        grad_middle,
        branch,
        out_sums,
        g_up_bias,
        g_vectors,
        probs,
        h1.reshape(8 * rows, width),
        g_up.reshape(8, 160, 640),
        g_down,
    )

    def whole(pieces):
        return jnp.concatenate([pieces[0], pieces[1], pieces[2], pieces[3, 32:]]).astype(F32)

    return (
        output[None],
        input_grad[None],
        whole(fin_qkv[:, 0]),
        whole(fin_qkv[:, 1]),
        whole(fin_qkv[:, 2]),
        whole(fin_out),
        whole(fin_up),
        fin_down.astype(F32),
        hb_out[1, :160],
        hb_out[2, :160],
        vec_out[0],
        hb_out[0],
        vec_out[1],
        vec_out[4],
        vec_out[5],
        vec_out[2],
        vec_out[3],
    )


def solution(mesh):
    by_clip, matrix, vector = P("rep", "shard", None), P("shard", None), P("shard")
    return jax.shard_map(
        per_device,
        mesh=mesh,
        in_specs=(by_clip, P("rep")) + (matrix,) * 6 + (vector,) * 9 + (by_clip,),
        out_specs=(by_clip, by_clip) + (matrix,) * 6 + (vector,) * 9,
        check_vma=False,
    )
```

```python
import jax
import jax.numpy as jnp
from jax import lax
from jax.experimental import pallas as pl
from jax.experimental.pallas import tpu as pltpu
from jax.sharding import PartitionSpec as P

HD = 80
EPS = 1e-05
F32 = jnp.float32
BF16 = jnp.bfloat16
NT = (((1,), (1,)), ((), ()))
TN = (((0,), (0,)), ((), ()))


MESH = pl.DeviceIdType.MESH
VMEM = pl.BlockSpec(memory_space=pltpu.VMEM)
HBM = pl.BlockSpec(memory_space=pl.ANY)


class Net:
    def __init__(self, sent, got, still):
        rep, shard = lax.axis_index("rep"), lax.axis_index("shard")
        self.y, self.zh, self.c = rep // 4, rep // 2 % 2, rep % 2
        self.x, self.zl = shard // 2, shard % 2
        self.me, self.shard = 2 * self.x + self.c, shard
        self.sent, self.got, self.still, self.used, self.started = sent, got, still, 0, []

    def device(self, dx=0, dc=0, dz=0, dy=0):
        z = (2 * self.zh + self.zl + dz) % 4
        return (
            (self.y + dy) % 4 * 4 + z // 2 * 2 + (self.c + dc) % 2,
            (self.x + dx) % 4 * 2 + z % 2,
        )

    def in_pair(self, dx, dz):
        return (
            self.y * 4 + self.zh * 2 + self.c,
            (self.x + dx) % 4 * 2 + (self.zl + dz) % 2,
        )

    def partner(self):
        return (self.y * 4 + self.zh * 2 + self.zl, 2 * self.x + self.c)

    def greet(self, devices):
        barrier = pltpu.get_barrier_semaphore()
        for device in devices:
            pl.semaphore_signal(barrier, inc=1, device_id=device, device_id_type=MESH)
        return lambda: pl.semaphore_wait(barrier, len(devices))

    def reserve(self, count):
        first = self.used
        self.used += count
        return first

    def copy(self, index, source, target, device):
        return pltpu.make_async_remote_copy(
            src_ref=source,
            dst_ref=target,
            send_sem=self.sent.at[index],
            recv_sem=self.got.at[index],
            device_id=device,
            device_id_type=MESH,
        )

    def go(self, source, target, device):
        copy = self.copy(self.reserve(1), source, target, device)
        copy.start()
        self.started.append(copy)
        return copy

    def cross(self, source, target):
        index = self.reserve(1)
        copy = self.copy(index, source, target, self.partner())
        local = pltpu.make_async_copy(source, target, self.still.at[index])

        @pl.when(self.c != self.zl)
        def _():
            copy.start()

        @pl.when(self.c == self.zl)
        def _():
            local.start()

        def arrived():
            @pl.when(self.c != self.zl)
            def _():
                copy.wait_recv()

            @pl.when(self.c == self.zl)
            def _():
                local.wait()

        def left():
            @pl.when(self.c != self.zl)
            def _():
                copy.wait_send()

        return arrived, left

    def all_sent(self):
        for copy in self.started:
            copy.wait_send()


def order(k):
    return 1 + 2 * k - 3 * (k // 2)


def aligned(index, size):
    return pl.ds(pl.multiple_of(index * size, size), size)


def scratch_for(copies):
    return [pltpu.SemaphoreType.DMA((copies,)) for _ in range(3)]


def begin_kernel(
    tokens,
    w_query,
    w_key,
    w_value,
    small,
    up_bias,
    w_out,
    w_up,
    w_down,
    cotangent,
    length,
    h1,
    heads,
    probs,
    mixed,
    attended,
    w_qkv,
    smalls,
    bias_up,
    own,
    clip,
    out_full,
    up_mine,
    down_mine,
    top,
    out_own,
    gathered,
    cut,
    lens,
    vectors,
    sent,
    got,
    still,
):
    net = Net(sent, got, still)
    x, y, c, zh, zl, me, shard = net.x, net.y, net.c, net.zh, net.zl, net.me, net.shard
    rows, width = tokens.shape
    plane = [net.device(dx, dc) for dx in range(4) for dc in range(2) if dx or dc]
    across = [net.in_pair(dx, 1) for dx in range(4)]
    rings = [net.device(dy=d) for d in (1, 2, 3)] + [net.device(dz=d) for d in (1, 2, 3)]
    wait = net.greet(plane + across + rings + [(y * 4 + zh * 2 + 1 - c, 2 * x + 1 - zl)])
    for block in range(8):
        cols = slice(160 * block, 160 * block + 160)
        for half in range(2):
            part = slice(80 * half, 80 * half + 80)
            cut[block, half, :, :160] = w_query[part, cols]
            cut[block, half, :, 160:320] = w_key[part, cols]
            cut[block, half, :, 320:] = w_value[part, cols]
    wait()

    token_arrived, token_left = net.cross(tokens, gathered.at[2 * x + zl])
    base = net.reserve(4)

    def token_send(k, source):
        dx = order(k)
        return net.copy(base + dx, source, gathered.at[me], net.device(dx))

    cut_near, cut_ring, up_near, up_ring = (net.reserve(4) for _ in range(4))

    def cut_copy(d):
        source = cut.at[2 * ((x + d) % 4) + c, zh]
        return net.copy(cut_near + d, source, w_qkv.at[x, zl, zh], net.device(d))

    def cut_share(d):
        here = w_qkv.at[:, zl, zh]
        return net.copy(cut_ring + d, here, here, net.device(dz=d))

    def up_part(index):
        cols = pl.ds(pl.multiple_of(index * 640, 128), 640)
        return w_up.at[aligned(zh, 80), cols]

    def up_copy(d):
        source = up_part(2 * ((x + d) % 4) + c)
        return net.copy(up_near + d, source, up_mine.at[x, zl, zh], net.device(d))

    def up_share(d):
        here = up_mine.at[:, zl, zh]
        return net.copy(up_ring + d, here, here, net.device(dz=d))

    up_local = pltpu.make_async_copy(up_part(me), up_mine.at[x, zl, zh], still.at[up_near])

    for d in (2, 1, 3):
        cut_copy(d).start()

    @pl.when(c == zl)
    def _():
        for k in range(3):
            token_send(k, tokens).start()

    @pl.when(c == 0)
    def _():
        lens[0] = length[...]

    @pl.when(c == 1)
    def _():
        lens[1] = length[...]

    lens_copy = net.go(length, lens.at[c], net.device(0, 1))
    arriving = []
    for dx in (0, 1, 3, 2):
        for dz in range(2):
            if dx or dz:
                arriving.append(net.go(small, smalls.at[shard], net.in_pair(dx, dz)))
    smalls[shard] = small[...]
    w_qkv[x, zl, zh] = cut[me, zh]
    token_arrived()

    @pl.when(c != zl)
    def _():
        for k in range(3):
            token_send(k, gathered.at[me]).start()

    sibling = net.device(0, 1)
    own_over = net.go(gathered.at[me], gathered.at[me], sibling)
    for d in (1, 3, 2):
        cut_copy(d).wait_recv()
    for d in (2, 1, 3):
        cut_share(d).start()
    up_local.start()
    for d in (2, 1, 3):
        up_copy(d).start()
    bias_arrived, bias_left = net.cross(up_bias, bias_up)
    top_arrived, top_left = net.cross(cotangent, top.at[2 * x + zl])
    out_arrived, out_left = net.cross(w_out, out_own)

    down_index, down_ring = net.reserve(1), net.reserve(4)
    down_cross = net.copy(
        down_index, w_down.at[aligned(y, 160)], down_mine.at[aligned(y, 160)], net.partner()
    )
    down_local = pltpu.make_async_copy(w_down, down_mine, still.at[down_index])

    def down_share(d):
        here = down_mine.at[aligned(y, 160)]
        return net.copy(down_ring + d, here, here, net.device(dy=d))

    @pl.when(c == zl)
    def _():
        down_local.start()

    @pl.when(c != zl)
    def _():
        down_cross.start()

    own[...] = gathered[me]
    for copy in arriving:
        copy.wait_recv()
    for block in range(8):
        vectors[:, 160 * block : 160 * block + 160] = smalls[block, :8, :].astype(F32)
    gain, shift = vectors[4:5, :], vectors[5:6, :]
    bias_q = smalls[me, 0:1, :].astype(F32)
    bias_v = smalls[me, 1:2, :].astype(F32)

    def project(slot):
        values = gathered[slot].astype(F32)
        center = values - jnp.mean(values, axis=-1, keepdims=True)
        inverse = lax.rsqrt(jnp.mean(center * center, axis=-1, keepdims=True) + EPS)
        normed = (center * inverse * gain + shift).astype(BF16)
        h1[slot] = normed
        made = jnp.dot(normed, w_qkv[...].reshape(width, 480), preferred_element_type=F32)
        here = aligned(slot, rows)
        for h in range(2):
            cols = slice(h * HD, (h + 1) * HD)
            heads[h, here, :] = (made[:, cols] + bias_q[:, cols]).astype(BF16)
            heads[2 + h, here, :] = made[:, 160 + h * HD : 240 + h * HD].astype(BF16)
            heads[4 + h, here, :] = (
                made[:, 320 + h * HD : 400 + h * HD] + bias_v[:, cols]
            ).astype(BF16)

    top_near, top_over, out_near, out_ring, out_over = (net.reserve(4) for _ in range(5))

    def top_copy(d):
        return net.copy(top_near + d, top.at[me], top.at[me], net.device(d))

    def top_pass(d):
        here = top.at[2 * ((x - d + 4) % 4) + c]
        return net.copy(top_over + d, here, here, sibling)

    half = pl.ds(pl.multiple_of(y % 2 * 640, 128), 640)
    out_piece = out_own.at[aligned(y // 2, 80), half]

    def out_copy(d):
        return net.copy(out_near + d, out_piece, out_full.at[x, c, y // 2, :, half], net.device(d))

    def out_share(d):
        here = out_full.at[:, c, y // 2, :, half]
        return net.copy(out_ring + d, here, here, net.device(dy=d))

    def out_pass(d):
        from_y = (y - d + 4) % 4
        cols = pl.ds(pl.multiple_of(from_y % 2 * 640, 128), 640)
        here = out_full.at[:, c, from_y // 2, :, cols]
        return net.copy(out_over + d, here, here, sibling)

    out_local = pltpu.make_async_copy(
        out_piece, out_full.at[x, c, y // 2, :, half], still.at[out_near]
    )
    out_arrived()
    out_local.start()
    for d in (2, 1, 3):
        out_copy(d).start()
    for d in (1, 3, 2):
        cut_share(d).wait_recv()
    up_local.wait()
    for d in (1, 3, 2):
        up_copy(d).wait_recv()
    for d in (2, 1, 3):
        up_share(d).start()
    project(me)
    out_local.wait()
    for d in (1, 3, 2):
        out_copy(d).wait_recv()
    for d in (2, 1, 3):
        out_share(d).start()
    out_pass(0).start()
    own_over.wait_recv()
    project(2 * x + 1 - c)

    top_arrived()
    for d in (2, 1, 3):
        top_copy(d).start()

    @pl.when(c != zl)
    def _():
        down_cross.wait_recv()
        for d in (2, 1, 3):
            down_share(d).start()

    over = net.reserve(4)

    def passed(dx, slot):
        return net.copy(over + dx, gathered.at[slot], gathered.at[slot], sibling)

    @pl.loop(0, 3)
    def _(k):
        dx = order(k)
        from_x = (x - dx + 4) % 4
        token_send(k, gathered.at[me]).wait_recv()
        passed(dx, 2 * from_x + c).start()
        project(2 * from_x + c)
        passed(dx, 2 * from_x + c).wait_recv()
        project(2 * from_x + 1 - c)

    top_pass(0).start()

    lens_copy.wait_recv()
    clip[...] = lens[zl]
    clip_length = clip[0:1, 0:1]
    position = lax.broadcasted_iota(jnp.int32, (1, 8 * rows), 1).astype(F32)
    mask = jnp.where(position < clip_length, 0.0, -1e30)

    def attend_rows(to_x):
        here = aligned(to_x, 2 * rows)
        for h in range(2):
            cols = slice(h * HD, (h + 1) * HD)
            scores = lax.dot_general(heads[h, here, :], heads[2 + h], NT, preferred_element_type=F32)
            scores = scores * HD**-0.5 + mask
            risen = jnp.exp(scores - jnp.max(scores, axis=-1, keepdims=True))
            share = 1.0 / jnp.sum(risen, axis=-1, keepdims=True)
            low = (risen * share).astype(BF16)
            probs[h, here, :] = low
            made = jnp.dot(low, heads[4 + h], preferred_element_type=F32).astype(BF16)
            mixed[2 * to_x, :, cols] = made[:rows]
            mixed[2 * to_x + 1, :, cols] = made[rows:]

    mixed_base = net.reserve(8)

    def mixed_send(dx, dc):
        slot = 2 * ((x + dx) % 4) + (c + dc) % 2
        return net.copy(
            mixed_base + 2 * dx + dc, mixed.at[slot], attended.at[me], net.device(dx, dc)
        )

    @pl.loop(1, 5)
    def _(step):
        dx = step % 4
        attend_rows((x + dx) % 4)
        mixed_send(dx, 1).start()

        @pl.when(dx != 0)
        def _():
            mixed_send(dx, 0).start()

    attended[me] = mixed[me]
    for d in (1, 3, 2):
        top_copy(d).wait_recv()
        top_pass(d).start()
    for d in (1, 3, 2):
        out_share(d).wait_recv()
        out_pass(d).start()
    for dx in range(4):
        for dc in range(2):
            if dx or dc:
                mixed_send(dx, dc).wait()
    for d in range(4):
        top_pass(d).wait()
        out_pass(d).wait()
    for d in (1, 2, 3):
        up_share(d).wait()
        for copy in (cut_copy, cut_share, up_copy, top_copy, out_copy, out_share):
            copy(d).wait_send()

    @pl.when(c == zl)
    def _():
        down_local.wait()

    @pl.when(c != zl)
    def _():
        down_cross.wait_send()
        for d in (1, 2, 3):
            down_share(d).wait()

    bias_arrived()
    for left in (token_left, out_left, top_left, bias_left):
        left()
    for k in range(3):
        token_send(k, gathered.at[me]).wait_send()
        passed(order(k), me).wait_send()
    net.all_sent()


def begin(tokens, w_query, w_key, w_value, small, up_bias, w_out, w_up, w_down, cotangent, length):
    rows, width = tokens.shape

    def shape(*dims):
        return jax.ShapeDtypeStruct(dims, BF16)

    return pl.pallas_call(
        begin_kernel,
        in_specs=[VMEM] * 11,
        out_specs=[VMEM] * 10 + [HBM] * 4 + [VMEM],
        out_shape=[
            shape(8, rows, width),
            shape(6, 8 * rows, HD),
            shape(2, 8 * rows, 8 * rows),
            shape(8, rows, 160),
            shape(8, rows, 160),
            shape(4, 2, 2, 80, 480),
            shape(8, 16, 160),
            shape(16, 640),
            shape(rows, width),
            jax.ShapeDtypeStruct((8, 128), F32),
            shape(4, 2, 2, 80, width),
            shape(4, 2, 2, 80, 640),
            shape(640, width),
            shape(8, rows, width),
            shape(160, width),
        ],
        scratch_shapes=[
            pltpu.VMEM((8, rows, width), BF16),
            pltpu.VMEM((8, 2, 80, 480), BF16),
            pltpu.VMEM((2, 8, 128), F32),
            pltpu.VMEM((8, width), F32),
        ]
        + scratch_for(96),
        compiler_params=pltpu.CompilerParams(
            collective_id=0, has_side_effects=True, vmem_limit_bytes=58 << 20
        ),
    )(tokens, w_query, w_key, w_value, small, up_bias, w_out, w_up, w_down, cotangent, length)


def middle_kernel(
    attended,
    own,
    smalls,
    up_bias,
    clip,
    out_full,
    up_mine,
    down_mine,
    top,
    result,
    grad_middle,
    branch,
    out_sums,
    g_up,
    g_down,
    g_up_bias,
    g_vectors,
    grad_mixed,
    vectors,
    middle,
    second,
    masked,
    active,
    hidden,
    parts,
    over,
    sums,
    arrived,
    out_parts,
    out_over,
    joined,
    by_head,
    sent,
    got,
    still,
):
    net = Net(sent, got, still)
    x, c, me = net.x, net.c, net.me
    rows, width = own.shape
    wait = net.greet([net.device(dx, dc) for dx in range(4) for dc in range(2) if dx or dc])
    for block in range(8):
        vectors[:, 160 * block : 160 * block + 160] = smalls[block, :8, :].astype(F32)
    bias_up = up_bias[0:1, :].astype(F32)
    mine = aligned(me, rows)
    for block in range(8):
        joined[:, 160 * block : 160 * block + 160] = attended[block]
    made = jnp.dot(joined[...], out_full[...], preferred_element_type=F32)
    middle[...] = own[...].astype(F32) + made + vectors[2:3, :]

    def normalised():
        values = middle[...]
        center = values - jnp.mean(values, axis=-1, keepdims=True)
        inverse = lax.rsqrt(jnp.mean(center * center, axis=-1, keepdims=True) + EPS)
        return center * inverse, inverse

    second[mine, :] = (normalised()[0] * vectors[6:7, :] + vectors[7:8, :]).astype(BF16)
    wait()

    near, pass_on, swap, add, out_swap = (net.reserve(4) for _ in range(5))

    def out_copy(dx, to_x):
        source = out_parts.at[aligned(2 * to_x + 1 - c, rows)]
        return net.copy(out_swap + dx, source, out_over.at[to_x], net.device(0, 1))

    def near_copy(dx):
        return net.copy(near + dx, second.at[mine], second.at[mine], net.device(dx))

    def pass_copy(dx, slot):
        here = second.at[aligned(slot, rows)]
        return net.copy(pass_on + dx, here, here, net.device(0, 1))

    def swap_copy(dx, to_x):
        source = parts.at[aligned(2 * to_x + 1 - c, rows)]
        return net.copy(swap + dx, source, over.at[to_x], net.device(0, 1))

    def add_copy(dx, to_x):
        return net.copy(add + dx, sums.at[to_x], arrived.at[dx], net.device(4 - dx))

    for dx in (1, 3, 2):
        near_copy(dx).start()

    @pl.loop(0, 4)
    def _(k):
        dx = k ^ (k >> 1)
        to_x = (x - dx + 4) % 4

        @pl.when(dx != 0)
        def _():
            near_copy(dx).wait_recv()

        pass_copy(dx, 2 * to_x + c).start()
        here = aligned(to_x, 2 * rows)
        position = lax.broadcasted_iota(jnp.int32, (2 * rows, 1), 0) + to_x * 2 * rows
        live = position.astype(F32) < clip[0:1, 0:1]
        low_top = jnp.where(live, top[here, :].astype(F32), 0.0).astype(BF16)
        masked[here, :] = low_top
        grad_act = lax.dot_general(low_top, down_mine[...], NT, preferred_element_type=F32)
        pass_copy(dx, 2 * to_x + c).wait_recv()
        z = jnp.dot(second[here, :], up_mine[...], preferred_element_type=F32) + bias_up
        bell = 0.5 * (1.0 + lax.erf(z * 0.7071067811865476))
        active[here, :] = (z * bell).astype(BF16)
        slope = bell + z * jnp.exp(-0.5 * z * z) * 0.3989422804014327
        grad_z = (grad_act * slope).astype(BF16)
        hidden[here, :] = grad_z
        parts[here, :] = lax.dot_general(
            grad_z, up_mine[...], NT, preferred_element_type=F32
        ).astype(BF16)
        swap_copy(dx, to_x).start()
        out_parts[here, :] = jnp.dot(
            active[here, :], down_mine[...], preferred_element_type=F32
        ).astype(BF16)
        out_copy(dx, to_x).start()
        swap_copy(dx, to_x).wait_recv()

        @pl.when(dx != 0)
        def _():
            kept = parts[aligned(2 * to_x + c, rows), :].astype(F32)
            sums[to_x] = (kept + over[to_x].astype(F32)).astype(BF16)
            add_copy(dx, to_x).start()

    @pl.loop(0, 5)
    def _(i):
        cols = pl.ds(pl.multiple_of(i * 256, 256), 256)
        g_up[cols, :] = lax.dot_general(
            second[:, cols], hidden[...], TN, preferred_element_type=F32
        ).astype(BF16)
        cols = pl.ds(pl.multiple_of(i * 128, 128), 128)
        g_down[cols, :] = lax.dot_general(
            active[:, cols], masked[...], TN, preferred_element_type=F32
        ).astype(BF16)

    for dx in range(4):
        to_x = (x - dx + 4) % 4
        out_copy(dx, to_x).wait_recv()
        kept = out_parts[aligned(2 * to_x + c, rows), :].astype(F32) + out_over[to_x].astype(F32)
        if dx:
            out_sums[to_x] = kept.astype(BF16)
        else:
            result[...] = middle[...] + kept + vectors[3:4, :]
    g_up_bias[...] = jnp.sum(hidden[...].astype(F32), axis=0, keepdims=True)
    grad_second = parts[mine, :].astype(F32) + over[x].astype(F32)
    for dx in (1, 3, 2):
        add_copy(dx, (x - dx + 4) % 4).wait_recv()
        grad_second = grad_second + arrived[dx].astype(F32)
    normed, inverse = normalised()
    scaled = grad_second * vectors[6:7, :]
    back = inverse * (
        scaled
        - jnp.mean(scaled, axis=-1, keepdims=True)
        - normed * jnp.mean(scaled * normed, axis=-1, keepdims=True)
    )
    top_own = masked[mine, :].astype(F32)
    total = top_own + back
    grad_middle[...] = total
    low = total.astype(BF16)
    branch[...] = low
    grad_attended = lax.dot_general(low, out_full[...], NT, preferred_element_type=F32)
    grad_attended = grad_attended.astype(BF16)
    for block in range(8):
        by_head[block] = grad_attended[:, 160 * block : 160 * block + 160]
    mixing = []
    for dx in (2, 1, 3, 0):
        for dc in (1, 0):
            if dx or dc:
                slot = 2 * ((x + dx) % 4) + (c + dc) % 2
                mixing.append(net.go(by_head.at[slot], grad_mixed.at[me], net.device(dx, dc)))
    grad_mixed[me] = by_head[me]
    g_vectors[0:1, :] = jnp.sum(low.astype(F32), axis=0, keepdims=True)
    g_vectors[1:2, :] = jnp.sum(top_own, axis=0, keepdims=True)
    g_vectors[2:3, :] = jnp.sum(grad_second * normed, axis=0, keepdims=True)
    g_vectors[3:4, :] = jnp.sum(grad_second, axis=0, keepdims=True)
    for copy in mixing:
        copy.wait_recv()
    for dx in range(4):
        to_x = (x - dx + 4) % 4
        pass_copy(dx, 2 * to_x + c).wait_send()
        swap_copy(dx, to_x).wait_send()
        out_copy(dx, to_x).wait_send()
        if dx:
            near_copy(dx).wait_send()
            add_copy(dx, to_x).wait_send()
    net.all_sent()


def middle_part(attended, own, smalls, up_bias, clip, out_full, up_mine, down_mine, top):
    rows, width = own.shape

    def shape(*dims, dtype=BF16):
        return jax.ShapeDtypeStruct(dims, dtype)

    def buffer(*dims, dtype=BF16):
        return pltpu.VMEM(dims, dtype)

    return pl.pallas_call(
        middle_kernel,
        in_specs=[VMEM] * 9,
        out_specs=[VMEM] * 9,
        out_shape=[
            shape(rows, width, dtype=F32),
            shape(rows, width, dtype=F32),
            shape(rows, width),
            shape(4, rows, width),
            shape(width, 640),
            shape(640, width),
            shape(1, 640, dtype=F32),
            shape(4, width, dtype=F32),
            shape(8, rows, 160),
        ],
        scratch_shapes=[
            buffer(8, width, dtype=F32),
            buffer(rows, width, dtype=F32),
            buffer(8 * rows, width),
            buffer(8 * rows, width),
            buffer(8 * rows, 640),
            buffer(8 * rows, 640),
            buffer(8 * rows, width),
            buffer(4, rows, width),
            buffer(4, rows, width),
            buffer(4, rows, width),
            buffer(8 * rows, width),
            buffer(4, rows, width),
            buffer(rows, width),
            buffer(8, rows, 160),
        ]
        + scratch_for(32),
        compiler_params=pltpu.CompilerParams(
            collective_id=1, has_side_effects=True, vmem_limit_bytes=60 << 20
        ),
    )(attended, own, smalls, up_bias, clip, out_full, up_mine, down_mine, top)


def piece_start(index):
    return pl.multiple_of(48 * index - 32 * (index // 3), 16)


def column_flow(net, source, r1, s1, r2, s2, planes, landed, place_of):
    y, z, x, c = net.y, 2 * net.zh + net.zl, net.x, net.c
    b1, b2, b3, b4, b5 = (net.reserve(4) for _ in range(5))
    sibling = net.device(0, 1)

    def copy_1(d):
        rows = pl.ds(piece_start((y + d) % 4), 48)
        return net.copy(b1 + d, source.at[:, rows, :], r1.at[d], net.device(dy=d))

    mine = pltpu.make_async_copy(
        source.at[:, pl.ds(piece_start(y), 48), :], r1.at[0], net.still.at[b1]
    )

    def copy_2(d):
        part = s1.at[pl.ds(2 * ((z + d) % 4), 2)]
        return net.copy(b2 + d, part, r2.at[d], net.device(dz=d))

    def copy_3(d):
        return net.copy(b3 + d, s2.at[(z + d) % 2], planes.at[z], net.device(dz=d))

    def copy_4(d):
        target = place_of(landed, 2 * x + c)
        return net.copy(b4 + d, planes.at[(x + d) % 4], target, net.device(d))

    def copy_5(d):
        here = place_of(landed, 2 * ((x - d + 4) % 4) + c)
        return net.copy(b5 + d, here, here, sibling)

    def first():
        mine.start()
        for d in (2, 1, 3):
            copy_1(d).start()

    def second():
        mine.wait()
        for d in (1, 2, 3):
            copy_1(d).wait_recv()
        total = r1[0].astype(F32)
        for d in (1, 2, 3):
            total = total + r1[d].astype(F32)
        s1[...] = total.astype(BF16)
        for d in (2, 1, 3):
            copy_2(d).start()

    def third():
        total = s1[pl.ds(2 * z, 2)].astype(F32)
        for d in (1, 2, 3):
            copy_2(d).wait_recv()
            total = total + r2[d].astype(F32)
        s2[...] = total.astype(BF16)
        for d in (2, 1, 3):
            copy_3(d).start()
        planes[z] = s2[z % 2]

    def fourth():
        for d in (1, 2, 3):
            copy_3(d).wait_recv()
        for d in (2, 1, 3):
            copy_4(d).start()
        place_of(landed, 2 * x + c)[...] = planes[x]
        copy_5(0).start()

    def fifth():
        for d in (1, 3, 2):
            copy_4(d).wait_recv()
            copy_5(d).start()
        for d in range(4):
            copy_5(d).wait_recv()

    def sent():
        for d in range(4):
            copy_5(d).wait_send()
        for d in (1, 2, 3):
            for copy in (copy_1, copy_2, copy_3, copy_4):
                copy(d).wait_send()

    return first, second, third, fourth, fifth, sent


def share_over_y(net, whole, final, half_of):
    y = net.y
    near, over = net.reserve(4), net.reserve(4)
    own = pltpu.make_async_copy(whole, final.at[y], net.still.at[near])

    def copy(d):
        return net.copy(near + d, half_of(whole), half_of(final.at[y]), net.device(dy=d))

    def forward(d):
        here = half_of(final.at[(y - d + 4) % 4])
        return net.copy(over + d, here, here, net.device(0, 1))

    def first():
        own.start()
        for d in (2, 1, 3):
            copy(d).start()

    def second():
        for d in (1, 3, 2):
            copy(d).wait_recv()
            forward(d).start()

    def third():
        own.wait()
        for d in (1, 2, 3):
            forward(d).wait_recv()
            forward(d).wait_send()
            copy(d).wait_send()

    return first, second, third


def four_way(net, base, held, position, device_of):
    def copy(d):
        return net.copy(base + d, held.at[position], held.at[position], device_of(d))

    def go():
        for d in (2, 1, 3):
            copy(d).start()

    def total():
        for d in (1, 2, 3):
            copy(d).wait_recv()
        return (held[0].astype(F32) + held[1].astype(F32)) + (
            held[2].astype(F32) + held[3].astype(F32)
        )

    def sent():
        for d in (1, 2, 3):
            copy(d).wait_send()

    return go, total, sent


def finish_kernel(
    heads,
    mixed,
    grad_mixed,
    w_qkv,
    own,
    smalls,
    result,
    grad_middle,
    branch,
    out_sums,
    g_up_bias,
    g_vectors,
    probs,
    h1,
    g_up,
    g_down,
    hb_out,
    vec_out,
    output,
    input_grad,
    fin_up,
    fin_qkv,
    fin_down,
    fin_out,
    branch_all,
    tall,
    prob_buf,
    grads,
    sum_k,
    sum_v,
    give,
    over,
    sums,
    arrived,
    out_arrived,
    final_rows,
    final_grad,
    up_r1,
    up_s1,
    up_r2,
    up_s2,
    up_planes,
    up_landed,
    g_qkv,
    qkv_r1,
    qkv_s1,
    qkv_r2,
    qkv_s2,
    qkv_planes,
    qkv_landed,
    qkv_rows,
    down_r1,
    down_s1,
    down_r2,
    down_l3,
    down_p,
    g_out,
    out_r1,
    out_z,
    out_t,
    head_y,
    head_z,
    head_sib,
    vec_cut,
    vec_1,
    vec_1s,
    vec_2,
    vec_3,
    vectors,
    sent,
    got,
    still,
):
    net = Net(sent, got, still)
    x, y, c, zl, me = net.x, net.y, net.c, net.zl, net.me
    z = 2 * net.zh + zl
    rows, width = own.shape
    sibling = net.device(0, 1)
    wait = net.greet(
        [net.device(dx, dc) for dx in range(4) for dc in range(2) if dx or dc]
        + [net.device(dy=d) for d in (1, 2, 3)]
        + [net.device(dz=d) for d in (1, 2, 3)]
        + [(y * 4 + net.zh * 2 + 1 - c, 2 * x + 1 - zl)]
    )

    tile = 2 * rows
    slots = net.reserve(2)

    def load_probs(i):
        slot = i % 2
        return pltpu.make_async_copy(
            probs.at[:, aligned(i, tile), :], prob_buf.at[slot], still.at[slots + slot]
        )

    load_probs(0).start()
    load_h1 = pltpu.make_async_copy(h1, tall, still.at[net.reserve(1)])
    load_h1.start()
    own_branch = pltpu.make_async_copy(
        branch, branch_all.at[aligned(me, rows)], still.at[net.reserve(1)]
    )
    own_branch.start()
    for block in range(8):
        vectors[:, 160 * block : 160 * block + 160] = smalls[block, :8, :].astype(F32)
    sum_k[...] = jnp.zeros_like(sum_k)
    sum_v[...] = jnp.zeros_like(sum_v)

    up = column_flow(
        net,
        g_up,
        up_r1,
        up_s1,
        up_r2,
        up_s2,
        up_planes,
        up_landed,
        lambda ref, hb: ref.at[:, pl.ds(pl.multiple_of(hb * 640, 128), 640)],
    )
    three = column_flow(
        net,
        g_qkv,
        qkv_r1,
        qkv_s1,
        qkv_r2,
        qkv_s2,
        qkv_planes,
        qkv_landed,
        lambda ref, hb: ref.at[hb],
    )
    up_share = share_over_y(
        net,
        up_landed,
        fin_up,
        lambda ref: ref.at[:, pl.ds(pl.multiple_of(c * 2560, 128), 2560)],
    )
    three_share = share_over_y(
        net,
        qkv_rows,
        fin_qkv,
        lambda ref: ref.at[:, :, pl.ds(pl.multiple_of(c * 640, 128), 640)],
    )

    d1, d2, d4, d5 = (net.reserve(4) for _ in range(4))
    d3_go, _, d3_sent = four_way(net, d3 := net.reserve(4), down_l3, y, lambda d: net.device(dy=d))
    down_mine = pltpu.make_async_copy(
        g_down.at[aligned(z, 160)], down_r1.at[0], still.at[d1]
    )

    def down_1(d):
        return net.copy(d1 + d, g_down.at[aligned((z + d) % 4, 160)], down_r1.at[d], net.device(dz=d))

    def down_2(d):
        part = down_s1.at[pl.ds(piece_start((y + d) % 4), 48)]
        return net.copy(d2 + d, part, down_r2.at[d], net.device(dy=d))

    def down_4(k, source_z):
        to_z = c + 2 * k
        return pltpu.make_async_remote_copy(
            src_ref=down_p,
            dst_ref=fin_down.at[aligned(source_z, 160)],
            send_sem=sent.at[d4 + k],
            recv_sem=got.at[d4 + source_z],
            device_id=(y * 4 + to_z // 2 * 2 + c, 2 * x + to_z % 2),
            device_id_type=MESH,
        )

    down_local = pltpu.make_async_copy(down_p, fin_down.at[aligned(z, 160)], still.at[d4])

    def down_5(source_z):
        here = fin_down.at[aligned(source_z, 160)]
        return net.copy(d5 + source_z, here, here, sibling)

    e1, e3, e4 = (net.reserve(4) for _ in range(3))
    out_go, out_total, out_sent = four_way(
        net, net.reserve(4), out_z, z, lambda d: net.device(dz=d)
    )

    def out_1(d):
        part = g_out.at[pl.ds(piece_start((y + d) % 4), 48)]
        return net.copy(e1 + d, part, out_r1.at[d], net.device(dy=d))

    def out_3(d):
        return net.copy(e3 + d, out_t, fin_out.at[y], net.device(dy=d))

    out_local = pltpu.make_async_copy(out_t, fin_out.at[y], still.at[e3])

    def out_4(source_y):
        return net.copy(e4 + source_y, fin_out.at[source_y], fin_out.at[source_y], sibling)

    near, pass_on, swap, add, out_add = (net.reserve(4) for _ in range(5))

    def near_copy(dx):
        return net.copy(near + dx, branch, branch_all.at[aligned(me, rows)], net.device(dx))

    def pass_copy(dx):
        here = branch_all.at[aligned(2 * ((x - dx + 4) % 4) + c, rows)]
        return net.copy(pass_on + dx, here, here, sibling)

    def swap_copy(dx, to_x):
        return net.copy(swap + dx, give.at[to_x], over.at[to_x], sibling)

    def add_copy(dx, to_x):
        return net.copy(add + dx, sums.at[to_x], arrived.at[dx], net.device(4 - dx))

    def out_add_copy(dx):
        to_x = (x - dx + 4) % 4
        return net.copy(out_add + dx, out_sums.at[to_x], out_arrived.at[dx], net.device(4 - dx))

    wait()
    for dx in (1, 3, 2):
        near_copy(dx).start()
    up[0]()
    down_mine.start()
    for d in (2, 1, 3):
        down_1(d).start()

    @pl.loop(0, 4)
    def _(i):
        @pl.when(i < 3)
        def _():
            load_probs(i + 1).start()

        load_probs(i).wait()
        here = aligned(i, tile)
        for h in range(2):
            cols = slice(h * HD, (h + 1) * HD)
            back = jnp.concatenate([grad_mixed[2 * i, :, cols], grad_mixed[2 * i + 1, :, cols]])
            seen = jnp.concatenate([mixed[2 * i, :, cols], mixed[2 * i + 1, :, cols]])
            low = prob_buf[i % 2, h]
            row_total = jnp.sum(back.astype(F32) * seen.astype(F32), axis=-1, keepdims=True)
            grad_probs = lax.dot_general(back, heads[4 + h], NT, preferred_element_type=F32)
            grad_scores = (low.astype(F32) * (grad_probs - row_total)).astype(BF16)
            sum_v[h] += lax.dot_general(low, back, TN, preferred_element_type=F32)
            sum_k[h] += lax.dot_general(
                grad_scores, heads[h, here, :], TN, preferred_element_type=F32
            )
            grad_q = jnp.dot(grad_scores, heads[2 + h], preferred_element_type=F32)
            grads[here, cols] = (grad_q * HD**-0.5).astype(BF16)

    for h in range(2):
        grads[:, 160 + h * HD : 160 + (h + 1) * HD] = (sum_k[h] * HD**-0.5).astype(BF16)
        grads[:, 320 + h * HD : 320 + (h + 1) * HD] = sum_v[h].astype(BF16)

    load_h1.wait()

    @pl.loop(0, 2)
    def _(i):
        cols = pl.ds(pl.multiple_of(i * 640, 128), 640)
        made = lax.dot_general(tall[:, cols], grads[...], TN, preferred_element_type=F32)
        g_qkv[pl.ds(4 * i, 4)] = made.astype(BF16).reshape(4, 160, 480)

    three[0]()
    @pl.loop(0, 4)
    def _(k):
        dx = order(k)
        dx = jnp.where(k == 3, 0, dx)
        to_x = (x - dx + 4) % 4
        part = lax.dot_general(
            grads[aligned(to_x, tile), :], w_qkv[...], NT, preferred_element_type=F32
        )
        low, high = part[:rows], part[rows:]
        give[to_x] = jnp.where(c == 0, high, low).astype(BF16)
        swap_copy(dx, to_x).start()
        kept = jnp.where(c == 0, low, high)
        swap_copy(dx, to_x).wait_recv()
        kept = kept + over[to_x].astype(F32)

        @pl.when(dx != 0)
        def _():
            sums[to_x] = kept.astype(BF16)
            add_copy(dx, to_x).start()

        @pl.when(dx == 0)
        def _():
            final_grad[...] = kept

    own_branch.wait()
    pass_copy(0).start()
    for dx in (1, 3, 2):
        near_copy(dx).wait_recv()
        pass_copy(dx).start()

    up[1]()
    down_mine.wait()
    total = down_r1[0].astype(F32)
    for d in (1, 2, 3):
        down_1(d).wait_recv()
        total = total + down_r1[d].astype(F32)
    down_s1[...] = total.astype(BF16)
    for d in (2, 1, 3):
        down_2(d).start()

    for dx in range(4):
        pass_copy(dx).wait_recv()
        pass_copy(dx).wait_send()
    load_branch = pltpu.make_async_copy(branch_all, tall, still.at[net.reserve(1)])
    load_branch.start()
    load_branch.wait()
    seen = jnp.concatenate([mixed[block] for block in range(8)])
    g_out[...] = lax.dot_general(seen, tall[...], TN, preferred_element_type=F32).astype(BF16)
    for d in (2, 1, 3):
        out_1(d).start()

    head_y[y] = jnp.zeros((8, 640), F32)
    head_y[y, 0:1, :] = g_up_bias[...]
    column_sums = jnp.sum(grads[...].astype(F32), axis=0, keepdims=True)
    head_y[y, 1:2, :160] = column_sums[:, :160]
    head_y[y, 2:3, :160] = column_sums[:, 320:]
    head_y_go, head_y_total, head_y_sent = four_way(
        net, net.reserve(4), head_y, y, lambda d: net.device(dy=d)
    )
    head_y_go()

    three[1]()
    up[2]()
    total = down_s1[pl.ds(piece_start(y), 48), :].astype(F32)
    for d in (1, 2, 3):
        down_2(d).wait_recv()
        total = total + down_r2[d].astype(F32)
    down_l3[y] = total.astype(BF16)
    d3_go()

    three[2]()
    up[3]()
    for d in (1, 2, 3):
        net.copy(d3 + d, down_l3.at[y], down_l3.at[y], net.device(dy=d)).wait_recv()
    for i in range(3):
        down_p[48 * i : 48 * i + 48, :] = down_l3[i]
    down_p[144:160, :] = down_l3[3, 32:48, :]
    for k in range(2):

        @pl.when(c + 2 * k != z)
        def _():
            down_4(k, z).start()

    @pl.when(c == zl)
    def _():
        down_local.start()

    up[4]()
    up_share[0]()
    three[3]()
    grad_first = final_grad[...]
    for dx in (1, 3, 2):
        add_copy(dx, (x - dx + 4) % 4).wait_recv()
        grad_first = grad_first + arrived[dx].astype(F32)
    values = own[...].astype(F32)
    center = values - jnp.mean(values, axis=-1, keepdims=True)
    inverse = lax.rsqrt(jnp.mean(center * center, axis=-1, keepdims=True) + EPS)
    normed = center * inverse
    scaled = grad_first * vectors[4:5, :]
    back = inverse * (
        scaled
        - jnp.mean(scaled, axis=-1, keepdims=True)
        - normed * jnp.mean(scaled * normed, axis=-1, keepdims=True)
    )
    final_grad[...] = grad_middle[...] + back
    grad_arrived, grad_left = net.cross(final_grad, input_grad)
    gain = jnp.sum(grad_first * normed, axis=0, keepdims=True)
    shift = jnp.sum(grad_first, axis=0, keepdims=True)
    for block in range(8):
        cols = slice(160 * block, 160 * block + 160)
        here = vec_cut.at[block // 2, block % 2]
        here[0:4, :] = g_vectors[:, cols]
        here[4:5, :] = gain[:, cols]
        here[5:6, :] = shift[:, cols]
        here[6:8, :] = jnp.zeros((2, 160), F32)
    v1 = net.reserve(8)

    def vec_copy(dx, dc):
        return net.copy(
            v1 + 2 * dx + dc, vec_cut.at[(x + dx) % 4], vec_1.at[me], net.device(dx, dc)
        )

    others = [(dx, dc) for dx in (2, 1, 3, 0) for dc in (1, 0) if dx or dc]
    for dx, dc in others:
        vec_copy(dx, dc).start()
    vec_1[me] = vec_cut[x]

    for dx in (1, 3, 2):
        out_add_copy(dx).start()
    three[4]()
    for block in range(8):
        cols = slice(160 * block, 160 * block + 160)
        for k in range(3):
            qkv_rows[k, :, cols] = qkv_landed[block, :, 160 * k : 160 * k + 160]
    three_share[0]()
    total = g_out[pl.ds(piece_start(y), 48), :].astype(F32)
    for d in (1, 2, 3):
        out_1(d).wait_recv()
        total = total + out_r1[d].astype(F32)
    out_z[z] = total.astype(BF16)
    out_go()
    head_z[z] = head_y_total()
    head_z_go, head_z_total, head_z_sent = four_way(
        net, net.reserve(4), head_z, z, lambda d: net.device(dz=d)
    )
    head_z_go()
    for dx, dc in others:
        vec_copy(dx, dc).wait_recv()
    total = vec_1[0]
    for block in range(1, 8):
        total = total + vec_1[block]
    vec_1s[...] = total
    v2 = net.reserve(4)

    def vec_z(d):
        return net.copy(v2 + d, vec_1s.at[(z + d) % 2], vec_2.at[z], net.device(dz=d))

    for d in (2, 1, 3):
        vec_z(d).start()
    vec_2[z] = vec_1s[zl]
    out_t[...] = out_total().astype(BF16)

    @pl.when(c == zl)
    def _():
        out_local.start()
        for d in (2, 1, 3):
            out_3(d).start()

    head_sib[0] = head_z_total()
    head_copy = net.go(head_sib.at[0], head_sib.at[1], sibling)
    for d in (1, 2, 3):
        vec_z(d).wait_recv()
    vec_3[y] = (vec_2[0] + vec_2[1]) + (vec_2[2] + vec_2[3])
    vec_y_go, vec_y_total, vec_y_sent = four_way(
        net, net.reserve(4), vec_3, y, lambda d: net.device(dy=d)
    )
    vec_y_go()

    @pl.when(c == zl)
    def _():
        down_local.wait()
        down_5(z).start()
        for d in (1, 2, 3):
            source_z = (z + d) % 4
            down_4(0, source_z).wait_recv()
            down_5(source_z).start()
        out_local.wait()
        out_4(y).start()
        for d in (1, 2, 3):
            out_3(d).wait_recv()
            out_4((y + 4 - d) % 4).start()

    total = result[...]
    for dx in (1, 3, 2):
        out_add_copy(dx).wait_recv()
        total = total + out_arrived[dx].astype(F32)
    final_rows[...] = total.astype(BF16)
    output_arrived, output_left = net.cross(final_rows, output)

    up_share[1]()
    three_share[1]()
    head_copy.wait_recv()
    hb_out[...] = jnp.where(c == zl, head_sib[0], head_sib[1])
    vec_out[...] = vec_y_total()

    @pl.when(c == zl)
    def _():
        for i in range(4):
            down_5(i).wait_send()
            out_4(i).wait_send()
        for d in (1, 2, 3):
            out_3(d).wait_send()

    @pl.when(c != zl)
    def _():
        for i in range(4):
            down_5(i).wait_recv()
            out_4(i).wait_recv()

    for k in range(2):

        @pl.when(c + 2 * k != z)
        def _():
            down_4(k, z).wait_send()

    up_share[2]()
    three_share[2]()
    grad_arrived()
    grad_left()
    output_arrived()
    output_left()
    for done in (up[5], three[5], d3_sent, out_sent, head_y_sent, head_z_sent, vec_y_sent):
        done()
    for d in (1, 2, 3):
        down_1(d).wait_send()
        down_2(d).wait_send()
        out_1(d).wait_send()
        vec_z(d).wait_send()
        near_copy(d).wait_send()
        add_copy(d, (x - d + 4) % 4).wait_send()
        out_add_copy(d).wait_send()
    for d in range(4):
        swap_copy(d, (x - d + 4) % 4).wait_send()
    for dx, dc in others:
        vec_copy(dx, dc).wait_send()
    net.all_sent()


def finish(
    heads,
    mixed,
    grad_mixed,
    w_qkv,
    own,
    smalls,
    result,
    grad_middle,
    branch,
    out_sums,
    g_up_bias,
    g_vectors,
    probs,
    h1,
    g_up,
    g_down,
):
    rows, width = own.shape

    def shape(*dims, dtype=BF16):
        return jax.ShapeDtypeStruct(dims, dtype)

    def buffer(*dims, dtype=BF16):
        return pltpu.VMEM(dims, dtype)

    def column_buffers(columns):
        return [
            buffer(4, 8, 48, columns),
            buffer(8, 48, columns),
            buffer(4, 2, 48, columns),
            buffer(2, 48, columns),
            buffer(4, 48, columns),
        ]

    return pl.pallas_call(
        finish_kernel,
        in_specs=[VMEM] * 12 + [HBM] * 4,
        out_specs=[VMEM] * 2 + [HBM] * 7,
        out_shape=[
            shape(8, 640, dtype=F32),
            shape(8, 160, dtype=F32),
            shape(rows, width),
            shape(rows, width, dtype=F32),
            shape(4, 48, 5120),
            shape(4, 3, 48, width),
            shape(640, width),
            shape(4, 48, width),
            shape(8 * rows, width),
        ],
        scratch_shapes=[
            buffer(8 * rows, width),
            buffer(2, 2, 2 * rows, 8 * rows),
            buffer(8 * rows, 480),
            buffer(2, 8 * rows, HD, dtype=F32),
            buffer(2, 8 * rows, HD, dtype=F32),
            buffer(4, rows, width),
            buffer(4, rows, width),
            buffer(4, rows, width),
            buffer(4, rows, width),
            buffer(4, rows, width),
            buffer(rows, width),
            buffer(rows, width, dtype=F32),
        ]
        + column_buffers(640)
        + [buffer(48, 5120), buffer(8, 160, 480)]
        + column_buffers(480)
        + [
            buffer(8, 48, 480),
            buffer(3, 48, width),
            buffer(4, 160, width),
            buffer(160, width),
            buffer(4, 48, width),
            buffer(4, 48, width),
            buffer(160, width),
            buffer(160, width),
            buffer(4, 48, width),
            buffer(4, 48, width),
            buffer(48, width),
            buffer(4, 8, 640, dtype=F32),
            buffer(4, 8, 640, dtype=F32),
            buffer(2, 8, 640, dtype=F32),
            buffer(4, 2, 8, 160, dtype=F32),
            buffer(8, 2, 8, 160, dtype=F32),
            buffer(2, 8, 160, dtype=F32),
            buffer(4, 8, 160, dtype=F32),
            buffer(4, 8, 160, dtype=F32),
            buffer(8, width, dtype=F32),
        ]
        + scratch_for(192),
        compiler_params=pltpu.CompilerParams(
            collective_id=2, has_side_effects=True, vmem_limit_bytes=62 << 20
        ),
    )(
        heads,
        mixed,
        grad_mixed,
        w_qkv,
        own,
        smalls,
        result,
        grad_middle,
        branch,
        out_sums,
        g_up_bias,
        g_vectors,
        probs,
        h1,
        g_up,
        g_down,
    )


def widen_kernel(hb, vec, up, three, down, out, *results):
    (o_up, o_q, o_k, o_v, o_down, o_out, *small, f_up, f_three, f_down, f_out, done) = results
    copies = []

    def push(source, target):
        copy = pltpu.make_async_copy(source, target, done.at[len(copies)])
        copy.start()
        copies.append(copy)

    for i in range(4):
        here, there = slice(48 * i, min(48 * i + 48, 160)), slice(0, 48)
        if i == 3:
            there = slice(32, 48)
        f_up[here, :] = up[i, there, :].astype(F32)
        f_out[here, :] = out[i, there, :].astype(F32)
        for k in range(3):
            f_three[k, here, :] = three[i, k, there, :].astype(F32)
    push(f_up, o_up)
    for k, target in enumerate((o_q, o_k, o_v)):
        push(f_three.at[k], target)
    push(f_out, o_out)
    f_down[...] = down[...].astype(F32)
    push(f_down, o_down)
    rows = (hb[1, :160], hb[2, :160], hb[0, :]) + tuple(vec[k, :] for k in range(6))
    for target, row in zip(small, rows):
        target[...] = row
    for copy in copies:
        copy.wait()


def widen(hb, vec, up, three, down, out):
    width = down.shape[1]

    def shape(*dims):
        return jax.ShapeDtypeStruct(dims, F32)

    sizes = [160, 160, 640] + [160] * 6
    return pl.pallas_call(
        widen_kernel,
        in_specs=[VMEM] * 6,
        out_specs=[HBM] * 6 + [VMEM] * 9,
        out_shape=[shape(160, 5120)]
        + [shape(160, width)] * 3
        + [shape(640, width), shape(160, width)]
        + [shape(size) for size in sizes],
        scratch_shapes=[
            pltpu.VMEM((160, 5120), F32),
            pltpu.VMEM((3, 160, width), F32),
            pltpu.VMEM((640, width), F32),
            pltpu.VMEM((160, width), F32),
            pltpu.SemaphoreType.DMA((6,)),
        ],
        compiler_params=pltpu.CompilerParams(vmem_limit_bytes=48 << 20),
    )(hb, vec, up, three, down, out)


def per_device(
    tokens,
    lengths,
    w_query,
    w_key,
    w_value,
    w_out,
    w_up,
    w_down,
    b_query,
    b_value,
    b_out,
    b_up,
    b_down,
    gain_attn,
    shift_attn,
    gain_ffn,
    shift_ffn,
    cotangent,
):
    rows, width = tokens.shape[1:]

    eight = [b_query, b_value, b_out, b_down, gain_attn, shift_attn, gain_ffn, shift_ffn]
    row = lax.broadcasted_iota(jnp.int32, (16, 160), 0)
    small = jnp.zeros((16, 160), BF16)
    for index, vector in enumerate(eight):
        small = jnp.where(row == index, vector[None, :], small)
    up_bias = jnp.broadcast_to(b_up[None, :], (16, 640))
    known = jnp.full((8, 128), lengths[0], F32)
    (
        h1,
        heads,
        probs,
        mixed,
        attended,
        w_qkv,
        smalls,
        up_bias,
        own,
        clip,
        out_full,
        up_mine,
        down_mine,
        top,
        _,
    ) = begin(
        tokens[0],
        w_query,
        w_key,
        w_value,
        small,
        up_bias,
        w_out,
        w_up,
        w_down,
        cotangent[0],
        known,
    )
    w_qkv = w_qkv.reshape(width, 480)
    (
        result,
        grad_middle,
        branch,
        out_sums,
        g_up,
        g_down,
        g_up_bias,
        g_vectors,
        grad_mixed,
    ) = middle_part(
        attended,
        own,
        smalls,
        up_bias,
        clip,
        out_full.reshape(width, width),
        up_mine.reshape(width, 640),
        down_mine,
        top.reshape(8 * rows, width),
    )
    hb_out, vec_out, output, input_grad, fin_up, fin_qkv, fin_down, fin_out, _ = finish(
        heads,
        mixed,
        grad_mixed,
        w_qkv,
        own,
        smalls,
        result,
        grad_middle,
        branch,
        out_sums,
        g_up_bias,
        g_vectors,
        probs,
        h1.reshape(8 * rows, width),
        g_up.reshape(8, 160, 640),
        g_down,
    )

    g_up, g_q, g_k, g_v, g_down, g_out, *small = widen(
        hb_out, vec_out, fin_up, fin_qkv, fin_down, fin_out
    )
    b_q, b_v, b_u, b_o, b_d, gain_two, shift_two, gain_one, shift_one = small
    return (
        output[None],
        input_grad[None],
        g_q,
        g_k,
        g_v,
        g_out,
        g_up,
        g_down,
        b_q,
        b_v,
        b_o,
        b_u,
        b_d,
        gain_one,
        shift_one,
        gain_two,
        shift_two,
    )


def solution(mesh):
    by_clip, matrix, vector = P("rep", "shard", None), P("shard", None), P("shard")
    return jax.shard_map(
        per_device,
        mesh=mesh,
        in_specs=(by_clip, P("rep")) + (matrix,) * 6 + (vector,) * 9 + (by_clip,),
        out_specs=(by_clip, by_clip) + (matrix,) * 6 + (vector,) * 9,
        check_vma=False,
    )
```

```python
import jax
import jax.numpy as jnp
from jax import lax
from jax.experimental import pallas as pl
from jax.experimental.pallas import tpu as pltpu
from jax.sharding import PartitionSpec as P

HD = 80
EPS = 1e-05
F32 = jnp.float32
BF16 = jnp.bfloat16
NT = (((1,), (1,)), ((), ()))
TN = (((0,), (0,)), ((), ()))


MESH = pl.DeviceIdType.MESH
VMEM = pl.BlockSpec(memory_space=pltpu.VMEM)
HBM = pl.BlockSpec(memory_space=pl.ANY)


class Net:
    def __init__(self, sent, got, still):
        rep, shard = lax.axis_index("rep"), lax.axis_index("shard")
        self.y, self.zh, self.c = rep // 4, rep // 2 % 2, rep % 2
        self.x, self.zl = shard // 2, shard % 2
        self.me, self.shard = 2 * self.x + self.c, shard
        self.sent, self.got, self.still, self.used, self.started = sent, got, still, 0, []

    def device(self, dx=0, dc=0, dz=0, dy=0):
        z = (2 * self.zh + self.zl + dz) % 4
        return (
            (self.y + dy) % 4 * 4 + z // 2 * 2 + (self.c + dc) % 2,
            (self.x + dx) % 4 * 2 + z % 2,
        )

    def in_pair(self, dx, dz):
        return (
            self.y * 4 + self.zh * 2 + self.c,
            (self.x + dx) % 4 * 2 + (self.zl + dz) % 2,
        )

    def partner(self):
        return (self.y * 4 + self.zh * 2 + self.zl, 2 * self.x + self.c)

    def greet(self, devices):
        barrier = pltpu.get_barrier_semaphore()
        for device in devices:
            pl.semaphore_signal(barrier, inc=1, device_id=device, device_id_type=MESH)
        return lambda: pl.semaphore_wait(barrier, len(devices))

    def reserve(self, count):
        first = self.used
        self.used += count
        return first

    def copy(self, index, source, target, device):
        return pltpu.make_async_remote_copy(
            src_ref=source,
            dst_ref=target,
            send_sem=self.sent.at[index],
            recv_sem=self.got.at[index],
            device_id=device,
            device_id_type=MESH,
        )

    def go(self, source, target, device):
        copy = self.copy(self.reserve(1), source, target, device)
        copy.start()
        self.started.append(copy)
        return copy

    def cross(self, source, target):
        index = self.reserve(1)
        copy = self.copy(index, source, target, self.partner())
        local = pltpu.make_async_copy(source, target, self.still.at[index])

        @pl.when(self.c != self.zl)
        def _():
            copy.start()

        @pl.when(self.c == self.zl)
        def _():
            local.start()

        def arrived():
            @pl.when(self.c != self.zl)
            def _():
                copy.wait_recv()

            @pl.when(self.c == self.zl)
            def _():
                local.wait()

        def left():
            @pl.when(self.c != self.zl)
            def _():
                copy.wait_send()

        return arrived, left

    def all_sent(self):
        for copy in self.started:
            copy.wait_send()


def order(k):
    return 1 + 2 * k - 3 * (k // 2)


def aligned(index, size):
    return pl.ds(pl.multiple_of(index * size, size), size)


def scratch_for(copies):
    return [pltpu.SemaphoreType.DMA((copies,)) for _ in range(3)]


def begin_kernel(
    tokens,
    w_query,
    w_key,
    w_value,
    small,
    up_bias,
    w_out,
    w_up,
    w_down,
    cotangent,
    length,
    h1,
    heads,
    probs,
    mixed,
    attended,
    w_qkv,
    smalls,
    bias_up,
    own,
    clip,
    out_full,
    up_mine,
    down_mine,
    top,
    out_own,
    normed_rows,
    head_rows,
    prob_buf,
    gathered,
    cut,
    lens,
    vectors,
    sent,
    got,
    still,
):
    net = Net(sent, got, still)
    x, y, c, zh, zl, me, shard = net.x, net.y, net.c, net.zh, net.zl, net.me, net.shard
    rows, width = tokens.shape
    plane = [net.device(dx, dc) for dx in range(4) for dc in range(2) if dx or dc]
    across = [net.in_pair(dx, 1) for dx in range(4)]
    rings = [net.device(dy=d) for d in (1, 2, 3)] + [net.device(dz=d) for d in (1, 2, 3)]
    wait = net.greet(plane + across + rings + [(y * 4 + zh * 2 + 1 - c, 2 * x + 1 - zl)])
    for block in range(8):
        cols = slice(160 * block, 160 * block + 160)
        for half in range(2):
            part = slice(80 * half, 80 * half + 80)
            for k, weight in enumerate((w_query, w_key, w_value)):
                piece = weight[part, cols]
                for h in range(2):
                    first = 240 * h + 80 * k
                    cut[block, half, :, first : first + 80] = piece[:, 80 * h : 80 * h + 80]
    wait()

    token_arrived, token_left = net.cross(tokens, gathered.at[2 * x + zl])
    base = net.reserve(4)

    def token_send(k, source):
        dx = order(k)
        return net.copy(base + dx, source, gathered.at[me], net.device(dx))

    cut_near, cut_ring, up_near, up_ring = (net.reserve(4) for _ in range(4))

    def cut_copy(d):
        source = cut.at[2 * ((x + d) % 4) + c, zh]
        return net.copy(cut_near + d, source, w_qkv.at[x, zl, zh], net.device(d))

    def cut_share(d):
        here = w_qkv.at[:, zl, zh]
        return net.copy(cut_ring + d, here, here, net.device(dz=d))

    def up_part(index):
        cols = pl.ds(pl.multiple_of(index * 640, 128), 640)
        return w_up.at[aligned(zh, 80), cols]

    def up_copy(d):
        source = up_part(2 * ((x + d) % 4) + c)
        return net.copy(up_near + d, source, up_mine.at[x, zl, zh], net.device(d))

    def up_share(d):
        here = up_mine.at[:, zl, zh]
        return net.copy(up_ring + d, here, here, net.device(dz=d))

    up_local = pltpu.make_async_copy(up_part(me), up_mine.at[x, zl, zh], still.at[up_near])

    for d in (2, 1, 3):
        cut_copy(d).start()

    @pl.when(c == zl)
    def _():
        for k in range(2):
            token_send(k, tokens).start()

    @pl.when(c == 0)
    def _():
        lens[0] = length[...]

    @pl.when(c == 1)
    def _():
        lens[1] = length[...]

    lens_copy = net.go(length, lens.at[c], net.device(0, 1))
    arriving = []
    for dx in (0, 1, 3, 2):
        for dz in range(2):
            if dx or dz:
                arriving.append(net.go(small, smalls.at[shard], net.in_pair(dx, dz)))
    smalls[shard] = small[...]
    w_qkv[x, zl, zh] = cut[me, zh]
    token_arrived()

    @pl.when(c != zl)
    def _():
        for k in range(2):
            token_send(k, gathered.at[me]).start()

    sibling = net.device(0, 1)
    own_over = net.go(gathered.at[me], gathered.at[me], sibling)
    for d in (1, 3, 2):
        cut_copy(d).wait_recv()
    for d in (2, 1, 3):
        cut_share(d).start()
    up_local.start()
    for d in (2, 1, 3):
        up_copy(d).start()
    bias_arrived, bias_left = net.cross(up_bias, bias_up)
    top_arrived, top_left = net.cross(cotangent, top.at[2 * x + zl])
    out_arrived, out_left = net.cross(w_out, out_own)

    down_index, down_ring = net.reserve(1), net.reserve(4)
    down_cross = net.copy(
        down_index, w_down.at[aligned(y, 160)], down_mine.at[aligned(y, 160)], net.partner()
    )
    down_local = pltpu.make_async_copy(w_down, down_mine, still.at[down_index])

    def down_share(d):
        here = down_mine.at[aligned(y, 160)]
        return net.copy(down_ring + d, here, here, net.device(dy=d))

    @pl.when(c == zl)
    def _():
        down_local.start()

    @pl.when(c != zl)
    def _():
        down_cross.start()

    own[...] = gathered[me]
    for copy in arriving:
        copy.wait_recv()
    for block in range(8):
        vectors[:, 160 * block : 160 * block + 160] = smalls[block, :8, :].astype(F32)
    gain, shift = vectors[4:5, :], vectors[5:6, :]
    bias_q = smalls[me, 0:1, :].astype(F32)
    bias_v = smalls[me, 1:2, :].astype(F32)

    def project(slot):
        values = gathered[slot].astype(F32)
        center = values - jnp.mean(values, axis=-1, keepdims=True)
        inverse = lax.rsqrt(jnp.mean(center * center, axis=-1, keepdims=True) + EPS)
        normed = (center * inverse * gain + shift).astype(BF16)
        normed_rows[slot] = normed
        made = jnp.dot(normed, w_qkv[...].reshape(width, 480), preferred_element_type=F32)
        here = aligned(slot, rows)
        for h in range(2):
            cols = slice(h * HD, (h + 1) * HD)
            q, k, v = (made[:, 240 * h + 80 * j : 240 * h + 80 * j + 80] for j in range(3))
            head_rows[h, here, :] = (q + bias_q[:, cols]).astype(BF16)
            head_rows[2 + h, here, :] = k.astype(BF16)
            head_rows[4 + h, here, :] = (v + bias_v[:, cols]).astype(BF16)

    top_near, top_over, out_near, out_ring, out_over = (net.reserve(4) for _ in range(5))

    def top_copy(d):
        return net.copy(top_near + d, top.at[me], top.at[me], net.device(d))

    def top_pass(d):
        here = top.at[2 * ((x - d + 4) % 4) + c]
        return net.copy(top_over + d, here, here, sibling)

    half = pl.ds(pl.multiple_of(y % 2 * 640, 128), 640)
    out_piece = out_own.at[aligned(y // 2, 80), half]

    def out_copy(d):
        return net.copy(out_near + d, out_piece, out_full.at[x, c, y // 2, :, half], net.device(d))

    def out_share(d):
        here = out_full.at[:, c, y // 2, :, half]
        return net.copy(out_ring + d, here, here, net.device(dy=d))

    def out_pass(d):
        from_y = (y - d + 4) % 4
        cols = pl.ds(pl.multiple_of(from_y % 2 * 640, 128), 640)
        here = out_full.at[:, c, from_y // 2, :, cols]
        return net.copy(out_over + d, here, here, sibling)

    out_local = pltpu.make_async_copy(
        out_piece, out_full.at[x, c, y // 2, :, half], still.at[out_near]
    )
    out_arrived()
    out_local.start()
    for d in (2, 1, 3):
        out_copy(d).start()
    for d in (1, 3, 2):
        cut_share(d).wait_recv()
    project(me)
    out_local.wait()
    for d in (1, 3, 2):
        out_copy(d).wait_recv()
    for d in (2, 1, 3):
        out_share(d).start()
    out_pass(0).start()
    own_over.wait_recv()
    project(2 * x + 1 - c)
    top_arrived()
    for d in (2, 1, 3):
        top_copy(d).start()

    @pl.when(c != zl)
    def _():
        down_cross.wait_recv()
        for d in (2, 1, 3):
            down_share(d).start()

    over, halves = net.reserve(4), net.reserve(2)

    def token_half(i):
        slot = 2 * ((x + 3 + 2 * i) % 4) + c
        here = gathered.at[slot, pl.ds(i * rows // 2, rows // 2), :]
        return net.copy(halves + i, here, here, net.device(1 + 2 * i))

    def passed(dx, slot):
        return net.copy(over + dx, gathered.at[slot], gathered.at[slot], sibling)

    @pl.loop(0, 3)
    def _(k):
        dx = order(k)
        from_x = (x - dx + 4) % 4

        @pl.when(k == 0)
        def _():
            for i in range(2):
                token_send(i, gathered.at[me]).wait_recv()
                token_half(i).start()

        @pl.when(k == 2)
        def _():
            for i in range(2):
                token_half(i).wait_recv()

        passed(dx, 2 * from_x + c).start()
        project(2 * from_x + c)
        passed(dx, 2 * from_x + c).wait_recv()
        project(2 * from_x + 1 - c)

    up_local.wait()
    for d in (1, 3, 2):
        up_copy(d).wait_recv()
    for d in (2, 1, 3):
        up_share(d).start()
    top_pass(0).start()

    keep_h1 = pltpu.make_async_copy(normed_rows, h1, still.at[net.reserve(1)])
    keep_h1.start()
    keep_heads = pltpu.make_async_copy(head_rows, heads, still.at[net.reserve(1)])
    keep_heads.start()
    lens_copy.wait_recv()
    clip[...] = lens[zl]
    clip_length = clip[0:1, 0:1]
    position = lax.broadcasted_iota(jnp.int32, (1, 8 * rows), 1).astype(F32)
    mask = jnp.where(position < clip_length, 0.0, -1e30)

    def attend_rows(to_x, slot):
        here = aligned(to_x, 2 * rows)
        for h in range(2):
            cols = slice(h * HD, (h + 1) * HD)
            scores = lax.dot_general(
                head_rows[h, here, :], head_rows[2 + h], NT, preferred_element_type=F32
            )
            scores = scores * HD**-0.5 + mask
            risen = jnp.exp(scores - jnp.max(scores, axis=-1, keepdims=True))
            share = 1.0 / jnp.sum(risen, axis=-1, keepdims=True)
            low = (risen * share).astype(BF16)
            prob_buf[slot, h] = low
            made = jnp.dot(low, head_rows[4 + h], preferred_element_type=F32).astype(BF16)
            mixed[2 * to_x, :, cols] = made[:rows]
            mixed[2 * to_x + 1, :, cols] = made[rows:]

    prob_index = net.reserve(2)

    def keep_probs(to_x, slot):
        return pltpu.make_async_copy(
            prob_buf.at[slot], probs.at[:, aligned(to_x, 2 * rows), :], still.at[prob_index + slot]
        )

    mixed_base = net.reserve(8)

    def mixed_send(dx, dc):
        slot = 2 * ((x + dx) % 4) + (c + dc) % 2
        return net.copy(
            mixed_base + 2 * dx + dc, mixed.at[slot], attended.at[me], net.device(dx, dc)
        )

    @pl.loop(1, 5)
    def _(step):
        dx = step % 4
        to_x = (x + dx) % 4

        @pl.when(step > 2)
        def _():
            keep_probs(to_x, step % 2).wait()

        attend_rows(to_x, step % 2)
        keep_probs(to_x, step % 2).start()
        mixed_send(dx, 1).start()

        @pl.when(dx != 0)
        def _():
            mixed_send(dx, 0).start()

    attended[me] = mixed[me]
    for d in (1, 3, 2):
        top_copy(d).wait_recv()
        top_pass(d).start()
    for d in (1, 3, 2):
        out_share(d).wait_recv()
        out_pass(d).start()
    for dx in range(4):
        for dc in range(2):
            if dx or dc:
                mixed_send(dx, dc).wait()
    for d in range(4):
        top_pass(d).wait()
        out_pass(d).wait()
    for d in (1, 2, 3):
        up_share(d).wait()
        for copy in (cut_copy, cut_share, up_copy, top_copy, out_copy, out_share):
            copy(d).wait_send()

    @pl.when(c == zl)
    def _():
        down_local.wait()

    @pl.when(c != zl)
    def _():
        down_cross.wait_send()
        for d in (1, 2, 3):
            down_share(d).wait()

    keep_h1.wait()
    keep_heads.wait()
    for slot in range(2):
        keep_probs(slot, slot).wait()
    bias_arrived()
    for left in (token_left, out_left, top_left, bias_left):
        left()
    for k in range(2):
        token_send(k, gathered.at[me]).wait_send()
        token_half(k).wait_send()
    for k in range(3):
        passed(order(k), me).wait_send()
    net.all_sent()


def begin(tokens, w_query, w_key, w_value, small, up_bias, w_out, w_up, w_down, cotangent, length):
    rows, width = tokens.shape

    def shape(*dims):
        return jax.ShapeDtypeStruct(dims, BF16)

    return pl.pallas_call(
        begin_kernel,
        in_specs=[VMEM] * 11,
        out_specs=[HBM] * 3 + [VMEM] * 7 + [HBM] * 4 + [VMEM],
        out_shape=[
            shape(8, rows, width),
            shape(6, 8 * rows, HD),
            shape(2, 8 * rows, 8 * rows),
            shape(8, rows, 160),
            shape(8, rows, 160),
            shape(4, 2, 2, 80, 480),
            shape(8, 16, 160),
            shape(16, 640),
            shape(rows, width),
            jax.ShapeDtypeStruct((8, 128), F32),
            shape(4, 2, 2, 80, width),
            shape(4, 2, 2, 80, 640),
            shape(640, width),
            shape(8, rows, width),
            shape(160, width),
        ],
        scratch_shapes=[
            pltpu.VMEM((8, rows, width), BF16),
            pltpu.VMEM((6, 8 * rows, HD), BF16),
            pltpu.VMEM((2, 2, 2 * rows, 8 * rows), BF16),
            pltpu.VMEM((8, rows, width), BF16),
            pltpu.VMEM((8, 2, 80, 480), BF16),
            pltpu.VMEM((2, 8, 128), F32),
            pltpu.VMEM((8, width), F32),
        ]
        + scratch_for(96),
        compiler_params=pltpu.CompilerParams(
            collective_id=0, has_side_effects=True, vmem_limit_bytes=58 << 20
        ),
    )(tokens, w_query, w_key, w_value, small, up_bias, w_out, w_up, w_down, cotangent, length)


def middle_kernel(
    attended,
    own,
    smalls,
    up_bias,
    clip,
    out_full,
    up_mine,
    down_mine,
    top,
    result,
    grad_middle,
    branch,
    out_sums,
    g_up,
    g_down,
    g_up_bias,
    g_vectors,
    grad_mixed,
    vectors,
    middle,
    second,
    masked,
    active,
    hidden,
    parts,
    over,
    sums,
    arrived,
    out_parts,
    out_over,
    joined,
    by_head,
    sent,
    got,
    still,
):
    net = Net(sent, got, still)
    x, c, me = net.x, net.c, net.me
    rows, width = own.shape
    wait = net.greet([net.device(dx, dc) for dx in range(4) for dc in range(2) if dx or dc])
    for block in range(8):
        vectors[:, 160 * block : 160 * block + 160] = smalls[block, :8, :].astype(F32)
    bias_up = up_bias[0:1, :].astype(F32)
    mine = aligned(me, rows)
    for block in range(8):
        joined[:, 160 * block : 160 * block + 160] = attended[block]
    made = jnp.dot(joined[...], out_full[...], preferred_element_type=F32)
    middle[...] = own[...].astype(F32) + made + vectors[2:3, :]

    def normalised():
        values = middle[...]
        center = values - jnp.mean(values, axis=-1, keepdims=True)
        inverse = lax.rsqrt(jnp.mean(center * center, axis=-1, keepdims=True) + EPS)
        return center * inverse, inverse

    second[mine, :] = (normalised()[0] * vectors[6:7, :] + vectors[7:8, :]).astype(BF16)
    wait()

    near, pass_on, swap, add, out_swap = (net.reserve(4) for _ in range(5))

    def out_copy(dx, to_x):
        source = out_parts.at[aligned(2 * to_x + 1 - c, rows)]
        return net.copy(out_swap + dx, source, out_over.at[to_x], net.device(0, 1))

    def near_copy(dx):
        return net.copy(near + dx, second.at[mine], second.at[mine], net.device(dx))

    def pass_copy(dx, slot):
        here = second.at[aligned(slot, rows)]
        return net.copy(pass_on + dx, here, here, net.device(0, 1))

    def swap_copy(dx, to_x):
        source = parts.at[aligned(2 * to_x + 1 - c, rows)]
        return net.copy(swap + dx, source, over.at[to_x], net.device(0, 1))

    def add_copy(dx, to_x):
        return net.copy(add + dx, sums.at[to_x], arrived.at[dx], net.device(4 - dx))

    halves = net.reserve(2)

    def half_copy(i):
        slot = 2 * ((x + 3 + 2 * i) % 4) + c
        here = second.at[aligned(2 * slot + i, rows // 2)]
        return net.copy(halves + i, here, here, net.device(1 + 2 * i))

    for dx in (1, 3):
        near_copy(dx).start()

    @pl.loop(0, 4)
    def _(k):
        dx = k ^ (k >> 1)
        to_x = (x - dx + 4) % 4

        @pl.when(k == 1)
        def _():
            for i in range(2):
                near_copy(1 + 2 * i).wait_recv()
                half_copy(i).start()

        @pl.when(k == 3)
        def _():
            for i in range(2):
                half_copy(i).wait_recv()

        pass_copy(dx, 2 * to_x + c).start()
        here = aligned(to_x, 2 * rows)
        position = lax.broadcasted_iota(jnp.int32, (2 * rows, 1), 0) + to_x * 2 * rows
        live = position.astype(F32) < clip[0:1, 0:1]
        low_top = jnp.where(live, top[here, :].astype(F32), 0.0).astype(BF16)
        masked[here, :] = low_top
        grad_act = lax.dot_general(low_top, down_mine[...], NT, preferred_element_type=F32)
        pass_copy(dx, 2 * to_x + c).wait_recv()
        z = jnp.dot(second[here, :], up_mine[...], preferred_element_type=F32) + bias_up
        bell = 0.5 * (1.0 + lax.erf(z * 0.7071067811865476))
        active[here, :] = (z * bell).astype(BF16)
        slope = bell + z * jnp.exp(-0.5 * z * z) * 0.3989422804014327
        grad_z = (grad_act * slope).astype(BF16)
        hidden[here, :] = grad_z
        parts[here, :] = lax.dot_general(
            grad_z, up_mine[...], NT, preferred_element_type=F32
        ).astype(BF16)
        swap_copy(dx, to_x).start()
        out_parts[here, :] = jnp.dot(
            active[here, :], down_mine[...], preferred_element_type=F32
        ).astype(BF16)
        out_copy(dx, to_x).start()
        swap_copy(dx, to_x).wait_recv()

        @pl.when(dx != 0)
        def _():
            kept = parts[aligned(2 * to_x + c, rows), :].astype(F32)
            sums[to_x] = (kept + over[to_x].astype(F32)).astype(BF16)
            add_copy(dx, to_x).start()

    @pl.loop(0, 5)
    def _(i):
        cols = pl.ds(pl.multiple_of(i * 256, 256), 256)
        g_up[cols, :] = lax.dot_general(
            second[:, cols], hidden[...], TN, preferred_element_type=F32
        ).astype(BF16)
        cols = pl.ds(pl.multiple_of(i * 128, 128), 128)
        g_down[cols, :] = lax.dot_general(
            active[:, cols], masked[...], TN, preferred_element_type=F32
        ).astype(BF16)

    for dx in range(4):
        to_x = (x - dx + 4) % 4
        out_copy(dx, to_x).wait_recv()
        kept = out_parts[aligned(2 * to_x + c, rows), :].astype(F32) + out_over[to_x].astype(F32)
        if dx:
            out_sums[to_x] = kept.astype(BF16)
        else:
            result[...] = middle[...] + kept + vectors[3:4, :]
    g_up_bias[...] = jnp.sum(hidden[...].astype(F32), axis=0, keepdims=True)
    grad_second = parts[mine, :].astype(F32) + over[x].astype(F32)
    for dx in (1, 3, 2):
        add_copy(dx, (x - dx + 4) % 4).wait_recv()
        grad_second = grad_second + arrived[dx].astype(F32)
    normed, inverse = normalised()
    scaled = grad_second * vectors[6:7, :]
    back = inverse * (
        scaled
        - jnp.mean(scaled, axis=-1, keepdims=True)
        - normed * jnp.mean(scaled * normed, axis=-1, keepdims=True)
    )
    top_own = masked[mine, :].astype(F32)
    total = top_own + back
    grad_middle[...] = total
    low = total.astype(BF16)
    branch[...] = low
    grad_attended = lax.dot_general(low, out_full[...], NT, preferred_element_type=F32)
    grad_attended = grad_attended.astype(BF16)
    for block in range(8):
        by_head[block] = grad_attended[:, 160 * block : 160 * block + 160]
    mixing = []
    for dx in (2, 1, 3, 0):
        for dc in (1, 0):
            if dx or dc:
                slot = 2 * ((x + dx) % 4) + (c + dc) % 2
                mixing.append(net.go(by_head.at[slot], grad_mixed.at[me], net.device(dx, dc)))
    grad_mixed[me] = by_head[me]
    g_vectors[0:1, :] = jnp.sum(low.astype(F32), axis=0, keepdims=True)
    g_vectors[1:2, :] = jnp.sum(top_own, axis=0, keepdims=True)
    g_vectors[2:3, :] = jnp.sum(grad_second * normed, axis=0, keepdims=True)
    g_vectors[3:4, :] = jnp.sum(grad_second, axis=0, keepdims=True)
    for copy in mixing:
        copy.wait_recv()
    for dx in range(4):
        to_x = (x - dx + 4) % 4
        pass_copy(dx, 2 * to_x + c).wait_send()
        swap_copy(dx, to_x).wait_send()
        out_copy(dx, to_x).wait_send()
        if dx:
            add_copy(dx, to_x).wait_send()
    for i in range(2):
        near_copy(1 + 2 * i).wait_send()
        half_copy(i).wait_send()
    net.all_sent()


def middle_part(attended, own, smalls, up_bias, clip, out_full, up_mine, down_mine, top):
    rows, width = own.shape

    def shape(*dims, dtype=BF16):
        return jax.ShapeDtypeStruct(dims, dtype)

    def buffer(*dims, dtype=BF16):
        return pltpu.VMEM(dims, dtype)

    return pl.pallas_call(
        middle_kernel,
        in_specs=[VMEM] * 9,
        out_specs=[VMEM] * 9,
        out_shape=[
            shape(rows, width, dtype=F32),
            shape(rows, width, dtype=F32),
            shape(rows, width),
            shape(4, rows, width),
            shape(width, 640),
            shape(640, width),
            shape(1, 640, dtype=F32),
            shape(4, width, dtype=F32),
            shape(8, rows, 160),
        ],
        scratch_shapes=[
            buffer(8, width, dtype=F32),
            buffer(rows, width, dtype=F32),
            buffer(8 * rows, width),
            buffer(8 * rows, width),
            buffer(8 * rows, 640),
            buffer(8 * rows, 640),
            buffer(8 * rows, width),
            buffer(4, rows, width),
            buffer(4, rows, width),
            buffer(4, rows, width),
            buffer(8 * rows, width),
            buffer(4, rows, width),
            buffer(rows, width),
            buffer(8, rows, 160),
        ]
        + scratch_for(32),
        compiler_params=pltpu.CompilerParams(
            collective_id=1, has_side_effects=True, vmem_limit_bytes=60 << 20
        ),
    )(attended, own, smalls, up_bias, clip, out_full, up_mine, down_mine, top)


def piece_start(index):
    return pl.multiple_of(48 * index - 32 * (index // 3), 16)


def column_flow(net, source, r1, s1, r2, s2, planes, landed, place_of):
    y, z, x, c = net.y, 2 * net.zh + net.zl, net.x, net.c
    b1, b2, b3, b4, b5 = (net.reserve(4) for _ in range(5))
    sibling = net.device(0, 1)

    def copy_1(d):
        rows = pl.ds(piece_start((y + d) % 4), 48)
        return net.copy(b1 + d, source.at[:, rows, :], r1.at[d], net.device(dy=d))

    mine = pltpu.make_async_copy(
        source.at[:, pl.ds(piece_start(y), 48), :], r1.at[0], net.still.at[b1]
    )

    def copy_2(d):
        part = s1.at[pl.ds(2 * ((z + d) % 4), 2)]
        return net.copy(b2 + d, part, r2.at[d], net.device(dz=d))

    def copy_3(d):
        return net.copy(b3 + d, s2.at[(z + d) % 2], planes.at[z], net.device(dz=d))

    def copy_4(d):
        target = place_of(landed, 2 * x + c)
        return net.copy(b4 + d, planes.at[(x + d) % 4], target, net.device(d))

    def copy_5(d):
        here = place_of(landed, 2 * ((x - d + 4) % 4) + c)
        return net.copy(b5 + d, here, here, sibling)

    def first():
        mine.start()
        for d in (2, 1, 3):
            copy_1(d).start()

    def second():
        mine.wait()
        for d in (1, 2, 3):
            copy_1(d).wait_recv()
        total = r1[0].astype(F32)
        for d in (1, 2, 3):
            total = total + r1[d].astype(F32)
        s1[...] = total.astype(BF16)
        for d in (2, 1, 3):
            copy_2(d).start()

    def third():
        total = s1[pl.ds(2 * z, 2)].astype(F32)
        for d in (1, 2, 3):
            copy_2(d).wait_recv()
            total = total + r2[d].astype(F32)
        s2[...] = total.astype(BF16)
        for d in (2, 1, 3):
            copy_3(d).start()
        planes[z] = s2[z % 2]

    def fourth():
        for d in (1, 2, 3):
            copy_3(d).wait_recv()
        for d in (2, 1, 3):
            copy_4(d).start()
        place_of(landed, 2 * x + c)[...] = planes[x]
        copy_5(0).start()

    def fifth():
        for d in (1, 3, 2):
            copy_4(d).wait_recv()
            copy_5(d).start()
        for d in range(4):
            copy_5(d).wait_recv()

    def sent():
        for d in range(4):
            copy_5(d).wait_send()
        for d in (1, 2, 3):
            for copy in (copy_1, copy_2, copy_3, copy_4):
                copy(d).wait_send()

    return first, second, third, fourth, fifth, sent


def share_over_y(net, whole, final, half_of):
    y = net.y
    near, over = net.reserve(4), net.reserve(4)
    own = pltpu.make_async_copy(whole, final.at[y], net.still.at[near])

    def copy(d):
        return net.copy(near + d, half_of(whole), half_of(final.at[y]), net.device(dy=d))

    def forward(d):
        here = half_of(final.at[(y - d + 4) % 4])
        return net.copy(over + d, here, here, net.device(0, 1))

    def first():
        own.start()
        for d in (2, 1, 3):
            copy(d).start()

    def second():
        for d in (1, 3, 2):
            copy(d).wait_recv()
            forward(d).start()

    def third():
        own.wait()
        for d in (1, 2, 3):
            forward(d).wait_recv()
            forward(d).wait_send()
            copy(d).wait_send()

    return first, second, third


def four_way(net, base, held, position, device_of):
    def copy(d):
        return net.copy(base + d, held.at[position], held.at[position], device_of(d))

    def go():
        for d in (2, 1, 3):
            copy(d).start()

    def total():
        for d in (1, 2, 3):
            copy(d).wait_recv()
        return (held[0].astype(F32) + held[1].astype(F32)) + (
            held[2].astype(F32) + held[3].astype(F32)
        )

    def sent():
        for d in (1, 2, 3):
            copy(d).wait_send()

    return go, total, sent


def finish_kernel(
    heads,
    mixed,
    grad_mixed,
    w_qkv,
    own,
    smalls,
    result,
    grad_middle,
    branch,
    g_up_bias,
    g_vectors,
    out_sums,
    probs,
    h1,
    g_up,
    g_down,
    hb_out,
    vec_out,
    output,
    input_grad,
    fin_up,
    fin_qkv,
    fin_down,
    fin_out,
    branch_all,
    tall,
    prob_buf,
    grads,
    sum_k,
    sum_v,
    give,
    over,
    sums,
    arrived,
    out_arrived,
    final_rows,
    final_grad,
    low_grad,
    up_r1,
    up_s1,
    up_r2,
    up_s2,
    up_planes,
    up_landed,
    g_head_0,
    r1_head_0,
    s1_head_0,
    r2_head_0,
    s2_head_0,
    planes_head_0,
    landed_head_0,
    g_head_1,
    r1_head_1,
    s1_head_1,
    r2_head_1,
    s2_head_1,
    planes_head_1,
    landed_head_1,
    qkv_rows,
    w_heads,
    down_r1,
    down_s1,
    down_r2,
    down_l3,
    down_p,
    g_out,
    out_r1,
    out_z,
    out_t,
    head_y,
    head_z,
    head_sib,
    vec_cut,
    vec_1,
    vec_1s,
    vec_2,
    vec_3,
    vectors,
    sent,
    got,
    still,
):
    net = Net(sent, got, still)
    x, y, c, zl, me = net.x, net.y, net.c, net.zl, net.me
    z = 2 * net.zh + zl
    rows, width = own.shape
    sibling = net.device(0, 1)
    wait = net.greet(
        [net.device(dx, dc) for dx in range(4) for dc in range(2) if dx or dc]
        + [net.device(dy=d) for d in (1, 2, 3)]
        + [net.device(dz=d) for d in (1, 2, 3)]
        + [(y * 4 + net.zh * 2 + 1 - c, 2 * x + 1 - zl)]
    )

    tile = 2 * rows
    slots = net.reserve(2)

    def load_probs(j):
        slot = j % 2
        return pltpu.make_async_copy(
            probs.at[j // 4, aligned(j % 4, tile), :], prob_buf.at[slot], still.at[slots + slot]
        )

    load_probs(0).start()
    load_h1 = pltpu.make_async_copy(h1, tall, still.at[net.reserve(1)])
    load_h1.start()
    own_branch = pltpu.make_async_copy(
        branch, branch_all.at[aligned(me, rows)], still.at[net.reserve(1)]
    )
    own_branch.start()
    for block in range(8):
        vectors[:, 160 * block : 160 * block + 160] = smalls[block, :8, :].astype(F32)
    for h in range(2):
        w_heads[h] = w_qkv[:, 240 * h : 240 * h + 240]

    up = column_flow(
        net,
        g_up,
        up_r1,
        up_s1,
        up_r2,
        up_s2,
        up_planes,
        up_landed,
        lambda ref, hb: ref.at[:, pl.ds(pl.multiple_of(hb * 640, 128), 640)],
    )
    head_buffers = (
        (g_head_0, r1_head_0, s1_head_0, r2_head_0, s2_head_0, planes_head_0, landed_head_0),
        (g_head_1, r1_head_1, s1_head_1, r2_head_1, s2_head_1, planes_head_1, landed_head_1),
    )
    flows = [column_flow(net, *held, lambda ref, hb: ref.at[hb]) for held in head_buffers]
    up_share = share_over_y(
        net,
        up_landed,
        fin_up,
        lambda ref: ref.at[:, pl.ds(pl.multiple_of(c * 2560, 128), 2560)],
    )
    three_share = share_over_y(
        net,
        qkv_rows,
        fin_qkv,
        lambda ref: ref.at[:, :, pl.ds(pl.multiple_of(c * 640, 128), 640)],
    )

    d1, d2, d4, d5 = (net.reserve(4) for _ in range(4))
    d3_go, _, d3_sent = four_way(net, d3 := net.reserve(4), down_l3, y, lambda d: net.device(dy=d))
    down_mine = pltpu.make_async_copy(
        g_down.at[aligned(z, 160)], down_r1.at[0], still.at[d1]
    )

    def down_1(d):
        return net.copy(d1 + d, g_down.at[aligned((z + d) % 4, 160)], down_r1.at[d], net.device(dz=d))

    def down_2(d):
        part = down_s1.at[pl.ds(piece_start((y + d) % 4), 48)]
        return net.copy(d2 + d, part, down_r2.at[d], net.device(dy=d))

    def down_4(k, source_z):
        to_z = c + 2 * k
        return pltpu.make_async_remote_copy(
            src_ref=down_p,
            dst_ref=fin_down.at[aligned(source_z, 160)],
            send_sem=sent.at[d4 + k],
            recv_sem=got.at[d4 + source_z],
            device_id=(y * 4 + to_z // 2 * 2 + c, 2 * x + to_z % 2),
            device_id_type=MESH,
        )

    down_local = pltpu.make_async_copy(down_p, fin_down.at[aligned(z, 160)], still.at[d4])

    def down_5(source_z):
        here = fin_down.at[aligned(source_z, 160)]
        return net.copy(d5 + source_z, here, here, sibling)

    e1, e3, e4 = (net.reserve(4) for _ in range(3))
    out_go, out_total, out_sent = four_way(
        net, net.reserve(4), out_z, z, lambda d: net.device(dz=d)
    )

    def out_1(d):
        part = g_out.at[pl.ds(piece_start((y + d) % 4), 48)]
        return net.copy(e1 + d, part, out_r1.at[d], net.device(dy=d))

    def out_3(d):
        return net.copy(e3 + d, out_t, fin_out.at[y], net.device(dy=d))

    out_local = pltpu.make_async_copy(out_t, fin_out.at[y], still.at[e3])

    def out_4(source_y):
        return net.copy(e4 + source_y, fin_out.at[source_y], fin_out.at[source_y], sibling)

    near, pass_on, swap, add, out_add = (net.reserve(4) for _ in range(5))

    def near_copy(dx):
        return net.copy(near + dx, branch, branch_all.at[aligned(me, rows)], net.device(dx))

    def pass_copy(dx):
        here = branch_all.at[aligned(2 * ((x - dx + 4) % 4) + c, rows)]
        return net.copy(pass_on + dx, here, here, sibling)

    def swap_copy(dx, to_x):
        return net.copy(swap + dx, give.at[to_x], over.at[to_x], sibling)

    def add_copy(dx, to_x):
        return net.copy(add + dx, sums.at[to_x], arrived.at[dx], net.device(4 - dx))

    def out_add_copy(dx):
        to_x = (x - dx + 4) % 4
        return net.copy(out_add + dx, out_sums.at[to_x], out_arrived.at[dx], net.device(4 - dx))

    wait()
    for dx in (1, 3, 2):
        near_copy(dx).start()
    up[0]()
    down_mine.start()
    for d in (2, 1, 3):
        down_1(d).start()

    for h in range(2):
        cols = slice(h * HD, (h + 1) * HD)
        sum_k[...] = jnp.zeros_like(sum_k)
        sum_v[...] = jnp.zeros_like(sum_v)

        @pl.loop(0, 4)
        def _(i, h=h, cols=cols):
            j = 4 * h + i

            @pl.when(j < 7)
            def _():
                load_probs(j + 1).start()

            load_probs(j).wait()
            here = aligned(i, tile)
            back = jnp.concatenate([grad_mixed[2 * i, :, cols], grad_mixed[2 * i + 1, :, cols]])
            seen = jnp.concatenate([mixed[2 * i, :, cols], mixed[2 * i + 1, :, cols]])
            low = prob_buf[j % 2]
            row_total = jnp.sum(back.astype(F32) * seen.astype(F32), axis=-1, keepdims=True)
            grad_probs = lax.dot_general(back, heads[4 + h], NT, preferred_element_type=F32)
            grad_scores = (low.astype(F32) * (grad_probs - row_total)).astype(BF16)
            sum_v[...] += lax.dot_general(low, back, TN, preferred_element_type=F32)
            sum_k[...] += lax.dot_general(
                grad_scores, heads[h, here, :], TN, preferred_element_type=F32
            )
            grad_q = jnp.dot(grad_scores, heads[2 + h], preferred_element_type=F32)
            grads[h, here, :80] = (grad_q * HD**-0.5).astype(BF16)

        grads[h, :, 80:160] = (sum_k[...] * HD**-0.5).astype(BF16)
        grads[h, :, 160:] = sum_v[...].astype(BF16)
        if h == 0:
            load_h1.wait()

        @pl.loop(0, 2)
        def _(i, h=h):
            cols = pl.ds(pl.multiple_of(i * 640, 128), 640)
            made = lax.dot_general(tall[:, cols], grads[h], TN, preferred_element_type=F32)
            head_buffers[h][0][pl.ds(4 * i, 4)] = made.astype(BF16).reshape(4, 160, 240)

        flows[h][0]()

    def back_rows(block):
        made = [
            lax.dot_general(
                grads[h, aligned(block, rows), :], w_heads[h], NT, preferred_element_type=F32
            )
            for h in range(2)
        ]
        return made[0] + made[1]

    @pl.loop(0, 4)
    def _(k):
        dx = jnp.where(k == 3, 0, order(k))
        to_x = (x - dx + 4) % 4
        give[to_x] = back_rows(2 * to_x + 1 - c).astype(BF16)
        swap_copy(dx, to_x).start()

    @pl.loop(0, 4)
    def _(k):
        dx = jnp.where(k == 3, 0, order(k))
        to_x = (x - dx + 4) % 4
        kept = back_rows(2 * to_x + c)
        swap_copy(dx, to_x).wait_recv()
        kept = kept + over[to_x].astype(F32)

        @pl.when(dx != 0)
        def _():
            sums[to_x] = kept.astype(BF16)
            add_copy(dx, to_x).start()

        @pl.when(dx == 0)
        def _():
            final_grad[...] = kept

    own_branch.wait()
    pass_copy(0).start()
    for dx in (1, 3, 2):
        near_copy(dx).wait_recv()
        pass_copy(dx).start()

    up[1]()
    down_mine.wait()
    total = down_r1[0].astype(F32)
    for d in (1, 2, 3):
        down_1(d).wait_recv()
        total = total + down_r1[d].astype(F32)
    down_s1[...] = total.astype(BF16)
    for d in (2, 1, 3):
        down_2(d).start()

    for dx in range(4):
        pass_copy(dx).wait_recv()
        pass_copy(dx).wait_send()
    load_branch = pltpu.make_async_copy(branch_all, tall, still.at[net.reserve(1)])
    load_branch.start()
    load_branch.wait()
    seen = jnp.concatenate([mixed[block] for block in range(8)])
    g_out[...] = lax.dot_general(seen, tall[...], TN, preferred_element_type=F32).astype(BF16)
    for d in (2, 1, 3):
        out_1(d).start()

    head_y[y] = jnp.zeros((8, 640), F32)
    head_y[y, 0:1, :] = g_up_bias[...]
    for h in range(2):
        cols = slice(h * HD, (h + 1) * HD)
        column_sums = jnp.sum(grads[h].astype(F32), axis=0, keepdims=True)
        head_y[y, 1:2, cols] = column_sums[:, :80]
        head_y[y, 2:3, cols] = column_sums[:, 160:]
    head_y_go, head_y_total, head_y_sent = four_way(
        net, net.reserve(4), head_y, y, lambda d: net.device(dy=d)
    )
    head_y_go()

    for flow in flows:
        flow[1]()
    up[2]()
    total = down_s1[pl.ds(piece_start(y), 48), :].astype(F32)
    for d in (1, 2, 3):
        down_2(d).wait_recv()
        total = total + down_r2[d].astype(F32)
    down_l3[y] = total.astype(BF16)
    d3_go()

    for flow in flows:
        flow[2]()
    up[3]()
    for d in (1, 2, 3):
        net.copy(d3 + d, down_l3.at[y], down_l3.at[y], net.device(dy=d)).wait_recv()
    for i in range(3):
        down_p[48 * i : 48 * i + 48, :] = down_l3[i]
    down_p[144:160, :] = down_l3[3, 32:48, :]
    for k in range(2):

        @pl.when(c + 2 * k != z)
        def _():
            down_4(k, z).start()

    @pl.when(c == zl)
    def _():
        down_local.start()

    up[4]()
    up_share[0]()
    for flow in flows:
        flow[3]()
    grad_first = final_grad[...]
    for dx in (1, 3, 2):
        add_copy(dx, (x - dx + 4) % 4).wait_recv()
        grad_first = grad_first + arrived[dx].astype(F32)
    values = own[...].astype(F32)
    center = values - jnp.mean(values, axis=-1, keepdims=True)
    inverse = lax.rsqrt(jnp.mean(center * center, axis=-1, keepdims=True) + EPS)
    normed = center * inverse
    scaled = grad_first * vectors[4:5, :]
    back = inverse * (
        scaled
        - jnp.mean(scaled, axis=-1, keepdims=True)
        - normed * jnp.mean(scaled * normed, axis=-1, keepdims=True)
    )
    low_grad[...] = (grad_middle[...] + back).astype(BF16)
    grad_arrived, grad_left = net.cross(low_grad, input_grad)
    gain = jnp.sum(grad_first * normed, axis=0, keepdims=True)
    shift = jnp.sum(grad_first, axis=0, keepdims=True)
    for block in range(8):
        cols = slice(160 * block, 160 * block + 160)
        here = vec_cut.at[block // 2, block % 2]
        here[0:4, :] = g_vectors[:, cols]
        here[4:5, :] = gain[:, cols]
        here[5:6, :] = shift[:, cols]
        here[6:8, :] = jnp.zeros((2, 160), F32)
    v1 = net.reserve(8)

    def vec_copy(dx, dc):
        return net.copy(
            v1 + 2 * dx + dc, vec_cut.at[(x + dx) % 4], vec_1.at[me], net.device(dx, dc)
        )

    others = [(dx, dc) for dx in (2, 1, 3, 0) for dc in (1, 0) if dx or dc]
    for dx, dc in others:
        vec_copy(dx, dc).start()
    vec_1[me] = vec_cut[x]

    for dx in (1, 3, 2):
        out_add_copy(dx).start()
    for flow in flows:
        flow[4]()
    for block in range(8):
        cols = slice(160 * block, 160 * block + 160)
        for k in range(3):
            qkv_rows[k, :, cols] = jnp.concatenate(
                [held[6][block, :, 80 * k : 80 * k + 80] for held in head_buffers], axis=1
            )
    three_share[0]()
    total = g_out[pl.ds(piece_start(y), 48), :].astype(F32)
    for d in (1, 2, 3):
        out_1(d).wait_recv()
        total = total + out_r1[d].astype(F32)
    out_z[z] = total.astype(BF16)
    out_go()
    head_z[z] = head_y_total()
    head_z_go, head_z_total, head_z_sent = four_way(
        net, net.reserve(4), head_z, z, lambda d: net.device(dz=d)
    )
    head_z_go()
    for dx, dc in others:
        vec_copy(dx, dc).wait_recv()
    total = vec_1[0]
    for block in range(1, 8):
        total = total + vec_1[block]
    vec_1s[...] = total
    v2 = net.reserve(4)

    def vec_z(d):
        return net.copy(v2 + d, vec_1s.at[(z + d) % 2], vec_2.at[z], net.device(dz=d))

    for d in (2, 1, 3):
        vec_z(d).start()
    vec_2[z] = vec_1s[zl]
    out_t[...] = out_total().astype(BF16)

    @pl.when(c == zl)
    def _():
        out_local.start()
        for d in (2, 1, 3):
            out_3(d).start()

    head_sib[0] = head_z_total()
    head_copy = net.go(head_sib.at[0], head_sib.at[1], sibling)
    for d in (1, 2, 3):
        vec_z(d).wait_recv()
    vec_3[y] = (vec_2[0] + vec_2[1]) + (vec_2[2] + vec_2[3])
    vec_y_go, vec_y_total, vec_y_sent = four_way(
        net, net.reserve(4), vec_3, y, lambda d: net.device(dy=d)
    )
    vec_y_go()

    @pl.when(c == zl)
    def _():
        down_local.wait()
        down_5(z).start()
        for d in (1, 2, 3):
            source_z = (z + d) % 4
            down_4(0, source_z).wait_recv()
            down_5(source_z).start()
        out_local.wait()
        out_4(y).start()
        for d in (1, 2, 3):
            out_3(d).wait_recv()
            out_4((y + 4 - d) % 4).start()

    total = result[...]
    for dx in (1, 3, 2):
        out_add_copy(dx).wait_recv()
        total = total + out_arrived[dx].astype(F32)
    final_rows[...] = total.astype(BF16)
    output_arrived, output_left = net.cross(final_rows, output)

    up_share[1]()
    three_share[1]()
    head_copy.wait_recv()
    hb_out[...] = jnp.where(c == zl, head_sib[0], head_sib[1])
    vec_out[...] = vec_y_total()

    @pl.when(c == zl)
    def _():
        for i in range(4):
            down_5(i).wait_send()
            out_4(i).wait_send()
        for d in (1, 2, 3):
            out_3(d).wait_send()

    @pl.when(c != zl)
    def _():
        for i in range(4):
            down_5(i).wait_recv()
            out_4(i).wait_recv()

    for k in range(2):

        @pl.when(c + 2 * k != z)
        def _():
            down_4(k, z).wait_send()

    up_share[2]()
    three_share[2]()
    grad_arrived()
    grad_left()
    output_arrived()
    output_left()
    for done in (up[5], flows[0][5], flows[1][5], d3_sent, out_sent, head_y_sent, head_z_sent, vec_y_sent):
        done()
    for d in (1, 2, 3):
        down_1(d).wait_send()
        down_2(d).wait_send()
        out_1(d).wait_send()
        vec_z(d).wait_send()
        near_copy(d).wait_send()
        add_copy(d, (x - d + 4) % 4).wait_send()
        out_add_copy(d).wait_send()
    for d in range(4):
        swap_copy(d, (x - d + 4) % 4).wait_send()
    for dx, dc in others:
        vec_copy(dx, dc).wait_send()
    net.all_sent()


def finish(
    heads,
    mixed,
    grad_mixed,
    w_qkv,
    own,
    smalls,
    result,
    grad_middle,
    branch,
    out_sums,
    g_up_bias,
    g_vectors,
    probs,
    h1,
    g_up,
    g_down,
):
    rows, width = own.shape

    def shape(*dims, dtype=BF16):
        return jax.ShapeDtypeStruct(dims, dtype)

    def buffer(*dims, dtype=BF16):
        return pltpu.VMEM(dims, dtype)

    def column_buffers(columns):
        return [
            buffer(4, 8, 48, columns),
            buffer(8, 48, columns),
            buffer(4, 2, 48, columns),
            buffer(2, 48, columns),
            buffer(4, 48, columns),
        ]

    return pl.pallas_call(
        finish_kernel,
        in_specs=[VMEM] * 11 + [HBM] * 5,
        out_specs=[VMEM] * 2 + [HBM] * 7,
        out_shape=[
            shape(8, 640, dtype=F32),
            shape(8, 160, dtype=F32),
            shape(rows, width),
            shape(rows, width),
            shape(4, 48, 5120),
            shape(4, 3, 48, width),
            shape(640, width),
            shape(4, 48, width),
            shape(8 * rows, width),
        ],
        scratch_shapes=[
            buffer(8 * rows, width),
            buffer(2, 2 * rows, 8 * rows),
            buffer(2, 8 * rows, 240),
            buffer(8 * rows, HD, dtype=F32),
            buffer(8 * rows, HD, dtype=F32),
            buffer(4, rows, width),
            buffer(4, rows, width),
            buffer(4, rows, width),
            buffer(4, rows, width),
            buffer(4, rows, width),
            buffer(rows, width),
            buffer(rows, width, dtype=F32),
            buffer(rows, width),
        ]
        + column_buffers(640)
        + [buffer(48, 5120)]
        + ([buffer(8, 160, 240)] + column_buffers(240) + [buffer(8, 48, 240)]) * 2
        + [
            buffer(3, 48, width),
            buffer(2, width, 240),
            buffer(4, 160, width),
            buffer(160, width),
            buffer(4, 48, width),
            buffer(4, 48, width),
            buffer(160, width),
            buffer(160, width),
            buffer(4, 48, width),
            buffer(4, 48, width),
            buffer(48, width),
            buffer(4, 8, 640, dtype=F32),
            buffer(4, 8, 640, dtype=F32),
            buffer(2, 8, 640, dtype=F32),
            buffer(4, 2, 8, 160, dtype=F32),
            buffer(8, 2, 8, 160, dtype=F32),
            buffer(2, 8, 160, dtype=F32),
            buffer(4, 8, 160, dtype=F32),
            buffer(4, 8, 160, dtype=F32),
            buffer(8, width, dtype=F32),
        ]
        + scratch_for(192),
        compiler_params=pltpu.CompilerParams(
            collective_id=2, has_side_effects=True, vmem_limit_bytes=62 << 20
        ),
    )(
        heads,
        mixed,
        grad_mixed,
        w_qkv,
        own,
        smalls,
        result,
        grad_middle,
        branch,
        g_up_bias,
        g_vectors,
        out_sums,
        probs,
        h1,
        g_up,
        g_down,
    )


def widen_kernel(hb, vec, up, three, down, out, rows, grad, *results):
    o_up, o_q, o_k, o_v, o_down, o_out, o_rows, o_grad = results[:8]
    small, scratch = results[8:17], results[17:]
    b_up, b_three, b_down, b_out, b_rows, b_grad, f_up, f_three, f_down, f_out, f_grad, came, done = scratch
    loads, copies = [], []
    sources = ((up, b_up), (three, b_three), (down, b_down), (out, b_out), (grad, b_grad), (rows, b_rows))
    for source, target in sources:
        loads.append(pltpu.make_async_copy(source, target, came.at[len(loads)]))
        loads[-1].start()

    def push(source, target):
        copy = pltpu.make_async_copy(source, target, done.at[len(copies)])
        copy.start()
        copies.append(copy)

    pieces = ((slice(0, 48), 0, slice(0, 48)), (slice(48, 96), 1, slice(0, 48)))
    pieces += ((slice(96, 144), 2, slice(0, 48)), (slice(144, 160), 3, slice(32, 48)))
    loads[0].wait()
    for here, i, there in pieces:
        f_up[here, :] = b_up[i, there, :].astype(F32)
    push(f_up, o_up)
    loads[1].wait()
    for k, target in enumerate((o_q, o_k, o_v)):
        for here, i, there in pieces:
            f_three[k, here, :] = b_three[i, k, there, :].astype(F32)
        push(f_three.at[k], target)
    loads[2].wait()
    f_down[...] = b_down[...].astype(F32)
    push(f_down, o_down)
    loads[3].wait()
    for here, i, there in pieces:
        f_out[here, :] = b_out[i, there, :].astype(F32)
    push(f_out, o_out)
    loads[4].wait()
    f_grad[...] = b_grad[...].astype(F32)
    push(f_grad, o_grad)
    loads[5].wait()
    push(b_rows, o_rows)
    for target, row in zip(small, (hb[1, :160], hb[2, :160], hb[0, :])):
        target[...] = row
    for k in range(6):
        small[3 + k][...] = vec[k, :]
    for copy in copies:
        copy.wait()


def widen(hb, vec, up, three, down, out, rows, grad):
    width = down.shape[1]

    def shape(*dims):
        return jax.ShapeDtypeStruct(dims, F32)

    sizes = [160, 160, 640] + [160] * 6
    arrays = (up, three, down, out, rows, grad)
    return pl.pallas_call(
        widen_kernel,
        in_specs=[VMEM] * 2 + [HBM] * 6,
        out_specs=[HBM] * 8 + [VMEM] * 9,
        out_shape=[shape(160, 5120)]
        + [shape(160, width)] * 3
        + [shape(640, width), shape(160, width)]
        + [jax.ShapeDtypeStruct(rows.shape, BF16), shape(*grad.shape)]
        + [shape(size) for size in sizes],
        scratch_shapes=[pltpu.VMEM(array.shape, BF16) for array in arrays]
        + [
            pltpu.VMEM((160, 5120), F32),
            pltpu.VMEM((3, 160, width), F32),
            pltpu.VMEM((640, width), F32),
            pltpu.VMEM((160, width), F32),
            pltpu.VMEM(grad.shape, F32),
            pltpu.SemaphoreType.DMA((6,)),
            pltpu.SemaphoreType.DMA((8,)),
        ],
        compiler_params=pltpu.CompilerParams(vmem_limit_bytes=60 << 20),
    )(hb, vec, up, three, down, out, rows, grad)


def per_device(
    tokens,
    lengths,
    w_query,
    w_key,
    w_value,
    w_out,
    w_up,
    w_down,
    b_query,
    b_value,
    b_out,
    b_up,
    b_down,
    gain_attn,
    shift_attn,
    gain_ffn,
    shift_ffn,
    cotangent,
):
    rows, width = tokens.shape[1:]

    eight = [b_query, b_value, b_out, b_down, gain_attn, shift_attn, gain_ffn, shift_ffn]
    row = lax.broadcasted_iota(jnp.int32, (16, 160), 0)
    small = jnp.zeros((16, 160), BF16)
    for index, vector in enumerate(eight):
        small = jnp.where(row == index, vector[None, :], small)
    up_bias = jnp.broadcast_to(b_up[None, :], (16, 640))
    known = jnp.full((8, 128), lengths[0], F32)
    (
        h1,
        heads,
        probs,
        mixed,
        attended,
        w_qkv,
        smalls,
        up_bias,
        own,
        clip,
        out_full,
        up_mine,
        down_mine,
        top,
        _,
    ) = begin(
        tokens[0],
        w_query,
        w_key,
        w_value,
        small,
        up_bias,
        w_out,
        w_up,
        w_down,
        cotangent[0],
        known,
    )
    w_qkv = w_qkv.reshape(width, 480)
    (
        result,
        grad_middle,
        branch,
        out_sums,
        g_up,
        g_down,
        g_up_bias,
        g_vectors,
        grad_mixed,
    ) = middle_part(
        attended,
        own,
        smalls,
        up_bias,
        clip,
        out_full.reshape(width, width),
        up_mine.reshape(width, 640),
        down_mine,
        top.reshape(8 * rows, width),
    )
    hb_out, vec_out, output, input_grad, fin_up, fin_qkv, fin_down, fin_out, _ = finish(
        heads,
        mixed,
        grad_mixed,
        w_qkv,
        own,
        smalls,
        result,
        grad_middle,
        branch,
        out_sums,
        g_up_bias,
        g_vectors,
        probs,
        h1.reshape(8 * rows, width),
        g_up.reshape(8, 160, 640),
        g_down,
    )

    g_up, g_q, g_k, g_v, g_down, g_out, output, input_grad, *small = widen(
        hb_out, vec_out, fin_up, fin_qkv, fin_down, fin_out, output, input_grad
    )
    b_q, b_v, b_u, b_o, b_d, gain_two, shift_two, gain_one, shift_one = small
    return (
        output[None],
        input_grad[None],
        g_q,
        g_k,
        g_v,
        g_out,
        g_up,
        g_down,
        b_q,
        b_v,
        b_o,
        b_u,
        b_d,
        gain_one,
        shift_one,
        gain_two,
        shift_two,
    )


def solution(mesh):
    by_clip, matrix, vector = P("rep", "shard", None), P("shard", None), P("shard")
    return jax.shard_map(
        per_device,
        mesh=mesh,
        in_specs=(by_clip, P("rep")) + (matrix,) * 6 + (vector,) * 9 + (by_clip,),
        out_specs=(by_clip, by_clip) + (matrix,) * 6 + (vector,) * 9,
        check_vma=False,
    )
```

```python
import jax
import jax.numpy as jnp
from jax import lax
from jax.experimental import pallas as pl
from jax.experimental.pallas import tpu as pltpu
from jax.sharding import PartitionSpec as P

HD = 80
EPS = 1e-05
F32 = jnp.float32
BF16 = jnp.bfloat16
NT = (((1,), (1,)), ((), ()))
TN = (((0,), (0,)), ((), ()))


MESH = pl.DeviceIdType.MESH
VMEM = pl.BlockSpec(memory_space=pltpu.VMEM)
HBM = pl.BlockSpec(memory_space=pl.ANY)


class Net:
    def __init__(self, sent, got, still):
        rep, shard = lax.axis_index("rep"), lax.axis_index("shard")
        self.y, self.zh, self.c = rep // 4, rep // 2 % 2, rep % 2
        self.x, self.zl = shard // 2, shard % 2
        self.me, self.shard = 2 * self.x + self.c, shard
        self.sent, self.got, self.still, self.used, self.started = sent, got, still, 0, []

    def device(self, dx=0, dc=0, dz=0, dy=0):
        z = (2 * self.zh + self.zl + dz) % 4
        return (
            (self.y + dy) % 4 * 4 + z // 2 * 2 + (self.c + dc) % 2,
            (self.x + dx) % 4 * 2 + z % 2,
        )

    def in_pair(self, dx, dz):
        return (
            self.y * 4 + self.zh * 2 + self.c,
            (self.x + dx) % 4 * 2 + (self.zl + dz) % 2,
        )

    def partner(self):
        return (self.y * 4 + self.zh * 2 + self.zl, 2 * self.x + self.c)

    def greet(self, devices):
        barrier = pltpu.get_barrier_semaphore()
        for device in devices:
            pl.semaphore_signal(barrier, inc=1, device_id=device, device_id_type=MESH)
        return lambda: pl.semaphore_wait(barrier, len(devices))

    def reserve(self, count):
        first = self.used
        self.used += count
        return first

    def copy(self, index, source, target, device):
        return pltpu.make_async_remote_copy(
            src_ref=source,
            dst_ref=target,
            send_sem=self.sent.at[index],
            recv_sem=self.got.at[index],
            device_id=device,
            device_id_type=MESH,
        )

    def go(self, source, target, device):
        copy = self.copy(self.reserve(1), source, target, device)
        copy.start()
        self.started.append(copy)
        return copy

    def cross(self, source, target):
        index = self.reserve(1)
        copy = self.copy(index, source, target, self.partner())
        local = pltpu.make_async_copy(source, target, self.still.at[index])

        @pl.when(self.c != self.zl)
        def _():
            copy.start()

        @pl.when(self.c == self.zl)
        def _():
            local.start()

        def arrived():
            @pl.when(self.c != self.zl)
            def _():
                copy.wait_recv()

            @pl.when(self.c == self.zl)
            def _():
                local.wait()

        def left():
            @pl.when(self.c != self.zl)
            def _():
                copy.wait_send()

        return arrived, left

    def all_sent(self):
        for copy in self.started:
            copy.wait_send()


def order(k):
    return 1 + 2 * k - 3 * (k // 2)


def aligned(index, size):
    return pl.ds(pl.multiple_of(index * size, size), size)


def scratch_for(copies):
    return [pltpu.SemaphoreType.DMA((copies,)) for _ in range(3)]


def begin_kernel(
    tokens,
    w_query,
    w_key,
    w_value,
    small,
    up_bias,
    w_out,
    w_up,
    w_down,
    cotangent,
    length,
    h1,
    heads,
    probs,
    mixed,
    attended,
    w_qkv,
    smalls,
    bias_up,
    own,
    clip,
    out_full,
    up_mine,
    down_mine,
    top,
    out_own,
    normed_rows,
    head_rows,
    prob_buf,
    gathered,
    cut,
    lens,
    vectors,
    sent,
    got,
    still,
):
    net = Net(sent, got, still)
    x, y, c, zh, zl, me, shard = net.x, net.y, net.c, net.zh, net.zl, net.me, net.shard
    rows, width = tokens.shape
    plane = [net.device(dx, dc) for dx in range(4) for dc in range(2) if dx or dc]
    across = [net.in_pair(dx, 1) for dx in range(4)]
    rings = [net.device(dy=d) for d in (1, 2, 3)] + [net.device(dz=d) for d in (1, 2, 3)]
    wait = net.greet(plane + across + rings + [(y * 4 + zh * 2 + 1 - c, 2 * x + 1 - zl)])
    for block in range(8):
        cols = slice(160 * block, 160 * block + 160)
        for half in range(2):
            part = slice(80 * half, 80 * half + 80)
            for k, weight in enumerate((w_query, w_key, w_value)):
                piece = weight[part, cols]
                for h in range(2):
                    first = 240 * h + 80 * k
                    cut[block, half, :, first : first + 80] = piece[:, 80 * h : 80 * h + 80]
    wait()

    token_arrived, token_left = net.cross(tokens, gathered.at[2 * x + zl])
    base = net.reserve(4)

    def token_send(k, source):
        dx = order(k)
        return net.copy(base + dx, source, gathered.at[me], net.device(dx))

    cut_near, cut_ring, up_near, up_ring = (net.reserve(4) for _ in range(4))

    def cut_copy(d):
        source = cut.at[2 * ((x + d) % 4) + c, zh]
        return net.copy(cut_near + d, source, w_qkv.at[x, zl, zh], net.device(d))

    def cut_share(d):
        here = w_qkv.at[:, zl, zh]
        return net.copy(cut_ring + d, here, here, net.device(dz=d))

    cut_half = net.reserve(2)

    def cut_on(i):
        from_z = (2 * zh + zl + 3 + 2 * i) % 4
        here = w_qkv.at[pl.ds(2 * i, 2), from_z % 2, from_z // 2]
        return net.copy(cut_half + i, here, here, net.device(dz=1 + 2 * i))

    def up_part(index):
        cols = pl.ds(pl.multiple_of(index * 640, 128), 640)
        return w_up.at[aligned(zh, 80), cols]

    def up_copy(d):
        source = up_part(2 * ((x + d) % 4) + c)
        return net.copy(up_near + d, source, up_mine.at[x, zl, zh], net.device(d))

    def up_share(d):
        here = up_mine.at[:, zl, zh]
        return net.copy(up_ring + d, here, here, net.device(dz=d))

    up_local = pltpu.make_async_copy(up_part(me), up_mine.at[x, zl, zh], still.at[up_near])

    for d in (2, 1, 3):
        cut_copy(d).start()

    @pl.when(c == zl)
    def _():
        for k in range(2):
            token_send(k, tokens).start()

    @pl.when(c == 0)
    def _():
        lens[0] = length[...]

    @pl.when(c == 1)
    def _():
        lens[1] = length[...]

    lens_copy = net.go(length, lens.at[c], net.device(0, 1))
    arriving = []
    for dx in (0, 1, 3, 2):
        for dz in range(2):
            if dx or dz:
                arriving.append(net.go(small, smalls.at[shard], net.in_pair(dx, dz)))
    smalls[shard] = small[...]
    w_qkv[x, zl, zh] = cut[me, zh]
    token_arrived()

    @pl.when(c != zl)
    def _():
        for k in range(2):
            token_send(k, gathered.at[me]).start()

    sibling = net.device(0, 1)
    own_over = net.go(gathered.at[me], gathered.at[me], sibling)
    for d in (1, 3, 2):
        cut_copy(d).wait_recv()
    for d in (1, 3):
        cut_share(d).start()
    up_local.start()
    for d in (2, 1, 3):
        up_copy(d).start()
    own[...] = gathered[me]
    for copy in arriving:
        copy.wait_recv()
    for block in range(8):
        vectors[:, 160 * block : 160 * block + 160] = smalls[block, :8, :].astype(F32)
    gain, shift = vectors[4:5, :], vectors[5:6, :]
    bias_q = smalls[me, 0:1, :].astype(F32)
    bias_v = smalls[me, 1:2, :].astype(F32)

    def project(slot):
        values = gathered[slot].astype(F32)
        center = values - jnp.mean(values, axis=-1, keepdims=True)
        inverse = lax.rsqrt(jnp.mean(center * center, axis=-1, keepdims=True) + EPS)
        normed = (center * inverse * gain + shift).astype(BF16)
        normed_rows[slot] = normed
        made = jnp.dot(normed, w_qkv[...].reshape(width, 480), preferred_element_type=F32)
        here = aligned(slot, rows)
        for h in range(2):
            cols = slice(h * HD, (h + 1) * HD)
            q, k, v = (made[:, 240 * h + 80 * j : 240 * h + 80 * j + 80] for j in range(3))
            head_rows[h, here, :] = (q + bias_q[:, cols]).astype(BF16)
            head_rows[2 + h, here, :] = k.astype(BF16)
            head_rows[4 + h, here, :] = (v + bias_v[:, cols]).astype(BF16)

    for i in range(2):
        cut_share(1 + 2 * i).wait_recv()
        cut_on(i).start()
    bias_arrived, bias_left = net.cross(up_bias, bias_up)
    top_arrived, top_left = net.cross(cotangent, top.at[2 * x + zl])
    out_arrived, out_left = net.cross(w_out, out_own)

    down_index, down_ring = net.reserve(1), net.reserve(4)
    down_cross = net.copy(
        down_index, w_down.at[aligned(y, 160)], down_mine.at[aligned(y, 160)], net.partner()
    )
    down_local = pltpu.make_async_copy(w_down, down_mine, still.at[down_index])

    def down_share(d):
        here = down_mine.at[aligned(y, 160)]
        return net.copy(down_ring + d, here, here, net.device(dy=d))

    @pl.when(c == zl)
    def _():
        down_local.start()

    @pl.when(c != zl)
    def _():
        down_cross.start()

    top_near, top_over, out_near, out_ring, out_over = (net.reserve(4) for _ in range(5))

    def top_copy(d):
        return net.copy(top_near + d, top.at[me], top.at[me], net.device(d))

    top_halves = net.reserve(2)

    def top_half(i):
        slot = 2 * ((x + 3 + 2 * i) % 4) + c
        here = top.at[slot, pl.ds(i * rows // 2, rows // 2), :]
        return net.copy(top_halves + i, here, here, net.device(1 + 2 * i))

    def top_pass(d):
        here = top.at[2 * ((x - d + 4) % 4) + c]
        return net.copy(top_over + d, here, here, sibling)

    half = pl.ds(pl.multiple_of(y % 2 * 640, 128), 640)
    out_piece = out_own.at[aligned(y // 2, 80), half]

    def out_copy(d):
        return net.copy(out_near + d, out_piece, out_full.at[x, c, y // 2, :, half], net.device(d))

    def out_share(d):
        here = out_full.at[:, c, y // 2, :, half]
        return net.copy(out_ring + d, here, here, net.device(dy=d))

    def out_pass(d):
        from_y = (y - d + 4) % 4
        cols = pl.ds(pl.multiple_of(from_y % 2 * 640, 128), 640)
        here = out_full.at[:, c, from_y // 2, :, cols]
        return net.copy(out_over + d, here, here, sibling)

    out_local = pltpu.make_async_copy(
        out_piece, out_full.at[x, c, y // 2, :, half], still.at[out_near]
    )
    for i in range(2):
        cut_on(i).wait_recv()
    project(me)
    own_over.wait_recv()
    project(2 * x + 1 - c)
    out_arrived()
    out_local.start()
    for d in (2, 1, 3):
        out_copy(d).start()

    @pl.when(c != zl)
    def _():
        down_cross.wait_recv()
        for d in (2, 1, 3):
            down_share(d).start()

    over, halves = net.reserve(4), net.reserve(2)

    def token_half(i):
        slot = 2 * ((x + 3 + 2 * i) % 4) + c
        here = gathered.at[slot, pl.ds(i * rows // 2, rows // 2), :]
        return net.copy(halves + i, here, here, net.device(1 + 2 * i))

    def passed(dx, slot):
        return net.copy(over + dx, gathered.at[slot], gathered.at[slot], sibling)

    @pl.loop(0, 3)
    def _(k):
        dx = order(k)
        from_x = (x - dx + 4) % 4

        @pl.when(k == 0)
        def _():
            for i in range(2):
                token_send(i, gathered.at[me]).wait_recv()
                token_half(i).start()

        @pl.when(k == 1)
        def _():
            top_arrived()
            for i in range(2):
                top_copy(1 + 2 * i).start()

        @pl.when(k == 2)
        def _():
            for i in range(2):
                token_half(i).wait_recv()

        passed(dx, 2 * from_x + c).start()
        project(2 * from_x + c)
        passed(dx, 2 * from_x + c).wait_recv()
        project(2 * from_x + 1 - c)

    out_local.wait()
    for d in (1, 3, 2):
        out_copy(d).wait_recv()
    for d in (2, 1, 3):
        out_share(d).start()
    out_pass(0).start()
    up_local.wait()
    for d in (1, 3, 2):
        up_copy(d).wait_recv()
    for d in (2, 1, 3):
        up_share(d).start()
    top_pass(0).start()

    keep_h1 = pltpu.make_async_copy(normed_rows, h1, still.at[net.reserve(1)])
    keep_h1.start()
    keep_heads = pltpu.make_async_copy(head_rows, heads, still.at[net.reserve(1)])
    keep_heads.start()
    lens_copy.wait_recv()
    clip[...] = lens[zl]
    clip_length = clip[0:1, 0:1]
    position = lax.broadcasted_iota(jnp.int32, (1, 8 * rows), 1).astype(F32)
    mask = jnp.where(position < clip_length, 0.0, -1e30)

    def attend_rows(to_x, slot):
        here = aligned(to_x, 2 * rows)
        for h in range(2):
            cols = slice(h * HD, (h + 1) * HD)
            scores = lax.dot_general(
                head_rows[h, here, :], head_rows[2 + h], NT, preferred_element_type=F32
            )
            scores = scores * HD**-0.5 + mask
            risen = jnp.exp(scores - jnp.max(scores, axis=-1, keepdims=True))
            share = 1.0 / jnp.sum(risen, axis=-1, keepdims=True)
            low = (risen * share).astype(BF16)
            prob_buf[slot, h] = low
            made = jnp.dot(low, head_rows[4 + h], preferred_element_type=F32).astype(BF16)
            mixed[2 * to_x, :, cols] = made[:rows]
            mixed[2 * to_x + 1, :, cols] = made[rows:]

    prob_index = net.reserve(2)

    def keep_probs(to_x, slot):
        return pltpu.make_async_copy(
            prob_buf.at[slot], probs.at[:, aligned(to_x, 2 * rows), :], still.at[prob_index + slot]
        )

    mixed_base = net.reserve(8)

    def mixed_send(dx, dc):
        slot = 2 * ((x + dx) % 4) + (c + dc) % 2
        return net.copy(
            mixed_base + 2 * dx + dc, mixed.at[slot], attended.at[me], net.device(dx, dc)
        )

    @pl.loop(1, 5)
    def _(step):
        dx = step % 4
        to_x = (x + dx) % 4

        @pl.when(step == 2)
        def _():
            for i in range(2):
                top_copy(1 + 2 * i).wait_recv()
                top_half(i).start()
                top_pass(1 + 2 * i).start()

        @pl.when(step > 2)
        def _():
            keep_probs(to_x, step % 2).wait()

        attend_rows(to_x, step % 2)
        keep_probs(to_x, step % 2).start()
        mixed_send(dx, 1).start()

        @pl.when(dx != 0)
        def _():
            mixed_send(dx, 0).start()

    attended[me] = mixed[me]
    for i in range(2):
        top_half(i).wait_recv()
    top_pass(2).start()
    for d in (1, 3, 2):
        out_share(d).wait_recv()
        out_pass(d).start()
    for dx in range(4):
        for dc in range(2):
            if dx or dc:
                mixed_send(dx, dc).wait()
    for d in range(4):
        top_pass(d).wait()
        out_pass(d).wait()
    for d in (1, 2, 3):
        up_share(d).wait()
        for copy in (cut_copy, up_copy, out_copy, out_share):
            copy(d).wait_send()
    for i in range(2):
        for copy in (cut_share, top_copy):
            copy(1 + 2 * i).wait_send()
        cut_on(i).wait_send()
        top_half(i).wait_send()

    @pl.when(c == zl)
    def _():
        down_local.wait()

    @pl.when(c != zl)
    def _():
        down_cross.wait_send()
        for d in (1, 2, 3):
            down_share(d).wait()

    keep_h1.wait()
    keep_heads.wait()
    for slot in range(2):
        keep_probs(slot, slot).wait()
    bias_arrived()
    for left in (token_left, out_left, top_left, bias_left):
        left()
    for k in range(2):
        token_send(k, gathered.at[me]).wait_send()
        token_half(k).wait_send()
    for k in range(3):
        passed(order(k), me).wait_send()
    net.all_sent()


def begin(tokens, w_query, w_key, w_value, small, up_bias, w_out, w_up, w_down, cotangent, length):
    rows, width = tokens.shape

    def shape(*dims):
        return jax.ShapeDtypeStruct(dims, BF16)

    return pl.pallas_call(
        begin_kernel,
        in_specs=[VMEM] * 11,
        out_specs=[HBM] * 3 + [VMEM] * 7 + [HBM] * 4 + [VMEM],
        out_shape=[
            shape(8, rows, width),
            shape(6, 8 * rows, HD),
            shape(2, 8 * rows, 8 * rows),
            shape(8, rows, 160),
            shape(8, rows, 160),
            shape(4, 2, 2, 80, 480),
            shape(8, 16, 160),
            shape(16, 640),
            shape(rows, width),
            jax.ShapeDtypeStruct((8, 128), F32),
            shape(4, 2, 2, 80, width),
            shape(4, 2, 2, 80, 640),
            shape(640, width),
            shape(8, rows, width),
            shape(160, width),
        ],
        scratch_shapes=[
            pltpu.VMEM((8, rows, width), BF16),
            pltpu.VMEM((6, 8 * rows, HD), BF16),
            pltpu.VMEM((2, 2, 2 * rows, 8 * rows), BF16),
            pltpu.VMEM((8, rows, width), BF16),
            pltpu.VMEM((8, 2, 80, 480), BF16),
            pltpu.VMEM((2, 8, 128), F32),
            pltpu.VMEM((8, width), F32),
        ]
        + scratch_for(96),
        compiler_params=pltpu.CompilerParams(
            collective_id=0, has_side_effects=True, vmem_limit_bytes=58 << 20
        ),
    )(tokens, w_query, w_key, w_value, small, up_bias, w_out, w_up, w_down, cotangent, length)


def middle_kernel(
    attended,
    own,
    smalls,
    up_bias,
    clip,
    out_full,
    up_mine,
    down_mine,
    top,
    result,
    grad_middle,
    branch,
    out_sums,
    g_up,
    g_down,
    g_up_bias,
    g_vectors,
    grad_mixed,
    vectors,
    middle,
    second,
    masked,
    active,
    hidden,
    parts,
    over,
    sums,
    arrived,
    out_parts,
    out_over,
    joined,
    by_head,
    sent,
    got,
    still,
):
    net = Net(sent, got, still)
    x, c, me = net.x, net.c, net.me
    rows, width = own.shape
    wait = net.greet([net.device(dx, dc) for dx in range(4) for dc in range(2) if dx or dc])
    for block in range(8):
        vectors[:, 160 * block : 160 * block + 160] = smalls[block, :8, :].astype(F32)
    bias_up = up_bias[0:1, :].astype(F32)
    mine = aligned(me, rows)
    for block in range(8):
        joined[:, 160 * block : 160 * block + 160] = attended[block]
    made = jnp.dot(joined[...], out_full[...], preferred_element_type=F32)
    middle[...] = own[...].astype(F32) + made + vectors[2:3, :]

    def normalised():
        values = middle[...]
        center = values - jnp.mean(values, axis=-1, keepdims=True)
        inverse = lax.rsqrt(jnp.mean(center * center, axis=-1, keepdims=True) + EPS)
        return center * inverse, inverse

    second[mine, :] = (normalised()[0] * vectors[6:7, :] + vectors[7:8, :]).astype(BF16)
    wait()

    near, pass_on, swap, add, out_swap = (net.reserve(4) for _ in range(5))

    def out_copy(dx, to_x):
        source = out_parts.at[aligned(2 * to_x + 1 - c, rows)]
        return net.copy(out_swap + dx, source, out_over.at[to_x], net.device(0, 1))

    def near_copy(dx):
        return net.copy(near + dx, second.at[mine], second.at[mine], net.device(dx))

    def pass_copy(dx, slot):
        here = second.at[aligned(slot, rows)]
        return net.copy(pass_on + dx, here, here, net.device(0, 1))

    def swap_copy(dx, to_x):
        source = parts.at[aligned(2 * to_x + 1 - c, rows)]
        return net.copy(swap + dx, source, over.at[to_x], net.device(0, 1))

    def add_copy(dx, to_x):
        return net.copy(add + dx, sums.at[to_x], arrived.at[dx], net.device(4 - dx))

    halves = net.reserve(2)

    def half_copy(i):
        slot = 2 * ((x + 3 + 2 * i) % 4) + c
        here = second.at[aligned(2 * slot + i, rows // 2)]
        return net.copy(halves + i, here, here, net.device(1 + 2 * i))

    for dx in (1, 3):
        near_copy(dx).start()

    @pl.loop(0, 4)
    def _(k):
        dx = k ^ (k >> 1)
        to_x = (x - dx + 4) % 4

        @pl.when(k == 1)
        def _():
            for i in range(2):
                near_copy(1 + 2 * i).wait_recv()
                half_copy(i).start()

        @pl.when(k == 3)
        def _():
            for i in range(2):
                half_copy(i).wait_recv()

        pass_copy(dx, 2 * to_x + c).start()
        here = aligned(to_x, 2 * rows)
        position = lax.broadcasted_iota(jnp.int32, (2 * rows, 1), 0) + to_x * 2 * rows
        live = position.astype(F32) < clip[0:1, 0:1]
        low_top = jnp.where(live, top[here, :].astype(F32), 0.0).astype(BF16)
        masked[here, :] = low_top
        grad_act = lax.dot_general(low_top, down_mine[...], NT, preferred_element_type=F32)
        pass_copy(dx, 2 * to_x + c).wait_recv()
        z = jnp.dot(second[here, :], up_mine[...], preferred_element_type=F32) + bias_up
        bell = 0.5 * (1.0 + lax.erf(z * 0.7071067811865476))
        active[here, :] = (z * bell).astype(BF16)
        slope = bell + z * jnp.exp(-0.5 * z * z) * 0.3989422804014327
        grad_z = (grad_act * slope).astype(BF16)
        hidden[here, :] = grad_z
        parts[here, :] = lax.dot_general(
            grad_z, up_mine[...], NT, preferred_element_type=F32
        ).astype(BF16)
        swap_copy(dx, to_x).start()
        out_parts[here, :] = jnp.dot(
            active[here, :], down_mine[...], preferred_element_type=F32
        ).astype(BF16)
        out_copy(dx, to_x).start()
        swap_copy(dx, to_x).wait_recv()

        @pl.when(dx != 0)
        def _():
            kept = parts[aligned(2 * to_x + c, rows), :].astype(F32)
            sums[to_x] = (kept + over[to_x].astype(F32)).astype(BF16)
            add_copy(dx, to_x).start()

    @pl.loop(0, 5)
    def _(i):
        cols = pl.ds(pl.multiple_of(i * 256, 256), 256)
        g_up[cols, :] = lax.dot_general(
            second[:, cols], hidden[...], TN, preferred_element_type=F32
        ).astype(BF16)
        cols = pl.ds(pl.multiple_of(i * 128, 128), 128)
        g_down[cols, :] = lax.dot_general(
            active[:, cols], masked[...], TN, preferred_element_type=F32
        ).astype(BF16)

    for dx in range(4):
        to_x = (x - dx + 4) % 4
        out_copy(dx, to_x).wait_recv()
        kept = out_parts[aligned(2 * to_x + c, rows), :].astype(F32) + out_over[to_x].astype(F32)
        if dx:
            out_sums[to_x] = kept.astype(BF16)
        else:
            result[...] = middle[...] + kept + vectors[3:4, :]
    g_up_bias[...] = jnp.sum(hidden[...].astype(F32), axis=0, keepdims=True)
    grad_second = parts[mine, :].astype(F32) + over[x].astype(F32)
    for dx in (1, 3, 2):
        add_copy(dx, (x - dx + 4) % 4).wait_recv()
        grad_second = grad_second + arrived[dx].astype(F32)
    normed, inverse = normalised()
    scaled = grad_second * vectors[6:7, :]
    back = inverse * (
        scaled
        - jnp.mean(scaled, axis=-1, keepdims=True)
        - normed * jnp.mean(scaled * normed, axis=-1, keepdims=True)
    )
    top_own = masked[mine, :].astype(F32)
    total = top_own + back
    grad_middle[...] = total
    low = total.astype(BF16)
    branch[...] = low
    grad_attended = lax.dot_general(low, out_full[...], NT, preferred_element_type=F32)
    grad_attended = grad_attended.astype(BF16)
    for block in range(8):
        by_head[block] = grad_attended[:, 160 * block : 160 * block + 160]
    mixing = []
    for dx in (2, 1, 3, 0):
        for dc in (1, 0):
            if dx or dc:
                slot = 2 * ((x + dx) % 4) + (c + dc) % 2
                mixing.append(net.go(by_head.at[slot], grad_mixed.at[me], net.device(dx, dc)))
    grad_mixed[me] = by_head[me]
    g_vectors[0:1, :] = jnp.sum(low.astype(F32), axis=0, keepdims=True)
    g_vectors[1:2, :] = jnp.sum(top_own, axis=0, keepdims=True)
    g_vectors[2:3, :] = jnp.sum(grad_second * normed, axis=0, keepdims=True)
    g_vectors[3:4, :] = jnp.sum(grad_second, axis=0, keepdims=True)
    for copy in mixing:
        copy.wait_recv()
    for dx in range(4):
        to_x = (x - dx + 4) % 4
        pass_copy(dx, 2 * to_x + c).wait_send()
        swap_copy(dx, to_x).wait_send()
        out_copy(dx, to_x).wait_send()
        if dx:
            add_copy(dx, to_x).wait_send()
    for i in range(2):
        near_copy(1 + 2 * i).wait_send()
        half_copy(i).wait_send()
    net.all_sent()


def middle_part(attended, own, smalls, up_bias, clip, out_full, up_mine, down_mine, top):
    rows, width = own.shape

    def shape(*dims, dtype=BF16):
        return jax.ShapeDtypeStruct(dims, dtype)

    def buffer(*dims, dtype=BF16):
        return pltpu.VMEM(dims, dtype)

    return pl.pallas_call(
        middle_kernel,
        in_specs=[VMEM] * 9,
        out_specs=[VMEM] * 9,
        out_shape=[
            shape(rows, width, dtype=F32),
            shape(rows, width, dtype=F32),
            shape(rows, width),
            shape(4, rows, width),
            shape(width, 640),
            shape(640, width),
            shape(1, 640, dtype=F32),
            shape(4, width, dtype=F32),
            shape(8, rows, 160),
        ],
        scratch_shapes=[
            buffer(8, width, dtype=F32),
            buffer(rows, width, dtype=F32),
            buffer(8 * rows, width),
            buffer(8 * rows, width),
            buffer(8 * rows, 640),
            buffer(8 * rows, 640),
            buffer(8 * rows, width),
            buffer(4, rows, width),
            buffer(4, rows, width),
            buffer(4, rows, width),
            buffer(8 * rows, width),
            buffer(4, rows, width),
            buffer(rows, width),
            buffer(8, rows, 160),
        ]
        + scratch_for(32),
        compiler_params=pltpu.CompilerParams(
            collective_id=1, has_side_effects=True, vmem_limit_bytes=60 << 20
        ),
    )(attended, own, smalls, up_bias, clip, out_full, up_mine, down_mine, top)


def piece_start(index):
    return pl.multiple_of(48 * index - 32 * (index // 3), 16)


def beside(p, way):
    return p + 1 - 2 * (p % 2) if way == 0 else 3 - p


def halving(net, piece, r1, t1, r3):
    x = net.x
    b1, b2 = net.reserve(4), net.reserve(2)
    both = [(half, slot) for slot in (1, 0) for half in range(2)]

    def copy_1(half, slot):
        near = beside(x, half)
        wanted = near if slot == 0 else beside(near, 1 - half)
        return net.copy(
            b1 + 2 * half + slot, piece(half, wanted), r1.at[half, slot], net.device(near - x + 4)
        )

    def copy_2(half):
        device = net.device(beside(x, 1 - half) - x + 4)
        return net.copy(b2 + half, t1.at[half], r3.at[half], device)

    def first():
        for half, slot in both:
            copy_1(half, slot).start()

    def halfway(kept):
        for half in range(2):
            copy_1(half, 1).wait_recv()
            t1[half] = (kept(half).astype(F32) + r1[half, 1].astype(F32)).astype(BF16)
            copy_2(half).start()

    def total(half):
        copy_1(half, 0).wait_recv()
        copy_2(half).wait_recv()
        return r1[half, 0].astype(F32) + r3[half].astype(F32)

    def sent():
        for half, slot in both:
            copy_1(half, slot).wait_send()
        for half in range(2):
            copy_2(half).wait_send()

    return first, halfway, total, sent


def column_flow(net, source, m1, r1, t1, r3, s1, r2, s2, planes, landed, place_of):
    y, z, x, c = net.y, 2 * net.zh + net.zl, net.x, net.c
    b1, b2, b3, b4, b5 = (net.reserve(4) for _ in range(5))
    b6 = net.reserve(2)
    sibling = net.device(0, 1)

    def piece(half, p):
        return source.at[pl.ds(4 * half, 4), pl.ds(piece_start(p), 48), :]

    def copy_1(half, slot):
        near = beside(y, half)
        wanted = near if slot == 0 else beside(near, 1 - half)
        return net.copy(
            b1 + 2 * half + slot,
            piece(half, wanted),
            r1.at[half, slot],
            net.device(dy=near - y + 4),
        )

    def load(half, slot):
        wanted = y if slot == 0 else beside(y, 1 - half)
        return pltpu.make_async_copy(
            piece(half, wanted), m1.at[half, slot], net.still.at[b1 + 2 * half + slot]
        )

    def copy_6(half):
        device = net.device(dy=beside(y, 1 - half) - y + 4)
        return net.copy(b6 + half, t1.at[half], r3.at[half], device)

    def copy_2(d):
        part = s1.at[pl.ds(2 * ((z + d) % 4), 2)]
        return net.copy(b2 + d, part, r2.at[d], net.device(dz=d))

    def copy_3(d):
        return net.copy(b3 + d, s2.at[(z + d) % 2], planes.at[z], net.device(dz=d))

    def copy_4(d):
        target = place_of(landed, 2 * x + c)
        return net.copy(b4 + d, planes.at[(x + d) % 4], target, net.device(d))

    def copy_5(d):
        here = place_of(landed, 2 * ((x - d + 4) % 4) + c)
        return net.copy(b5 + d, here, here, sibling)

    both = [(half, slot) for half in range(2) for slot in range(2)]

    def first():
        for half, slot in both:
            copy_1(half, slot).start()
        for half, slot in both:
            load(half, slot).start()

    def halfway():
        for half, slot in both:
            load(half, slot).wait()
            copy_1(half, slot).wait_recv()
        for half in range(2):
            t1[half] = (m1[half, 1].astype(F32) + r1[half, 1].astype(F32)).astype(BF16)
            copy_6(half).start()

    def second():
        for half in range(2):
            copy_6(half).wait_recv()
            total = m1[half, 0].astype(F32) + r1[half, 0].astype(F32) + r3[half].astype(F32)
            s1[pl.ds(4 * half, 4)] = total.astype(BF16)
        for d in (2, 1, 3):
            copy_2(d).start()

    def third():
        total = s1[pl.ds(2 * z, 2)].astype(F32)
        for d in (1, 2, 3):
            copy_2(d).wait_recv()
            total = total + r2[d].astype(F32)
        s2[...] = total.astype(BF16)
        for d in (2, 1, 3):
            copy_3(d).start()
        planes[z] = s2[z % 2]

    def fourth():
        for d in (1, 2, 3):
            copy_3(d).wait_recv()
        for d in (2, 1, 3):
            copy_4(d).start()
        place_of(landed, 2 * x + c)[...] = planes[x]
        copy_5(0).start()

    def fifth():
        for d in (1, 3, 2):
            copy_4(d).wait_recv()
            copy_5(d).start()
        for d in range(4):
            copy_5(d).wait_recv()

    def sent():
        for d in range(4):
            copy_5(d).wait_send()
        for d in (1, 2, 3):
            for copy in (copy_2, copy_3, copy_4):
                copy(d).wait_send()
        for half in range(2):
            copy_6(half).wait_send()
        for half, slot in both:
            copy_1(half, slot).wait_send()

    return first, halfway, second, third, fourth, fifth, sent


def share_over_y(net, whole, final, half_of):
    y = net.y
    near, over = net.reserve(4), net.reserve(4)
    own = pltpu.make_async_copy(whole, final.at[y], net.still.at[near])

    def copy(d):
        return net.copy(near + d, half_of(whole), half_of(final.at[y]), net.device(dy=d))

    def forward(d):
        here = half_of(final.at[(y - d + 4) % 4])
        return net.copy(over + d, here, here, net.device(0, 1))

    def first():
        own.start()
        for d in (2, 1, 3):
            copy(d).start()

    def second():
        for d in (1, 3, 2):
            copy(d).wait_recv()
            forward(d).start()

    def third():
        own.wait()
        for d in (1, 2, 3):
            forward(d).wait_recv()
            forward(d).wait_send()
            copy(d).wait_send()

    return first, second, third


def four_way(net, base, held, position, device_of):
    def copy(d):
        return net.copy(base + d, held.at[position], held.at[position], device_of(d))

    def go():
        for d in (2, 1, 3):
            copy(d).start()

    def total():
        for d in (1, 2, 3):
            copy(d).wait_recv()
        return (held[0].astype(F32) + held[1].astype(F32)) + (
            held[2].astype(F32) + held[3].astype(F32)
        )

    def sent():
        for d in (1, 2, 3):
            copy(d).wait_send()

    return go, total, sent


def finish_kernel(
    heads,
    mixed,
    grad_mixed,
    w_qkv,
    own,
    smalls,
    result,
    grad_middle,
    branch,
    g_up_bias,
    g_vectors,
    out_sums,
    probs,
    h1,
    g_up,
    g_down,
    hb_out,
    vec_out,
    output,
    input_grad,
    fin_up,
    fin_qkv,
    fin_down,
    fin_out,
    branch_all,
    tall,
    prob_buf,
    grads,
    sum_k,
    sum_v,
    give,
    over,
    sums,
    back_r1,
    back_t1,
    back_r3,
    out_r1_x,
    out_t1_x,
    out_r3_x,
    out_kept,
    final_rows,
    final_grad,
    low_grad,
    up_m1,
    up_r1,
    up_t1,
    up_r3,
    up_s1,
    up_r2,
    up_s2,
    up_planes,
    up_landed,
    g_head_0,
    m1_head_0,
    r1_head_0,
    t1_head_0,
    r3_head_0,
    s1_head_0,
    r2_head_0,
    s2_head_0,
    planes_head_0,
    landed_head_0,
    g_head_1,
    m1_head_1,
    r1_head_1,
    t1_head_1,
    r3_head_1,
    s1_head_1,
    r2_head_1,
    s2_head_1,
    planes_head_1,
    landed_head_1,
    qkv_rows,
    w_heads,
    down_r1,
    down_s1,
    down_r2,
    down_l3,
    down_p,
    g_out,
    out_r1,
    out_z,
    out_t,
    head_y,
    head_z,
    head_sib,
    vec_cut,
    vec_1,
    vec_1s,
    vec_2,
    vec_3,
    vectors,
    sent,
    got,
    still,
):
    net = Net(sent, got, still)
    x, y, c, zl, me = net.x, net.y, net.c, net.zl, net.me
    z = 2 * net.zh + zl
    rows, width = own.shape
    sibling = net.device(0, 1)
    wait = net.greet(
        [net.device(dx, dc) for dx in range(4) for dc in range(2) if dx or dc]
        + [net.device(dy=d) for d in (1, 2, 3)]
        + [net.device(dz=d) for d in (1, 2, 3)]
        + [(y * 4 + net.zh * 2 + 1 - c, 2 * x + 1 - zl)]
    )

    tile = 2 * rows
    slots = net.reserve(2)

    def load_probs(j):
        slot = j % 2
        return pltpu.make_async_copy(
            probs.at[j // 4, aligned(j % 4, tile), :], prob_buf.at[slot], still.at[slots + slot]
        )

    load_probs(0).start()
    load_h1 = pltpu.make_async_copy(h1, tall, still.at[net.reserve(1)])
    load_h1.start()
    own_branch = pltpu.make_async_copy(
        branch, branch_all.at[aligned(me, rows)], still.at[net.reserve(1)]
    )
    own_branch.start()
    for block in range(8):
        vectors[:, 160 * block : 160 * block + 160] = smalls[block, :8, :].astype(F32)
    for h in range(2):
        w_heads[h] = w_qkv[:, 240 * h : 240 * h + 240]

    up = column_flow(
        net,
        g_up,
        up_m1,
        up_r1,
        up_t1,
        up_r3,
        up_s1,
        up_r2,
        up_s2,
        up_planes,
        up_landed,
        lambda ref, hb: ref.at[:, pl.ds(pl.multiple_of(hb * 640, 128), 640)],
    )
    head_buffers = (
        (
            g_head_0,
            m1_head_0,
            r1_head_0,
            t1_head_0,
            r3_head_0,
            s1_head_0,
            r2_head_0,
            s2_head_0,
            planes_head_0,
            landed_head_0,
        ),
        (
            g_head_1,
            m1_head_1,
            r1_head_1,
            t1_head_1,
            r3_head_1,
            s1_head_1,
            r2_head_1,
            s2_head_1,
            planes_head_1,
            landed_head_1,
        ),
    )
    flows = [column_flow(net, *held, lambda ref, hb: ref.at[hb]) for held in head_buffers]
    up_share = share_over_y(
        net,
        up_landed,
        fin_up,
        lambda ref: ref.at[:, pl.ds(pl.multiple_of(c * 2560, 128), 2560)],
    )
    three_share = share_over_y(
        net,
        qkv_rows,
        fin_qkv,
        lambda ref: ref.at[:, :, pl.ds(pl.multiple_of(c * 640, 128), 640)],
    )

    d1, d2, d4, d5 = (net.reserve(4) for _ in range(4))
    d3_go, _, d3_sent = four_way(net, d3 := net.reserve(4), down_l3, y, lambda d: net.device(dy=d))
    down_mine = pltpu.make_async_copy(
        g_down.at[aligned(z, 160)], down_r1.at[0], still.at[d1]
    )

    def down_1(d):
        return net.copy(d1 + d, g_down.at[aligned((z + d) % 4, 160)], down_r1.at[d], net.device(dz=d))

    def down_2(d):
        part = down_s1.at[pl.ds(piece_start((y + d) % 4), 48)]
        return net.copy(d2 + d, part, down_r2.at[d], net.device(dy=d))

    def down_4(k, source_z):
        to_z = c + 2 * k
        return pltpu.make_async_remote_copy(
            src_ref=down_p,
            dst_ref=fin_down.at[aligned(source_z, 160)],
            send_sem=sent.at[d4 + k],
            recv_sem=got.at[d4 + source_z],
            device_id=(y * 4 + to_z // 2 * 2 + c, 2 * x + to_z % 2),
            device_id_type=MESH,
        )

    down_local = pltpu.make_async_copy(down_p, fin_down.at[aligned(z, 160)], still.at[d4])

    def down_5(source_z):
        here = fin_down.at[aligned(source_z, 160)]
        return net.copy(d5 + source_z, here, here, sibling)

    e1, e3, e4 = (net.reserve(4) for _ in range(3))
    out_go, out_total, out_sent = four_way(
        net, net.reserve(4), out_z, z, lambda d: net.device(dz=d)
    )

    def out_1(d):
        part = g_out.at[pl.ds(piece_start((y + d) % 4), 48)]
        return net.copy(e1 + d, part, out_r1.at[d], net.device(dy=d))

    def out_3(d):
        return net.copy(e3 + d, out_t, fin_out.at[y], net.device(dy=d))

    out_local = pltpu.make_async_copy(out_t, fin_out.at[y], still.at[e3])

    def out_4(source_y):
        return net.copy(e4 + source_y, fin_out.at[source_y], fin_out.at[source_y], sibling)

    near, pass_on, swap = (net.reserve(4) for _ in range(3))
    branch_halves = net.reserve(2)

    def near_copy(dx):
        return net.copy(near + dx, branch, branch_all.at[aligned(me, rows)], net.device(dx))

    def pass_copy(dx):
        here = branch_all.at[aligned(2 * ((x - dx + 4) % 4) + c, rows)]
        return net.copy(pass_on + dx, here, here, sibling)

    def swap_copy(dx, to_x):
        return net.copy(swap + dx, give.at[to_x], over.at[to_x], sibling)

    half_rows = rows // 2

    def branch_half(i):
        here = branch_all.at[aligned(2 * (2 * ((x + 3 + 2 * i) % 4) + c) + i, half_rows)]
        return net.copy(branch_halves + i, here, here, net.device(1 + 2 * i))

    def in_half(half):
        return pl.ds(half_rows * half, half_rows)

    back_sum = halving(
        net, lambda half, p: sums.at[p, in_half(half)], back_r1, back_t1, back_r3
    )
    out_sum = halving(
        net, lambda half, p: out_sums.at[p, in_half(half)], out_r1_x, out_t1_x, out_r3_x
    )
    out_load = [
        pltpu.make_async_copy(
            out_sums.at[beside(x, 1 - half), in_half(half)],
            out_kept.at[half],
            still.at[net.reserve(1)],
        )
        for half in range(2)
    ]
    for load in out_load:
        load.start()

    wait()
    out_sum[0]()
    for dx in (1, 3):
        near_copy(dx).start()
    up[0]()
    down_mine.start()
    for d in (2, 1, 3):
        down_1(d).start()

    for h in range(2):
        cols = slice(h * HD, (h + 1) * HD)
        sum_k[...] = jnp.zeros_like(sum_k)
        sum_v[...] = jnp.zeros_like(sum_v)

        @pl.loop(0, 4)
        def _(i, h=h, cols=cols):
            j = 4 * h + i

            @pl.when(j < 7)
            def _():
                load_probs(j + 1).start()

            load_probs(j).wait()
            here = aligned(i, tile)
            back = jnp.concatenate([grad_mixed[2 * i, :, cols], grad_mixed[2 * i + 1, :, cols]])
            seen = jnp.concatenate([mixed[2 * i, :, cols], mixed[2 * i + 1, :, cols]])
            low = prob_buf[j % 2]
            row_total = jnp.sum(back.astype(F32) * seen.astype(F32), axis=-1, keepdims=True)
            grad_probs = lax.dot_general(back, heads[4 + h], NT, preferred_element_type=F32)
            grad_scores = (low.astype(F32) * (grad_probs - row_total)).astype(BF16)
            sum_v[...] += lax.dot_general(low, back, TN, preferred_element_type=F32)
            sum_k[...] += lax.dot_general(
                grad_scores, heads[h, here, :], TN, preferred_element_type=F32
            )
            grad_q = jnp.dot(grad_scores, heads[2 + h], preferred_element_type=F32)
            grads[h, here, :80] = (grad_q * HD**-0.5).astype(BF16)

        grads[h, :, 80:160] = (sum_k[...] * HD**-0.5).astype(BF16)
        grads[h, :, 160:] = sum_v[...].astype(BF16)
        if h == 0:
            load_h1.wait()

        @pl.loop(0, 2)
        def _(i, h=h):
            cols = pl.ds(pl.multiple_of(i * 640, 128), 640)
            made = lax.dot_general(tall[:, cols], grads[h], TN, preferred_element_type=F32)
            head_buffers[h][0][pl.ds(4 * i, 4)] = made.astype(BF16).reshape(4, 160, 240)

        if h == 0:
            up[1]()
            for load in out_load:
                load.wait()
            out_sum[1](lambda half: out_kept[half])
        flows[h][0]()
        if h == 1:
            flows[0][1]()
            for i in range(2):
                near_copy(1 + 2 * i).wait_recv()
                branch_half(i).start()
            up[2]()

    def back_rows(block):
        made = [
            lax.dot_general(
                grads[h, aligned(block, rows), :], w_heads[h], NT, preferred_element_type=F32
            )
            for h in range(2)
        ]
        return made[0] + made[1]

    @pl.loop(0, 4)
    def _(k):
        dx = jnp.where(k == 3, 0, order(k))
        to_x = (x - dx + 4) % 4
        give[to_x] = back_rows(2 * to_x + 1 - c).astype(BF16)
        swap_copy(dx, to_x).start()

    flows[1][1]()
    up[3]()

    @pl.loop(0, 4)
    def _(k):
        dx = jnp.where(k == 3, 0, order(k))
        to_x = (x - dx + 4) % 4
        kept = back_rows(2 * to_x + c)
        swap_copy(dx, to_x).wait_recv()
        kept = kept + over[to_x].astype(F32)

        @pl.when(dx != 0)
        def _():
            sums[to_x] = kept.astype(BF16)

        @pl.when(dx == 0)
        def _():
            final_grad[...] = kept

    back_sum[0]()
    flows[0][2]()
    own_branch.wait()
    pass_copy(0).start()
    for dx in (1, 3):
        pass_copy(dx).start()
    for i in range(2):
        branch_half(i).wait_recv()
    pass_copy(2).start()

    down_mine.wait()
    total = down_r1[0].astype(F32)
    for d in (1, 2, 3):
        down_1(d).wait_recv()
        total = total + down_r1[d].astype(F32)
    down_s1[...] = total.astype(BF16)
    for d in (2, 1, 3):
        down_2(d).start()

    for dx in range(4):
        pass_copy(dx).wait_recv()
        pass_copy(dx).wait_send()
    load_branch = pltpu.make_async_copy(branch_all, tall, still.at[net.reserve(1)])
    load_branch.start()
    load_branch.wait()
    seen = jnp.concatenate([mixed[block] for block in range(8)])
    g_out[...] = lax.dot_general(seen, tall[...], TN, preferred_element_type=F32).astype(BF16)
    for d in (2, 1, 3):
        out_1(d).start()

    head_y[y] = jnp.zeros((8, 640), F32)
    head_y[y, 0:1, :] = g_up_bias[...]
    for h in range(2):
        cols = slice(h * HD, (h + 1) * HD)
        column_sums = jnp.sum(grads[h].astype(F32), axis=0, keepdims=True)
        head_y[y, 1:2, cols] = column_sums[:, :80]
        head_y[y, 2:3, cols] = column_sums[:, 160:]
    head_y_go, head_y_total, head_y_sent = four_way(
        net, net.reserve(4), head_y, y, lambda d: net.device(dy=d)
    )
    head_y_go()

    flows[1][2]()
    up[4]()
    back_sum[1](lambda half: sums[beside(x, 1 - half), in_half(half), :])
    total = down_s1[pl.ds(piece_start(y), 48), :].astype(F32)
    for d in (1, 2, 3):
        down_2(d).wait_recv()
        total = total + down_r2[d].astype(F32)
    down_l3[y] = total.astype(BF16)
    d3_go()

    for flow in flows:
        flow[3]()
    for d in (1, 2, 3):
        net.copy(d3 + d, down_l3.at[y], down_l3.at[y], net.device(dy=d)).wait_recv()
    for i in range(3):
        down_p[48 * i : 48 * i + 48, :] = down_l3[i]
    down_p[144:160, :] = down_l3[3, 32:48, :]
    for k in range(2):

        @pl.when(c + 2 * k != z)
        def _():
            down_4(k, z).start()

    @pl.when(c == zl)
    def _():
        down_local.start()

    up[5]()
    up_share[0]()
    for flow in flows:
        flow[4]()
    total = result[...] + jnp.concatenate([out_sum[2](half) for half in range(2)])
    final_rows[...] = total.astype(BF16)
    output_arrived, output_left = net.cross(final_rows, output)

    grad_first = final_grad[...] + jnp.concatenate([back_sum[2](half) for half in range(2)])
    values = own[...].astype(F32)
    center = values - jnp.mean(values, axis=-1, keepdims=True)
    inverse = lax.rsqrt(jnp.mean(center * center, axis=-1, keepdims=True) + EPS)
    normed = center * inverse
    scaled = grad_first * vectors[4:5, :]
    back = inverse * (
        scaled
        - jnp.mean(scaled, axis=-1, keepdims=True)
        - normed * jnp.mean(scaled * normed, axis=-1, keepdims=True)
    )
    low_grad[...] = (grad_middle[...] + back).astype(BF16)
    grad_arrived, grad_left = net.cross(low_grad, input_grad)
    gain = jnp.sum(grad_first * normed, axis=0, keepdims=True)
    shift = jnp.sum(grad_first, axis=0, keepdims=True)
    for block in range(8):
        cols = slice(160 * block, 160 * block + 160)
        here = vec_cut.at[block // 2, block % 2]
        here[0:4, :] = g_vectors[:, cols]
        here[4:5, :] = gain[:, cols]
        here[5:6, :] = shift[:, cols]
        here[6:8, :] = jnp.zeros((2, 160), F32)
    v1 = net.reserve(8)

    def vec_copy(dx, dc):
        return net.copy(
            v1 + 2 * dx + dc, vec_cut.at[(x + dx) % 4], vec_1.at[me], net.device(dx, dc)
        )

    others = [(dx, dc) for dx in (2, 1, 3, 0) for dc in (1, 0) if dx or dc]
    for dx, dc in others:
        vec_copy(dx, dc).start()
    vec_1[me] = vec_cut[x]

    for flow in flows:
        flow[5]()
    for block in range(8):
        cols = slice(160 * block, 160 * block + 160)
        for k in range(3):
            qkv_rows[k, :, cols] = jnp.concatenate(
                [held[9][block, :, 80 * k : 80 * k + 80] for held in head_buffers], axis=1
            )
    three_share[0]()
    total = g_out[pl.ds(piece_start(y), 48), :].astype(F32)
    for d in (1, 2, 3):
        out_1(d).wait_recv()
        total = total + out_r1[d].astype(F32)
    out_z[z] = total.astype(BF16)
    out_go()
    head_z[z] = head_y_total()
    head_z_go, head_z_total, head_z_sent = four_way(
        net, net.reserve(4), head_z, z, lambda d: net.device(dz=d)
    )
    head_z_go()
    for dx, dc in others:
        vec_copy(dx, dc).wait_recv()
    total = vec_1[0]
    for block in range(1, 8):
        total = total + vec_1[block]
    vec_1s[...] = total
    v2 = net.reserve(4)

    def vec_z(d):
        return net.copy(v2 + d, vec_1s.at[(z + d) % 2], vec_2.at[z], net.device(dz=d))

    for d in (2, 1, 3):
        vec_z(d).start()
    vec_2[z] = vec_1s[zl]
    out_t[...] = out_total().astype(BF16)

    @pl.when(c == zl)
    def _():
        out_local.start()
        for d in (2, 1, 3):
            out_3(d).start()

    head_sib[0] = head_z_total()
    head_copy = net.go(head_sib.at[0], head_sib.at[1], sibling)
    for d in (1, 2, 3):
        vec_z(d).wait_recv()
    vec_3[y] = (vec_2[0] + vec_2[1]) + (vec_2[2] + vec_2[3])
    vec_y_go, vec_y_total, vec_y_sent = four_way(
        net, net.reserve(4), vec_3, y, lambda d: net.device(dy=d)
    )
    vec_y_go()

    @pl.when(c == zl)
    def _():
        down_local.wait()
        down_5(z).start()
        for d in (1, 2, 3):
            source_z = (z + d) % 4
            down_4(0, source_z).wait_recv()
            down_5(source_z).start()
        out_local.wait()
        out_4(y).start()
        for d in (1, 2, 3):
            out_3(d).wait_recv()
            out_4((y + 4 - d) % 4).start()


    up_share[1]()
    three_share[1]()
    head_copy.wait_recv()
    hb_out[...] = jnp.where(c == zl, head_sib[0], head_sib[1])
    vec_out[...] = vec_y_total()

    @pl.when(c == zl)
    def _():
        for i in range(4):
            down_5(i).wait_send()
            out_4(i).wait_send()
        for d in (1, 2, 3):
            out_3(d).wait_send()

    @pl.when(c != zl)
    def _():
        for i in range(4):
            down_5(i).wait_recv()
            out_4(i).wait_recv()

    for k in range(2):

        @pl.when(c + 2 * k != z)
        def _():
            down_4(k, z).wait_send()

    up_share[2]()
    three_share[2]()
    grad_arrived()
    grad_left()
    output_arrived()
    output_left()
    for done in (up[6], flows[0][6], flows[1][6], d3_sent, out_sent, head_y_sent, head_z_sent, vec_y_sent):
        done()
    for d in (1, 2, 3):
        down_1(d).wait_send()
        down_2(d).wait_send()
        out_1(d).wait_send()
        vec_z(d).wait_send()
    for d in range(4):
        swap_copy(d, (x - d + 4) % 4).wait_send()
    for i in range(2):
        near_copy(1 + 2 * i).wait_send()
        branch_half(i).wait_send()
    back_sum[3]()
    out_sum[3]()
    for dx, dc in others:
        vec_copy(dx, dc).wait_send()
    net.all_sent()


def finish(
    heads,
    mixed,
    grad_mixed,
    w_qkv,
    own,
    smalls,
    result,
    grad_middle,
    branch,
    out_sums,
    g_up_bias,
    g_vectors,
    probs,
    h1,
    g_up,
    g_down,
):
    rows, width = own.shape

    def shape(*dims, dtype=BF16):
        return jax.ShapeDtypeStruct(dims, dtype)

    def buffer(*dims, dtype=BF16):
        return pltpu.VMEM(dims, dtype)

    def column_buffers(columns):
        return [
            buffer(2, 2, 4, 48, columns),
            buffer(2, 2, 4, 48, columns),
            buffer(2, 4, 48, columns),
            buffer(2, 4, 48, columns),
            buffer(8, 48, columns),
            buffer(4, 2, 48, columns),
            buffer(2, 48, columns),
            buffer(4, 48, columns),
        ]

    return pl.pallas_call(
        finish_kernel,
        in_specs=[VMEM] * 11 + [HBM] * 5,
        out_specs=[VMEM] * 2 + [HBM] * 7,
        out_shape=[
            shape(8, 640, dtype=F32),
            shape(8, 160, dtype=F32),
            shape(rows, width),
            shape(rows, width),
            shape(4, 48, 5120),
            shape(4, 3, 48, width),
            shape(640, width),
            shape(4, 48, width),
            shape(8 * rows, width),
        ],
        scratch_shapes=[
            buffer(8 * rows, width),
            buffer(2, 2 * rows, 8 * rows),
            buffer(2, 8 * rows, 240),
            buffer(8 * rows, HD, dtype=F32),
            buffer(8 * rows, HD, dtype=F32),
            buffer(4, rows, width),
            buffer(4, rows, width),
            buffer(4, rows, width),
            buffer(2, 2, rows // 2, width),
            buffer(2, rows // 2, width),
            buffer(2, rows // 2, width),
            buffer(2, 2, rows // 2, width),
            buffer(2, rows // 2, width),
            buffer(2, rows // 2, width),
            buffer(2, rows // 2, width),
            buffer(rows, width),
            buffer(rows, width, dtype=F32),
            buffer(rows, width),
        ]
        + column_buffers(640)
        + [buffer(48, 5120)]
        + ([buffer(8, 160, 240)] + column_buffers(240) + [buffer(8, 48, 240)]) * 2
        + [
            buffer(3, 48, width),
            buffer(2, width, 240),
            buffer(4, 160, width),
            buffer(160, width),
            buffer(4, 48, width),
            buffer(4, 48, width),
            buffer(160, width),
            buffer(160, width),
            buffer(4, 48, width),
            buffer(4, 48, width),
            buffer(48, width),
            buffer(4, 8, 640, dtype=F32),
            buffer(4, 8, 640, dtype=F32),
            buffer(2, 8, 640, dtype=F32),
            buffer(4, 2, 8, 160, dtype=F32),
            buffer(8, 2, 8, 160, dtype=F32),
            buffer(2, 8, 160, dtype=F32),
            buffer(4, 8, 160, dtype=F32),
            buffer(4, 8, 160, dtype=F32),
            buffer(8, width, dtype=F32),
        ]
        + scratch_for(192),
        compiler_params=pltpu.CompilerParams(
            collective_id=2, has_side_effects=True, vmem_limit_bytes=62 << 20
        ),
    )(
        heads,
        mixed,
        grad_mixed,
        w_qkv,
        own,
        smalls,
        result,
        grad_middle,
        branch,
        g_up_bias,
        g_vectors,
        out_sums,
        probs,
        h1,
        g_up,
        g_down,
    )


def widen_kernel(hb, vec, up, three, down, out, rows, grad, *results):
    o_up, o_q, o_k, o_v, o_down, o_out, o_rows, o_grad = results[:8]
    small, scratch = results[8:17], results[17:]
    b_up, b_three, b_down, b_out, b_rows, b_grad, f_up, f_three, f_down, f_out, f_grad, came, done = scratch
    loads, copies = [], []
    sources = ((up, b_up), (three, b_three), (down, b_down), (out, b_out), (grad, b_grad), (rows, b_rows))
    for source, target in sources:
        loads.append(pltpu.make_async_copy(source, target, came.at[len(loads)]))
        loads[-1].start()

    def push(source, target):
        copy = pltpu.make_async_copy(source, target, done.at[len(copies)])
        copy.start()
        copies.append(copy)

    pieces = ((slice(0, 48), 0, slice(0, 48)), (slice(48, 96), 1, slice(0, 48)))
    pieces += ((slice(96, 144), 2, slice(0, 48)), (slice(144, 160), 3, slice(32, 48)))
    loads[0].wait()
    for here, i, there in pieces:
        f_up[here, :] = b_up[i, there, :].astype(F32)
    push(f_up, o_up)
    loads[1].wait()
    for k, target in enumerate((o_q, o_k, o_v)):
        for here, i, there in pieces:
            f_three[k, here, :] = b_three[i, k, there, :].astype(F32)
        push(f_three.at[k], target)
    loads[2].wait()
    f_down[...] = b_down[...].astype(F32)
    push(f_down, o_down)
    loads[3].wait()
    for here, i, there in pieces:
        f_out[here, :] = b_out[i, there, :].astype(F32)
    push(f_out, o_out)
    loads[4].wait()
    f_grad[...] = b_grad[...].astype(F32)
    push(f_grad, o_grad)
    loads[5].wait()
    push(b_rows, o_rows)
    for target, row in zip(small, (hb[1, :160], hb[2, :160], hb[0, :])):
        target[...] = row
    for k in range(6):
        small[3 + k][...] = vec[k, :]
    for copy in copies:
        copy.wait()


def widen(hb, vec, up, three, down, out, rows, grad):
    width = down.shape[1]

    def shape(*dims):
        return jax.ShapeDtypeStruct(dims, F32)

    sizes = [160, 160, 640] + [160] * 6
    arrays = (up, three, down, out, rows, grad)
    return pl.pallas_call(
        widen_kernel,
        in_specs=[VMEM] * 2 + [HBM] * 6,
        out_specs=[HBM] * 8 + [VMEM] * 9,
        out_shape=[shape(160, 5120)]
        + [shape(160, width)] * 3
        + [shape(640, width), shape(160, width)]
        + [jax.ShapeDtypeStruct(rows.shape, BF16), shape(*grad.shape)]
        + [shape(size) for size in sizes],
        scratch_shapes=[pltpu.VMEM(array.shape, BF16) for array in arrays]
        + [
            pltpu.VMEM((160, 5120), F32),
            pltpu.VMEM((3, 160, width), F32),
            pltpu.VMEM((640, width), F32),
            pltpu.VMEM((160, width), F32),
            pltpu.VMEM(grad.shape, F32),
            pltpu.SemaphoreType.DMA((6,)),
            pltpu.SemaphoreType.DMA((8,)),
        ],
        compiler_params=pltpu.CompilerParams(vmem_limit_bytes=60 << 20),
    )(hb, vec, up, three, down, out, rows, grad)


def per_device(
    tokens,
    lengths,
    w_query,
    w_key,
    w_value,
    w_out,
    w_up,
    w_down,
    b_query,
    b_value,
    b_out,
    b_up,
    b_down,
    gain_attn,
    shift_attn,
    gain_ffn,
    shift_ffn,
    cotangent,
):
    rows, width = tokens.shape[1:]

    eight = [b_query, b_value, b_out, b_down, gain_attn, shift_attn, gain_ffn, shift_ffn]
    row = lax.broadcasted_iota(jnp.int32, (16, 160), 0)
    small = jnp.zeros((16, 160), BF16)
    for index, vector in enumerate(eight):
        small = jnp.where(row == index, vector[None, :], small)
    up_bias = jnp.broadcast_to(b_up[None, :], (16, 640))
    known = jnp.full((8, 128), lengths[0], F32)
    (
        h1,
        heads,
        probs,
        mixed,
        attended,
        w_qkv,
        smalls,
        up_bias,
        own,
        clip,
        out_full,
        up_mine,
        down_mine,
        top,
        _,
    ) = begin(
        tokens[0],
        w_query,
        w_key,
        w_value,
        small,
        up_bias,
        w_out,
        w_up,
        w_down,
        cotangent[0],
        known,
    )
    w_qkv = w_qkv.reshape(width, 480)
    (
        result,
        grad_middle,
        branch,
        out_sums,
        g_up,
        g_down,
        g_up_bias,
        g_vectors,
        grad_mixed,
    ) = middle_part(
        attended,
        own,
        smalls,
        up_bias,
        clip,
        out_full.reshape(width, width),
        up_mine.reshape(width, 640),
        down_mine,
        top.reshape(8 * rows, width),
    )
    hb_out, vec_out, output, input_grad, fin_up, fin_qkv, fin_down, fin_out, _ = finish(
        heads,
        mixed,
        grad_mixed,
        w_qkv,
        own,
        smalls,
        result,
        grad_middle,
        branch,
        out_sums,
        g_up_bias,
        g_vectors,
        probs,
        h1.reshape(8 * rows, width),
        g_up.reshape(8, 160, 640),
        g_down,
    )

    g_up, g_q, g_k, g_v, g_down, g_out, output, input_grad, *small = widen(
        hb_out, vec_out, fin_up, fin_qkv, fin_down, fin_out, output, input_grad
    )
    b_q, b_v, b_u, b_o, b_d, gain_two, shift_two, gain_one, shift_one = small
    return (
        output[None],
        input_grad[None],
        g_q,
        g_k,
        g_v,
        g_out,
        g_up,
        g_down,
        b_q,
        b_v,
        b_o,
        b_u,
        b_d,
        gain_one,
        shift_one,
        gain_two,
        shift_two,
    )


def solution(mesh):
    by_clip, matrix, vector = P("rep", "shard", None), P("shard", None), P("shard")
    return jax.shard_map(
        per_device,
        mesh=mesh,
        in_specs=(by_clip, P("rep")) + (matrix,) * 6 + (vector,) * 9 + (by_clip,),
        out_specs=(by_clip, by_clip) + (matrix,) * 6 + (vector,) * 9,
        check_vma=False,
    )
```

```python
import jax
import jax.numpy as jnp
from jax import lax
from jax.experimental import pallas as pl
from jax.experimental.pallas import tpu as pltpu
from jax.sharding import PartitionSpec as P

HD = 80
EPS = 1e-05
F32 = jnp.float32
BF16 = jnp.bfloat16
NT = (((1,), (1,)), ((), ()))
TN = (((0,), (0,)), ((), ()))


MESH = pl.DeviceIdType.MESH
VMEM = pl.BlockSpec(memory_space=pltpu.VMEM)
HBM = pl.BlockSpec(memory_space=pl.ANY)


class Net:
    def __init__(self, sent, got, still):
        rep, shard = lax.axis_index("rep"), lax.axis_index("shard")
        self.y, self.zh, self.c = rep // 4, rep // 2 % 2, rep % 2
        self.x, self.zl = shard // 2, shard % 2
        self.me, self.shard = 2 * self.x + self.c, shard
        self.sent, self.got, self.still, self.used, self.started = sent, got, still, 0, []

    def device(self, dx=0, dc=0, dz=0, dy=0):
        z = (2 * self.zh + self.zl + dz) % 4
        return (
            (self.y + dy) % 4 * 4 + z // 2 * 2 + (self.c + dc) % 2,
            (self.x + dx) % 4 * 2 + z % 2,
        )

    def in_pair(self, dx, dz):
        return (
            self.y * 4 + self.zh * 2 + self.c,
            (self.x + dx) % 4 * 2 + (self.zl + dz) % 2,
        )

    def partner(self):
        return (self.y * 4 + self.zh * 2 + self.zl, 2 * self.x + self.c)

    def greet(self, devices):
        barrier = pltpu.get_barrier_semaphore()
        for device in devices:
            pl.semaphore_signal(barrier, inc=1, device_id=device, device_id_type=MESH)
        return lambda: pl.semaphore_wait(barrier, len(devices))

    def reserve(self, count):
        first = self.used
        self.used += count
        return first

    def copy(self, index, source, target, device):
        return pltpu.make_async_remote_copy(
            src_ref=source,
            dst_ref=target,
            send_sem=self.sent.at[index],
            recv_sem=self.got.at[index],
            device_id=device,
            device_id_type=MESH,
        )

    def go(self, source, target, device):
        copy = self.copy(self.reserve(1), source, target, device)
        copy.start()
        self.started.append(copy)
        return copy

    def cross(self, source, target):
        index = self.reserve(1)
        copy = self.copy(index, source, target, self.partner())
        local = pltpu.make_async_copy(source, target, self.still.at[index])

        @pl.when(self.c != self.zl)
        def _():
            copy.start()

        @pl.when(self.c == self.zl)
        def _():
            local.start()

        def arrived():
            @pl.when(self.c != self.zl)
            def _():
                copy.wait_recv()

            @pl.when(self.c == self.zl)
            def _():
                local.wait()

        def left():
            @pl.when(self.c != self.zl)
            def _():
                copy.wait_send()

        return arrived, left

    def all_sent(self):
        for copy in self.started:
            copy.wait_send()


def order(k):
    return 1 + 2 * k - 3 * (k // 2)


def aligned(index, size):
    return pl.ds(pl.multiple_of(index * size, size), size)


def scratch_for(copies):
    return [pltpu.SemaphoreType.DMA((copies,)) for _ in range(3)]


def begin_kernel(
    tokens,
    w_query,
    w_key,
    w_value,
    small,
    up_bias,
    w_out,
    w_up,
    w_down,
    cotangent,
    length,
    h1,
    heads,
    probs,
    mixed,
    attended,
    w_qkv,
    smalls,
    bias_up,
    own,
    clip,
    out_full,
    up_mine,
    down_mine,
    top,
    out_own,
    normed_rows,
    head_rows,
    prob_buf,
    gathered,
    cut,
    lens,
    vectors,
    sent,
    got,
    still,
):
    net = Net(sent, got, still)
    x, y, c, zh, zl, me, shard = net.x, net.y, net.c, net.zh, net.zl, net.me, net.shard
    rows, width = tokens.shape
    plane = [net.device(dx, dc) for dx in range(4) for dc in range(2) if dx or dc]
    across = [net.in_pair(dx, 1) for dx in range(4)]
    rings = [net.device(dy=d) for d in (1, 2, 3)] + [net.device(dz=d) for d in (1, 2, 3)]
    wait = net.greet(plane + across + rings + [(y * 4 + zh * 2 + 1 - c, 2 * x + 1 - zl)])
    for block in range(8):
        cols = slice(160 * block, 160 * block + 160)
        for half in range(2):
            part = slice(80 * half, 80 * half + 80)
            for k, weight in enumerate((w_query, w_key, w_value)):
                piece = weight[part, cols]
                for h in range(2):
                    first = 240 * h + 80 * k
                    cut[block, half, :, first : first + 80] = piece[:, 80 * h : 80 * h + 80]
    wait()

    token_arrived, token_left = net.cross(tokens, gathered.at[2 * x + zl])
    base = net.reserve(4)

    def token_send(k, source):
        dx = order(k)
        return net.copy(base + dx, source, gathered.at[me], net.device(dx))

    cut_near, cut_ring, up_near, up_ring = (net.reserve(4) for _ in range(4))

    def cut_copy(d):
        source = cut.at[2 * ((x + d) % 4) + c, zh]
        return net.copy(cut_near + d, source, w_qkv.at[x, zl, zh], net.device(d))

    def cut_share(d):
        here = w_qkv.at[:, zl, zh]
        return net.copy(cut_ring + d, here, here, net.device(dz=d))

    cut_half = net.reserve(2)

    def cut_on(i):
        from_z = (2 * zh + zl + 3 + 2 * i) % 4
        here = w_qkv.at[pl.ds(2 * i, 2), from_z % 2, from_z // 2]
        return net.copy(cut_half + i, here, here, net.device(dz=1 + 2 * i))

    def up_part(index):
        cols = pl.ds(pl.multiple_of(index * 640, 128), 640)
        return w_up.at[aligned(zh, 80), cols]

    def up_copy(d):
        source = up_part(2 * ((x + d) % 4) + c)
        return net.copy(up_near + d, source, up_mine.at[x, zl, zh], net.device(d))

    def up_share(d):
        here = up_mine.at[:, zl, zh]
        return net.copy(up_ring + d, here, here, net.device(dz=d))

    up_local = pltpu.make_async_copy(up_part(me), up_mine.at[x, zl, zh], still.at[up_near])

    for d in (2, 1, 3):
        cut_copy(d).start()

    @pl.when(c == zl)
    def _():
        for k in range(2):
            token_send(k, tokens).start()

    @pl.when(c == 0)
    def _():
        lens[0] = length[...]

    @pl.when(c == 1)
    def _():
        lens[1] = length[...]

    lens_copy = net.go(length, lens.at[c], net.device(0, 1))
    arriving = []
    for dx in (0, 1, 3, 2):
        for dz in range(2):
            if dx or dz:
                arriving.append(net.go(small, smalls.at[shard], net.in_pair(dx, dz)))
    smalls[shard] = small[...]
    w_qkv[x, zl, zh] = cut[me, zh]
    token_arrived()

    @pl.when(c != zl)
    def _():
        for k in range(2):
            token_send(k, gathered.at[me]).start()

    sibling = net.device(0, 1)
    own_over = net.go(gathered.at[me], gathered.at[me], sibling)
    for d in (1, 3, 2):
        cut_copy(d).wait_recv()
    for d in (1, 3):
        cut_share(d).start()
    up_local.start()
    for d in (2, 1, 3):
        up_copy(d).start()
    own[...] = gathered[me]
    for copy in arriving:
        copy.wait_recv()
    for block in range(8):
        vectors[:, 160 * block : 160 * block + 160] = smalls[block, :8, :].astype(F32)
    gain, shift = vectors[4:5, :], vectors[5:6, :]
    bias_q = smalls[me, 0:1, :].astype(F32)
    bias_v = smalls[me, 1:2, :].astype(F32)

    def project(slot):
        values = gathered[slot].astype(F32)
        center = values - jnp.mean(values, axis=-1, keepdims=True)
        inverse = lax.rsqrt(jnp.mean(center * center, axis=-1, keepdims=True) + EPS)
        normed = (center * inverse * gain + shift).astype(BF16)
        normed_rows[slot] = normed
        made = jnp.dot(normed, w_qkv[...].reshape(width, 480), preferred_element_type=F32)
        here = aligned(slot, rows)
        for h in range(2):
            cols = slice(h * HD, (h + 1) * HD)
            q, k, v = (made[:, 240 * h + 80 * j : 240 * h + 80 * j + 80] for j in range(3))
            head_rows[h, here, :] = (q + bias_q[:, cols]).astype(BF16)
            head_rows[2 + h, here, :] = k.astype(BF16)
            head_rows[4 + h, here, :] = (v + bias_v[:, cols]).astype(BF16)

    for i in range(2):
        cut_share(1 + 2 * i).wait_recv()
        cut_on(i).start()
    bias_arrived, bias_left = net.cross(up_bias, bias_up)
    top_arrived, top_left = net.cross(cotangent, top.at[2 * x + zl])
    out_arrived, out_left = net.cross(w_out, out_own)

    down_index, down_ring = net.reserve(1), net.reserve(4)
    down_cross = net.copy(
        down_index, w_down.at[aligned(y, 160)], down_mine.at[aligned(y, 160)], net.partner()
    )
    down_local = pltpu.make_async_copy(w_down, down_mine, still.at[down_index])

    def down_share(d):
        here = down_mine.at[aligned(y, 160)]
        return net.copy(down_ring + d, here, here, net.device(dy=d))

    @pl.when(c == zl)
    def _():
        down_local.start()

    @pl.when(c != zl)
    def _():
        down_cross.start()

    top_near, top_over, out_near, out_ring, out_over = (net.reserve(4) for _ in range(5))

    def top_copy(d):
        return net.copy(top_near + d, top.at[me], top.at[me], net.device(d))

    top_halves = net.reserve(2)

    def top_half(i):
        slot = 2 * ((x + 3 + 2 * i) % 4) + c
        here = top.at[slot, pl.ds(i * rows // 2, rows // 2), :]
        return net.copy(top_halves + i, here, here, net.device(1 + 2 * i))

    def top_pass(d):
        here = top.at[2 * ((x - d + 4) % 4) + c]
        return net.copy(top_over + d, here, here, sibling)

    half = pl.ds(pl.multiple_of(y % 2 * 640, 128), 640)
    out_piece = out_own.at[aligned(y // 2, 80), half]

    def out_copy(d):
        return net.copy(out_near + d, out_piece, out_full.at[x, c, y // 2, :, half], net.device(d))

    def out_share(d):
        here = out_full.at[:, c, y // 2, :, half]
        return net.copy(out_ring + d, here, here, net.device(dy=d))

    def out_pass(d):
        from_y = (y - d + 4) % 4
        cols = pl.ds(pl.multiple_of(from_y % 2 * 640, 128), 640)
        here = out_full.at[:, c, from_y // 2, :, cols]
        return net.copy(out_over + d, here, here, sibling)

    out_local = pltpu.make_async_copy(
        out_piece, out_full.at[x, c, y // 2, :, half], still.at[out_near]
    )
    for i in range(2):
        cut_on(i).wait_recv()
    project(me)
    own_over.wait_recv()
    project(2 * x + 1 - c)
    out_arrived()
    out_local.start()
    for d in (2, 1, 3):
        out_copy(d).start()

    @pl.when(c != zl)
    def _():
        down_cross.wait_recv()
        for d in (2, 1, 3):
            down_share(d).start()

    over, halves = net.reserve(4), net.reserve(2)

    def token_half(i):
        slot = 2 * ((x + 3 + 2 * i) % 4) + c
        here = gathered.at[slot, pl.ds(i * rows // 2, rows // 2), :]
        return net.copy(halves + i, here, here, net.device(1 + 2 * i))

    def passed(dx, slot):
        return net.copy(over + dx, gathered.at[slot], gathered.at[slot], sibling)

    @pl.loop(0, 3)
    def _(k):
        dx = order(k)
        from_x = (x - dx + 4) % 4

        @pl.when(k == 0)
        def _():
            for i in range(2):
                token_send(i, gathered.at[me]).wait_recv()
                token_half(i).start()

        @pl.when(k == 1)
        def _():
            top_arrived()
            for i in range(2):
                top_copy(1 + 2 * i).start()

        @pl.when(k == 2)
        def _():
            for i in range(2):
                token_half(i).wait_recv()

        passed(dx, 2 * from_x + c).start()
        project(2 * from_x + c)
        passed(dx, 2 * from_x + c).wait_recv()
        project(2 * from_x + 1 - c)

    out_local.wait()
    for d in (1, 3, 2):
        out_copy(d).wait_recv()
    for d in (2, 1, 3):
        out_share(d).start()
    out_pass(0).start()
    up_local.wait()
    for d in (1, 3, 2):
        up_copy(d).wait_recv()
    for d in (2, 1, 3):
        up_share(d).start()
    top_pass(0).start()

    keep_h1 = pltpu.make_async_copy(normed_rows, h1, still.at[net.reserve(1)])
    keep_h1.start()
    keep_heads = pltpu.make_async_copy(head_rows, heads, still.at[net.reserve(1)])
    keep_heads.start()
    lens_copy.wait_recv()
    clip[...] = lens[zl]
    clip_length = clip[0:1, 0:1]
    position = lax.broadcasted_iota(jnp.int32, (1, 8 * rows), 1).astype(F32)
    mask = jnp.where(position < clip_length, 0.0, -1e30)

    def attend_rows(to_x, slot):
        here = aligned(to_x, 2 * rows)
        for h in range(2):
            cols = slice(h * HD, (h + 1) * HD)
            scores = lax.dot_general(
                head_rows[h, here, :], head_rows[2 + h], NT, preferred_element_type=F32
            )
            scores = scores * HD**-0.5 + mask
            risen = jnp.exp(scores - jnp.max(scores, axis=-1, keepdims=True))
            share = 1.0 / jnp.sum(risen, axis=-1, keepdims=True)
            low = (risen * share).astype(BF16)
            prob_buf[slot, h] = low
            made = jnp.dot(low, head_rows[4 + h], preferred_element_type=F32).astype(BF16)
            mixed[2 * to_x, :, cols] = made[:rows]
            mixed[2 * to_x + 1, :, cols] = made[rows:]

    prob_index = net.reserve(2)

    def keep_probs(to_x, slot):
        return pltpu.make_async_copy(
            prob_buf.at[slot], probs.at[:, aligned(to_x, 2 * rows), :], still.at[prob_index + slot]
        )

    mixed_base = net.reserve(8)

    def mixed_send(dx, dc):
        slot = 2 * ((x + dx) % 4) + (c + dc) % 2
        return net.copy(
            mixed_base + 2 * dx + dc, mixed.at[slot], attended.at[me], net.device(dx, dc)
        )

    @pl.loop(1, 5)
    def _(step):
        dx = step % 4
        to_x = (x + dx) % 4

        @pl.when(step == 2)
        def _():
            for i in range(2):
                top_copy(1 + 2 * i).wait_recv()
                top_half(i).start()
                top_pass(1 + 2 * i).start()

        @pl.when(step > 2)
        def _():
            keep_probs(to_x, step % 2).wait()

        attend_rows(to_x, step % 2)
        keep_probs(to_x, step % 2).start()
        mixed_send(dx, 1).start()

        @pl.when(dx != 0)
        def _():
            mixed_send(dx, 0).start()

    attended[me] = mixed[me]
    for i in range(2):
        top_half(i).wait_recv()
    top_pass(2).start()
    for d in (1, 3, 2):
        out_share(d).wait_recv()
        out_pass(d).start()
    for dx in range(4):
        for dc in range(2):
            if dx or dc:
                mixed_send(dx, dc).wait()
    for d in range(4):
        top_pass(d).wait()
        out_pass(d).wait()
    for d in (1, 2, 3):
        up_share(d).wait()
        for copy in (cut_copy, up_copy, out_copy, out_share):
            copy(d).wait_send()
    for i in range(2):
        for copy in (cut_share, top_copy):
            copy(1 + 2 * i).wait_send()
        cut_on(i).wait_send()
        top_half(i).wait_send()

    @pl.when(c == zl)
    def _():
        down_local.wait()

    @pl.when(c != zl)
    def _():
        down_cross.wait_send()
        for d in (1, 2, 3):
            down_share(d).wait()

    keep_h1.wait()
    keep_heads.wait()
    for slot in range(2):
        keep_probs(slot, slot).wait()
    bias_arrived()
    for left in (token_left, out_left, top_left, bias_left):
        left()
    for k in range(2):
        token_send(k, gathered.at[me]).wait_send()
        token_half(k).wait_send()
    for k in range(3):
        passed(order(k), me).wait_send()
    net.all_sent()


def begin(tokens, w_query, w_key, w_value, small, up_bias, w_out, w_up, w_down, cotangent, length):
    rows, width = tokens.shape

    def shape(*dims):
        return jax.ShapeDtypeStruct(dims, BF16)

    return pl.pallas_call(
        begin_kernel,
        in_specs=[VMEM] * 11,
        out_specs=[HBM] * 3 + [VMEM] * 7 + [HBM] * 4 + [VMEM],
        out_shape=[
            shape(8, rows, width),
            shape(6, 8 * rows, HD),
            shape(2, 8 * rows, 8 * rows),
            shape(8, rows, 160),
            shape(8, rows, 160),
            shape(4, 2, 2, 80, 480),
            shape(8, 16, 160),
            shape(16, 640),
            shape(rows, width),
            jax.ShapeDtypeStruct((8, 128), F32),
            shape(4, 2, 2, 80, width),
            shape(4, 2, 2, 80, 640),
            shape(640, width),
            shape(8, rows, width),
            shape(160, width),
        ],
        scratch_shapes=[
            pltpu.VMEM((8, rows, width), BF16),
            pltpu.VMEM((6, 8 * rows, HD), BF16),
            pltpu.VMEM((2, 2, 2 * rows, 8 * rows), BF16),
            pltpu.VMEM((8, rows, width), BF16),
            pltpu.VMEM((8, 2, 80, 480), BF16),
            pltpu.VMEM((2, 8, 128), F32),
            pltpu.VMEM((8, width), F32),
        ]
        + scratch_for(96),
        compiler_params=pltpu.CompilerParams(
            collective_id=0, has_side_effects=True, vmem_limit_bytes=58 << 20
        ),
    )(tokens, w_query, w_key, w_value, small, up_bias, w_out, w_up, w_down, cotangent, length)


def middle_kernel(
    attended,
    own,
    smalls,
    up_bias,
    clip,
    out_full,
    up_mine,
    down_mine,
    top,
    result,
    grad_middle,
    branch,
    out_sums,
    g_up,
    g_down,
    g_up_bias,
    g_vectors,
    grad_mixed,
    vectors,
    middle,
    second,
    masked,
    active,
    hidden,
    parts,
    over,
    sums,
    arrived,
    out_parts,
    out_over,
    joined,
    by_head,
    sent,
    got,
    still,
):
    net = Net(sent, got, still)
    x, c, me = net.x, net.c, net.me
    rows, width = own.shape
    wait = net.greet([net.device(dx, dc) for dx in range(4) for dc in range(2) if dx or dc])
    for block in range(8):
        vectors[:, 160 * block : 160 * block + 160] = smalls[block, :8, :].astype(F32)
    bias_up = up_bias[0:1, :].astype(F32)
    mine = aligned(me, rows)
    for block in range(8):
        joined[:, 160 * block : 160 * block + 160] = attended[block]
    made = jnp.dot(joined[...], out_full[...], preferred_element_type=F32)
    middle[...] = own[...].astype(F32) + made + vectors[2:3, :]

    def normalised():
        values = middle[...]
        center = values - jnp.mean(values, axis=-1, keepdims=True)
        inverse = lax.rsqrt(jnp.mean(center * center, axis=-1, keepdims=True) + EPS)
        return center * inverse, inverse

    second[mine, :] = (normalised()[0] * vectors[6:7, :] + vectors[7:8, :]).astype(BF16)
    wait()

    near, pass_on, swap, add, out_swap = (net.reserve(4) for _ in range(5))

    def out_copy(dx, to_x):
        source = out_parts.at[aligned(2 * to_x + 1 - c, rows)]
        return net.copy(out_swap + dx, source, out_over.at[to_x], net.device(0, 1))

    def near_copy(dx):
        return net.copy(near + dx, second.at[mine], second.at[mine], net.device(dx))

    def pass_copy(dx, slot):
        here = second.at[aligned(slot, rows)]
        return net.copy(pass_on + dx, here, here, net.device(0, 1))

    def swap_copy(dx, to_x):
        source = parts.at[aligned(2 * to_x + 1 - c, rows)]
        return net.copy(swap + dx, source, over.at[to_x], net.device(0, 1))

    def add_copy(dx, to_x):
        return net.copy(add + dx, sums.at[to_x], arrived.at[dx], net.device(4 - dx))

    halves = net.reserve(2)

    def half_copy(i):
        slot = 2 * ((x + 3 + 2 * i) % 4) + c
        here = second.at[aligned(2 * slot + i, rows // 2)]
        return net.copy(halves + i, here, here, net.device(1 + 2 * i))

    for dx in (1, 3):
        near_copy(dx).start()

    @pl.loop(0, 4)
    def _(k):
        dx = k ^ (k >> 1)
        to_x = (x - dx + 4) % 4

        @pl.when(k == 1)
        def _():
            for i in range(2):
                near_copy(1 + 2 * i).wait_recv()
                half_copy(i).start()

        @pl.when(k == 3)
        def _():
            for i in range(2):
                half_copy(i).wait_recv()

        pass_copy(dx, 2 * to_x + c).start()
        here = aligned(to_x, 2 * rows)
        position = lax.broadcasted_iota(jnp.int32, (2 * rows, 1), 0) + to_x * 2 * rows
        live = position.astype(F32) < clip[0:1, 0:1]
        low_top = jnp.where(live, top[here, :].astype(F32), 0.0).astype(BF16)
        masked[here, :] = low_top
        grad_act = lax.dot_general(low_top, down_mine[...], NT, preferred_element_type=F32)
        pass_copy(dx, 2 * to_x + c).wait_recv()
        z = jnp.dot(second[here, :], up_mine[...], preferred_element_type=F32) + bias_up
        bell = 0.5 * (1.0 + lax.erf(z * 0.7071067811865476))
        active[here, :] = (z * bell).astype(BF16)
        slope = bell + z * jnp.exp(-0.5 * z * z) * 0.3989422804014327
        grad_z = (grad_act * slope).astype(BF16)
        hidden[here, :] = grad_z
        parts[here, :] = lax.dot_general(
            grad_z, up_mine[...], NT, preferred_element_type=F32
        ).astype(BF16)
        swap_copy(dx, to_x).start()
        out_parts[here, :] = jnp.dot(
            active[here, :], down_mine[...], preferred_element_type=F32
        ).astype(BF16)
        out_copy(dx, to_x).start()
        swap_copy(dx, to_x).wait_recv()

        @pl.when(dx != 0)
        def _():
            kept = parts[aligned(2 * to_x + c, rows), :].astype(F32)
            sums[to_x] = (kept + over[to_x].astype(F32)).astype(BF16)
            add_copy(dx, to_x).start()

    @pl.loop(0, 5)
    def _(i):
        cols = pl.ds(pl.multiple_of(i * 256, 256), 256)
        g_up[cols, :] = lax.dot_general(
            second[:, cols], hidden[...], TN, preferred_element_type=F32
        ).astype(BF16)
        cols = pl.ds(pl.multiple_of(i * 128, 128), 128)
        g_down[cols, :] = lax.dot_general(
            active[:, cols], masked[...], TN, preferred_element_type=F32
        ).astype(BF16)

    for dx in range(4):
        to_x = (x - dx + 4) % 4
        out_copy(dx, to_x).wait_recv()
        kept = out_parts[aligned(2 * to_x + c, rows), :].astype(F32) + out_over[to_x].astype(F32)
        if dx:
            out_sums[to_x] = kept.astype(BF16)
        else:
            result[...] = middle[...] + kept + vectors[3:4, :]
    g_up_bias[...] = jnp.sum(hidden[...].astype(F32), axis=0, keepdims=True)
    grad_second = parts[mine, :].astype(F32) + over[x].astype(F32)
    for dx in (1, 3, 2):
        add_copy(dx, (x - dx + 4) % 4).wait_recv()
        grad_second = grad_second + arrived[dx].astype(F32)
    normed, inverse = normalised()
    scaled = grad_second * vectors[6:7, :]
    back = inverse * (
        scaled
        - jnp.mean(scaled, axis=-1, keepdims=True)
        - normed * jnp.mean(scaled * normed, axis=-1, keepdims=True)
    )
    top_own = masked[mine, :].astype(F32)
    total = top_own + back
    grad_middle[...] = total
    low = total.astype(BF16)
    branch[...] = low
    grad_attended = lax.dot_general(low, out_full[...], NT, preferred_element_type=F32)
    grad_attended = grad_attended.astype(BF16)
    for block in range(8):
        by_head[block] = grad_attended[:, 160 * block : 160 * block + 160]
    mixing = []
    for dx in (2, 1, 3, 0):
        for dc in (1, 0):
            if dx or dc:
                slot = 2 * ((x + dx) % 4) + (c + dc) % 2
                mixing.append(net.go(by_head.at[slot], grad_mixed.at[me], net.device(dx, dc)))
    grad_mixed[me] = by_head[me]
    g_vectors[0:1, :] = jnp.sum(low.astype(F32), axis=0, keepdims=True)
    g_vectors[1:2, :] = jnp.sum(top_own, axis=0, keepdims=True)
    g_vectors[2:3, :] = jnp.sum(grad_second * normed, axis=0, keepdims=True)
    g_vectors[3:4, :] = jnp.sum(grad_second, axis=0, keepdims=True)
    for copy in mixing:
        copy.wait_recv()
    for dx in range(4):
        to_x = (x - dx + 4) % 4
        pass_copy(dx, 2 * to_x + c).wait_send()
        swap_copy(dx, to_x).wait_send()
        out_copy(dx, to_x).wait_send()
        if dx:
            add_copy(dx, to_x).wait_send()
    for i in range(2):
        near_copy(1 + 2 * i).wait_send()
        half_copy(i).wait_send()
    net.all_sent()


def middle_part(attended, own, smalls, up_bias, clip, out_full, up_mine, down_mine, top):
    rows, width = own.shape

    def shape(*dims, dtype=BF16):
        return jax.ShapeDtypeStruct(dims, dtype)

    def buffer(*dims, dtype=BF16):
        return pltpu.VMEM(dims, dtype)

    return pl.pallas_call(
        middle_kernel,
        in_specs=[VMEM] * 9,
        out_specs=[VMEM] * 9,
        out_shape=[
            shape(rows, width, dtype=F32),
            shape(rows, width, dtype=F32),
            shape(rows, width),
            shape(4, rows, width),
            shape(width, 640),
            shape(640, width),
            shape(1, 640, dtype=F32),
            shape(4, width, dtype=F32),
            shape(8, rows, 160),
        ],
        scratch_shapes=[
            buffer(8, width, dtype=F32),
            buffer(rows, width, dtype=F32),
            buffer(8 * rows, width),
            buffer(8 * rows, width),
            buffer(8 * rows, 640),
            buffer(8 * rows, 640),
            buffer(8 * rows, width),
            buffer(4, rows, width),
            buffer(4, rows, width),
            buffer(4, rows, width),
            buffer(8 * rows, width),
            buffer(4, rows, width),
            buffer(rows, width),
            buffer(8, rows, 160),
        ]
        + scratch_for(32),
        compiler_params=pltpu.CompilerParams(
            collective_id=1, has_side_effects=True, vmem_limit_bytes=60 << 20
        ),
    )(attended, own, smalls, up_bias, clip, out_full, up_mine, down_mine, top)


def piece_start(index):
    return pl.multiple_of(48 * index - 32 * (index // 3), 16)


def beside(p, way):
    return p + 1 - 2 * (p % 2) if way == 0 else 3 - p


def halving(net, piece, r1, t1, r3):
    x = net.x
    b1, b2 = net.reserve(4), net.reserve(2)
    both = [(half, slot) for slot in (1, 0) for half in range(2)]

    def copy_1(half, slot):
        near = beside(x, half)
        wanted = near if slot == 0 else beside(near, 1 - half)
        return net.copy(
            b1 + 2 * half + slot, piece(half, wanted), r1.at[half, slot], net.device(near - x + 4)
        )

    def copy_2(half):
        device = net.device(beside(x, 1 - half) - x + 4)
        return net.copy(b2 + half, t1.at[half], r3.at[half], device)

    def first():
        for half, slot in both:
            copy_1(half, slot).start()

    def halfway(kept):
        for half in range(2):
            copy_1(half, 1).wait_recv()
            t1[half] = (kept(half).astype(F32) + r1[half, 1].astype(F32)).astype(BF16)
            copy_2(half).start()

    def total(half):
        copy_1(half, 0).wait_recv()
        copy_2(half).wait_recv()
        return r1[half, 0].astype(F32) + r3[half].astype(F32)

    def sent():
        for half, slot in both:
            copy_1(half, slot).wait_send()
        for half in range(2):
            copy_2(half).wait_send()

    return first, halfway, total, sent


def column_flow(net, source, m1, r1, t1, r3, s1, r2, s2, planes, landed, place_of):
    y, z, x, c = net.y, 2 * net.zh + net.zl, net.x, net.c
    b1, b2, b3, b4, b5 = (net.reserve(4) for _ in range(5))
    b6 = net.reserve(2)
    sibling = net.device(0, 1)

    def piece(half, p):
        return source.at[pl.ds(4 * half, 4), pl.ds(piece_start(p), 48), :]

    def copy_1(half, slot):
        near = beside(y, half)
        wanted = near if slot == 0 else beside(near, 1 - half)
        return net.copy(
            b1 + 2 * half + slot,
            piece(half, wanted),
            r1.at[half, slot],
            net.device(dy=near - y + 4),
        )

    def load(half, slot):
        wanted = y if slot == 0 else beside(y, 1 - half)
        return pltpu.make_async_copy(
            piece(half, wanted), m1.at[half, slot], net.still.at[b1 + 2 * half + slot]
        )

    def copy_6(half):
        device = net.device(dy=beside(y, 1 - half) - y + 4)
        return net.copy(b6 + half, t1.at[half], r3.at[half], device)

    def copy_2(d):
        part = s1.at[pl.ds(2 * ((z + d) % 4), 2)]
        return net.copy(b2 + d, part, r2.at[d], net.device(dz=d))

    def copy_3(d):
        return net.copy(b3 + d, s2.at[(z + d) % 2], planes.at[z], net.device(dz=d))

    def copy_4(d):
        target = place_of(landed, 2 * x + c)
        return net.copy(b4 + d, planes.at[(x + d) % 4], target, net.device(d))

    def copy_5(d):
        here = place_of(landed, 2 * ((x - d + 4) % 4) + c)
        return net.copy(b5 + d, here, here, sibling)

    both = [(half, slot) for half in range(2) for slot in range(2)]

    def first():
        for half, slot in both:
            copy_1(half, slot).start()
        for half, slot in both:
            load(half, slot).start()

    def halfway():
        for half, slot in both:
            load(half, slot).wait()
            copy_1(half, slot).wait_recv()
        for half in range(2):
            t1[half] = (m1[half, 1].astype(F32) + r1[half, 1].astype(F32)).astype(BF16)
            copy_6(half).start()

    def second():
        for half in range(2):
            copy_6(half).wait_recv()
            total = m1[half, 0].astype(F32) + r1[half, 0].astype(F32) + r3[half].astype(F32)
            s1[pl.ds(4 * half, 4)] = total.astype(BF16)
        for d in (2, 1, 3):
            copy_2(d).start()

    def third():
        total = s1[pl.ds(2 * z, 2)].astype(F32)
        for d in (1, 2, 3):
            copy_2(d).wait_recv()
            total = total + r2[d].astype(F32)
        s2[...] = total.astype(BF16)
        for d in (2, 1, 3):
            copy_3(d).start()
        planes[z] = s2[z % 2]

    def fourth():
        for d in (1, 2, 3):
            copy_3(d).wait_recv()
        for d in (2, 1, 3):
            copy_4(d).start()
        place_of(landed, 2 * x + c)[...] = planes[x]
        copy_5(0).start()

    def fifth():
        for d in (1, 3, 2):
            copy_4(d).wait_recv()
            copy_5(d).start()
        for d in range(4):
            copy_5(d).wait_recv()

    def sent():
        for d in range(4):
            copy_5(d).wait_send()
        for d in (1, 2, 3):
            for copy in (copy_2, copy_3, copy_4):
                copy(d).wait_send()
        for half in range(2):
            copy_6(half).wait_send()
        for half, slot in both:
            copy_1(half, slot).wait_send()

    return first, halfway, second, third, fourth, fifth, sent


def share_over_y(net, whole, final, half_of):
    y = net.y
    near, over = net.reserve(4), net.reserve(4)
    own = pltpu.make_async_copy(whole, final.at[y], net.still.at[near])

    def copy(d):
        return net.copy(near + d, half_of(whole), half_of(final.at[y]), net.device(dy=d))

    def forward(d):
        here = half_of(final.at[(y - d + 4) % 4])
        return net.copy(over + d, here, here, net.device(0, 1))

    def first():
        own.start()
        for d in (2, 1, 3):
            copy(d).start()

    def second():
        for d in (1, 3, 2):
            copy(d).wait_recv()
            forward(d).start()

    def third():
        own.wait()
        for d in (1, 2, 3):
            forward(d).wait_recv()
            forward(d).wait_send()
            copy(d).wait_send()

    return first, second, third


def four_way(net, base, held, position, device_of):
    def copy(d):
        return net.copy(base + d, held.at[position], held.at[position], device_of(d))

    def go():
        for d in (2, 1, 3):
            copy(d).start()

    def total():
        for d in (1, 2, 3):
            copy(d).wait_recv()
        return (held[0].astype(F32) + held[1].astype(F32)) + (
            held[2].astype(F32) + held[3].astype(F32)
        )

    def sent():
        for d in (1, 2, 3):
            copy(d).wait_send()

    return go, total, sent


def finish_kernel(
    heads,
    mixed,
    grad_mixed,
    w_qkv,
    own,
    smalls,
    result,
    grad_middle,
    branch,
    g_up_bias,
    g_vectors,
    out_sums,
    probs,
    h1,
    g_up,
    g_down,
    hb_out,
    vec_out,
    output,
    input_grad,
    fin_up,
    fin_qkv,
    fin_down,
    fin_out,
    branch_all,
    tall,
    prob_buf,
    grads,
    sum_k,
    sum_v,
    give,
    over,
    sums,
    back_r1,
    back_t1,
    back_r3,
    out_r1_x,
    out_t1_x,
    out_r3_x,
    out_kept,
    final_rows,
    final_grad,
    low_grad,
    up_m1,
    up_r1,
    up_t1,
    up_r3,
    up_s1,
    up_r2,
    up_s2,
    up_planes,
    up_landed,
    g_head_0,
    m1_head_0,
    r1_head_0,
    t1_head_0,
    r3_head_0,
    s1_head_0,
    r2_head_0,
    s2_head_0,
    planes_head_0,
    landed_head_0,
    g_head_1,
    m1_head_1,
    r1_head_1,
    t1_head_1,
    r3_head_1,
    s1_head_1,
    r2_head_1,
    s2_head_1,
    planes_head_1,
    landed_head_1,
    qkv_rows,
    w_heads,
    down_r1,
    down_s1,
    down_r2,
    down_l3,
    down_p,
    g_out,
    out_r1,
    out_z,
    out_t,
    head_y,
    head_z,
    head_sib,
    vec_cut,
    vec_1,
    vec_1s,
    vec_2,
    vec_3,
    vectors,
    sent,
    got,
    still,
):
    net = Net(sent, got, still)
    x, y, c, zl, me = net.x, net.y, net.c, net.zl, net.me
    z = 2 * net.zh + zl
    rows, width = own.shape
    sibling = net.device(0, 1)
    wait = net.greet(
        [net.device(dx, dc) for dx in range(4) for dc in range(2) if dx or dc]
        + [net.device(dy=d) for d in (1, 2, 3)]
        + [net.device(dz=d) for d in (1, 2, 3)]
        + [(y * 4 + net.zh * 2 + 1 - c, 2 * x + 1 - zl)]
    )

    tile = 2 * rows
    slots = net.reserve(2)

    def load_probs(j):
        slot = j % 2
        return pltpu.make_async_copy(
            probs.at[j // 4, aligned(j % 4, tile), :], prob_buf.at[slot], still.at[slots + slot]
        )

    load_probs(0).start()
    load_h1 = pltpu.make_async_copy(h1, tall, still.at[net.reserve(1)])
    load_h1.start()
    own_branch = pltpu.make_async_copy(
        branch, branch_all.at[aligned(me, rows)], still.at[net.reserve(1)]
    )
    own_branch.start()
    for block in range(8):
        vectors[:, 160 * block : 160 * block + 160] = smalls[block, :8, :].astype(F32)
    for h in range(2):
        w_heads[h] = w_qkv[:, 240 * h : 240 * h + 240]

    up = column_flow(
        net,
        g_up,
        up_m1,
        up_r1,
        up_t1,
        up_r3,
        up_s1,
        up_r2,
        up_s2,
        up_planes,
        up_landed,
        lambda ref, hb: ref.at[:, pl.ds(pl.multiple_of(hb * 640, 128), 640)],
    )
    head_buffers = (
        (
            g_head_0,
            m1_head_0,
            r1_head_0,
            t1_head_0,
            r3_head_0,
            s1_head_0,
            r2_head_0,
            s2_head_0,
            planes_head_0,
            landed_head_0,
        ),
        (
            g_head_1,
            m1_head_1,
            r1_head_1,
            t1_head_1,
            r3_head_1,
            s1_head_1,
            r2_head_1,
            s2_head_1,
            planes_head_1,
            landed_head_1,
        ),
    )
    flows = [column_flow(net, *held, lambda ref, hb: ref.at[hb]) for held in head_buffers]
    up_share = share_over_y(
        net,
        up_landed,
        fin_up,
        lambda ref: ref.at[:, pl.ds(pl.multiple_of(c * 2560, 128), 2560)],
    )
    three_share = share_over_y(
        net,
        qkv_rows,
        fin_qkv,
        lambda ref: ref.at[:, :, pl.ds(pl.multiple_of(c * 640, 128), 640)],
    )

    d1, d2, d4, d5 = (net.reserve(4) for _ in range(4))
    d3_go, _, d3_sent = four_way(net, d3 := net.reserve(4), down_l3, y, lambda d: net.device(dy=d))
    down_mine = pltpu.make_async_copy(
        g_down.at[aligned(z, 160)], down_r1.at[0], still.at[d1]
    )

    def down_1(d):
        return net.copy(d1 + d, g_down.at[aligned((z + d) % 4, 160)], down_r1.at[d], net.device(dz=d))

    def down_2(d):
        part = down_s1.at[pl.ds(piece_start((y + d) % 4), 48)]
        return net.copy(d2 + d, part, down_r2.at[d], net.device(dy=d))

    def down_4(k, source_z):
        to_z = c + 2 * k
        return pltpu.make_async_remote_copy(
            src_ref=down_p,
            dst_ref=fin_down.at[aligned(source_z, 160)],
            send_sem=sent.at[d4 + k],
            recv_sem=got.at[d4 + source_z],
            device_id=(y * 4 + to_z // 2 * 2 + c, 2 * x + to_z % 2),
            device_id_type=MESH,
        )

    down_local = pltpu.make_async_copy(down_p, fin_down.at[aligned(z, 160)], still.at[d4])

    def down_5(source_z):
        here = fin_down.at[aligned(source_z, 160)]
        return net.copy(d5 + source_z, here, here, sibling)

    e1, e3, e4 = (net.reserve(4) for _ in range(3))
    out_go, out_total, out_sent = four_way(
        net, net.reserve(4), out_z, z, lambda d: net.device(dz=d)
    )

    def out_1(d):
        part = g_out.at[pl.ds(piece_start((y + d) % 4), 48)]
        return net.copy(e1 + d, part, out_r1.at[d], net.device(dy=d))

    def out_3(d):
        return net.copy(e3 + d, out_t, fin_out.at[y], net.device(dy=d))

    out_local = pltpu.make_async_copy(out_t, fin_out.at[y], still.at[e3])

    def out_4(source_y):
        return net.copy(e4 + source_y, fin_out.at[source_y], fin_out.at[source_y], sibling)

    near, pass_on, swap = (net.reserve(4) for _ in range(3))
    branch_halves = net.reserve(2)

    def near_copy(dx):
        return net.copy(near + dx, branch, branch_all.at[aligned(me, rows)], net.device(dx))

    def pass_copy(dx):
        here = branch_all.at[aligned(2 * ((x - dx + 4) % 4) + c, rows)]
        return net.copy(pass_on + dx, here, here, sibling)

    def swap_copy(dx, to_x):
        return net.copy(swap + dx, give.at[to_x], over.at[to_x], sibling)

    half_rows = rows // 2

    def branch_half(i):
        here = branch_all.at[aligned(2 * (2 * ((x + 3 + 2 * i) % 4) + c) + i, half_rows)]
        return net.copy(branch_halves + i, here, here, net.device(1 + 2 * i))

    def in_half(half):
        return pl.ds(half_rows * half, half_rows)

    back_sum = halving(
        net, lambda half, p: sums.at[p, in_half(half)], back_r1, back_t1, back_r3
    )
    out_sum = halving(
        net, lambda half, p: out_sums.at[p, in_half(half)], out_r1_x, out_t1_x, out_r3_x
    )
    out_load = [
        pltpu.make_async_copy(
            out_sums.at[beside(x, 1 - half), in_half(half)],
            out_kept.at[half],
            still.at[net.reserve(1)],
        )
        for half in range(2)
    ]
    for load in out_load:
        load.start()

    wait()
    out_sum[0]()
    for dx in (1, 3):
        near_copy(dx).start()
    up[0]()
    down_mine.start()
    for d in (2, 1, 3):
        down_1(d).start()

    for h in range(2):
        cols = slice(h * HD, (h + 1) * HD)
        sum_k[...] = jnp.zeros_like(sum_k)
        sum_v[...] = jnp.zeros_like(sum_v)

        @pl.loop(0, 4)
        def _(i, h=h, cols=cols):
            j = 4 * h + i

            @pl.when(j < 7)
            def _():
                load_probs(j + 1).start()

            load_probs(j).wait()
            here = aligned(i, tile)
            back = jnp.concatenate([grad_mixed[2 * i, :, cols], grad_mixed[2 * i + 1, :, cols]])
            seen = jnp.concatenate([mixed[2 * i, :, cols], mixed[2 * i + 1, :, cols]])
            low = prob_buf[j % 2]
            row_total = jnp.sum(back.astype(F32) * seen.astype(F32), axis=-1, keepdims=True)
            grad_probs = lax.dot_general(back, heads[4 + h], NT, preferred_element_type=F32)
            grad_scores = (low.astype(F32) * (grad_probs - row_total)).astype(BF16)
            sum_v[...] += lax.dot_general(low, back, TN, preferred_element_type=F32)
            sum_k[...] += lax.dot_general(
                grad_scores, heads[h, here, :], TN, preferred_element_type=F32
            )
            grad_q = jnp.dot(grad_scores, heads[2 + h], preferred_element_type=F32)
            grads[h, here, :80] = (grad_q * HD**-0.5).astype(BF16)

        grads[h, :, 80:160] = (sum_k[...] * HD**-0.5).astype(BF16)
        grads[h, :, 160:] = sum_v[...].astype(BF16)
        if h == 0:
            load_h1.wait()

        @pl.loop(0, 2)
        def _(i, h=h):
            cols = pl.ds(pl.multiple_of(i * 640, 128), 640)
            made = lax.dot_general(tall[:, cols], grads[h], TN, preferred_element_type=F32)
            head_buffers[h][0][pl.ds(4 * i, 4)] = made.astype(BF16).reshape(4, 160, 240)

        if h == 0:
            up[1]()
            for load in out_load:
                load.wait()
            out_sum[1](lambda half: out_kept[half])
        flows[h][0]()
        if h == 1:
            flows[0][1]()
            for i in range(2):
                near_copy(1 + 2 * i).wait_recv()
                branch_half(i).start()
            up[2]()

    def back_rows(block):
        made = [
            lax.dot_general(
                grads[h, aligned(block, rows), :], w_heads[h], NT, preferred_element_type=F32
            )
            for h in range(2)
        ]
        return made[0] + made[1]

    head_y[y] = jnp.zeros((8, 640), F32)
    head_y[y, 0:1, :] = g_up_bias[...]
    for h in range(2):
        cols = slice(h * HD, (h + 1) * HD)
        column_sums = jnp.sum(grads[h].astype(F32), axis=0, keepdims=True)
        head_y[y, 1:2, cols] = column_sums[:, :80]
        head_y[y, 2:3, cols] = column_sums[:, 160:]
    head_y_go, head_y_total, head_y_sent = four_way(
        net, net.reserve(4), head_y, y, lambda d: net.device(dy=d)
    )
    head_y_go()

    @pl.loop(0, 4)
    def _(k):
        dx = jnp.where(k == 3, 0, order(k))
        to_x = (x - dx + 4) % 4
        give[to_x] = back_rows(2 * to_x + 1 - c).astype(BF16)
        swap_copy(dx, to_x).start()

    flows[1][1]()
    up[3]()
    down_mine.wait()
    total = down_r1[0].astype(F32)
    for d in (1, 2, 3):
        down_1(d).wait_recv()
        total = total + down_r1[d].astype(F32)
    down_s1[...] = total.astype(BF16)
    for d in (2, 1, 3):
        down_2(d).start()


    @pl.loop(0, 4)
    def _(k):
        dx = jnp.where(k == 3, 0, order(k))
        to_x = (x - dx + 4) % 4
        kept = back_rows(2 * to_x + c)
        swap_copy(dx, to_x).wait_recv()
        kept = kept + over[to_x].astype(F32)

        @pl.when(dx != 0)
        def _():
            sums[to_x] = kept.astype(BF16)

        @pl.when(dx == 0)
        def _():
            final_grad[...] = kept

    back_sum[0]()
    flows[0][2]()
    own_branch.wait()
    pass_copy(0).start()
    for dx in (1, 3):
        pass_copy(dx).start()
    for i in range(2):
        branch_half(i).wait_recv()
    pass_copy(2).start()

    head_z[z] = head_y_total()
    head_z_go, head_z_total, head_z_sent = four_way(
        net, net.reserve(4), head_z, z, lambda d: net.device(dz=d)
    )
    head_z_go()
    flows[1][2]()
    up[4]()
    total = down_s1[pl.ds(piece_start(y), 48), :].astype(F32)
    for d in (1, 2, 3):
        down_2(d).wait_recv()
        total = total + down_r2[d].astype(F32)
    down_l3[y] = total.astype(BF16)
    d3_go()

    for dx in range(4):
        pass_copy(dx).wait_recv()
        pass_copy(dx).wait_send()
    load_branch = pltpu.make_async_copy(branch_all, tall, still.at[net.reserve(1)])
    load_branch.start()
    load_branch.wait()
    seen = jnp.concatenate([mixed[block] for block in range(8)])
    g_out[...] = lax.dot_general(seen, tall[...], TN, preferred_element_type=F32).astype(BF16)
    for d in (2, 1, 3):
        out_1(d).start()

    back_sum[1](lambda half: sums[beside(x, 1 - half), in_half(half), :])
    for flow in flows:
        flow[3]()
    up[5]()
    for d in (1, 2, 3):
        net.copy(d3 + d, down_l3.at[y], down_l3.at[y], net.device(dy=d)).wait_recv()
    for i in range(3):
        down_p[48 * i : 48 * i + 48, :] = down_l3[i]
    down_p[144:160, :] = down_l3[3, 32:48, :]
    for k in range(2):

        @pl.when(c + 2 * k != z)
        def _():
            down_4(k, z).start()

    @pl.when(c == zl)
    def _():
        down_local.start()

    total = g_out[pl.ds(piece_start(y), 48), :].astype(F32)
    for d in (1, 2, 3):
        out_1(d).wait_recv()
        total = total + out_r1[d].astype(F32)
    out_z[z] = total.astype(BF16)
    out_go()
    for flow in flows:
        flow[4]()
    up_share[0]()
    total = result[...] + jnp.concatenate([out_sum[2](half) for half in range(2)])
    final_rows[...] = total.astype(BF16)
    output_arrived, output_left = net.cross(final_rows, output)

    head_sib[0] = head_z_total()
    head_copy = net.go(head_sib.at[0], head_sib.at[1], sibling)
    grad_first = final_grad[...] + jnp.concatenate([back_sum[2](half) for half in range(2)])
    values = own[...].astype(F32)
    center = values - jnp.mean(values, axis=-1, keepdims=True)
    inverse = lax.rsqrt(jnp.mean(center * center, axis=-1, keepdims=True) + EPS)
    normed = center * inverse
    scaled = grad_first * vectors[4:5, :]
    back = inverse * (
        scaled
        - jnp.mean(scaled, axis=-1, keepdims=True)
        - normed * jnp.mean(scaled * normed, axis=-1, keepdims=True)
    )
    low_grad[...] = (grad_middle[...] + back).astype(BF16)
    grad_arrived, grad_left = net.cross(low_grad, input_grad)
    gain = jnp.sum(grad_first * normed, axis=0, keepdims=True)
    shift = jnp.sum(grad_first, axis=0, keepdims=True)
    for block in range(8):
        cols = slice(160 * block, 160 * block + 160)
        here = vec_cut.at[block // 2, block % 2]
        here[0:4, :] = g_vectors[:, cols]
        here[4:5, :] = gain[:, cols]
        here[5:6, :] = shift[:, cols]
        here[6:8, :] = jnp.zeros((2, 160), F32)
    v1 = net.reserve(8)

    def vec_copy(dx, dc):
        return net.copy(
            v1 + 2 * dx + dc, vec_cut.at[(x + dx) % 4], vec_1.at[me], net.device(dx, dc)
        )

    others = [(dx, dc) for dx in (2, 1, 3, 0) for dc in (1, 0) if dx or dc]
    for dx, dc in others:
        vec_copy(dx, dc).start()
    vec_1[me] = vec_cut[x]

    for flow in flows:
        flow[5]()
    for block in range(8):
        cols = slice(160 * block, 160 * block + 160)
        for k in range(3):
            qkv_rows[k, :, cols] = jnp.concatenate(
                [held[9][block, :, 80 * k : 80 * k + 80] for held in head_buffers], axis=1
            )
    three_share[0]()
    out_t[...] = out_total().astype(BF16)

    @pl.when(c == zl)
    def _():
        out_local.start()
        for d in (2, 1, 3):
            out_3(d).start()

    for dx, dc in others:
        vec_copy(dx, dc).wait_recv()
    total = vec_1[0]
    for block in range(1, 8):
        total = total + vec_1[block]
    vec_1s[...] = total
    v2 = net.reserve(4)

    def vec_z(d):
        return net.copy(v2 + d, vec_1s.at[(z + d) % 2], vec_2.at[z], net.device(dz=d))

    for d in (2, 1, 3):
        vec_z(d).start()
    vec_2[z] = vec_1s[zl]
    @pl.when(c == zl)
    def _():
        down_local.wait()
        down_5(z).start()
        for d in (1, 2, 3):
            source_z = (z + d) % 4
            down_4(0, source_z).wait_recv()
            down_5(source_z).start()

    for d in (1, 2, 3):
        vec_z(d).wait_recv()
    vec_3[y] = (vec_2[0] + vec_2[1]) + (vec_2[2] + vec_2[3])
    vec_y_go, vec_y_total, vec_y_sent = four_way(
        net, net.reserve(4), vec_3, y, lambda d: net.device(dy=d)
    )
    vec_y_go()

    @pl.when(c == zl)
    def _():
        out_local.wait()
        out_4(y).start()
        for d in (1, 2, 3):
            out_3(d).wait_recv()
            out_4((y + 4 - d) % 4).start()


    up_share[1]()
    three_share[1]()
    head_copy.wait_recv()
    hb_out[...] = jnp.where(c == zl, head_sib[0], head_sib[1])
    vec_out[...] = vec_y_total()

    @pl.when(c == zl)
    def _():
        for i in range(4):
            down_5(i).wait_send()
            out_4(i).wait_send()
        for d in (1, 2, 3):
            out_3(d).wait_send()

    @pl.when(c != zl)
    def _():
        for i in range(4):
            down_5(i).wait_recv()
            out_4(i).wait_recv()

    for k in range(2):

        @pl.when(c + 2 * k != z)
        def _():
            down_4(k, z).wait_send()

    up_share[2]()
    three_share[2]()
    grad_arrived()
    grad_left()
    output_arrived()
    output_left()
    for done in (up[6], flows[0][6], flows[1][6], d3_sent, out_sent, head_y_sent, head_z_sent, vec_y_sent):
        done()
    for d in (1, 2, 3):
        down_1(d).wait_send()
        down_2(d).wait_send()
        out_1(d).wait_send()
        vec_z(d).wait_send()
    for d in range(4):
        swap_copy(d, (x - d + 4) % 4).wait_send()
    for i in range(2):
        near_copy(1 + 2 * i).wait_send()
        branch_half(i).wait_send()
    back_sum[3]()
    out_sum[3]()
    for dx, dc in others:
        vec_copy(dx, dc).wait_send()
    net.all_sent()


def finish(
    heads,
    mixed,
    grad_mixed,
    w_qkv,
    own,
    smalls,
    result,
    grad_middle,
    branch,
    out_sums,
    g_up_bias,
    g_vectors,
    probs,
    h1,
    g_up,
    g_down,
):
    rows, width = own.shape

    def shape(*dims, dtype=BF16):
        return jax.ShapeDtypeStruct(dims, dtype)

    def buffer(*dims, dtype=BF16):
        return pltpu.VMEM(dims, dtype)

    def column_buffers(columns):
        return [
            buffer(2, 2, 4, 48, columns),
            buffer(2, 2, 4, 48, columns),
            buffer(2, 4, 48, columns),
            buffer(2, 4, 48, columns),
            buffer(8, 48, columns),
            buffer(4, 2, 48, columns),
            buffer(2, 48, columns),
            buffer(4, 48, columns),
        ]

    return pl.pallas_call(
        finish_kernel,
        in_specs=[VMEM] * 11 + [HBM] * 5,
        out_specs=[VMEM] * 2 + [HBM] * 7,
        out_shape=[
            shape(8, 640, dtype=F32),
            shape(8, 160, dtype=F32),
            shape(rows, width),
            shape(rows, width),
            shape(4, 48, 5120),
            shape(4, 3, 48, width),
            shape(640, width),
            shape(4, 48, width),
            shape(8 * rows, width),
        ],
        scratch_shapes=[
            buffer(8 * rows, width),
            buffer(2, 2 * rows, 8 * rows),
            buffer(2, 8 * rows, 240),
            buffer(8 * rows, HD, dtype=F32),
            buffer(8 * rows, HD, dtype=F32),
            buffer(4, rows, width),
            buffer(4, rows, width),
            buffer(4, rows, width),
            buffer(2, 2, rows // 2, width),
            buffer(2, rows // 2, width),
            buffer(2, rows // 2, width),
            buffer(2, 2, rows // 2, width),
            buffer(2, rows // 2, width),
            buffer(2, rows // 2, width),
            buffer(2, rows // 2, width),
            buffer(rows, width),
            buffer(rows, width, dtype=F32),
            buffer(rows, width),
        ]
        + column_buffers(640)
        + [buffer(48, 5120)]
        + ([buffer(8, 160, 240)] + column_buffers(240) + [buffer(8, 48, 240)]) * 2
        + [
            buffer(3, 48, width),
            buffer(2, width, 240),
            buffer(4, 160, width),
            buffer(160, width),
            buffer(4, 48, width),
            buffer(4, 48, width),
            buffer(160, width),
            buffer(160, width),
            buffer(4, 48, width),
            buffer(4, 48, width),
            buffer(48, width),
            buffer(4, 8, 640, dtype=F32),
            buffer(4, 8, 640, dtype=F32),
            buffer(2, 8, 640, dtype=F32),
            buffer(4, 2, 8, 160, dtype=F32),
            buffer(8, 2, 8, 160, dtype=F32),
            buffer(2, 8, 160, dtype=F32),
            buffer(4, 8, 160, dtype=F32),
            buffer(4, 8, 160, dtype=F32),
            buffer(8, width, dtype=F32),
        ]
        + scratch_for(192),
        compiler_params=pltpu.CompilerParams(
            collective_id=2, has_side_effects=True, vmem_limit_bytes=62 << 20
        ),
    )(
        heads,
        mixed,
        grad_mixed,
        w_qkv,
        own,
        smalls,
        result,
        grad_middle,
        branch,
        g_up_bias,
        g_vectors,
        out_sums,
        probs,
        h1,
        g_up,
        g_down,
    )


def widen_kernel(hb, vec, up, three, down, out, rows, grad, *results):
    o_up, o_q, o_k, o_v, o_down, o_out, o_rows, o_grad = results[:8]
    small, scratch = results[8:17], results[17:]
    b_up, b_three, b_down, b_out, b_rows, b_grad, f_up, f_three, f_down, f_out, f_grad, came, done = scratch
    loads, copies = [], []
    sources = ((up, b_up), (three, b_three), (down, b_down), (out, b_out), (grad, b_grad), (rows, b_rows))
    for source, target in sources:
        loads.append(pltpu.make_async_copy(source, target, came.at[len(loads)]))
        loads[-1].start()

    def push(source, target):
        copy = pltpu.make_async_copy(source, target, done.at[len(copies)])
        copy.start()
        copies.append(copy)

    pieces = ((slice(0, 48), 0, slice(0, 48)), (slice(48, 96), 1, slice(0, 48)))
    pieces += ((slice(96, 144), 2, slice(0, 48)), (slice(144, 160), 3, slice(32, 48)))
    loads[0].wait()
    for here, i, there in pieces:
        f_up[here, :] = b_up[i, there, :].astype(F32)
    push(f_up, o_up)
    loads[1].wait()
    for k, target in enumerate((o_q, o_k, o_v)):
        for here, i, there in pieces:
            f_three[k, here, :] = b_three[i, k, there, :].astype(F32)
        push(f_three.at[k], target)
    loads[2].wait()
    f_down[...] = b_down[...].astype(F32)
    push(f_down, o_down)
    loads[3].wait()
    for here, i, there in pieces:
        f_out[here, :] = b_out[i, there, :].astype(F32)
    push(f_out, o_out)
    loads[4].wait()
    f_grad[...] = b_grad[...].astype(F32)
    push(f_grad, o_grad)
    loads[5].wait()
    push(b_rows, o_rows)
    for target, row in zip(small, (hb[1, :160], hb[2, :160], hb[0, :])):
        target[...] = row
    for k in range(6):
        small[3 + k][...] = vec[k, :]
    for copy in copies:
        copy.wait()


def widen(hb, vec, up, three, down, out, rows, grad):
    width = down.shape[1]

    def shape(*dims):
        return jax.ShapeDtypeStruct(dims, F32)

    sizes = [160, 160, 640] + [160] * 6
    arrays = (up, three, down, out, rows, grad)
    return pl.pallas_call(
        widen_kernel,
        in_specs=[VMEM] * 2 + [HBM] * 6,
        out_specs=[HBM] * 8 + [VMEM] * 9,
        out_shape=[shape(160, 5120)]
        + [shape(160, width)] * 3
        + [shape(640, width), shape(160, width)]
        + [jax.ShapeDtypeStruct(rows.shape, BF16), shape(*grad.shape)]
        + [shape(size) for size in sizes],
        scratch_shapes=[pltpu.VMEM(array.shape, BF16) for array in arrays]
        + [
            pltpu.VMEM((160, 5120), F32),
            pltpu.VMEM((3, 160, width), F32),
            pltpu.VMEM((640, width), F32),
            pltpu.VMEM((160, width), F32),
            pltpu.VMEM(grad.shape, F32),
            pltpu.SemaphoreType.DMA((6,)),
            pltpu.SemaphoreType.DMA((8,)),
        ],
        compiler_params=pltpu.CompilerParams(vmem_limit_bytes=60 << 20),
    )(hb, vec, up, three, down, out, rows, grad)


def per_device(
    tokens,
    lengths,
    w_query,
    w_key,
    w_value,
    w_out,
    w_up,
    w_down,
    b_query,
    b_value,
    b_out,
    b_up,
    b_down,
    gain_attn,
    shift_attn,
    gain_ffn,
    shift_ffn,
    cotangent,
):
    rows, width = tokens.shape[1:]

    eight = [b_query, b_value, b_out, b_down, gain_attn, shift_attn, gain_ffn, shift_ffn]
    row = lax.broadcasted_iota(jnp.int32, (16, 160), 0)
    small = jnp.zeros((16, 160), BF16)
    for index, vector in enumerate(eight):
        small = jnp.where(row == index, vector[None, :], small)
    up_bias = jnp.broadcast_to(b_up[None, :], (16, 640))
    known = jnp.full((8, 128), lengths[0], F32)
    (
        h1,
        heads,
        probs,
        mixed,
        attended,
        w_qkv,
        smalls,
        up_bias,
        own,
        clip,
        out_full,
        up_mine,
        down_mine,
        top,
        _,
    ) = begin(
        tokens[0],
        w_query,
        w_key,
        w_value,
        small,
        up_bias,
        w_out,
        w_up,
        w_down,
        cotangent[0],
        known,
    )
    w_qkv = w_qkv.reshape(width, 480)
    (
        result,
        grad_middle,
        branch,
        out_sums,
        g_up,
        g_down,
        g_up_bias,
        g_vectors,
        grad_mixed,
    ) = middle_part(
        attended,
        own,
        smalls,
        up_bias,
        clip,
        out_full.reshape(width, width),
        up_mine.reshape(width, 640),
        down_mine,
        top.reshape(8 * rows, width),
    )
    hb_out, vec_out, output, input_grad, fin_up, fin_qkv, fin_down, fin_out, _ = finish(
        heads,
        mixed,
        grad_mixed,
        w_qkv,
        own,
        smalls,
        result,
        grad_middle,
        branch,
        out_sums,
        g_up_bias,
        g_vectors,
        probs,
        h1.reshape(8 * rows, width),
        g_up.reshape(8, 160, 640),
        g_down,
    )

    g_up, g_q, g_k, g_v, g_down, g_out, output, input_grad, *small = widen(
        hb_out, vec_out, fin_up, fin_qkv, fin_down, fin_out, output, input_grad
    )
    b_q, b_v, b_u, b_o, b_d, gain_two, shift_two, gain_one, shift_one = small
    return (
        output[None],
        input_grad[None],
        g_q,
        g_k,
        g_v,
        g_out,
        g_up,
        g_down,
        b_q,
        b_v,
        b_o,
        b_u,
        b_d,
        gain_one,
        shift_one,
        gain_two,
        shift_two,
    )


def solution(mesh):
    by_clip, matrix, vector = P("rep", "shard", None), P("shard", None), P("shard")
    return jax.shard_map(
        per_device,
        mesh=mesh,
        in_specs=(by_clip, P("rep")) + (matrix,) * 6 + (vector,) * 9 + (by_clip,),
        out_specs=(by_clip, by_clip) + (matrix,) * 6 + (vector,) * 9,
        check_vma=False,
    )
```

```python
import jax
import jax.numpy as jnp
from jax import lax
from jax.experimental import pallas as pl
from jax.experimental.pallas import tpu as pltpu
from jax.sharding import PartitionSpec as P

HD = 80
EPS = 1e-05
F32 = jnp.float32
BF16 = jnp.bfloat16
NT = (((1,), (1,)), ((), ()))
TN = (((0,), (0,)), ((), ()))


MESH = pl.DeviceIdType.MESH
VMEM = pl.BlockSpec(memory_space=pltpu.VMEM)
HBM = pl.BlockSpec(memory_space=pl.ANY)


class Net:
    def __init__(self, sent, got, still):
        rep, shard = lax.axis_index("rep"), lax.axis_index("shard")
        self.y, self.zh, self.c = rep // 4, rep // 2 % 2, rep % 2
        self.x, self.zl = shard // 2, shard % 2
        self.me, self.shard = 2 * self.x + self.c, shard
        self.sent, self.got, self.still, self.used, self.started = sent, got, still, 0, []

    def device(self, dx=0, dc=0, dz=0, dy=0):
        z = (2 * self.zh + self.zl + dz) % 4
        return (
            (self.y + dy) % 4 * 4 + z // 2 * 2 + (self.c + dc) % 2,
            (self.x + dx) % 4 * 2 + z % 2,
        )

    def in_pair(self, dx, dz):
        return (
            self.y * 4 + self.zh * 2 + self.c,
            (self.x + dx) % 4 * 2 + (self.zl + dz) % 2,
        )

    def partner(self):
        return (self.y * 4 + self.zh * 2 + self.zl, 2 * self.x + self.c)

    def greet(self, devices):
        barrier = pltpu.get_barrier_semaphore()
        for device in devices:
            pl.semaphore_signal(barrier, inc=1, device_id=device, device_id_type=MESH)
        return lambda: pl.semaphore_wait(barrier, len(devices))

    def reserve(self, count):
        first = self.used
        self.used += count
        return first

    def copy(self, index, source, target, device):
        return pltpu.make_async_remote_copy(
            src_ref=source,
            dst_ref=target,
            send_sem=self.sent.at[index],
            recv_sem=self.got.at[index],
            device_id=device,
            device_id_type=MESH,
        )

    def go(self, source, target, device):
        copy = self.copy(self.reserve(1), source, target, device)
        copy.start()
        self.started.append(copy)
        return copy

    def cross(self, source, target):
        index = self.reserve(1)
        copy = self.copy(index, source, target, self.partner())
        local = pltpu.make_async_copy(source, target, self.still.at[index])

        @pl.when(self.c != self.zl)
        def _():
            copy.start()

        @pl.when(self.c == self.zl)
        def _():
            local.start()

        def arrived():
            @pl.when(self.c != self.zl)
            def _():
                copy.wait_recv()

            @pl.when(self.c == self.zl)
            def _():
                local.wait()

        def left():
            @pl.when(self.c != self.zl)
            def _():
                copy.wait_send()

        return arrived, left

    def all_sent(self):
        for copy in self.started:
            copy.wait_send()


def order(k):
    return 1 + 2 * k - 3 * (k // 2)


def aligned(index, size):
    return pl.ds(pl.multiple_of(index * size, size), size)


def scratch_for(copies):
    return [pltpu.SemaphoreType.DMA((copies,)) for _ in range(3)]


def begin_kernel(
    tokens,
    w_query,
    w_key,
    w_value,
    small,
    up_bias,
    w_out,
    w_up,
    w_down,
    cotangent,
    length,
    h1,
    heads,
    probs,
    mixed,
    attended,
    w_qkv,
    smalls,
    bias_up,
    own,
    clip,
    out_full,
    up_mine,
    down_mine,
    top,
    out_own,
    normed_rows,
    head_rows,
    prob_buf,
    gathered,
    cut,
    lens,
    vectors,
    sent,
    got,
    still,
):
    net = Net(sent, got, still)
    x, y, c, zh, zl, me, shard = net.x, net.y, net.c, net.zh, net.zl, net.me, net.shard
    rows, width = tokens.shape
    plane = [net.device(dx, dc) for dx in range(4) for dc in range(2) if dx or dc]
    across = [net.in_pair(dx, 1) for dx in range(4)]
    rings = [net.device(dy=d) for d in (1, 2, 3)] + [net.device(dz=d) for d in (1, 2, 3)]
    wait = net.greet(plane + across + rings + [(y * 4 + zh * 2 + 1 - c, 2 * x + 1 - zl)])
    for block in range(8):
        cols = slice(160 * block, 160 * block + 160)
        for half in range(2):
            part = slice(80 * half, 80 * half + 80)
            for k, weight in enumerate((w_query, w_key, w_value)):
                piece = weight[part, cols]
                for h in range(2):
                    first = 240 * h + 80 * k
                    cut[block, half, :, first : first + 80] = piece[:, 80 * h : 80 * h + 80]
    wait()

    token_arrived, token_left = net.cross(tokens, gathered.at[2 * x + zl])
    base = net.reserve(4)

    def token_send(k, source):
        dx = order(k)
        return net.copy(base + dx, source, gathered.at[me], net.device(dx))

    cut_near, cut_ring, up_near, up_ring = (net.reserve(4) for _ in range(4))

    def cut_copy(d):
        source = cut.at[2 * ((x + d) % 4) + c, zh]
        return net.copy(cut_near + d, source, w_qkv.at[x, zl, zh], net.device(d))

    def cut_share(d):
        here = w_qkv.at[:, zl, zh]
        return net.copy(cut_ring + d, here, here, net.device(dz=d))

    cut_half = net.reserve(2)

    def cut_on(i):
        from_z = (2 * zh + zl + 3 + 2 * i) % 4
        here = w_qkv.at[pl.ds(2 * i, 2), from_z % 2, from_z // 2]
        return net.copy(cut_half + i, here, here, net.device(dz=1 + 2 * i))

    def up_part(index):
        cols = pl.ds(pl.multiple_of(index * 640, 128), 640)
        return w_up.at[aligned(zh, 80), cols]

    def up_copy(d):
        source = up_part(2 * ((x + d) % 4) + c)
        return net.copy(up_near + d, source, up_mine.at[x, zl, zh], net.device(d))

    def up_share(d):
        here = up_mine.at[:, zl, zh]
        return net.copy(up_ring + d, here, here, net.device(dz=d))

    up_local = pltpu.make_async_copy(up_part(me), up_mine.at[x, zl, zh], still.at[up_near])

    for d in (2, 1, 3):
        cut_copy(d).start()

    @pl.when(c == zl)
    def _():
        for k in range(2):
            token_send(k, tokens).start()

    @pl.when(c == 0)
    def _():
        lens[0] = length[...]

    @pl.when(c == 1)
    def _():
        lens[1] = length[...]

    lens_copy = net.go(length, lens.at[c], net.device(0, 1))
    arriving = []
    for dx in (0, 1, 3, 2):
        for dz in range(2):
            if dx or dz:
                arriving.append(net.go(small, smalls.at[shard], net.in_pair(dx, dz)))
    smalls[shard] = small[...]
    w_qkv[x, zl, zh] = cut[me, zh]
    token_arrived()

    @pl.when(c != zl)
    def _():
        for k in range(2):
            token_send(k, gathered.at[me]).start()

    sibling = net.device(0, 1)
    own_over = net.go(gathered.at[me], gathered.at[me], sibling)
    for d in (1, 3, 2):
        cut_copy(d).wait_recv()
    for d in (1, 3):
        cut_share(d).start()
    up_local.start()
    for d in (2, 1, 3):
        up_copy(d).start()
    own[...] = gathered[me]
    for copy in arriving:
        copy.wait_recv()
    for block in range(8):
        vectors[:, 160 * block : 160 * block + 160] = smalls[block, :8, :].astype(F32)
    gain, shift = vectors[4:5, :], vectors[5:6, :]
    bias_q = smalls[me, 0:1, :].astype(F32)
    bias_v = smalls[me, 1:2, :].astype(F32)

    def project(slot):
        values = gathered[slot].astype(F32)
        center = values - jnp.mean(values, axis=-1, keepdims=True)
        inverse = lax.rsqrt(jnp.mean(center * center, axis=-1, keepdims=True) + EPS)
        normed = (center * inverse * gain + shift).astype(BF16)
        normed_rows[slot] = normed
        made = jnp.dot(normed, w_qkv[...].reshape(width, 480), preferred_element_type=F32)
        here = aligned(slot, rows)
        for h in range(2):
            cols = slice(h * HD, (h + 1) * HD)
            q, k, v = (made[:, 240 * h + 80 * j : 240 * h + 80 * j + 80] for j in range(3))
            head_rows[h, here, :] = (q + bias_q[:, cols]).astype(BF16)
            head_rows[2 + h, here, :] = k.astype(BF16)
            head_rows[4 + h, here, :] = (v + bias_v[:, cols]).astype(BF16)

    for i in range(2):
        cut_share(1 + 2 * i).wait_recv()
        cut_on(i).start()
    bias_arrived, bias_left = net.cross(up_bias, bias_up)
    top_arrived, top_left = net.cross(cotangent, top.at[2 * x + zl])
    out_arrived, out_left = net.cross(w_out, out_own)

    down_index, down_ring = net.reserve(1), net.reserve(4)
    down_cross = net.copy(
        down_index, w_down.at[aligned(y, 160)], down_mine.at[aligned(y, 160)], net.partner()
    )
    down_local = pltpu.make_async_copy(w_down, down_mine, still.at[down_index])

    def down_share(d):
        here = down_mine.at[aligned(y, 160)]
        return net.copy(down_ring + d, here, here, net.device(dy=d))

    @pl.when(c == zl)
    def _():
        down_local.start()

    @pl.when(c != zl)
    def _():
        down_cross.start()

    top_near, top_over, out_near, out_ring, out_over = (net.reserve(4) for _ in range(5))

    def top_copy(d):
        return net.copy(top_near + d, top.at[me], top.at[me], net.device(d))

    top_halves = net.reserve(2)

    def top_half(i):
        slot = 2 * ((x + 3 + 2 * i) % 4) + c
        here = top.at[slot, pl.ds(i * rows // 2, rows // 2), :]
        return net.copy(top_halves + i, here, here, net.device(1 + 2 * i))

    def top_pass(d):
        here = top.at[2 * ((x - d + 4) % 4) + c]
        return net.copy(top_over + d, here, here, sibling)

    half = pl.ds(pl.multiple_of(y % 2 * 640, 128), 640)
    out_piece = out_own.at[aligned(y // 2, 80), half]

    def out_copy(d):
        return net.copy(out_near + d, out_piece, out_full.at[x, c, y // 2, :, half], net.device(d))

    def out_share(d):
        here = out_full.at[:, c, y // 2, :, half]
        return net.copy(out_ring + d, here, here, net.device(dy=d))

    def out_pass(d):
        from_y = (y - d + 4) % 4
        cols = pl.ds(pl.multiple_of(from_y % 2 * 640, 128), 640)
        here = out_full.at[:, c, from_y // 2, :, cols]
        return net.copy(out_over + d, here, here, sibling)

    out_local = pltpu.make_async_copy(
        out_piece, out_full.at[x, c, y // 2, :, half], still.at[out_near]
    )
    for i in range(2):
        cut_on(i).wait_recv()
    project(me)
    own_over.wait_recv()
    project(2 * x + 1 - c)
    out_arrived()
    out_local.start()
    for d in (2, 1, 3):
        out_copy(d).start()

    @pl.when(c != zl)
    def _():
        down_cross.wait_recv()
        for d in (2, 1, 3):
            down_share(d).start()

    over, halves = net.reserve(4), net.reserve(2)

    def token_half(i):
        slot = 2 * ((x + 3 + 2 * i) % 4) + c
        here = gathered.at[slot, pl.ds(i * rows // 2, rows // 2), :]
        return net.copy(halves + i, here, here, net.device(1 + 2 * i))

    def passed(dx, slot):
        return net.copy(over + dx, gathered.at[slot], gathered.at[slot], sibling)

    @pl.loop(0, 3)
    def _(k):
        dx = order(k)
        from_x = (x - dx + 4) % 4

        @pl.when(k == 0)
        def _():
            for i in range(2):
                token_send(i, gathered.at[me]).wait_recv()
                token_half(i).start()

        @pl.when(k == 1)
        def _():
            top_arrived()
            for i in range(2):
                top_copy(1 + 2 * i).start()

        @pl.when(k == 2)
        def _():
            for i in range(2):
                token_half(i).wait_recv()
            out_local.wait()
            for d in (1, 3, 2):
                out_copy(d).wait_recv()
            for d in (2, 1, 3):
                out_share(d).start()
            out_pass(0).start()
            up_local.wait()
            for d in (1, 3, 2):
                up_copy(d).wait_recv()
            for d in (2, 1, 3):
                up_share(d).start()

        passed(dx, 2 * from_x + c).start()
        project(2 * from_x + c)
        passed(dx, 2 * from_x + c).wait_recv()
        project(2 * from_x + 1 - c)

    top_pass(0).start()

    keep_h1 = pltpu.make_async_copy(normed_rows, h1, still.at[net.reserve(1)])
    keep_h1.start()
    keep_heads = pltpu.make_async_copy(head_rows, heads, still.at[net.reserve(1)])
    keep_heads.start()
    lens_copy.wait_recv()
    clip[...] = lens[zl]
    clip_length = clip[0:1, 0:1]
    position = lax.broadcasted_iota(jnp.int32, (1, 8 * rows), 1).astype(F32)
    mask = jnp.where(position < clip_length, 0.0, -1e30)

    def attend_rows(to_x, slot):
        here = aligned(to_x, 2 * rows)
        for h in range(2):
            cols = slice(h * HD, (h + 1) * HD)
            scores = lax.dot_general(
                head_rows[h, here, :], head_rows[2 + h], NT, preferred_element_type=F32
            )
            scores = scores * HD**-0.5 + mask
            risen = jnp.exp(scores - jnp.max(scores, axis=-1, keepdims=True))
            share = 1.0 / jnp.sum(risen, axis=-1, keepdims=True)
            low = (risen * share).astype(BF16)
            prob_buf[slot, h] = low
            made = jnp.dot(low, head_rows[4 + h], preferred_element_type=F32).astype(BF16)
            mixed[2 * to_x, :, cols] = made[:rows]
            mixed[2 * to_x + 1, :, cols] = made[rows:]

    prob_index = net.reserve(2)

    def keep_probs(to_x, slot):
        return pltpu.make_async_copy(
            prob_buf.at[slot], probs.at[:, aligned(to_x, 2 * rows), :], still.at[prob_index + slot]
        )

    mixed_base = net.reserve(8)

    def mixed_send(dx, dc):
        slot = 2 * ((x + dx) % 4) + (c + dc) % 2
        return net.copy(
            mixed_base + 2 * dx + dc, mixed.at[slot], attended.at[me], net.device(dx, dc)
        )

    @pl.loop(1, 5)
    def _(step):
        dx = step % 4
        to_x = (x + dx) % 4

        @pl.when(step == 2)
        def _():
            for i in range(2):
                top_copy(1 + 2 * i).wait_recv()
                top_half(i).start()
                top_pass(1 + 2 * i).start()

        @pl.when(step > 2)
        def _():
            keep_probs(to_x, step % 2).wait()

        attend_rows(to_x, step % 2)
        keep_probs(to_x, step % 2).start()
        mixed_send(dx, 1).start()

        @pl.when(dx != 0)
        def _():
            mixed_send(dx, 0).start()

    attended[me] = mixed[me]
    for i in range(2):
        top_half(i).wait_recv()
    top_pass(2).start()
    for d in (1, 3, 2):
        out_share(d).wait_recv()
        out_pass(d).start()
    for dx in range(4):
        for dc in range(2):
            if dx or dc:
                mixed_send(dx, dc).wait()
    for d in range(4):
        top_pass(d).wait()
        out_pass(d).wait()
    for d in (1, 2, 3):
        up_share(d).wait()
        for copy in (cut_copy, up_copy, out_copy, out_share):
            copy(d).wait_send()
    for i in range(2):
        for copy in (cut_share, top_copy):
            copy(1 + 2 * i).wait_send()
        cut_on(i).wait_send()
        top_half(i).wait_send()

    @pl.when(c == zl)
    def _():
        down_local.wait()

    @pl.when(c != zl)
    def _():
        down_cross.wait_send()
        for d in (1, 2, 3):
            down_share(d).wait()

    keep_h1.wait()
    keep_heads.wait()
    for slot in range(2):
        keep_probs(slot, slot).wait()
    bias_arrived()
    for left in (token_left, out_left, top_left, bias_left):
        left()
    for k in range(2):
        token_send(k, gathered.at[me]).wait_send()
        token_half(k).wait_send()
    for k in range(3):
        passed(order(k), me).wait_send()
    net.all_sent()


def begin(tokens, w_query, w_key, w_value, small, up_bias, w_out, w_up, w_down, cotangent, length):
    rows, width = tokens.shape

    def shape(*dims):
        return jax.ShapeDtypeStruct(dims, BF16)

    return pl.pallas_call(
        begin_kernel,
        in_specs=[VMEM] * 11,
        out_specs=[HBM] * 3 + [VMEM] * 7 + [HBM] * 4 + [VMEM],
        out_shape=[
            shape(8, rows, width),
            shape(6, 8 * rows, HD),
            shape(2, 8 * rows, 8 * rows),
            shape(8, rows, 160),
            shape(8, rows, 160),
            shape(4, 2, 2, 80, 480),
            shape(8, 16, 160),
            shape(16, 640),
            shape(rows, width),
            jax.ShapeDtypeStruct((8, 128), F32),
            shape(4, 2, 2, 80, width),
            shape(4, 2, 2, 80, 640),
            shape(640, width),
            shape(8, rows, width),
            shape(160, width),
        ],
        scratch_shapes=[
            pltpu.VMEM((8, rows, width), BF16),
            pltpu.VMEM((6, 8 * rows, HD), BF16),
            pltpu.VMEM((2, 2, 2 * rows, 8 * rows), BF16),
            pltpu.VMEM((8, rows, width), BF16),
            pltpu.VMEM((8, 2, 80, 480), BF16),
            pltpu.VMEM((2, 8, 128), F32),
            pltpu.VMEM((8, width), F32),
        ]
        + scratch_for(96),
        compiler_params=pltpu.CompilerParams(
            collective_id=0, has_side_effects=True, vmem_limit_bytes=58 << 20
        ),
    )(tokens, w_query, w_key, w_value, small, up_bias, w_out, w_up, w_down, cotangent, length)


def middle_kernel(
    attended,
    own,
    smalls,
    up_bias,
    clip,
    out_full,
    up_mine,
    down_mine,
    top,
    result,
    grad_middle,
    branch,
    out_sums,
    g_up,
    g_down,
    g_up_bias,
    g_vectors,
    grad_mixed,
    vectors,
    middle,
    second,
    masked,
    active,
    hidden,
    parts,
    over,
    sums,
    arrived,
    out_parts,
    out_over,
    joined,
    by_head,
    sent,
    got,
    still,
):
    net = Net(sent, got, still)
    x, c, me = net.x, net.c, net.me
    rows, width = own.shape
    wait = net.greet([net.device(dx, dc) for dx in range(4) for dc in range(2) if dx or dc])
    for block in range(8):
        vectors[:, 160 * block : 160 * block + 160] = smalls[block, :8, :].astype(F32)
    bias_up = up_bias[0:1, :].astype(F32)
    mine = aligned(me, rows)
    for block in range(8):
        joined[:, 160 * block : 160 * block + 160] = attended[block]
    made = jnp.dot(joined[...], out_full[...], preferred_element_type=F32)
    middle[...] = own[...].astype(F32) + made + vectors[2:3, :]

    def normalised():
        values = middle[...]
        center = values - jnp.mean(values, axis=-1, keepdims=True)
        inverse = lax.rsqrt(jnp.mean(center * center, axis=-1, keepdims=True) + EPS)
        return center * inverse, inverse

    second[mine, :] = (normalised()[0] * vectors[6:7, :] + vectors[7:8, :]).astype(BF16)
    wait()

    near, pass_on, swap, add, out_swap = (net.reserve(4) for _ in range(5))

    def out_copy(dx, to_x):
        source = out_parts.at[aligned(2 * to_x + 1 - c, rows)]
        return net.copy(out_swap + dx, source, out_over.at[to_x], net.device(0, 1))

    def near_copy(dx):
        return net.copy(near + dx, second.at[mine], second.at[mine], net.device(dx))

    def pass_copy(dx, slot):
        here = second.at[aligned(slot, rows)]
        return net.copy(pass_on + dx, here, here, net.device(0, 1))

    def swap_copy(dx, to_x):
        source = parts.at[aligned(2 * to_x + 1 - c, rows)]
        return net.copy(swap + dx, source, over.at[to_x], net.device(0, 1))

    def add_copy(dx, to_x):
        return net.copy(add + dx, sums.at[to_x], arrived.at[dx], net.device(4 - dx))

    halves = net.reserve(2)

    def half_copy(i):
        slot = 2 * ((x + 3 + 2 * i) % 4) + c
        here = second.at[aligned(2 * slot + i, rows // 2)]
        return net.copy(halves + i, here, here, net.device(1 + 2 * i))

    for dx in (1, 3):
        near_copy(dx).start()

    @pl.loop(0, 4)
    def _(k):
        dx = k ^ (k >> 1)
        to_x = (x - dx + 4) % 4

        @pl.when(k == 1)
        def _():
            for i in range(2):
                near_copy(1 + 2 * i).wait_recv()
                half_copy(i).start()

        @pl.when(k == 3)
        def _():
            for i in range(2):
                half_copy(i).wait_recv()

        pass_copy(dx, 2 * to_x + c).start()
        here = aligned(to_x, 2 * rows)
        position = lax.broadcasted_iota(jnp.int32, (2 * rows, 1), 0) + to_x * 2 * rows
        live = position.astype(F32) < clip[0:1, 0:1]
        low_top = jnp.where(live, top[here, :].astype(F32), 0.0).astype(BF16)
        masked[here, :] = low_top
        grad_act = lax.dot_general(low_top, down_mine[...], NT, preferred_element_type=F32)
        pass_copy(dx, 2 * to_x + c).wait_recv()
        z = jnp.dot(second[here, :], up_mine[...], preferred_element_type=F32) + bias_up
        bell = 0.5 * (1.0 + lax.erf(z * 0.7071067811865476))
        active[here, :] = (z * bell).astype(BF16)
        slope = bell + z * jnp.exp(-0.5 * z * z) * 0.3989422804014327
        grad_z = (grad_act * slope).astype(BF16)
        hidden[here, :] = grad_z
        parts[here, :] = lax.dot_general(
            grad_z, up_mine[...], NT, preferred_element_type=F32
        ).astype(BF16)
        swap_copy(dx, to_x).start()
        out_parts[here, :] = jnp.dot(
            active[here, :], down_mine[...], preferred_element_type=F32
        ).astype(BF16)
        out_copy(dx, to_x).start()
        swap_copy(dx, to_x).wait_recv()

        @pl.when(dx != 0)
        def _():
            kept = parts[aligned(2 * to_x + c, rows), :].astype(F32)
            sums[to_x] = (kept + over[to_x].astype(F32)).astype(BF16)
            add_copy(dx, to_x).start()

    @pl.loop(0, 5)
    def _(i):
        cols = pl.ds(pl.multiple_of(i * 256, 256), 256)
        g_up[cols, :] = lax.dot_general(
            second[:, cols], hidden[...], TN, preferred_element_type=F32
        ).astype(BF16)
        cols = pl.ds(pl.multiple_of(i * 128, 128), 128)
        g_down[cols, :] = lax.dot_general(
            active[:, cols], masked[...], TN, preferred_element_type=F32
        ).astype(BF16)

    for dx in range(4):
        to_x = (x - dx + 4) % 4
        out_copy(dx, to_x).wait_recv()
        kept = out_parts[aligned(2 * to_x + c, rows), :].astype(F32) + out_over[to_x].astype(F32)
        if dx:
            out_sums[to_x] = kept.astype(BF16)
        else:
            result[...] = middle[...] + kept + vectors[3:4, :]
    g_up_bias[...] = jnp.sum(hidden[...].astype(F32), axis=0, keepdims=True)
    grad_second = parts[mine, :].astype(F32) + over[x].astype(F32)
    for dx in (1, 3, 2):
        add_copy(dx, (x - dx + 4) % 4).wait_recv()
        grad_second = grad_second + arrived[dx].astype(F32)
    normed, inverse = normalised()
    scaled = grad_second * vectors[6:7, :]
    back = inverse * (
        scaled
        - jnp.mean(scaled, axis=-1, keepdims=True)
        - normed * jnp.mean(scaled * normed, axis=-1, keepdims=True)
    )
    top_own = masked[mine, :].astype(F32)
    total = top_own + back
    grad_middle[...] = total
    low = total.astype(BF16)
    branch[...] = low
    grad_attended = lax.dot_general(low, out_full[...], NT, preferred_element_type=F32)
    grad_attended = grad_attended.astype(BF16)
    for block in range(8):
        by_head[block] = grad_attended[:, 160 * block : 160 * block + 160]
    mixing = []
    for dx in (2, 1, 3, 0):
        for dc in (1, 0):
            if dx or dc:
                slot = 2 * ((x + dx) % 4) + (c + dc) % 2
                mixing.append(net.go(by_head.at[slot], grad_mixed.at[me], net.device(dx, dc)))
    grad_mixed[me] = by_head[me]
    g_vectors[0:1, :] = jnp.sum(low.astype(F32), axis=0, keepdims=True)
    g_vectors[1:2, :] = jnp.sum(top_own, axis=0, keepdims=True)
    g_vectors[2:3, :] = jnp.sum(grad_second * normed, axis=0, keepdims=True)
    g_vectors[3:4, :] = jnp.sum(grad_second, axis=0, keepdims=True)
    for copy in mixing:
        copy.wait_recv()
    for dx in range(4):
        to_x = (x - dx + 4) % 4
        pass_copy(dx, 2 * to_x + c).wait_send()
        swap_copy(dx, to_x).wait_send()
        out_copy(dx, to_x).wait_send()
        if dx:
            add_copy(dx, to_x).wait_send()
    for i in range(2):
        near_copy(1 + 2 * i).wait_send()
        half_copy(i).wait_send()
    net.all_sent()


def middle_part(attended, own, smalls, up_bias, clip, out_full, up_mine, down_mine, top):
    rows, width = own.shape

    def shape(*dims, dtype=BF16):
        return jax.ShapeDtypeStruct(dims, dtype)

    def buffer(*dims, dtype=BF16):
        return pltpu.VMEM(dims, dtype)

    return pl.pallas_call(
        middle_kernel,
        in_specs=[VMEM] * 9,
        out_specs=[VMEM] * 9,
        out_shape=[
            shape(rows, width, dtype=F32),
            shape(rows, width, dtype=F32),
            shape(rows, width),
            shape(4, rows, width),
            shape(width, 640),
            shape(640, width),
            shape(1, 640, dtype=F32),
            shape(4, width, dtype=F32),
            shape(8, rows, 160),
        ],
        scratch_shapes=[
            buffer(8, width, dtype=F32),
            buffer(rows, width, dtype=F32),
            buffer(8 * rows, width),
            buffer(8 * rows, width),
            buffer(8 * rows, 640),
            buffer(8 * rows, 640),
            buffer(8 * rows, width),
            buffer(4, rows, width),
            buffer(4, rows, width),
            buffer(4, rows, width),
            buffer(8 * rows, width),
            buffer(4, rows, width),
            buffer(rows, width),
            buffer(8, rows, 160),
        ]
        + scratch_for(32),
        compiler_params=pltpu.CompilerParams(
            collective_id=1, has_side_effects=True, vmem_limit_bytes=60 << 20
        ),
    )(attended, own, smalls, up_bias, clip, out_full, up_mine, down_mine, top)


def piece_start(index):
    return pl.multiple_of(48 * index - 32 * (index // 3), 16)


def beside(p, way):
    return p + 1 - 2 * (p % 2) if way == 0 else 3 - p


def halving(net, piece, r1, t1, r3):
    x = net.x
    b1, b2 = net.reserve(4), net.reserve(2)
    both = [(half, slot) for slot in (1, 0) for half in range(2)]

    def copy_1(half, slot):
        near = beside(x, half)
        wanted = near if slot == 0 else beside(near, 1 - half)
        return net.copy(
            b1 + 2 * half + slot, piece(half, wanted), r1.at[half, slot], net.device(near - x + 4)
        )

    def copy_2(half):
        device = net.device(beside(x, 1 - half) - x + 4)
        return net.copy(b2 + half, t1.at[half], r3.at[half], device)

    def first():
        for half, slot in both:
            copy_1(half, slot).start()

    def halfway(kept):
        for half in range(2):
            copy_1(half, 1).wait_recv()
            t1[half] = (kept(half).astype(F32) + r1[half, 1].astype(F32)).astype(BF16)
            copy_2(half).start()

    def total(half):
        copy_1(half, 0).wait_recv()
        copy_2(half).wait_recv()
        return r1[half, 0].astype(F32) + r3[half].astype(F32)

    def sent():
        for half, slot in both:
            copy_1(half, slot).wait_send()
        for half in range(2):
            copy_2(half).wait_send()

    return first, halfway, total, sent


def column_flow(net, source, m1, r1, t1, r3, s1, r2, s2, planes, landed, place_of):
    y, z, x, c = net.y, 2 * net.zh + net.zl, net.x, net.c
    b1, b2, b3, b4, b5 = (net.reserve(4) for _ in range(5))
    b6 = net.reserve(2)
    sibling = net.device(0, 1)

    def piece(half, p):
        return source.at[pl.ds(4 * half, 4), pl.ds(piece_start(p), 48), :]

    def copy_1(half, slot):
        near = beside(y, half)
        wanted = near if slot == 0 else beside(near, 1 - half)
        return net.copy(
            b1 + 2 * half + slot,
            piece(half, wanted),
            r1.at[half, slot],
            net.device(dy=near - y + 4),
        )

    def load(half, slot):
        wanted = y if slot == 0 else beside(y, 1 - half)
        return pltpu.make_async_copy(
            piece(half, wanted), m1.at[half, slot], net.still.at[b1 + 2 * half + slot]
        )

    def copy_6(half):
        device = net.device(dy=beside(y, 1 - half) - y + 4)
        return net.copy(b6 + half, t1.at[half], r3.at[half], device)

    def copy_2(d):
        part = s1.at[pl.ds(2 * ((z + d) % 4), 2)]
        return net.copy(b2 + d, part, r2.at[d], net.device(dz=d))

    def copy_3(d):
        return net.copy(b3 + d, s2.at[(z + d) % 2], planes.at[z], net.device(dz=d))

    def copy_4(d):
        target = place_of(landed, 2 * x + c)
        return net.copy(b4 + d, planes.at[(x + d) % 4], target, net.device(d))

    def copy_5(d):
        here = place_of(landed, 2 * ((x - d + 4) % 4) + c)
        return net.copy(b5 + d, here, here, sibling)

    both = [(half, slot) for half in range(2) for slot in range(2)]

    def first():
        for half, slot in both:
            copy_1(half, slot).start()
        for half, slot in both:
            load(half, slot).start()

    def halfway():
        for half, slot in both:
            load(half, slot).wait()
            copy_1(half, slot).wait_recv()
        for half in range(2):
            t1[half] = (m1[half, 1].astype(F32) + r1[half, 1].astype(F32)).astype(BF16)
            copy_6(half).start()

    def second():
        for half in range(2):
            copy_6(half).wait_recv()
            total = m1[half, 0].astype(F32) + r1[half, 0].astype(F32) + r3[half].astype(F32)
            s1[pl.ds(4 * half, 4)] = total.astype(BF16)
        for d in (2, 1, 3):
            copy_2(d).start()

    def third():
        total = s1[pl.ds(2 * z, 2)].astype(F32)
        for d in (1, 2, 3):
            copy_2(d).wait_recv()
            total = total + r2[d].astype(F32)
        s2[...] = total.astype(BF16)
        for d in (2, 1, 3):
            copy_3(d).start()
        planes[z] = s2[z % 2]

    def fourth():
        for d in (1, 2, 3):
            copy_3(d).wait_recv()
        for d in (2, 1, 3):
            copy_4(d).start()
        place_of(landed, 2 * x + c)[...] = planes[x]
        copy_5(0).start()

    def fifth():
        for d in (1, 3, 2):
            copy_4(d).wait_recv()
            copy_5(d).start()
        for d in range(4):
            copy_5(d).wait_recv()

    def sent():
        for d in range(4):
            copy_5(d).wait_send()
        for d in (1, 2, 3):
            for copy in (copy_2, copy_3, copy_4):
                copy(d).wait_send()
        for half in range(2):
            copy_6(half).wait_send()
        for half, slot in both:
            copy_1(half, slot).wait_send()

    return first, halfway, second, third, fourth, fifth, sent


def share_over_y(net, whole, final, half_of):
    y = net.y
    near, over = net.reserve(4), net.reserve(4)
    own = pltpu.make_async_copy(whole, final.at[y], net.still.at[near])

    def copy(d):
        return net.copy(near + d, half_of(whole), half_of(final.at[y]), net.device(dy=d))

    def forward(d):
        here = half_of(final.at[(y - d + 4) % 4])
        return net.copy(over + d, here, here, net.device(0, 1))

    def first():
        own.start()
        for d in (2, 1, 3):
            copy(d).start()

    def second():
        for d in (1, 3, 2):
            copy(d).wait_recv()
            forward(d).start()

    def third():
        own.wait()
        for d in (1, 2, 3):
            forward(d).wait_recv()
            forward(d).wait_send()
            copy(d).wait_send()

    return first, second, third


def four_way(net, base, held, position, device_of):
    def copy(d):
        return net.copy(base + d, held.at[position], held.at[position], device_of(d))

    def go():
        for d in (2, 1, 3):
            copy(d).start()

    def total():
        for d in (1, 2, 3):
            copy(d).wait_recv()
        return (held[0].astype(F32) + held[1].astype(F32)) + (
            held[2].astype(F32) + held[3].astype(F32)
        )

    def sent():
        for d in (1, 2, 3):
            copy(d).wait_send()

    return go, total, sent


def finish_kernel(
    heads,
    mixed,
    grad_mixed,
    w_qkv,
    own,
    smalls,
    result,
    grad_middle,
    branch,
    g_up_bias,
    g_vectors,
    out_sums,
    probs,
    h1,
    g_up,
    g_down,
    hb_out,
    vec_out,
    output,
    input_grad,
    fin_up,
    fin_qkv,
    fin_down,
    fin_out,
    branch_all,
    tall,
    prob_buf,
    grads,
    sum_k,
    sum_v,
    give,
    over,
    sums,
    back_r1,
    back_t1,
    back_r3,
    out_r1_x,
    out_t1_x,
    out_r3_x,
    out_kept,
    final_rows,
    final_grad,
    low_grad,
    up_m1,
    up_r1,
    up_t1,
    up_r3,
    up_s1,
    up_r2,
    up_s2,
    up_planes,
    up_landed,
    g_head_0,
    m1_head_0,
    r1_head_0,
    t1_head_0,
    r3_head_0,
    s1_head_0,
    r2_head_0,
    s2_head_0,
    planes_head_0,
    landed_head_0,
    g_head_1,
    m1_head_1,
    r1_head_1,
    t1_head_1,
    r3_head_1,
    s1_head_1,
    r2_head_1,
    s2_head_1,
    planes_head_1,
    landed_head_1,
    qkv_rows,
    w_heads,
    down_r1,
    down_s1,
    down_r2,
    down_l3,
    down_p,
    g_out,
    out_r1,
    out_z,
    out_t,
    head_y,
    head_z,
    head_sib,
    vec_cut,
    vec_1,
    vec_1s,
    vec_2,
    vec_3,
    vectors,
    sent,
    got,
    still,
):
    net = Net(sent, got, still)
    x, y, c, zl, me = net.x, net.y, net.c, net.zl, net.me
    z = 2 * net.zh + zl
    rows, width = own.shape
    sibling = net.device(0, 1)
    wait = net.greet(
        [net.device(dx, dc) for dx in range(4) for dc in range(2) if dx or dc]
        + [net.device(dy=d) for d in (1, 2, 3)]
        + [net.device(dz=d) for d in (1, 2, 3)]
        + [(y * 4 + net.zh * 2 + 1 - c, 2 * x + 1 - zl)]
    )

    tile = 2 * rows
    slots = net.reserve(2)

    def load_probs(j):
        slot = j % 2
        return pltpu.make_async_copy(
            probs.at[j // 4, aligned(j % 4, tile), :], prob_buf.at[slot], still.at[slots + slot]
        )

    load_probs(0).start()
    load_h1 = pltpu.make_async_copy(h1, tall, still.at[net.reserve(1)])
    load_h1.start()
    own_branch = pltpu.make_async_copy(
        branch, branch_all.at[aligned(me, rows)], still.at[net.reserve(1)]
    )
    own_branch.start()
    for block in range(8):
        vectors[:, 160 * block : 160 * block + 160] = smalls[block, :8, :].astype(F32)
    for h in range(2):
        w_heads[h] = w_qkv[:, 240 * h : 240 * h + 240]

    up = column_flow(
        net,
        g_up,
        up_m1,
        up_r1,
        up_t1,
        up_r3,
        up_s1,
        up_r2,
        up_s2,
        up_planes,
        up_landed,
        lambda ref, hb: ref.at[:, pl.ds(pl.multiple_of(hb * 640, 128), 640)],
    )
    head_buffers = (
        (
            g_head_0,
            m1_head_0,
            r1_head_0,
            t1_head_0,
            r3_head_0,
            s1_head_0,
            r2_head_0,
            s2_head_0,
            planes_head_0,
            landed_head_0,
        ),
        (
            g_head_1,
            m1_head_1,
            r1_head_1,
            t1_head_1,
            r3_head_1,
            s1_head_1,
            r2_head_1,
            s2_head_1,
            planes_head_1,
            landed_head_1,
        ),
    )
    flows = [column_flow(net, *held, lambda ref, hb: ref.at[hb]) for held in head_buffers]
    up_share = share_over_y(
        net,
        up_landed,
        fin_up,
        lambda ref: ref.at[:, pl.ds(pl.multiple_of(c * 2560, 128), 2560)],
    )
    three_share = share_over_y(
        net,
        qkv_rows,
        fin_qkv,
        lambda ref: ref.at[:, :, pl.ds(pl.multiple_of(c * 640, 128), 640)],
    )

    d1, d2, d4, d5 = (net.reserve(4) for _ in range(4))
    d3_go, _, d3_sent = four_way(net, d3 := net.reserve(4), down_l3, y, lambda d: net.device(dy=d))
    down_mine = pltpu.make_async_copy(
        g_down.at[aligned(z, 160)], down_r1.at[0], still.at[d1]
    )

    def down_1(d):
        return net.copy(d1 + d, g_down.at[aligned((z + d) % 4, 160)], down_r1.at[d], net.device(dz=d))

    def down_2(d):
        part = down_s1.at[pl.ds(piece_start((y + d) % 4), 48)]
        return net.copy(d2 + d, part, down_r2.at[d], net.device(dy=d))

    def down_4(k, source_z):
        to_z = c + 2 * k
        return pltpu.make_async_remote_copy(
            src_ref=down_p,
            dst_ref=fin_down.at[aligned(source_z, 160)],
            send_sem=sent.at[d4 + k],
            recv_sem=got.at[d4 + source_z],
            device_id=(y * 4 + to_z // 2 * 2 + c, 2 * x + to_z % 2),
            device_id_type=MESH,
        )

    down_local = pltpu.make_async_copy(down_p, fin_down.at[aligned(z, 160)], still.at[d4])

    def down_5(source_z):
        here = fin_down.at[aligned(source_z, 160)]
        return net.copy(d5 + source_z, here, here, sibling)

    e1, e3, e4 = (net.reserve(4) for _ in range(3))
    out_go, out_total, out_sent = four_way(
        net, net.reserve(4), out_z, z, lambda d: net.device(dz=d)
    )

    def out_1(d):
        part = g_out.at[pl.ds(piece_start((y + d) % 4), 48)]
        return net.copy(e1 + d, part, out_r1.at[d], net.device(dy=d))

    def out_3(d):
        return net.copy(e3 + d, out_t, fin_out.at[y], net.device(dy=d))

    out_local = pltpu.make_async_copy(out_t, fin_out.at[y], still.at[e3])

    def out_4(source_y):
        return net.copy(e4 + source_y, fin_out.at[source_y], fin_out.at[source_y], sibling)

    near, pass_on, swap = (net.reserve(4) for _ in range(3))
    branch_halves = net.reserve(2)

    def near_copy(dx):
        return net.copy(near + dx, branch, branch_all.at[aligned(me, rows)], net.device(dx))

    def pass_copy(dx):
        here = branch_all.at[aligned(2 * ((x - dx + 4) % 4) + c, rows)]
        return net.copy(pass_on + dx, here, here, sibling)

    def swap_copy(dx, to_x):
        return net.copy(swap + dx, give.at[to_x], over.at[to_x], sibling)

    half_rows = rows // 2

    def branch_half(i):
        here = branch_all.at[aligned(2 * (2 * ((x + 3 + 2 * i) % 4) + c) + i, half_rows)]
        return net.copy(branch_halves + i, here, here, net.device(1 + 2 * i))

    def in_half(half):
        return pl.ds(half_rows * half, half_rows)

    back_sum = halving(
        net, lambda half, p: sums.at[p, in_half(half)], back_r1, back_t1, back_r3
    )
    out_sum = halving(
        net, lambda half, p: out_sums.at[p, in_half(half)], out_r1_x, out_t1_x, out_r3_x
    )
    out_load = [
        pltpu.make_async_copy(
            out_sums.at[beside(x, 1 - half), in_half(half)],
            out_kept.at[half],
            still.at[net.reserve(1)],
        )
        for half in range(2)
    ]
    for load in out_load:
        load.start()

    wait()
    out_sum[0]()
    for dx in (1, 3):
        near_copy(dx).start()
    up[0]()
    down_mine.start()
    for d in (2, 1, 3):
        down_1(d).start()

    for h in range(2):
        cols = slice(h * HD, (h + 1) * HD)
        sum_k[...] = jnp.zeros_like(sum_k)
        sum_v[...] = jnp.zeros_like(sum_v)

        @pl.loop(0, 4)
        def _(i, h=h, cols=cols):
            j = 4 * h + i

            @pl.when(j < 7)
            def _():
                load_probs(j + 1).start()

            load_probs(j).wait()
            here = aligned(i, tile)
            back = jnp.concatenate([grad_mixed[2 * i, :, cols], grad_mixed[2 * i + 1, :, cols]])
            seen = jnp.concatenate([mixed[2 * i, :, cols], mixed[2 * i + 1, :, cols]])
            low = prob_buf[j % 2]
            row_total = jnp.sum(back.astype(F32) * seen.astype(F32), axis=-1, keepdims=True)
            grad_probs = lax.dot_general(back, heads[4 + h], NT, preferred_element_type=F32)
            grad_scores = (low.astype(F32) * (grad_probs - row_total)).astype(BF16)
            sum_v[...] += lax.dot_general(low, back, TN, preferred_element_type=F32)
            sum_k[...] += lax.dot_general(
                grad_scores, heads[h, here, :], TN, preferred_element_type=F32
            )
            grad_q = jnp.dot(grad_scores, heads[2 + h], preferred_element_type=F32)
            grads[h, here, :80] = (grad_q * HD**-0.5).astype(BF16)

        grads[h, :, 80:160] = (sum_k[...] * HD**-0.5).astype(BF16)
        grads[h, :, 160:] = sum_v[...].astype(BF16)
        if h == 0:
            load_h1.wait()

        @pl.loop(0, 2)
        def _(i, h=h):
            cols = pl.ds(pl.multiple_of(i * 640, 128), 640)
            made = lax.dot_general(tall[:, cols], grads[h], TN, preferred_element_type=F32)
            head_buffers[h][0][pl.ds(4 * i, 4)] = made.astype(BF16).reshape(4, 160, 240)

        if h == 0:
            up[1]()
            for load in out_load:
                load.wait()
            out_sum[1](lambda half: out_kept[half])
        flows[h][0]()
        if h == 1:
            flows[0][1]()
            for i in range(2):
                near_copy(1 + 2 * i).wait_recv()
                branch_half(i).start()
            up[2]()

    def back_rows(block):
        made = [
            lax.dot_general(
                grads[h, aligned(block, rows), :], w_heads[h], NT, preferred_element_type=F32
            )
            for h in range(2)
        ]
        return made[0] + made[1]

    head_y[y] = jnp.zeros((8, 640), F32)
    head_y[y, 0:1, :] = g_up_bias[...]
    for h in range(2):
        cols = slice(h * HD, (h + 1) * HD)
        column_sums = jnp.sum(grads[h].astype(F32), axis=0, keepdims=True)
        head_y[y, 1:2, cols] = column_sums[:, :80]
        head_y[y, 2:3, cols] = column_sums[:, 160:]
    head_y_go, head_y_total, head_y_sent = four_way(
        net, net.reserve(4), head_y, y, lambda d: net.device(dy=d)
    )
    head_y_go()

    @pl.loop(0, 4)
    def _(k):
        dx = jnp.where(k == 3, 0, order(k))
        to_x = (x - dx + 4) % 4
        give[to_x] = back_rows(2 * to_x + 1 - c).astype(BF16)
        swap_copy(dx, to_x).start()

    flows[1][1]()
    up[3]()
    down_mine.wait()
    total = down_r1[0].astype(F32)
    for d in (1, 2, 3):
        down_1(d).wait_recv()
        total = total + down_r1[d].astype(F32)
    down_s1[...] = total.astype(BF16)
    for d in (2, 1, 3):
        down_2(d).start()


    @pl.loop(0, 4)
    def _(k):
        dx = jnp.where(k == 3, 0, order(k))
        to_x = (x - dx + 4) % 4
        kept = back_rows(2 * to_x + c)
        swap_copy(dx, to_x).wait_recv()
        kept = kept + over[to_x].astype(F32)

        @pl.when(dx != 0)
        def _():
            sums[to_x] = kept.astype(BF16)

        @pl.when(dx == 0)
        def _():
            final_grad[...] = kept

    back_sum[0]()
    flows[0][2]()
    own_branch.wait()
    pass_copy(0).start()
    for dx in (1, 3):
        pass_copy(dx).start()
    for i in range(2):
        branch_half(i).wait_recv()
    pass_copy(2).start()

    head_z[z] = head_y_total()
    head_z_go, head_z_total, head_z_sent = four_way(
        net, net.reserve(4), head_z, z, lambda d: net.device(dz=d)
    )
    head_z_go()
    flows[1][2]()
    up[4]()
    total = down_s1[pl.ds(piece_start(y), 48), :].astype(F32)
    for d in (1, 2, 3):
        down_2(d).wait_recv()
        total = total + down_r2[d].astype(F32)
    down_l3[y] = total.astype(BF16)
    d3_go()

    for dx in range(4):
        pass_copy(dx).wait_recv()
        pass_copy(dx).wait_send()
    load_branch = pltpu.make_async_copy(branch_all, tall, still.at[net.reserve(1)])
    load_branch.start()
    load_branch.wait()
    seen = jnp.concatenate([mixed[block] for block in range(8)])
    g_out[...] = lax.dot_general(seen, tall[...], TN, preferred_element_type=F32).astype(BF16)
    for d in (2, 1, 3):
        out_1(d).start()

    back_sum[1](lambda half: sums[beside(x, 1 - half), in_half(half), :])
    for flow in flows:
        flow[3]()
    up[5]()
    for d in (1, 2, 3):
        net.copy(d3 + d, down_l3.at[y], down_l3.at[y], net.device(dy=d)).wait_recv()
    for i in range(3):
        down_p[48 * i : 48 * i + 48, :] = down_l3[i]
    down_p[144:160, :] = down_l3[3, 32:48, :]
    for k in range(2):

        @pl.when(c + 2 * k != z)
        def _():
            down_4(k, z).start()

    @pl.when(c == zl)
    def _():
        down_local.start()

    total = g_out[pl.ds(piece_start(y), 48), :].astype(F32)
    for d in (1, 2, 3):
        out_1(d).wait_recv()
        total = total + out_r1[d].astype(F32)
    out_z[z] = total.astype(BF16)
    out_go()
    for flow in flows:
        flow[4]()
    up_share[0]()
    total = result[...] + jnp.concatenate([out_sum[2](half) for half in range(2)])
    final_rows[...] = total.astype(BF16)
    output_arrived, output_left = net.cross(final_rows, output)

    head_sib[0] = head_z_total()
    head_copy = net.go(head_sib.at[0], head_sib.at[1], sibling)
    grad_first = final_grad[...] + jnp.concatenate([back_sum[2](half) for half in range(2)])
    values = own[...].astype(F32)
    center = values - jnp.mean(values, axis=-1, keepdims=True)
    inverse = lax.rsqrt(jnp.mean(center * center, axis=-1, keepdims=True) + EPS)
    normed = center * inverse
    scaled = grad_first * vectors[4:5, :]
    back = inverse * (
        scaled
        - jnp.mean(scaled, axis=-1, keepdims=True)
        - normed * jnp.mean(scaled * normed, axis=-1, keepdims=True)
    )
    low_grad[...] = (grad_middle[...] + back).astype(BF16)
    grad_arrived, grad_left = net.cross(low_grad, input_grad)
    gain = jnp.sum(grad_first * normed, axis=0, keepdims=True)
    shift = jnp.sum(grad_first, axis=0, keepdims=True)
    for block in range(8):
        cols = slice(160 * block, 160 * block + 160)
        here = vec_cut.at[block // 2, block % 2]
        here[0:4, :] = g_vectors[:, cols]
        here[4:5, :] = gain[:, cols]
        here[5:6, :] = shift[:, cols]
        here[6:8, :] = jnp.zeros((2, 160), F32)
    v1 = net.reserve(8)

    def vec_copy(dx, dc):
        return net.copy(
            v1 + 2 * dx + dc, vec_cut.at[(x + dx) % 4], vec_1.at[me], net.device(dx, dc)
        )

    others = [(dx, dc) for dx in (2, 1, 3, 0) for dc in (1, 0) if dx or dc]
    for dx, dc in others:
        vec_copy(dx, dc).start()
    vec_1[me] = vec_cut[x]

    for flow in flows:
        flow[5]()
    for block in range(8):
        cols = slice(160 * block, 160 * block + 160)
        for k in range(3):
            qkv_rows[k, :, cols] = jnp.concatenate(
                [held[9][block, :, 80 * k : 80 * k + 80] for held in head_buffers], axis=1
            )
    three_share[0]()
    out_t[...] = out_total().astype(BF16)

    @pl.when(c == zl)
    def _():
        out_local.start()
        for d in (2, 1, 3):
            out_3(d).start()

    for dx, dc in others:
        vec_copy(dx, dc).wait_recv()
    total = vec_1[0]
    for block in range(1, 8):
        total = total + vec_1[block]
    vec_1s[...] = total
    v2 = net.reserve(4)

    def vec_z(d):
        return net.copy(v2 + d, vec_1s.at[(z + d) % 2], vec_2.at[z], net.device(dz=d))

    for d in (2, 1, 3):
        vec_z(d).start()
    vec_2[z] = vec_1s[zl]
    @pl.when(c == zl)
    def _():
        down_local.wait()
        down_5(z).start()
        for d in (1, 2, 3):
            source_z = (z + d) % 4
            down_4(0, source_z).wait_recv()
            down_5(source_z).start()

    for d in (1, 2, 3):
        vec_z(d).wait_recv()
    vec_3[y] = (vec_2[0] + vec_2[1]) + (vec_2[2] + vec_2[3])
    vec_y_go, vec_y_total, vec_y_sent = four_way(
        net, net.reserve(4), vec_3, y, lambda d: net.device(dy=d)
    )
    vec_y_go()

    @pl.when(c == zl)
    def _():
        out_local.wait()
        out_4(y).start()
        for d in (1, 2, 3):
            out_3(d).wait_recv()
            out_4((y + 4 - d) % 4).start()


    up_share[1]()
    three_share[1]()
    head_copy.wait_recv()
    hb_out[...] = jnp.where(c == zl, head_sib[0], head_sib[1])
    vec_out[...] = vec_y_total()

    @pl.when(c == zl)
    def _():
        for i in range(4):
            down_5(i).wait_send()
            out_4(i).wait_send()
        for d in (1, 2, 3):
            out_3(d).wait_send()

    @pl.when(c != zl)
    def _():
        for i in range(4):
            down_5(i).wait_recv()
            out_4(i).wait_recv()

    for k in range(2):

        @pl.when(c + 2 * k != z)
        def _():
            down_4(k, z).wait_send()

    up_share[2]()
    three_share[2]()
    grad_arrived()
    grad_left()
    output_arrived()
    output_left()
    for done in (up[6], flows[0][6], flows[1][6], d3_sent, out_sent, head_y_sent, head_z_sent, vec_y_sent):
        done()
    for d in (1, 2, 3):
        down_1(d).wait_send()
        down_2(d).wait_send()
        out_1(d).wait_send()
        vec_z(d).wait_send()
    for d in range(4):
        swap_copy(d, (x - d + 4) % 4).wait_send()
    for i in range(2):
        near_copy(1 + 2 * i).wait_send()
        branch_half(i).wait_send()
    back_sum[3]()
    out_sum[3]()
    for dx, dc in others:
        vec_copy(dx, dc).wait_send()
    net.all_sent()


def finish(
    heads,
    mixed,
    grad_mixed,
    w_qkv,
    own,
    smalls,
    result,
    grad_middle,
    branch,
    out_sums,
    g_up_bias,
    g_vectors,
    probs,
    h1,
    g_up,
    g_down,
):
    rows, width = own.shape

    def shape(*dims, dtype=BF16):
        return jax.ShapeDtypeStruct(dims, dtype)

    def buffer(*dims, dtype=BF16):
        return pltpu.VMEM(dims, dtype)

    def column_buffers(columns):
        return [
            buffer(2, 2, 4, 48, columns),
            buffer(2, 2, 4, 48, columns),
            buffer(2, 4, 48, columns),
            buffer(2, 4, 48, columns),
            buffer(8, 48, columns),
            buffer(4, 2, 48, columns),
            buffer(2, 48, columns),
            buffer(4, 48, columns),
        ]

    return pl.pallas_call(
        finish_kernel,
        in_specs=[VMEM] * 11 + [HBM] * 5,
        out_specs=[VMEM] * 2 + [HBM] * 7,
        out_shape=[
            shape(8, 640, dtype=F32),
            shape(8, 160, dtype=F32),
            shape(rows, width),
            shape(rows, width),
            shape(4, 48, 5120),
            shape(4, 3, 48, width),
            shape(640, width),
            shape(4, 48, width),
            shape(8 * rows, width),
        ],
        scratch_shapes=[
            buffer(8 * rows, width),
            buffer(2, 2 * rows, 8 * rows),
            buffer(2, 8 * rows, 240),
            buffer(8 * rows, HD, dtype=F32),
            buffer(8 * rows, HD, dtype=F32),
            buffer(4, rows, width),
            buffer(4, rows, width),
            buffer(4, rows, width),
            buffer(2, 2, rows // 2, width),
            buffer(2, rows // 2, width),
            buffer(2, rows // 2, width),
            buffer(2, 2, rows // 2, width),
            buffer(2, rows // 2, width),
            buffer(2, rows // 2, width),
            buffer(2, rows // 2, width),
            buffer(rows, width),
            buffer(rows, width, dtype=F32),
            buffer(rows, width),
        ]
        + column_buffers(640)
        + [buffer(48, 5120)]
        + ([buffer(8, 160, 240)] + column_buffers(240) + [buffer(8, 48, 240)]) * 2
        + [
            buffer(3, 48, width),
            buffer(2, width, 240),
            buffer(4, 160, width),
            buffer(160, width),
            buffer(4, 48, width),
            buffer(4, 48, width),
            buffer(160, width),
            buffer(160, width),
            buffer(4, 48, width),
            buffer(4, 48, width),
            buffer(48, width),
            buffer(4, 8, 640, dtype=F32),
            buffer(4, 8, 640, dtype=F32),
            buffer(2, 8, 640, dtype=F32),
            buffer(4, 2, 8, 160, dtype=F32),
            buffer(8, 2, 8, 160, dtype=F32),
            buffer(2, 8, 160, dtype=F32),
            buffer(4, 8, 160, dtype=F32),
            buffer(4, 8, 160, dtype=F32),
            buffer(8, width, dtype=F32),
        ]
        + scratch_for(192),
        compiler_params=pltpu.CompilerParams(
            collective_id=2, has_side_effects=True, vmem_limit_bytes=62 << 20
        ),
    )(
        heads,
        mixed,
        grad_mixed,
        w_qkv,
        own,
        smalls,
        result,
        grad_middle,
        branch,
        g_up_bias,
        g_vectors,
        out_sums,
        probs,
        h1,
        g_up,
        g_down,
    )


def widen_kernel(hb, vec, up, three, down, out, rows, grad, *results):
    o_up, o_q, o_k, o_v, o_down, o_out, o_rows, o_grad = results[:8]
    small, scratch = results[8:17], results[17:]
    b_up, b_three, b_down, b_out, b_rows, b_grad, f_up, f_three, f_down, f_out, f_grad, came, done = scratch
    loads, copies = [], []
    sources = ((up, b_up), (three, b_three), (down, b_down), (out, b_out), (grad, b_grad), (rows, b_rows))
    for source, target in sources:
        loads.append(pltpu.make_async_copy(source, target, came.at[len(loads)]))
        loads[-1].start()

    def push(source, target):
        copy = pltpu.make_async_copy(source, target, done.at[len(copies)])
        copy.start()
        copies.append(copy)

    pieces = ((slice(0, 48), 0, slice(0, 48)), (slice(48, 96), 1, slice(0, 48)))
    pieces += ((slice(96, 144), 2, slice(0, 48)), (slice(144, 160), 3, slice(32, 48)))
    loads[0].wait()
    for here, i, there in pieces:
        f_up[here, :] = b_up[i, there, :].astype(F32)
    push(f_up, o_up)
    loads[1].wait()
    for k, target in enumerate((o_q, o_k, o_v)):
        for here, i, there in pieces:
            f_three[k, here, :] = b_three[i, k, there, :].astype(F32)
        push(f_three.at[k], target)
    loads[2].wait()
    f_down[...] = b_down[...].astype(F32)
    push(f_down, o_down)
    loads[3].wait()
    for here, i, there in pieces:
        f_out[here, :] = b_out[i, there, :].astype(F32)
    push(f_out, o_out)
    loads[4].wait()
    f_grad[...] = b_grad[...].astype(F32)
    push(f_grad, o_grad)
    loads[5].wait()
    push(b_rows, o_rows)
    for target, row in zip(small, (hb[1, :160], hb[2, :160], hb[0, :])):
        target[...] = row
    for k in range(6):
        small[3 + k][...] = vec[k, :]
    for copy in copies:
        copy.wait()


def widen(hb, vec, up, three, down, out, rows, grad):
    width = down.shape[1]

    def shape(*dims):
        return jax.ShapeDtypeStruct(dims, F32)

    sizes = [160, 160, 640] + [160] * 6
    arrays = (up, three, down, out, rows, grad)
    return pl.pallas_call(
        widen_kernel,
        in_specs=[VMEM] * 2 + [HBM] * 6,
        out_specs=[HBM] * 8 + [VMEM] * 9,
        out_shape=[shape(160, 5120)]
        + [shape(160, width)] * 3
        + [shape(640, width), shape(160, width)]
        + [jax.ShapeDtypeStruct(rows.shape, BF16), shape(*grad.shape)]
        + [shape(size) for size in sizes],
        scratch_shapes=[pltpu.VMEM(array.shape, BF16) for array in arrays]
        + [
            pltpu.VMEM((160, 5120), F32),
            pltpu.VMEM((3, 160, width), F32),
            pltpu.VMEM((640, width), F32),
            pltpu.VMEM((160, width), F32),
            pltpu.VMEM(grad.shape, F32),
            pltpu.SemaphoreType.DMA((6,)),
            pltpu.SemaphoreType.DMA((8,)),
        ],
        compiler_params=pltpu.CompilerParams(vmem_limit_bytes=60 << 20),
    )(hb, vec, up, three, down, out, rows, grad)


def per_device(
    tokens,
    lengths,
    w_query,
    w_key,
    w_value,
    w_out,
    w_up,
    w_down,
    b_query,
    b_value,
    b_out,
    b_up,
    b_down,
    gain_attn,
    shift_attn,
    gain_ffn,
    shift_ffn,
    cotangent,
):
    rows, width = tokens.shape[1:]

    eight = [b_query, b_value, b_out, b_down, gain_attn, shift_attn, gain_ffn, shift_ffn]
    row = lax.broadcasted_iota(jnp.int32, (16, 160), 0)
    small = jnp.zeros((16, 160), BF16)
    for index, vector in enumerate(eight):
        small = jnp.where(row == index, vector[None, :], small)
    up_bias = jnp.broadcast_to(b_up[None, :], (16, 640))
    known = jnp.full((8, 128), lengths[0], F32)
    (
        h1,
        heads,
        probs,
        mixed,
        attended,
        w_qkv,
        smalls,
        up_bias,
        own,
        clip,
        out_full,
        up_mine,
        down_mine,
        top,
        _,
    ) = begin(
        tokens[0],
        w_query,
        w_key,
        w_value,
        small,
        up_bias,
        w_out,
        w_up,
        w_down,
        cotangent[0],
        known,
    )
    w_qkv = w_qkv.reshape(width, 480)
    (
        result,
        grad_middle,
        branch,
        out_sums,
        g_up,
        g_down,
        g_up_bias,
        g_vectors,
        grad_mixed,
    ) = middle_part(
        attended,
        own,
        smalls,
        up_bias,
        clip,
        out_full.reshape(width, width),
        up_mine.reshape(width, 640),
        down_mine,
        top.reshape(8 * rows, width),
    )
    hb_out, vec_out, output, input_grad, fin_up, fin_qkv, fin_down, fin_out, _ = finish(
        heads,
        mixed,
        grad_mixed,
        w_qkv,
        own,
        smalls,
        result,
        grad_middle,
        branch,
        out_sums,
        g_up_bias,
        g_vectors,
        probs,
        h1.reshape(8 * rows, width),
        g_up.reshape(8, 160, 640),
        g_down,
    )

    g_up, g_q, g_k, g_v, g_down, g_out, output, input_grad, *small = widen(
        hb_out, vec_out, fin_up, fin_qkv, fin_down, fin_out, output, input_grad
    )
    b_q, b_v, b_u, b_o, b_d, gain_two, shift_two, gain_one, shift_one = small
    return (
        output[None],
        input_grad[None],
        g_q,
        g_k,
        g_v,
        g_out,
        g_up,
        g_down,
        b_q,
        b_v,
        b_o,
        b_u,
        b_d,
        gain_one,
        shift_one,
        gain_two,
        shift_two,
    )


def solution(mesh):
    by_clip, matrix, vector = P("rep", "shard", None), P("shard", None), P("shard")
    return jax.shard_map(
        per_device,
        mesh=mesh,
        in_specs=(by_clip, P("rep")) + (matrix,) * 6 + (vector,) * 9 + (by_clip,),
        out_specs=(by_clip, by_clip) + (matrix,) * 6 + (vector,) * 9,
        check_vma=False,
    )
```
